32 devices in a mesh: dp: 16 (over z, x, core), fsdp: 2 (over y).
Axes of the slice: x: 2, y: 2, z: 4, core: 2. Of those that a mesh axis runs over, the one named last changes fastest.
Arguments:
- partials: bfloat16 [16, 3840, 1024], P('dp', None, 'fsdp'), may hold values from -16 to 16
- scales: float32 [16, 30, 1024], P('dp', None, 'fsdp'), may hold values from 0.25 to 4
Outputs:
- update: bfloat16 [3840, 1024], P('dp', 'fsdp')
The draws below stay inside these ranges and needn't reach their ends.
All inputs are finite; a program needn't handle non-finite values.
Results may differ from the reference program's by a relative error of at most 0.0004.
Values may be sent and summed in bfloat16 or wider, within the bound.
No kernel may reach another device: no remote copies, remote signals or barrier semaphores. Data moves between devices by JAX's collectives and lax.ppermute only.
A program may use at most 64 MiB of HBM per device.

```python
import math
import jax
import jax.numpy as jnp
from jax import lax

C = 3840
H = 1024
BLOCK = 128
REPLICAS = 16


def draw_partials(key, part):
    key = jax.random.fold_in(key, 17)
    keys = jax.random.split(key, 7)
    rank = min(256, H // 2)
    order = jnp.arange(1, rank + 1).astype(jnp.float32)
    spectrum = (1.0 + order / 12.0) ** (-1.5)
    spectrum = spectrum / jnp.sqrt(jnp.sum(spectrum * spectrum))
    left = jax.random.normal(keys[0], (C, rank), jnp.float32)
    right = jax.random.normal(keys[1], (H, rank), jnp.float32)
    spread = math.log(10.0)
    row_scale = jnp.exp(jax.random.uniform(keys[2], (C, 1), jnp.float32, -0.5, 0.5) * spread)
    col_scale = jnp.exp(jax.random.uniform(keys[3], (1, H), jnp.float32, -0.5, 0.5) * spread)
    common = jnp.dot(left * spectrum, right.T, precision=lax.Precision.HIGHEST, preferred_element_type=jnp.float32)
    common = common * row_scale * col_scale
    weights = jax.random.uniform(keys[4], (REPLICAS,), jnp.float32, 0.5, 1.5)
    paired = jax.random.permutation(keys[5], REPLICAS).astype(jnp.int32)
    row_block = (jnp.arange(C) // (C // REPLICAS)).astype(jnp.int32)
    share = 0.14

    def replica(index):
        sub = jax.random.fold_in(keys[6], index)
        noise = jax.random.normal(sub, (C, H), jnp.float32)
        boost = jnp.where(row_block == paired[index], 6.0, 1.0).astype(jnp.float32)[:, None]
        value = share * weights[index] * common + boost * noise
        return jnp.clip(value, -16.0, 16.0).astype(jnp.bfloat16)
    return lax.map(replica, jnp.arange(REPLICAS).astype(jnp.int32))


def shard_levels(stream_key, extent, cuts, low, high):
    factor_of, own = 1.0, jax.random.fold_in(stream_key, 6)
    for axis_at, blocks in cuts:
        draws = jnp.exp(jax.random.uniform(jax.random.fold_in(own, axis_at), (blocks,), jnp.float32, low / len(cuts), high / len(cuts)))
        factor_of = factor_of * jnp.repeat(draws, extent[axis_at] // blocks).reshape([-1 if axis == axis_at else 1 for axis in range(len(extent))])
    return factor_of


def setup_inputs(seed: int = 0) -> dict:
    splits = jax.random.split(jax.random.key(seed), 3)
    partials = draw_partials(jax.random.fold_in(splits[2], 71), 0)
    scales = jnp.clip(jnp.exp(math.log(4.0) - 2.7725887 * jax.random.uniform(splits[1], (REPLICAS, C // BLOCK, H), jnp.float32) ** shard_levels(splits[1], (REPLICAS, C // BLOCK, H), ((0, 16), (2, 2)), -0.2, 0.2)), 0.25, 4.0)
    return {"partials": partials, "scales": scales}


def reference(partials, scales):

    def add_one(total, pair):
        values, block_scales = pair
        full = jnp.repeat(block_scales, BLOCK, axis=0)
        return (total + values.astype(jnp.float32) * full, None)
    grad, _ = lax.scan(add_one, jnp.zeros((C, H), jnp.float32), (partials, scales))
    gram = jnp.dot(grad.T, grad, precision=lax.Precision.HIGHEST, preferred_element_type=jnp.float32)
    inv = 1.0 / (jnp.sqrt(jnp.trace(gram)) + 1e-07)
    scaled = gram * (inv * inv)
    poly = -4.775 * scaled + 2.0315 * jnp.dot(scaled, scaled, precision=lax.Precision.HIGHEST, preferred_element_type=jnp.float32)
    unit = grad * inv
    result = 3.4445 * unit + jnp.dot(unit, poly, precision=lax.Precision.HIGHEST, preferred_element_type=jnp.float32)
    return (0.25 * jnp.sqrt(jnp.float32(C * H)) * result).astype(jnp.bfloat16)
```

```python
import functools

import jax
import jax.numpy as jnp
import numpy as np
from jax import lax
from jax.experimental import pallas as pl
from jax.experimental.pallas import tpu as pltpu
from jax.sharding import PartitionSpec as P

BLOCK = 128
GRAIN = 16
CHUNKS = 1
PIECE = 256
F32 = jnp.float32
BF16 = jnp.bfloat16
VMEM = 48 * 1024 * 1024


def params():
    return pltpu.CompilerParams(vmem_limit_bytes=VMEM)


def split(value):
    high = value.astype(BF16)
    return high, (value - high.astype(F32)).astype(BF16)


def dot3(a, b, contract):
    dims = (contract, ((), ()))

    def one(u, v):
        return lax.dot_general(u, v, dims, preferred_element_type=F32)

    return one(a[0], b[0]) + (one(a[0], b[1]) + one(a[1], b[0]))


def dequant_kernel(inner_count, own_rows, start, at, values, *refs):
    raws, scales, out = refs[:3], refs[3:7], refs[7]
    step = pl.program_id(0)
    base = (step * inner_count + at[0]) * own_rows + start
    rows = out.shape[1]
    for g in range(rows // GRAIN):
        block = (base + g * GRAIN) // BLOCK
        here = slice(g * GRAIN, (g + 1) * GRAIN)
        total = values[0, here, :].astype(F32) * scales[0][pl.ds(block, 1), :]
        for raw, scale in zip(raws, scales[1:]):
            total += raw[0, here, :].astype(F32) * scale[pl.ds(block, 1), :]
        out[0, here, :] = total


def dequant(values, raws, scales, inner, inner_count, own_rows, start, rows):
    outer, width = raws[0].shape[0], raws[0].shape[2]
    per = own_rows // rows
    part = start // rows
    raw_spec = pl.BlockSpec((1, rows, width), lambda i, at: (i, 0, 0))
    scale_spec = pl.BlockSpec(scales[0].shape, lambda i, at: (0, 0))
    return pl.pallas_call(
        functools.partial(dequant_kernel, inner_count, own_rows, start),
        grid_spec=pltpu.PrefetchScalarGridSpec(
            num_scalar_prefetch=1,
            grid=(outer,),
            in_specs=[
                pl.BlockSpec(
                    (1, rows, width), lambda i, at: ((i * inner_count + at[0]) * per + part, 0, 0)
                )
            ]
            + [raw_spec] * 3
            + [scale_spec] * 4,
            out_specs=raw_spec,
        ),
        out_shape=jax.ShapeDtypeStruct((outer, rows, width), F32),
        compiler_params=params(),
        name="dequant_sum",
    )(inner[None], values.reshape(-1, rows, width), *raws, *scales)


def gram_kernel(at, *refs):
    slabs, out, high, low = refs[:4], refs[4], refs[5], refs[6]
    quarter, half = at[0], at[1]
    rows, share = slabs[0].shape
    for i, slab in enumerate(slabs):
        column = half if i % 2 == 0 else 1 - half
        lanes = pl.ds(pl.multiple_of(column * share, share), share)
        here = slice(i // 2 * rows, (i // 2 + 1) * rows)
        h, l = split(slab[...])
        high[here, lanes] = h
        low[here, lanes] = l

    def take(start, width):
        lanes = pl.ds(pl.multiple_of(start, 128), width)
        return high[:, lanes], low[:, lanes]

    contract = ((0,), (0,))
    own = take(quarter * PIECE, PIECE)
    out[0:PIECE, :] = dot3(own, own, contract)
    for k in range(1, 4):
        bit = lax.rem(lax.div(quarter, 1 if k == 1 else 2), 2)
        other = lax.bitwise_xor(quarter, k)
        left = jnp.where(bit == 0, quarter * PIECE, other * PIECE + PIECE // 2)
        right = jnp.where(bit == 0, other * PIECE, quarter * PIECE)
        row = PIECE + (k - 1) * (PIECE // 2)
        out[row : row + PIECE // 2, :] = dot3(take(left, PIECE // 2), take(right, PIECE), contract)


def gram_share(slabs, quarter, half):
    rows, share = slabs[0].shape
    whole = pl.BlockSpec(memory_space=pltpu.VMEM)
    return pl.pallas_call(
        gram_kernel,
        in_specs=[pl.BlockSpec(memory_space=pltpu.SMEM)] + [whole] * 4,
        out_specs=whole,
        out_shape=jax.ShapeDtypeStruct((PIECE + 3 * (PIECE // 2), PIECE), F32),
        scratch_shapes=[pltpu.VMEM((2 * rows, 2 * share), BF16)] * 2,
        compiler_params=params(),
        name="gram_share",
    )(jnp.stack([quarter, half]), *slabs)


def update_kernel(chips, scale, at, pieces, own, across, out, packed, gram, high, low):
    chip, quarter, half = at[0], at[1], at[2]
    part = pieces.shape[1]
    for q in range(4):
        for s in range(chips):
            slot = lax.bitwise_xor(quarter, q) * chips + lax.bitwise_xor(chip, s)
            packed[q, s * part : (s + 1) * part, :] = pieces[slot]
    trace = jnp.zeros((1, 1), F32)
    rows = lax.broadcasted_iota(jnp.int32, (PIECE, PIECE), 0)
    columns = lax.broadcasted_iota(jnp.int32, (PIECE, PIECE), 1)
    for q in range(4):
        block = packed[q, 0:PIECE, :]
        trace += jnp.sum(jnp.where(rows == columns, block, 0.0), keepdims=True)
        span = slice(q * PIECE, (q + 1) * PIECE)
        high[span, span], low[span, span] = split(block)
        for k in range(1, 4):
            other = q ^ k
            if q > other:
                continue
            row = PIECE + (k - 1) * (PIECE // 2)
            for first, owner in ((0, q), (PIECE // 2, other)):
                block = packed[owner, row : row + PIECE // 2, :]
                here = slice(q * PIECE + first, q * PIECE + first + PIECE // 2)
                there = slice(other * PIECE, (other + 1) * PIECE)
                high[here, there], low[here, there] = split(block)
                high[there, here], low[there, here] = split(block.T)
    inv = 1.0 / (jnp.sqrt(trace) + 1e-07)
    share = own.shape[1]
    contract = ((1,), (0,))

    def mine(which):
        return pl.ds(pl.multiple_of(which * share, share), share)

    unit = own[...] * inv
    far = across[...] * inv
    first = dot3(split(unit), (high[mine(half), :], low[mine(half), :]), contract)
    first += dot3(split(far), (high[mine(1 - half), :], low[mine(1 - half), :]), contract)
    first = first * (inv * inv)
    gram[...] = first
    second = dot3(split(first), (high[:, mine(half)], low[:, mine(half)]), contract)
    second = second * (inv * inv)
    result = 3.4445 * unit + (-4.775 * gram[:, mine(half)] + 2.0315 * second)
    out[...] = (scale * result).astype(out.dtype)


def update(pieces, own, across, chip, quarter, half, scale):
    rows, share = own.shape
    width = 2 * share
    whole = pl.BlockSpec(memory_space=pltpu.VMEM)
    chips = pieces.shape[0] // 4
    return pl.pallas_call(
        functools.partial(update_kernel, chips, scale),
        in_specs=[pl.BlockSpec(memory_space=pltpu.SMEM)] + [whole] * 3,
        out_specs=whole,
        out_shape=jax.ShapeDtypeStruct((rows, share), BF16),
        scratch_shapes=[
            pltpu.VMEM((4, chips * pieces.shape[1], pieces.shape[2]), F32),
            pltpu.VMEM((rows, width), F32),
            pltpu.VMEM((width, width), BF16),
            pltpu.VMEM((width, width), BF16),
        ],
        compiler_params=params(),
        name="update",
    )(jnp.stack([chip, quarter, half]), pieces, own, across)


def flip(value, axis, mask):
    count = lax.axis_size(axis)
    return lax.ppermute(value, axis, [(i, i ^ mask) for i in range(count)])


def pick(value, index):
    return lax.dynamic_index_in_dim(value, index, 0, keepdims=False)


def fast_body(partials, scales):
    values, scales = partials[0], scales[0]
    dp = lax.axis_size("dp")
    features, share = values.shape
    inner_count, outer = 4, dp // 4
    own_rows = features // dp
    rank = lax.axis_index("dp")
    half = lax.axis_index("fsdp")
    inner, zed = rank % inner_count, rank // inner_count
    core, chip = rank % 2, rank // 2
    quarter = 2 * half + core

    other_scales = [flip(scales, "dp", k) for k in range(1, 4)]
    parts = values.reshape(outer, inner_count, own_rows, share)
    rows = own_rows // CHUNKS
    owns, acrosses, own_cores, across_cores = [], [], [], []
    for chunk in range(CHUNKS):
        start = chunk * rows
        raws = []
        for k in range(1, 4):
            sent = lax.dynamic_slice(
                parts,
                (jnp.int32(0), lax.bitwise_xor(inner, k), jnp.int32(start), jnp.int32(0)),
                (outer, 1, rows, share),
            )
            raws.append(flip(sent.reshape(outer, rows, share), "dp", k))
        summed = dequant(
            values, raws, [scales] + other_scales, inner, inner_count, own_rows, start, rows
        )
        grad = pick(summed, zed)
        for k in range(1, outer):
            grad = grad + flip(pick(summed, lax.bitwise_xor(zed, k)), "dp", inner_count * k)
        across = flip(grad, "fsdp", 1)
        owns.append(grad)
        acrosses.append(across)
        own_cores.append(flip(grad, "dp", 1))
        across_cores.append(flip(across, "dp", 1))
    slabs = [jnp.concatenate(x, 0) for x in (owns, acrosses, own_cores, across_cores)]

    shared = gram_share(slabs, quarter, half)
    chips = dp // 2
    shared = shared.reshape(chips, -1, shared.shape[1])
    piece = pick(shared, chip)
    for k in range(1, chips):
        piece = piece + flip(pick(shared, lax.bitwise_xor(chip, k)), "dp", 2 * k)
    along = [piece] + [flip(piece, "dp", inner_count * k) for k in range(1, outer)]
    held = jnp.stack(along)
    held = jnp.stack([held, flip(held, "dp", 2)], 1).reshape(chips, *piece.shape)
    held = jnp.stack([held, flip(held, "dp", 1)])
    held = jnp.stack([held, flip(held, "fsdp", 1)])
    held = held.reshape(4 * chips, *piece.shape)
    scale = float(0.25 * np.sqrt(np.float32(features * 2 * share)))
    return update(held, slabs[0], slabs[1], chip, quarter, half, scale)


def plain_body(partials, scales):
    values, scales = partials[0], scales[0]
    features, share = values.shape
    dp = lax.axis_size("dp")
    rows = values.reshape(scales.shape[0], -1, share).astype(F32) * scales[:, None, :]
    summed = lax.psum_scatter(
        rows.reshape(features, share), "dp", scatter_dimension=0, tiled=True
    )
    slab = lax.all_gather(summed, "fsdp", axis=1, tiled=True)
    width = slab.shape[1]
    highest = functools.partial(
        jnp.dot, precision=lax.Precision.HIGHEST, preferred_element_type=F32
    )
    half = lax.axis_index("fsdp")
    gram = lax.psum(highest(summed.T, slab), "dp")
    gram = lax.all_gather(gram, "fsdp", axis=0, tiled=True)
    inv = 1.0 / (jnp.sqrt(jnp.trace(gram)) + 1e-07)
    scaled = gram * (inv * inv)
    first = highest(slab * inv, scaled)
    mine = lambda value: lax.dynamic_slice_in_dim(value, half * share, share, 1)
    second = highest(first, mine(scaled))
    result = 3.4445 * (summed * inv) + (-4.775 * mine(first) + 2.0315 * second)
    return (0.25 * jnp.sqrt(F32(features * width)) * result).astype(BF16)


def solution(mesh):
    dp, fsdp = mesh.shape["dp"], mesh.shape["fsdp"]

    def run(partials, scales):
        features, width = partials.shape[1:]
        fast = (
            fsdp == 2
            and dp >= 4
            and dp & (dp - 1) == 0
            and features % (dp * GRAIN) == 0
            and width == 4 * PIECE
            and (PIECE + 3 * (PIECE // 2)) % (8 * dp // 2) == 0
        )
        return jax.shard_map(
            fast_body if fast else plain_body,
            mesh=mesh,
            in_specs=(P("dp", None, "fsdp"), P("dp", None, "fsdp")),
            out_specs=P("dp", "fsdp"),
            check_vma=False,
        )(partials, scales)

    return run
```

```python
import functools

import jax
import jax.numpy as jnp
import numpy as np
from jax import lax
from jax.experimental import pallas as pl
from jax.experimental.pallas import tpu as pltpu
from jax.sharding import PartitionSpec as P

BLOCK = 128
GRAIN = 16
CHUNKS = 3
PIECE = 256
F32 = jnp.float32
BF16 = jnp.bfloat16
VMEM = 48 * 1024 * 1024


def params():
    return pltpu.CompilerParams(vmem_limit_bytes=VMEM)


def split(value):
    high = value.astype(BF16)
    return high, (value - high.astype(F32)).astype(BF16)


def dot3(a, b, contract):
    dims = (contract, ((), ()))

    def one(u, v):
        return lax.dot_general(u, v, dims, preferred_element_type=F32)

    return one(a[0], b[0]) + (one(a[0], b[1]) + one(a[1], b[0]))


def dequant_kernel(inner_count, own_rows, start, at, values, *refs):
    raws, scales, out = refs[:3], refs[3:7], refs[7]
    step = pl.program_id(0)
    base = (step * inner_count + at[0]) * own_rows + start
    rows = out.shape[1]
    for g in range(rows // GRAIN):
        block = (base + g * GRAIN) // BLOCK
        here = slice(g * GRAIN, (g + 1) * GRAIN)
        total = values[0, here, :].astype(F32) * scales[0][pl.ds(block, 1), :]
        for raw, scale in zip(raws, scales[1:]):
            total += raw[0, here, :].astype(F32) * scale[pl.ds(block, 1), :]
        out[0, here, :] = total


def dequant(values, raws, scales, inner, inner_count, own_rows, start, rows):
    outer, width = raws[0].shape[0], raws[0].shape[2]
    per = own_rows // rows
    part = start // rows
    raw_spec = pl.BlockSpec((1, rows, width), lambda i, at: (i, 0, 0))
    scale_spec = pl.BlockSpec(scales[0].shape, lambda i, at: (0, 0))
    return pl.pallas_call(
        functools.partial(dequant_kernel, inner_count, own_rows, start),
        grid_spec=pltpu.PrefetchScalarGridSpec(
            num_scalar_prefetch=1,
            grid=(outer,),
            in_specs=[
                pl.BlockSpec(
                    (1, rows, width), lambda i, at: ((i * inner_count + at[0]) * per + part, 0, 0)
                )
            ]
            + [raw_spec] * 3
            + [scale_spec] * 4,
            out_specs=raw_spec,
        ),
        out_shape=jax.ShapeDtypeStruct((outer, rows, width), F32),
        compiler_params=params(),
        name="dequant_sum",
    )(inner[None], values.reshape(-1, rows, width), *raws, *scales)


def gram_kernel(at, *refs):
    slabs, out, high, low = refs[:4], refs[4], refs[5], refs[6]
    quarter, half = at[0], at[1]
    rows, share = slabs[0].shape
    for i, slab in enumerate(slabs):
        column = half if i % 2 == 0 else 1 - half
        lanes = pl.ds(pl.multiple_of(column * share, share), share)
        here = slice(i // 2 * rows, (i // 2 + 1) * rows)
        h, l = split(slab[...])
        high[here, lanes] = h
        low[here, lanes] = l

    def take(start, width):
        lanes = pl.ds(pl.multiple_of(start, 128), width)
        return high[:, lanes], low[:, lanes]

    contract = ((0,), (0,))
    own = take(quarter * PIECE, PIECE)
    out[0:PIECE, :] = dot3(own, own, contract)
    for k in range(1, 4):
        bit = lax.rem(lax.div(quarter, 1 if k == 1 else 2), 2)
        other = lax.bitwise_xor(quarter, k)
        left = jnp.where(bit == 0, quarter * PIECE, other * PIECE + PIECE // 2)
        right = jnp.where(bit == 0, other * PIECE, quarter * PIECE)
        row = PIECE + (k - 1) * (PIECE // 2)
        out[row : row + PIECE // 2, :] = dot3(take(left, PIECE // 2), take(right, PIECE), contract)


def gram_share(slabs, quarter, half):
    rows, share = slabs[0].shape
    whole = pl.BlockSpec(memory_space=pltpu.VMEM)
    return pl.pallas_call(
        gram_kernel,
        in_specs=[pl.BlockSpec(memory_space=pltpu.SMEM)] + [whole] * 4,
        out_specs=whole,
        out_shape=jax.ShapeDtypeStruct((PIECE + 3 * (PIECE // 2), PIECE), F32),
        scratch_shapes=[pltpu.VMEM((2 * rows, 2 * share), BF16)] * 2,
        compiler_params=params(),
        name="gram_share",
    )(jnp.stack([quarter, half]), *slabs)


def update_kernel(chips, scale, at, pieces, own, across, out, packed, gram, high, low):
    chip, quarter, half = at[0], at[1], at[2]
    part = pieces.shape[1]
    for q in range(4):
        for s in range(chips):
            slot = lax.bitwise_xor(quarter, q) * chips + lax.bitwise_xor(chip, s)
            packed[q, s * part : (s + 1) * part, :] = pieces[slot]
    trace = jnp.zeros((1, 1), F32)
    rows = lax.broadcasted_iota(jnp.int32, (PIECE, PIECE), 0)
    columns = lax.broadcasted_iota(jnp.int32, (PIECE, PIECE), 1)
    for q in range(4):
        block = packed[q, 0:PIECE, :]
        trace += jnp.sum(jnp.where(rows == columns, block, 0.0), keepdims=True)
        span = slice(q * PIECE, (q + 1) * PIECE)
        high[span, span], low[span, span] = split(block)
        for k in range(1, 4):
            other = q ^ k
            if q > other:
                continue
            row = PIECE + (k - 1) * (PIECE // 2)
            for first, owner in ((0, q), (PIECE // 2, other)):
                block = packed[owner, row : row + PIECE // 2, :]
                here = slice(q * PIECE + first, q * PIECE + first + PIECE // 2)
                there = slice(other * PIECE, (other + 1) * PIECE)
                high[here, there], low[here, there] = split(block)
                high[there, here], low[there, here] = split(block.T)
    inv = 1.0 / (jnp.sqrt(trace) + 1e-07)
    share = own.shape[1]
    contract = ((1,), (0,))

    def mine(which):
        return pl.ds(pl.multiple_of(which * share, share), share)

    unit = own[...] * inv
    far = across[...] * inv
    first = dot3(split(unit), (high[mine(half), :], low[mine(half), :]), contract)
    first += dot3(split(far), (high[mine(1 - half), :], low[mine(1 - half), :]), contract)
    first = first * (inv * inv)
    gram[...] = first
    second = dot3(split(first), (high[:, mine(half)], low[:, mine(half)]), contract)
    second = second * (inv * inv)
    result = 3.4445 * unit + (-4.775 * gram[:, mine(half)] + 2.0315 * second)
    out[...] = (scale * result).astype(out.dtype)


def update(pieces, own, across, chip, quarter, half, scale):
    rows, share = own.shape
    width = 2 * share
    whole = pl.BlockSpec(memory_space=pltpu.VMEM)
    chips = pieces.shape[0] // 4
    return pl.pallas_call(
        functools.partial(update_kernel, chips, scale),
        in_specs=[pl.BlockSpec(memory_space=pltpu.SMEM)] + [whole] * 3,
        out_specs=whole,
        out_shape=jax.ShapeDtypeStruct((rows, share), BF16),
        scratch_shapes=[
            pltpu.VMEM((4, chips * pieces.shape[1], pieces.shape[2]), F32),
            pltpu.VMEM((rows, width), F32),
            pltpu.VMEM((width, width), BF16),
            pltpu.VMEM((width, width), BF16),
        ],
        compiler_params=params(),
        name="update",
    )(jnp.stack([chip, quarter, half]), pieces, own, across)


def flip(value, axis, mask):
    count = lax.axis_size(axis)
    return lax.ppermute(value, axis, [(i, i ^ mask) for i in range(count)])


def pick(value, index):
    return lax.dynamic_index_in_dim(value, index, 0, keepdims=False)


def fast_body(partials, scales):
    values, scales = partials[0], scales[0]
    dp = lax.axis_size("dp")
    features, share = values.shape
    inner_count, outer = 4, dp // 4
    own_rows = features // dp
    rank = lax.axis_index("dp")
    half = lax.axis_index("fsdp")
    inner, zed = rank % inner_count, rank // inner_count
    core, chip = rank % 2, rank // 2
    quarter = 2 * half + core

    other_scales = [flip(scales, "dp", k) for k in range(1, 4)]
    parts = values.reshape(outer, inner_count, own_rows, share)
    rows = own_rows // CHUNKS
    owns, acrosses, own_cores, across_cores = [], [], [], []
    for chunk in range(CHUNKS):
        start = chunk * rows
        raws = []
        for k in range(1, 4):
            sent = lax.dynamic_slice(
                parts,
                (jnp.int32(0), lax.bitwise_xor(inner, k), jnp.int32(start), jnp.int32(0)),
                (outer, 1, rows, share),
            )
            raws.append(flip(sent.reshape(outer, rows, share), "dp", k))
        summed = dequant(
            values, raws, [scales] + other_scales, inner, inner_count, own_rows, start, rows
        )
        grad = pick(summed, zed)
        for k in range(1, outer):
            grad = grad + flip(pick(summed, lax.bitwise_xor(zed, k)), "dp", inner_count * k)
        across = flip(grad, "fsdp", 1)
        owns.append(grad)
        acrosses.append(across)
        own_cores.append(flip(grad, "dp", 1))
        across_cores.append(flip(across, "dp", 1))
    slabs = [jnp.concatenate(x, 0) for x in (owns, acrosses, own_cores, across_cores)]

    shared = gram_share(slabs, quarter, half)
    chips = dp // 2
    shared = shared.reshape(chips, -1, shared.shape[1])
    piece = pick(shared, chip)
    for k in range(1, chips):
        piece = piece + flip(pick(shared, lax.bitwise_xor(chip, k)), "dp", 2 * k)
    along = [piece] + [flip(piece, "dp", inner_count * k) for k in range(1, outer)]
    held = jnp.stack(along)
    held = jnp.stack([held, flip(held, "dp", 2)], 1).reshape(chips, *piece.shape)
    held = jnp.stack([held, flip(held, "fsdp", 1)])
    held = jnp.stack([held, flip(held, "dp", 1)], 1)
    held = held.reshape(4 * chips, *piece.shape)
    scale = float(0.25 * np.sqrt(np.float32(features * 2 * share)))
    return update(held, slabs[0], slabs[1], chip, quarter, half, scale)


def plain_body(partials, scales):
    values, scales = partials[0], scales[0]
    features, share = values.shape
    dp = lax.axis_size("dp")
    rows = values.reshape(scales.shape[0], -1, share).astype(F32) * scales[:, None, :]
    summed = lax.psum_scatter(
        rows.reshape(features, share), "dp", scatter_dimension=0, tiled=True
    )
    slab = lax.all_gather(summed, "fsdp", axis=1, tiled=True)
    width = slab.shape[1]
    highest = functools.partial(
        jnp.dot, precision=lax.Precision.HIGHEST, preferred_element_type=F32
    )
    half = lax.axis_index("fsdp")
    gram = lax.psum(highest(summed.T, slab), "dp")
    gram = lax.all_gather(gram, "fsdp", axis=0, tiled=True)
    inv = 1.0 / (jnp.sqrt(jnp.trace(gram)) + 1e-07)
    scaled = gram * (inv * inv)
    first = highest(slab * inv, scaled)
    mine = lambda value: lax.dynamic_slice_in_dim(value, half * share, share, 1)
    second = highest(first, mine(scaled))
    result = 3.4445 * (summed * inv) + (-4.775 * mine(first) + 2.0315 * second)
    return (0.25 * jnp.sqrt(F32(features * width)) * result).astype(BF16)


def solution(mesh):
    dp, fsdp = mesh.shape["dp"], mesh.shape["fsdp"]

    def run(partials, scales):
        features, width = partials.shape[1:]
        fast = (
            fsdp == 2
            and dp >= 4
            and dp & (dp - 1) == 0
            and features % (dp * GRAIN) == 0
            and width == 4 * PIECE
            and (PIECE + 3 * (PIECE // 2)) % (8 * dp // 2) == 0
        )
        return jax.shard_map(
            fast_body if fast else plain_body,
            mesh=mesh,
            in_specs=(P("dp", None, "fsdp"), P("dp", None, "fsdp")),
            out_specs=P("dp", "fsdp"),
            check_vma=False,
        )(partials, scales)

    return run
```

```python
import functools

import jax
import jax.numpy as jnp
import numpy as np
from jax import lax
from jax.experimental import pallas as pl
from jax.experimental.pallas import tpu as pltpu
from jax.sharding import PartitionSpec as P

BLOCK = 128
GRAIN = 16
CHUNKS = (2, 2, 1)
ORDER = (0, 2, 1, 3)
PIECE = 256
HALF = PIECE // 2
PACKED = HALF + HALF // 2 + 3 * HALF
F32 = jnp.float32
BF16 = jnp.bfloat16
VMEM = 48 * 1024 * 1024
WHOLE = pl.BlockSpec(memory_space=pltpu.VMEM)
SCALARS = pl.BlockSpec(memory_space=pltpu.SMEM)
ANYWHERE = pl.BlockSpec(memory_space=pl.ANY)


def params():
    return pltpu.CompilerParams(vmem_limit_bytes=VMEM)


def split(value):
    high = value.astype(BF16)
    return high, (value - high.astype(F32)).astype(BF16)


def dot3(a, b, contract):
    dims = (contract, ((), ()))

    def one(u, v):
        return lax.dot_general(u, v, dims, preferred_element_type=F32)

    return one(a[0], b[0]) + (one(a[0], b[1]) + one(a[1], b[0]))


def slot_row(at, side, slot, own_rows):
    zed, ex, core = at[0], at[1], at[2]
    z = lax.bitwise_xor(zed, ORDER[slot % 4])
    c = lax.bitwise_xor(core, slot // 4)
    x = lax.bitwise_xor(ex, side)
    return ((z * 2 + x) * 2 + c) * own_rows


def pack_kernel(side, own_rows, spans, after, at, values, *refs):
    outs, sem = refs[after:-1], refs[-1]
    copies = []
    for n, (start, rows) in enumerate(spans):
        for slot in range(8):
            base = pl.multiple_of(slot_row(at, side, slot, own_rows) + start, GRAIN)
            copy = pltpu.make_async_copy(
                values.at[pl.ds(base, rows), :], outs[n].at[slot], sem.at[n, slot]
            )
            copy.start()
            copies.append(copy)
    for copy in copies:
        copy.wait()


def pack(values, at, side, own_rows, spans, after):
    width = values.shape[1]
    return pl.pallas_call(
        functools.partial(pack_kernel, side, own_rows, spans, len(after)),
        in_specs=[SCALARS] + [ANYWHERE] * (1 + len(after)),
        out_specs=[ANYWHERE] * len(spans),
        out_shape=[jax.ShapeDtypeStruct((8, rows, width), BF16) for _, rows in spans],
        scratch_shapes=[pltpu.SemaphoreType.DMA((len(spans), 8))],
        compiler_params=params(),
        name="pack_rows",
    )(at, values, *after)


def dequant_kernel(own_rows, start, at, own, raw, scales, far_scales, *refs):
    keep, send = refs[-2:]
    rows = own.shape[1]
    for slot in range(8):
        base = slot_row(at, 0, slot, own_rows) + start
        out = keep if slot < 4 else send
        for g in range(rows // GRAIN):
            block = pl.ds((base + g * GRAIN) // BLOCK, 1)
            here = slice(g * GRAIN, (g + 1) * GRAIN)
            out[slot % 4, here, :] = (
                own[slot, here, :].astype(F32) * scales[block, :]
                + raw[slot, here, :].astype(F32) * far_scales[block, :]
            )


def dequant(at, own, raw, scales, far_scales, own_rows, start, after):
    _, rows, width = own.shape
    return pl.pallas_call(
        functools.partial(dequant_kernel, own_rows, start),
        in_specs=[SCALARS] + [WHOLE] * 4 + [ANYWHERE] * len(after),
        out_specs=[WHOLE] * 2,
        out_shape=[jax.ShapeDtypeStruct((4, rows, width), F32)] * 2,
        compiler_params=params(),
        name="dequant_sum",
    )(at, own, raw, scales, far_scales, *after)


def gram_kernel(count, at, *refs):
    slabs, (out, high, low, flat) = refs[: 4 * count], refs[4 * count :]
    zed, ex, half = at[0], at[1], at[3]
    quarter = 2 * half + at[2]
    share = slabs[0].shape[1]
    row = 0
    for i, slab in enumerate(slabs):
        column = half if i % 2 == 0 else 1 - half
        lanes = pl.ds(pl.multiple_of(column * share, share), share)
        here = slice(row, row + slab.shape[0])
        h, l = split(slab[...])
        high[here, lanes] = h
        low[here, lanes] = l
        row += slab.shape[0] if i % 2 == 1 else 0

    def take(start, width):
        lanes = pl.ds(pl.multiple_of(start, HALF), width)
        return high[:, lanes], low[:, lanes]

    contract = ((0,), (0,))
    own = take(quarter * PIECE, PIECE)
    block = dot3(own, own, contract)
    flat[0:HALF, :] = block[0:HALF, :]
    flat[HALF : HALF + HALF // 2, 0:HALF] = block[HALF : HALF + HALF // 2, HALF:]
    flat[HALF : HALF + HALF // 2, HALF:] = block[HALF + HALF // 2 :, HALF:]
    for k in range(1, 4):
        bit = lax.rem(lax.div(quarter, 1 if k == 1 else 2), 2)
        other = lax.bitwise_xor(quarter, k)
        left = jnp.where(bit == 0, quarter * PIECE, other * PIECE + HALF)
        right = jnp.where(bit == 0, other * PIECE, quarter * PIECE)
        row = PACKED + (k - 4) * HALF
        flat[row : row + HALF, :] = dot3(take(left, HALF), take(right, PIECE), contract)
    part = out.shape[1]
    for slot in range(8):
        z = lax.bitwise_xor(zed, ORDER[slot % 4])
        x = lax.bitwise_xor(ex, slot // 4)
        base = pl.multiple_of((z * 2 + x) * part, 8)
        out[slot] = flat[pl.ds(base, part), :]


def gram_share(at, slabs):
    rows = sum(slab.shape[0] for slab in slabs) // 2
    width = 2 * slabs[0].shape[1]
    return pl.pallas_call(
        functools.partial(gram_kernel, len(slabs) // 4),
        in_specs=[SCALARS] + [WHOLE] * len(slabs),
        out_specs=WHOLE,
        out_shape=jax.ShapeDtypeStruct((8, PACKED // 8, PIECE), F32),
        scratch_shapes=[pltpu.VMEM((rows, width), BF16)] * 2 + [pltpu.VMEM((PACKED, PIECE), F32)],
        compiler_params=params(),
        name="gram_share",
    )(at, *slabs)


def update_kernel(scale, places, count, at, *refs):
    pieces, refs = refs[: len(places)], refs[len(places) :]
    owns, acrosses, refs = refs[:count], refs[count : 2 * count], refs[2 * count :]
    out, packed, gram, high, low = refs
    zed, ex, core, half = at[0], at[1], at[2], at[3]
    part = pieces[0].shape[1]
    for ref, slots in zip(pieces, places):
        for n, (kz, kx, kc, kf) in enumerate(slots):
            quarter = 2 * lax.bitwise_xor(half, kf) + lax.bitwise_xor(core, kc)
            chip = 2 * lax.bitwise_xor(zed, kz) + lax.bitwise_xor(ex, kx)
            row = pl.multiple_of(quarter * PACKED + chip * part, 8)
            packed[pl.ds(row, part), :] = ref[n]
    trace = jnp.zeros((1, 1), F32)
    rows = lax.broadcasted_iota(jnp.int32, (HALF, HALF), 0)
    columns = lax.broadcasted_iota(jnp.int32, (HALF, HALF), 1)

    def put(block, row, column):
        h, l = split(block)
        here = (slice(row, row + block.shape[0]), slice(column, column + block.shape[1]))
        high[here] = h
        low[here] = l

    for q in range(4):
        base, edge = q * PACKED, q * PIECE
        top = packed[base : base + HALF, :]
        bottom = packed[base + HALF : base + HALF + HALF // 2, :]
        bottom = jnp.concatenate([bottom[:, :HALF], bottom[:, HALF:]], 0)
        for block in (top[:, :HALF], bottom):
            trace += jnp.sum(jnp.where(rows == columns, block, 0.0), keepdims=True)
        put(top, edge, edge)
        put(top[:, HALF:].T, edge + HALF, edge)
        put(bottom, edge + HALF, edge + HALF)
        for k in range(1, 4):
            other = q ^ k
            if q > other:
                continue
            row = PACKED + (k - 4) * HALF
            for first, owner in ((0, q), (HALF, other)):
                block = packed[owner * PACKED + row : owner * PACKED + row + HALF, :]
                put(block, edge + first, other * PIECE)
                put(block.T, other * PIECE, edge + first)
    inv = 1.0 / (jnp.sqrt(trace) + 1e-07)
    share = owns[0].shape[1]
    contract = ((1,), (0,))

    def mine(which):
        return pl.ds(pl.multiple_of(which * share, share), share)

    unit = jnp.concatenate([own[...] for own in owns], 0) * inv
    far = jnp.concatenate([across[...] for across in acrosses], 0) * inv
    first = dot3(split(unit), (high[mine(half), :], low[mine(half), :]), contract)
    first += dot3(split(far), (high[mine(1 - half), :], low[mine(1 - half), :]), contract)
    first = first * (inv * inv)
    gram[...] = first
    second = dot3(split(first), (high[:, mine(half)], low[:, mine(half)]), contract)
    second = second * (inv * inv)
    result = 3.4445 * unit + (-4.775 * gram[:, mine(half)] + 2.0315 * second)
    out[...] = (scale * result).astype(out.dtype)


def update(at, pieces, places, owns, acrosses, scale):
    rows = sum(own.shape[0] for own in owns)
    share = owns[0].shape[1]
    width = 2 * share
    return pl.pallas_call(
        functools.partial(update_kernel, scale, places, len(owns)),
        in_specs=[SCALARS] + [WHOLE] * (len(pieces) + 2 * len(owns)),
        out_specs=WHOLE,
        out_shape=jax.ShapeDtypeStruct((rows, share), BF16),
        scratch_shapes=[
            pltpu.VMEM((4 * PACKED, PIECE), F32),
            pltpu.VMEM((rows, width), F32),
            pltpu.VMEM((width, width), BF16),
            pltpu.VMEM((width, width), BF16),
        ],
        compiler_params=params(),
        name="update",
    )(at, *pieces, *owns, *acrosses)


AXIS_BITS = {"f": 1, "c": 2, "x": 4, "z1": 8, "z2": 16}


def flip(value, *names):
    mask = sum(AXIS_BITS[name] for name in names)
    count = lax.axis_size(("dp", "fsdp"))
    return lax.ppermute(value, ("dp", "fsdp"), [(i, i ^ mask) for i in range(count)])


def fast_body(partials, scales):
    values, scales = partials[0], scales[0]
    features, share = values.shape
    own_rows = features // lax.axis_size("dp")
    rank = lax.axis_index("dp")
    at = jnp.stack([rank // 4, rank // 2 % 2, rank % 2, lax.axis_index("fsdp")])
    unit = own_rows // sum(CHUNKS)
    spans, start = [], 0
    for size in CHUNKS:
        spans.append((start, size * unit))
        start += size * unit

    far_scales = flip(scales, "x")
    raws = [flip(sent, "x") for sent in pack(values, at, 1, own_rows, spans, [scales])]
    kept = pack(values, at, 0, own_rows, spans, [])
    after, later = [], []
    owns, acrosses, slabs = [], [], []
    for (start, rows), own, raw in zip(spans, kept, raws):
        keep, send = dequant(at, own, raw, scales, far_scales, own_rows, start, after)
        got = flip(send, "c")
        sent = keep[2:] + got[2:]
        after, later = later + [sent], []
        got_z = flip(sent, "z1")
        sent = keep[1] + got[1] + got_z[1]
        later.append(sent)
        last = flip(sent, "z2")
        grad = (keep[0] + got[0] + got_z[0]) + last
        across = flip(grad, "f")
        owns.append(grad)
        acrosses.append(across)
        slabs += [grad, across, flip(grad, "c"), flip(grad, "c", "f")]

    shared = gram_share(at, slabs)
    got = shared[:4] + flip(shared[4:], "x")
    got = got[:2] + flip(got[2:], "z1")
    piece = got[:1] + flip(got[1:], "z2")

    pair = jnp.concatenate([piece, flip(piece, "z2")])
    other = flip(pair, "z1")
    a, b = pair, other
    ax, bf = flip(a, "x"), flip(b, "f")
    near = jnp.concatenate([a, ax])
    far = jnp.concatenate([b, bf])
    near_f, far_x = flip(near, "f"), flip(far, "x")
    parts = [near, far, near_f, far_x]
    z_pair, z_other = ((0, 0), (2, 0)), ((1, 0), (3, 0))

    def places(zeds, first, second):
        return [(z, x, 0, f) for x, f in (first, second) for z, _ in zeds]

    slots = [
        places(z_pair, (0, 0), (1, 0)),
        places(z_other, (0, 0), (0, 1)),
        places(z_pair, (0, 1), (1, 1)),
        places(z_other, (1, 0), (1, 1)),
    ]
    parts += [flip(part, "c") for part in parts]
    slots += [[(z, x, 1, f) for z, x, _, f in group] for group in slots]
    scale = float(0.25 * np.sqrt(np.float32(features * 2 * share)))
    return update(at, parts, slots, owns, acrosses, scale)


def plain_body(partials, scales):
    values, scales = partials[0], scales[0]
    features, share = values.shape
    dp = lax.axis_size("dp")
    rows = values.reshape(scales.shape[0], -1, share).astype(F32) * scales[:, None, :]
    summed = lax.psum_scatter(
        rows.reshape(features, share), "dp", scatter_dimension=0, tiled=True
    )
    slab = lax.all_gather(summed, "fsdp", axis=1, tiled=True)
    width = slab.shape[1]
    highest = functools.partial(
        jnp.dot, precision=lax.Precision.HIGHEST, preferred_element_type=F32
    )
    half = lax.axis_index("fsdp")
    gram = lax.psum(highest(summed.T, slab), "dp")
    gram = lax.all_gather(gram, "fsdp", axis=0, tiled=True)
    inv = 1.0 / (jnp.sqrt(jnp.trace(gram)) + 1e-07)
    scaled = gram * (inv * inv)
    first = highest(slab * inv, scaled)
    mine = lambda value: lax.dynamic_slice_in_dim(value, half * share, share, 1)
    second = highest(first, mine(scaled))
    result = 3.4445 * (summed * inv) + (-4.775 * mine(first) + 2.0315 * second)
    return (0.25 * jnp.sqrt(F32(features * width)) * result).astype(BF16)


def solution(mesh):
    dp, fsdp = mesh.shape["dp"], mesh.shape["fsdp"]

    def run(partials, scales):
        features, width = partials.shape[1:]
        fast = (
            (dp, fsdp) == (16, 2)
            and features % (dp * GRAIN * sum(CHUNKS)) == 0
            and width == 4 * PIECE
        )
        return jax.shard_map(
            fast_body if fast else plain_body,
            mesh=mesh,
            in_specs=(P("dp", None, "fsdp"), P("dp", None, "fsdp")),
            out_specs=P("dp", "fsdp"),
            check_vma=False,
        )(partials, scales)

    return run
```

```python
import functools

import jax
import jax.numpy as jnp
import numpy as np
from jax import lax
from jax.experimental import pallas as pl
from jax.experimental.pallas import tpu as pltpu
from jax.sharding import PartitionSpec as P

BLOCK = 128
GRAIN = 16
CHUNKS = (2, 2, 1)
ORDER = (0, 2, 1, 3)
PIECE = 256
HALF = PIECE // 2
PACKED = HALF + HALF // 2 + 3 * HALF
F32 = jnp.float32
BF16 = jnp.bfloat16
VMEM = 48 * 1024 * 1024
WHOLE = pl.BlockSpec(memory_space=pltpu.VMEM)
SCALARS = pl.BlockSpec(memory_space=pltpu.SMEM)
ANYWHERE = pl.BlockSpec(memory_space=pl.ANY)


def params():
    return pltpu.CompilerParams(vmem_limit_bytes=VMEM)


def split(value):
    high = value.astype(BF16)
    return high, (value - high.astype(F32)).astype(BF16)


def dot3(a, b, contract):
    dims = (contract, ((), ()))

    def one(u, v):
        return lax.dot_general(u, v, dims, preferred_element_type=F32)

    return one(a[0], b[0]) + (one(a[0], b[1]) + one(a[1], b[0]))


def slot_row(at, side, slot, own_rows):
    zed, ex, core = at[0], at[1], at[2]
    z = lax.bitwise_xor(zed, ORDER[slot])
    c = lax.bitwise_xor(core, side % 2)
    x = lax.bitwise_xor(ex, side // 2)
    return ((z * 2 + x) * 2 + c) * own_rows


SLOTS = len(ORDER)
SPAN = 4


def pack_kernel(own_rows, spans, at, values, scales, core_out, *outs):
    blocks = scales.shape[0]
    for side in range(1, 4):
        for slot in range(SLOTS):
            base = slot_row(at, side, slot, own_rows)
            first = base // BLOCK
            for n in range(SPAN):
                row = pl.ds(jnp.minimum(first + n, blocks - 1), 1)
                outs[side - 1][slot * SPAN + n : slot * SPAN + n + 1, :] = scales[row, :]
    for slot in range(SLOTS):
        base = pl.multiple_of(slot_row(at, 1, slot, own_rows), GRAIN)
        core_out[slot] = values[pl.ds(base, own_rows), :]
    for n, (start, rows) in enumerate(spans):
        for side in (2, 3):
            for slot in range(SLOTS):
                base = pl.multiple_of(slot_row(at, side, slot, own_rows) + start, GRAIN)
                outs[3 + 2 * n + side - 2][slot] = values[pl.ds(base, rows), :]


def pack(values, scales, at, own_rows, spans):
    width = values.shape[1]
    shapes = [jax.ShapeDtypeStruct((SLOTS, own_rows, width), BF16)]
    shapes += [jax.ShapeDtypeStruct((SLOTS * SPAN, width), F32)] * 3
    for _, rows in spans:
        shapes += [jax.ShapeDtypeStruct((SLOTS, rows, width), BF16)] * 2
    return pl.pallas_call(
        functools.partial(pack_kernel, own_rows, spans),
        in_specs=[SCALARS, WHOLE, WHOLE],
        out_specs=[WHOLE] * len(shapes),
        out_shape=shapes,
        compiler_params=params(),
        name="pack_rows",
    )(at, values, scales)


def dequant_kernel(own_rows, start, at, values, scales, core_raw, *refs):
    raws, packed, outs = refs[:2], refs[2:5], refs[-3:]
    rows = raws[0].shape[1]
    for slot in range(SLOTS):
        base = slot_row(at, 0, slot, own_rows)
        for g in range(rows // GRAIN):
            row = base + (start + g * GRAIN)
            block = row // BLOCK
            near = pl.ds(block, 1)
            span = pl.ds(slot * SPAN + block - base // BLOCK, 1)
            here = slice(g * GRAIN, (g + 1) * GRAIN)
            there = pl.ds(pl.multiple_of(row, GRAIN), GRAIN)
            total = values[there, :].astype(F32) * scales[near, :]
            after = slice(start + g * GRAIN, start + (g + 1) * GRAIN)
            total += core_raw[slot, after, :].astype(F32) * packed[0][span, :]
            for raw, scale in zip(raws, packed[1:]):
                total += raw[slot, here, :].astype(F32) * scale[span, :]
            if slot < 2:
                outs[0][slot, here, :] = total
            else:
                outs[slot - 1][here, :] = total


def dequant(at, values, scales, core_raw, raws, packed, own_rows, start, after):
    _, rows, width = raws[0].shape
    part = jax.ShapeDtypeStruct((rows, width), F32)
    return pl.pallas_call(
        functools.partial(dequant_kernel, own_rows, start),
        in_specs=[SCALARS] + [WHOLE] * 8 + [ANYWHERE] * len(after),
        out_specs=[WHOLE] * 3,
        out_shape=[jax.ShapeDtypeStruct((2, rows, width), F32), part, part],
        compiler_params=params(),
        name="dequant_sum",
    )(at, values, scales, core_raw, *raws, *packed, *after)


def gram_kernel(count, at, *refs):
    slabs, (out, high, low, flat) = refs[: 4 * count], refs[4 * count :]
    zed, ex, half = at[0], at[1], at[3]
    quarter = 2 * half + at[2]
    share = slabs[0].shape[1]
    row = 0
    for i, slab in enumerate(slabs):
        column = half if i % 2 == 0 else 1 - half
        lanes = pl.ds(pl.multiple_of(column * share, share), share)
        here = slice(row, row + slab.shape[0])
        h, l = split(slab[...])
        high[here, lanes] = h
        low[here, lanes] = l
        row += slab.shape[0] if i % 2 == 1 else 0

    def take(start, width):
        lanes = pl.ds(pl.multiple_of(start, HALF), width)
        return high[:, lanes], low[:, lanes]

    contract = ((0,), (0,))
    own = take(quarter * PIECE, PIECE)
    block = dot3(own, own, contract)
    flat[0:HALF, :] = block[0:HALF, :]
    flat[HALF : HALF + HALF // 2, 0:HALF] = block[HALF : HALF + HALF // 2, HALF:]
    flat[HALF : HALF + HALF // 2, HALF:] = block[HALF + HALF // 2 :, HALF:]
    for k in range(1, 4):
        bit = lax.rem(lax.div(quarter, 1 if k == 1 else 2), 2)
        other = lax.bitwise_xor(quarter, k)
        left = jnp.where(bit == 0, quarter * PIECE, other * PIECE + HALF)
        right = jnp.where(bit == 0, other * PIECE, quarter * PIECE)
        row = PACKED + (k - 4) * HALF
        flat[row : row + HALF, :] = dot3(take(left, HALF), take(right, PIECE), contract)
    part = out.shape[1]
    for slot in range(8):
        z = lax.bitwise_xor(zed, ORDER[slot % 4])
        x = lax.bitwise_xor(ex, slot // 4)
        base = pl.multiple_of((z * 2 + x) * part, 8)
        out[slot] = flat[pl.ds(base, part), :]


def gram_share(at, slabs):
    rows = sum(slab.shape[0] for slab in slabs) // 2
    width = 2 * slabs[0].shape[1]
    return pl.pallas_call(
        functools.partial(gram_kernel, len(slabs) // 4),
        in_specs=[SCALARS] + [WHOLE] * len(slabs),
        out_specs=WHOLE,
        out_shape=jax.ShapeDtypeStruct((8, PACKED // 8, PIECE), F32),
        scratch_shapes=[pltpu.VMEM((rows, width), BF16)] * 2 + [pltpu.VMEM((PACKED, PIECE), F32)],
        compiler_params=params(),
        name="gram_share",
    )(at, *slabs)


def update_kernel(scale, places, count, at, *refs):
    pieces, refs = refs[: len(places)], refs[len(places) :]
    owns, acrosses, refs = refs[:count], refs[count : 2 * count], refs[2 * count :]
    out, packed, gram, high, low = refs
    zed, ex, core, half = at[0], at[1], at[2], at[3]
    part = pieces[0].shape[1]
    for ref, slots in zip(pieces, places):
        for n, (kz, kx, kc, kf) in enumerate(slots):
            quarter = 2 * lax.bitwise_xor(half, kf) + lax.bitwise_xor(core, kc)
            chip = 2 * lax.bitwise_xor(zed, kz) + lax.bitwise_xor(ex, kx)
            row = pl.multiple_of(quarter * PACKED + chip * part, 8)
            packed[pl.ds(row, part), :] = ref[n]
    trace = jnp.zeros((1, 1), F32)
    rows = lax.broadcasted_iota(jnp.int32, (HALF, HALF), 0)
    columns = lax.broadcasted_iota(jnp.int32, (HALF, HALF), 1)

    def put(block, row, column):
        h, l = split(block)
        here = (slice(row, row + block.shape[0]), slice(column, column + block.shape[1]))
        high[here] = h
        low[here] = l

    for q in range(4):
        base, edge = q * PACKED, q * PIECE
        top = packed[base : base + HALF, :]
        bottom = packed[base + HALF : base + HALF + HALF // 2, :]
        bottom = jnp.concatenate([bottom[:, :HALF], bottom[:, HALF:]], 0)
        for block in (top[:, :HALF], bottom):
            trace += jnp.sum(jnp.where(rows == columns, block, 0.0), keepdims=True)
        put(top, edge, edge)
        put(top[:, HALF:].T, edge + HALF, edge)
        put(bottom, edge + HALF, edge + HALF)
        for k in range(1, 4):
            other = q ^ k
            if q > other:
                continue
            row = PACKED + (k - 4) * HALF
            for first, owner in ((0, q), (HALF, other)):
                block = packed[owner * PACKED + row : owner * PACKED + row + HALF, :]
                put(block, edge + first, other * PIECE)
                put(block.T, other * PIECE, edge + first)
    inv = 1.0 / (jnp.sqrt(trace) + 1e-07)
    share = owns[0].shape[1]
    contract = ((1,), (0,))

    def mine(which):
        return pl.ds(pl.multiple_of(which * share, share), share)

    unit = jnp.concatenate([own[...] for own in owns], 0) * inv
    far = jnp.concatenate([across[...] for across in acrosses], 0) * inv
    first = dot3(split(unit), (high[mine(half), :], low[mine(half), :]), contract)
    first += dot3(split(far), (high[mine(1 - half), :], low[mine(1 - half), :]), contract)
    first = first * (inv * inv)
    gram[...] = first
    second = dot3(split(first), (high[:, mine(half)], low[:, mine(half)]), contract)
    second = second * (inv * inv)
    result = 3.4445 * unit + (-4.775 * gram[:, mine(half)] + 2.0315 * second)
    out[...] = (scale * result).astype(out.dtype)


def update(at, pieces, places, owns, acrosses, scale):
    rows = sum(own.shape[0] for own in owns)
    share = owns[0].shape[1]
    width = 2 * share
    return pl.pallas_call(
        functools.partial(update_kernel, scale, places, len(owns)),
        in_specs=[SCALARS] + [WHOLE] * (len(pieces) + 2 * len(owns)),
        out_specs=WHOLE,
        out_shape=jax.ShapeDtypeStruct((rows, share), BF16),
        scratch_shapes=[
            pltpu.VMEM((4 * PACKED, PIECE), F32),
            pltpu.VMEM((rows, width), F32),
            pltpu.VMEM((width, width), BF16),
            pltpu.VMEM((width, width), BF16),
        ],
        compiler_params=params(),
        name="update",
    )(at, *pieces, *owns, *acrosses)


AXIS_BITS = {"f": 1, "c": 2, "x": 4, "z1": 8, "z2": 16}


def flip(value, *names):
    mask = sum(AXIS_BITS[name] for name in names)
    count = lax.axis_size(("dp", "fsdp"))
    return lax.ppermute(value, ("dp", "fsdp"), [(i, i ^ mask) for i in range(count)])


SIDES = (("c",), ("x",), ("c", "x"))


def fast_body(partials, scales):
    values, scales = partials[0], scales[0]
    features, share = values.shape
    own_rows = features // lax.axis_size("dp")
    rank = lax.axis_index("dp")
    at = jnp.stack([rank // 4, rank // 2 % 2, rank % 2, lax.axis_index("fsdp")])
    unit = own_rows // sum(CHUNKS)
    spans, start = [], 0
    for size in CHUNKS:
        spans.append((start, size * unit))
        start += size * unit

    core_raw, *outs = pack(values, scales, at, own_rows, spans)
    packed = [flip(out, *names) for out, names in zip(outs, SIDES)]
    core_raw = flip(core_raw, "c")
    raws = [flip(out, *SIDES[1 + n % 2]) for n, out in enumerate(outs[3:])]
    owns, acrosses, slabs = [], [], []
    after, later = [], []
    for n, (start, rows) in enumerate(spans):
        pair = raws[2 * n : 2 * n + 2]
        keep, *go = dequant(
            at, values, scales, core_raw, pair, packed, own_rows, start, after
        )
        got = [flip(part, "z1") for part in go]
        sent = keep[1] + got[1]
        after, later = later + [sent], []
        grad = (keep[0] + got[0]) + flip(sent, "z2")
        later.append(grad)
        across = flip(grad, "f")
        owns.append(grad)
        acrosses.append(across)
        slabs += [grad, across, flip(grad, "c"), flip(grad, "c", "f")]

    shared = gram_share(at, slabs)
    got = shared[:4] + flip(shared[4:], "x")
    got = got[:2] + flip(got[2:], "z1")
    piece = got[:1] + flip(got[1:], "z2")

    pair = jnp.concatenate([piece, flip(piece, "z2")])
    other = flip(pair, "z1")
    a, b = pair, other
    ax, bf = flip(a, "x"), flip(b, "f")
    near = jnp.concatenate([a, ax])
    far = jnp.concatenate([b, bf])
    near_f, far_x = flip(near, "f"), flip(far, "x")
    parts = [near, far, near_f, far_x]
    z_pair, z_other = ((0, 0), (2, 0)), ((1, 0), (3, 0))

    def places(zeds, first, second):
        return [(z, x, 0, f) for x, f in (first, second) for z, _ in zeds]

    slots = [
        places(z_pair, (0, 0), (1, 0)),
        places(z_other, (0, 0), (0, 1)),
        places(z_pair, (0, 1), (1, 1)),
        places(z_other, (1, 0), (1, 1)),
    ]
    parts += [flip(part, "c") for part in parts]
    slots += [[(z, x, 1, f) for z, x, _, f in group] for group in slots]
    scale = float(0.25 * np.sqrt(np.float32(features * 2 * share)))
    return update(at, parts, slots, owns, acrosses, scale)


def plain_body(partials, scales):
    values, scales = partials[0], scales[0]
    features, share = values.shape
    dp = lax.axis_size("dp")
    rows = values.reshape(scales.shape[0], -1, share).astype(F32) * scales[:, None, :]
    summed = lax.psum_scatter(
        rows.reshape(features, share), "dp", scatter_dimension=0, tiled=True
    )
    slab = lax.all_gather(summed, "fsdp", axis=1, tiled=True)
    width = slab.shape[1]
    highest = functools.partial(
        jnp.dot, precision=lax.Precision.HIGHEST, preferred_element_type=F32
    )
    half = lax.axis_index("fsdp")
    gram = lax.psum(highest(summed.T, slab), "dp")
    gram = lax.all_gather(gram, "fsdp", axis=0, tiled=True)
    inv = 1.0 / (jnp.sqrt(jnp.trace(gram)) + 1e-07)
    scaled = gram * (inv * inv)
    first = highest(slab * inv, scaled)
    mine = lambda value: lax.dynamic_slice_in_dim(value, half * share, share, 1)
    second = highest(first, mine(scaled))
    result = 3.4445 * (summed * inv) + (-4.775 * mine(first) + 2.0315 * second)
    return (0.25 * jnp.sqrt(F32(features * width)) * result).astype(BF16)


def solution(mesh):
    dp, fsdp = mesh.shape["dp"], mesh.shape["fsdp"]

    def run(partials, scales):
        features, width = partials.shape[1:]
        fast = (
            (dp, fsdp) == (16, 2)
            and features % (dp * GRAIN * sum(CHUNKS)) == 0
            and width == 4 * PIECE
        )
        return jax.shard_map(
            fast_body if fast else plain_body,
            mesh=mesh,
            in_specs=(P("dp", None, "fsdp"), P("dp", None, "fsdp")),
            out_specs=P("dp", "fsdp"),
            check_vma=False,
        )(partials, scales)

    return run
```

```python
import functools

import jax
import jax.numpy as jnp
import numpy as np
from jax import lax
from jax.experimental import pallas as pl
from jax.experimental.pallas import tpu as pltpu
from jax.sharding import PartitionSpec as P

BLOCK = 128
GRAIN = 16
CHUNKS = (7, 5, 3)
ORDER = (0, 2, 1, 3)
PIECE = 256
HALF = PIECE // 2
PACKED = HALF + HALF // 2 + 3 * HALF
F32 = jnp.float32
BF16 = jnp.bfloat16
VMEM = 48 * 1024 * 1024
WHOLE = pl.BlockSpec(memory_space=pltpu.VMEM)
SCALARS = pl.BlockSpec(memory_space=pltpu.SMEM)
ANYWHERE = pl.BlockSpec(memory_space=pl.ANY)


def params():
    return pltpu.CompilerParams(vmem_limit_bytes=VMEM)


def split(value):
    high = value.astype(BF16)
    return high, (value - high.astype(F32)).astype(BF16)


def dot3(a, b, contract):
    dims = (contract, ((), ()))

    def one(u, v):
        return lax.dot_general(u, v, dims, preferred_element_type=F32)

    return one(a[0], b[0]) + (one(a[0], b[1]) + one(a[1], b[0]))


def slot_row(at, side, slot, own_rows):
    zed, ex, core = at[0], at[1], at[2]
    z = lax.bitwise_xor(zed, ORDER[slot])
    c = lax.bitwise_xor(core, side % 2)
    x = lax.bitwise_xor(ex, side // 2)
    return ((z * 2 + x) * 2 + c) * own_rows


SLOTS = len(ORDER)
SPAN = 4
TAIL = 3 * SLOTS * SPAN


def pack_kernel(own_rows, spans, at, values, scales, own, *refs):
    outs, gathered = refs[:-1], refs[-1]
    blocks = scales.shape[0]

    def copy(side, start, rows, out):
        for slot in range(SLOTS):
            base = pl.multiple_of(slot_row(at, side, slot, own_rows) + start, GRAIN)
            out[slot * rows : (slot + 1) * rows, :] = values[pl.ds(base, rows), :]

    def tail(side, out):
        for slot in range(SLOTS):
            first = slot_row(at, side, slot, own_rows) // BLOCK
            for n in range(SPAN):
                row = pl.ds(jnp.minimum(first + n, blocks - 1), 1)
                gathered[slot * SPAN + n : slot * SPAN + n + 1, :] = scales[row, :]
        left = gathered[...]
        for n in range(3):
            part = left.astype(BF16)
            row = out.shape[0] - TAIL + n * SLOTS * SPAN
            out[row : row + SLOTS * SPAN, :] = part
            left = left - part.astype(F32)

    copy(0, 0, own_rows, own)
    copy(1, 0, own_rows, outs[0])
    tail(1, outs[0])
    for n, (start, rows) in enumerate(spans):
        for side in (2, 3):
            out = outs[2 * n + side - 1]
            copy(side, start, rows, out)
            if n == 0:
                tail(side, out)


def pack(values, scales, at, own_rows, spans):
    width = values.shape[1]
    lengths = [SLOTS * own_rows, SLOTS * own_rows + TAIL]
    for n, (_, rows) in enumerate(spans):
        lengths += [SLOTS * rows + (TAIL if n == 0 else 0)] * 2
    return pl.pallas_call(
        functools.partial(pack_kernel, own_rows, spans),
        in_specs=[SCALARS, WHOLE, WHOLE],
        out_specs=[WHOLE] * len(lengths),
        out_shape=[jax.ShapeDtypeStruct((rows, width), BF16) for rows in lengths],
        scratch_shapes=[pltpu.VMEM((SLOTS * SPAN, width), F32)],
        compiler_params=params(),
        name="pack_rows",
    )(at, values, scales)


def dequant_kernel(own_rows, start, rows, at, scales, own, core_raw, *refs):
    heads, raws, refs = refs[:2], refs[2:4], refs[4:]
    outs, packed = refs[-4:-1], refs[-1]
    size = SLOTS * SPAN
    for n, ref in enumerate((core_raw, *heads)):
        row = ref.shape[0] - TAIL
        parts = [
            ref[row + k * size : row + (k + 1) * size, :].astype(F32) for k in range(3)
        ]
        packed[n * size : (n + 1) * size, :] = parts[0] + parts[1] + parts[2]
    for slot in range(SLOTS):
        base = slot_row(at, 0, slot, own_rows)
        for g in range(rows // GRAIN):
            block = (base + (start + g * GRAIN)) // BLOCK
            span = slot * SPAN + block - base // BLOCK
            here = slice(g * GRAIN, (g + 1) * GRAIN)
            row = slot * own_rows + start + g * GRAIN
            there = slice(row, row + GRAIN)
            row = slot * rows + g * GRAIN
            total = own[there, :].astype(F32) * scales[pl.ds(block, 1), :]
            total += core_raw[there, :].astype(F32) * packed[pl.ds(span, 1), :]
            for n, raw in enumerate(raws):
                part = raw[row : row + GRAIN, :].astype(F32)
                total += part * packed[pl.ds((n + 1) * size + span, 1), :]
            if slot < 2:
                outs[0][slot, here, :] = total
            else:
                outs[slot - 1][here, :] = total


def dequant(at, scales, own, core_raw, heads, raws, own_rows, start, rows, after):
    width = own.shape[1]
    part = jax.ShapeDtypeStruct((rows, width), F32)
    return pl.pallas_call(
        functools.partial(dequant_kernel, own_rows, start, rows),
        in_specs=[SCALARS] + [WHOLE] * 7 + [ANYWHERE] * len(after),
        out_specs=[WHOLE] * 3,
        out_shape=[jax.ShapeDtypeStruct((2, rows, width), F32), part, part],
        scratch_shapes=[pltpu.VMEM((3 * SLOTS * SPAN, width), F32)],
        compiler_params=params(),
        name="dequant_sum",
    )(at, scales, own, core_raw, *heads, *raws, *after)


def add(terms, after):
    def kernel(*refs):
        total = refs[0][...]
        for ref in refs[1 : len(terms)]:
            total = total + ref[...]
        refs[-1][...] = total

    return pl.pallas_call(
        kernel,
        in_specs=[WHOLE] * len(terms) + [ANYWHERE] * len(after),
        out_specs=WHOLE,
        out_shape=jax.ShapeDtypeStruct(terms[0].shape, F32),
        compiler_params=params(),
        name="add_rows",
    )(*terms, *after)


def gram_kernel(count, at, *refs):
    slabs, (out, high, low, flat) = refs[: 4 * count], refs[4 * count :]
    zed, ex, half = at[0], at[1], at[3]
    quarter = 2 * half + at[2]
    share = slabs[0].shape[1]
    row = 0
    for i, slab in enumerate(slabs):
        column = half if i % 2 == 0 else 1 - half
        lanes = pl.ds(pl.multiple_of(column * share, share), share)
        here = slice(row, row + slab.shape[0])
        h, l = split(slab[...])
        high[here, lanes] = h
        low[here, lanes] = l
        row += slab.shape[0] if i % 2 == 1 else 0

    def take(start, width):
        lanes = pl.ds(pl.multiple_of(start, HALF), width)
        return high[:, lanes], low[:, lanes]

    contract = ((0,), (0,))
    own = take(quarter * PIECE, PIECE)
    block = dot3(own, own, contract)
    flat[0:HALF, :] = block[0:HALF, :]
    flat[HALF : HALF + HALF // 2, 0:HALF] = block[HALF : HALF + HALF // 2, HALF:]
    flat[HALF : HALF + HALF // 2, HALF:] = block[HALF + HALF // 2 :, HALF:]
    for k in range(1, 4):
        bit = lax.rem(lax.div(quarter, 1 if k == 1 else 2), 2)
        other = lax.bitwise_xor(quarter, k)
        left = jnp.where(bit == 0, quarter * PIECE, other * PIECE + HALF)
        right = jnp.where(bit == 0, other * PIECE, quarter * PIECE)
        row = PACKED + (k - 4) * HALF
        flat[row : row + HALF, :] = dot3(take(left, HALF), take(right, PIECE), contract)
    part = out.shape[1]
    for slot in range(8):
        z = lax.bitwise_xor(zed, ORDER[slot % 4])
        x = lax.bitwise_xor(ex, slot // 4)
        base = pl.multiple_of((z * 2 + x) * part, 8)
        out[slot] = flat[pl.ds(base, part), :]


def gram_share(at, slabs):
    rows = sum(slab.shape[0] for slab in slabs) // 2
    width = 2 * slabs[0].shape[1]
    return pl.pallas_call(
        functools.partial(gram_kernel, len(slabs) // 4),
        in_specs=[SCALARS] + [WHOLE] * len(slabs),
        out_specs=WHOLE,
        out_shape=jax.ShapeDtypeStruct((8, PACKED // 8, PIECE), F32),
        scratch_shapes=[pltpu.VMEM((rows, width), BF16)] * 2 + [pltpu.VMEM((PACKED, PIECE), F32)],
        compiler_params=params(),
        name="gram_share",
    )(at, *slabs)


def update_kernel(scale, places, count, at, *refs):
    pieces, refs = refs[: len(places)], refs[len(places) :]
    owns, acrosses, refs = refs[:count], refs[count : 2 * count], refs[2 * count :]
    out, packed, gram, high, low = refs
    zed, ex, core, half = at[0], at[1], at[2], at[3]
    part = pieces[0].shape[1]
    for ref, slots in zip(pieces, places):
        for n, (kz, kx, kc, kf) in enumerate(slots):
            quarter = 2 * lax.bitwise_xor(half, kf) + lax.bitwise_xor(core, kc)
            chip = 2 * lax.bitwise_xor(zed, kz) + lax.bitwise_xor(ex, kx)
            row = pl.multiple_of(quarter * PACKED + chip * part, 8)
            packed[pl.ds(row, part), :] = ref[n]
    trace = jnp.zeros((1, 1), F32)
    rows = lax.broadcasted_iota(jnp.int32, (HALF, HALF), 0)
    columns = lax.broadcasted_iota(jnp.int32, (HALF, HALF), 1)

    def put(block, row, column):
        h, l = split(block)
        here = (slice(row, row + block.shape[0]), slice(column, column + block.shape[1]))
        high[here] = h
        low[here] = l

    for q in range(4):
        base, edge = q * PACKED, q * PIECE
        top = packed[base : base + HALF, :]
        bottom = packed[base + HALF : base + HALF + HALF // 2, :]
        bottom = jnp.concatenate([bottom[:, :HALF], bottom[:, HALF:]], 0)
        for block in (top[:, :HALF], bottom):
            trace += jnp.sum(jnp.where(rows == columns, block, 0.0), keepdims=True)
        put(top, edge, edge)
        put(top[:, HALF:].T, edge + HALF, edge)
        put(bottom, edge + HALF, edge + HALF)
        for k in range(1, 4):
            other = q ^ k
            if q > other:
                continue
            row = PACKED + (k - 4) * HALF
            for first, owner in ((0, q), (HALF, other)):
                block = packed[owner * PACKED + row : owner * PACKED + row + HALF, :]
                put(block, edge + first, other * PIECE)
                put(block.T, other * PIECE, edge + first)
    inv = 1.0 / (jnp.sqrt(trace) + 1e-07)
    share = owns[0].shape[1]
    contract = ((1,), (0,))

    def mine(which):
        return pl.ds(pl.multiple_of(which * share, share), share)

    unit = jnp.concatenate([own[...] for own in owns], 0) * inv
    far = jnp.concatenate([across[...] for across in acrosses], 0) * inv
    first = dot3(split(unit), (high[mine(half), :], low[mine(half), :]), contract)
    first += dot3(split(far), (high[mine(1 - half), :], low[mine(1 - half), :]), contract)
    first = first * (inv * inv)
    gram[...] = first
    second = dot3(split(first), (high[:, mine(half)], low[:, mine(half)]), contract)
    second = second * (inv * inv)
    result = 3.4445 * unit + (-4.775 * gram[:, mine(half)] + 2.0315 * second)
    out[...] = (scale * result).astype(out.dtype)


def update(at, pieces, places, owns, acrosses, scale):
    rows = sum(own.shape[0] for own in owns)
    share = owns[0].shape[1]
    width = 2 * share
    return pl.pallas_call(
        functools.partial(update_kernel, scale, places, len(owns)),
        in_specs=[SCALARS] + [WHOLE] * (len(pieces) + 2 * len(owns)),
        out_specs=WHOLE,
        out_shape=jax.ShapeDtypeStruct((rows, share), BF16),
        scratch_shapes=[
            pltpu.VMEM((4 * PACKED, PIECE), F32),
            pltpu.VMEM((rows, width), F32),
            pltpu.VMEM((width, width), BF16),
            pltpu.VMEM((width, width), BF16),
        ],
        compiler_params=params(),
        name="update",
    )(at, *pieces, *owns, *acrosses)


AXIS_BITS = {"f": 1, "c": 2, "x": 4, "z1": 8, "z2": 16}


def flip(value, *names):
    mask = sum(AXIS_BITS[name] for name in names)
    count = lax.axis_size(("dp", "fsdp"))
    return lax.ppermute(value, ("dp", "fsdp"), [(i, i ^ mask) for i in range(count)])


SIDES = (("x",), ("c", "x"))


def fast_body(partials, scales):
    values, scales = partials[0], scales[0]
    features, share = values.shape
    own_rows = features // lax.axis_size("dp")
    rank = lax.axis_index("dp")
    at = jnp.stack([rank // 4, rank // 2 % 2, rank % 2, lax.axis_index("fsdp")])
    unit = own_rows // sum(CHUNKS)
    spans, start = [], 0
    for size in CHUNKS:
        spans.append((start, size * unit))
        start += size * unit

    own, core_raw, *outs = pack(values, scales, at, own_rows, spans)
    core_raw = flip(core_raw, "c")
    raws = [flip(out, *SIDES[n % 2]) for n, out in enumerate(outs)]
    heads = raws[:2]
    owns, acrosses, slabs = [], [], []
    after, before = [], []
    for n, (start, rows) in enumerate(spans):
        pair = raws[2 * n : 2 * n + 2]
        keep, *go = dequant(
            at, scales, own, core_raw, heads, pair, own_rows, start, rows, after
        )
        got = [flip(part, "z1") for part in go]
        sent = add([keep[1], got[1]], owns[-1:])
        half = keep[0] + got[0]
        after = [sent, half]
        grad = add([half, flip(sent, "z2")], before)
        across = flip(grad, "f")
        owns.append(grad)
        acrosses.append(across)
        before = [across, flip(grad, "c"), flip(grad, "c", "f")]
        slabs += [grad] + before

    shared = gram_share(at, slabs)
    got = shared[:4] + flip(shared[4:], "x")
    got = got[:2] + flip(got[2:], "z1")
    piece = got[:1] + flip(got[1:], "z2")

    pair = jnp.concatenate([piece, flip(piece, "z2")])
    other = flip(pair, "z1")
    a, b = pair, other
    ax, bf = flip(a, "x"), flip(b, "f")
    near = jnp.concatenate([a, ax])
    far = jnp.concatenate([b, bf])
    near_f, far_x = flip(near, "f"), flip(far, "x")
    parts = [near, far, near_f, far_x]
    z_pair, z_other = ((0, 0), (2, 0)), ((1, 0), (3, 0))

    def places(zeds, first, second):
        return [(z, x, 0, f) for x, f in (first, second) for z, _ in zeds]

    slots = [
        places(z_pair, (0, 0), (1, 0)),
        places(z_other, (0, 0), (0, 1)),
        places(z_pair, (0, 1), (1, 1)),
        places(z_other, (1, 0), (1, 1)),
    ]
    parts += [flip(part, "c") for part in parts]
    slots += [[(z, x, 1, f) for z, x, _, f in group] for group in slots]
    scale = float(0.25 * np.sqrt(np.float32(features * 2 * share)))
    return update(at, parts, slots, owns, acrosses, scale)


def plain_body(partials, scales):
    values, scales = partials[0], scales[0]
    features, share = values.shape
    dp = lax.axis_size("dp")
    rows = values.reshape(scales.shape[0], -1, share).astype(F32) * scales[:, None, :]
    summed = lax.psum_scatter(
        rows.reshape(features, share), "dp", scatter_dimension=0, tiled=True
    )
    slab = lax.all_gather(summed, "fsdp", axis=1, tiled=True)
    width = slab.shape[1]
    highest = functools.partial(
        jnp.dot, precision=lax.Precision.HIGHEST, preferred_element_type=F32
    )
    half = lax.axis_index("fsdp")
    gram = lax.psum(highest(summed.T, slab), "dp")
    gram = lax.all_gather(gram, "fsdp", axis=0, tiled=True)
    inv = 1.0 / (jnp.sqrt(jnp.trace(gram)) + 1e-07)
    scaled = gram * (inv * inv)
    first = highest(slab * inv, scaled)
    mine = lambda value: lax.dynamic_slice_in_dim(value, half * share, share, 1)
    second = highest(first, mine(scaled))
    result = 3.4445 * (summed * inv) + (-4.775 * mine(first) + 2.0315 * second)
    return (0.25 * jnp.sqrt(F32(features * width)) * result).astype(BF16)


def solution(mesh):
    dp, fsdp = mesh.shape["dp"], mesh.shape["fsdp"]

    def run(partials, scales):
        features, width = partials.shape[1:]
        fast = (
            (dp, fsdp) == (16, 2)
            and features % (dp * GRAIN * sum(CHUNKS)) == 0
            and width == 4 * PIECE
        )
        return jax.shard_map(
            fast_body if fast else plain_body,
            mesh=mesh,
            in_specs=(P("dp", None, "fsdp"), P("dp", None, "fsdp")),
            out_specs=P("dp", "fsdp"),
            check_vma=False,
        )(partials, scales)

    return run
```

```python
import functools

import jax
import jax.numpy as jnp
import numpy as np
from jax import lax
from jax.experimental import pallas as pl
from jax.experimental.pallas import tpu as pltpu
from jax.sharding import PartitionSpec as P

BLOCK = 128
GRAIN = 16
CHUNKS = (3, 5, 4, 3)
ORDER = (0, 2, 1, 3)
PIECE = 256
HALF = PIECE // 2
PACKED = HALF + HALF // 2 + 3 * HALF
F32 = jnp.float32
BF16 = jnp.bfloat16
VMEM = 48 * 1024 * 1024
WHOLE = pl.BlockSpec(memory_space=pltpu.VMEM)
SCALARS = pl.BlockSpec(memory_space=pltpu.SMEM)
ANYWHERE = pl.BlockSpec(memory_space=pl.ANY)


def params():
    return pltpu.CompilerParams(vmem_limit_bytes=VMEM)


def split(value):
    high = value.astype(BF16)
    return high, (value - high.astype(F32)).astype(BF16)


def dot3(a, b, contract):
    dims = (contract, ((), ()))

    def one(u, v):
        return lax.dot_general(u, v, dims, preferred_element_type=F32)

    return one(a[0], b[0]) + (one(a[0], b[1]) + one(a[1], b[0]))


def slot_row(at, side, slot, own_rows):
    zed, ex, core = at[0], at[1], at[2]
    z = lax.bitwise_xor(zed, ORDER[slot])
    c = lax.bitwise_xor(core, side % 2)
    x = lax.bitwise_xor(ex, side // 2)
    return ((z * 2 + x) * 2 + c) * own_rows


SLOTS = len(ORDER)
SPAN = 4
TAIL = 3 * SLOTS * SPAN


def pack_kernel(own_rows, spans, at, values, scales, own, *refs):
    outs, gathered = refs[:-1], refs[-1]
    blocks = scales.shape[0]

    def copy(side, start, rows, out):
        for slot in range(SLOTS):
            base = pl.multiple_of(slot_row(at, side, slot, own_rows) + start, GRAIN)
            out[slot * rows : (slot + 1) * rows, :] = values[pl.ds(base, rows), :]

    def tail(side, out):
        for slot in range(SLOTS):
            first = slot_row(at, side, slot, own_rows) // BLOCK
            for n in range(SPAN):
                row = pl.ds(jnp.minimum(first + n, blocks - 1), 1)
                gathered[slot * SPAN + n : slot * SPAN + n + 1, :] = scales[row, :]
        left = gathered[...]
        for n in range(3):
            part = left.astype(BF16)
            row = out.shape[0] - TAIL + n * SLOTS * SPAN
            out[row : row + SLOTS * SPAN, :] = part
            left = left - part.astype(F32)

    copy(0, 0, own_rows, own)
    copy(1, 0, own_rows, outs[0])
    tail(1, outs[0])
    for n, (start, rows) in enumerate(spans):
        for side in (2, 3):
            out = outs[2 * n + side - 1]
            copy(side, start, rows, out)
            if n == 0:
                tail(side, out)


def pack(values, scales, at, own_rows, spans):
    width = values.shape[1]
    lengths = [SLOTS * own_rows, SLOTS * own_rows + TAIL]
    for n, (_, rows) in enumerate(spans):
        lengths += [SLOTS * rows + (TAIL if n == 0 else 0)] * 2
    return pl.pallas_call(
        functools.partial(pack_kernel, own_rows, spans),
        in_specs=[SCALARS, WHOLE, WHOLE],
        out_specs=[WHOLE] * len(lengths),
        out_shape=[jax.ShapeDtypeStruct((rows, width), BF16) for rows in lengths],
        scratch_shapes=[pltpu.VMEM((SLOTS * SPAN, width), F32)],
        compiler_params=params(),
        name="pack_rows",
    )(at, values, scales)


def dequant_kernel(own_rows, start, rows, at, scales, own, core_raw, *refs):
    heads, raws, refs = refs[:2], refs[2:4], refs[4:]
    outs, packed = refs[-4:-1], refs[-1]
    size = SLOTS * SPAN
    for n, ref in enumerate((core_raw, *heads)):
        row = ref.shape[0] - TAIL
        parts = [
            ref[row + k * size : row + (k + 1) * size, :].astype(F32) for k in range(3)
        ]
        packed[n * size : (n + 1) * size, :] = parts[0] + parts[1] + parts[2]
    for slot in range(SLOTS):
        base = slot_row(at, 0, slot, own_rows)
        for g in range(rows // GRAIN):
            block = (base + (start + g * GRAIN)) // BLOCK
            span = slot * SPAN + block - base // BLOCK
            here = slice(g * GRAIN, (g + 1) * GRAIN)
            row = slot * own_rows + start + g * GRAIN
            there = slice(row, row + GRAIN)
            row = slot * rows + g * GRAIN
            total = own[there, :].astype(F32) * scales[pl.ds(block, 1), :]
            total += core_raw[there, :].astype(F32) * packed[pl.ds(span, 1), :]
            for n, raw in enumerate(raws):
                part = raw[row : row + GRAIN, :].astype(F32)
                total += part * packed[pl.ds((n + 1) * size + span, 1), :]
            if slot < 2:
                outs[0][slot, here, :] = total
            else:
                outs[slot - 1][here, :] = total


def dequant(at, scales, own, core_raw, heads, raws, own_rows, start, rows, after):
    width = own.shape[1]
    part = jax.ShapeDtypeStruct((rows, width), F32)
    return pl.pallas_call(
        functools.partial(dequant_kernel, own_rows, start, rows),
        in_specs=[SCALARS] + [WHOLE] * 7 + [ANYWHERE] * len(after),
        out_specs=[WHOLE] * 3,
        out_shape=[jax.ShapeDtypeStruct((2, rows, width), F32), part, part],
        scratch_shapes=[pltpu.VMEM((3 * SLOTS * SPAN, width), F32)],
        compiler_params=params(),
        name="dequant_sum",
    )(at, scales, own, core_raw, *heads, *raws, *after)


def add(terms, after):
    def kernel(*refs):
        total = refs[0][...]
        for ref in refs[1 : len(terms)]:
            total = total + ref[...]
        refs[-1][...] = total

    return pl.pallas_call(
        kernel,
        in_specs=[WHOLE] * len(terms) + [ANYWHERE] * len(after),
        out_specs=WHOLE,
        out_shape=jax.ShapeDtypeStruct(terms[0].shape, F32),
        compiler_params=params(),
        name="add_rows",
    )(*terms, *after)


def gram_kernel(count, at, *refs):
    slabs, (out, high, low, flat) = refs[: 4 * count], refs[4 * count :]
    zed, ex, half = at[0], at[1], at[3]
    quarter = 2 * half + at[2]
    share = slabs[0].shape[1]
    row = 0
    for i, slab in enumerate(slabs):
        column = half if i % 2 == 0 else 1 - half
        lanes = pl.ds(pl.multiple_of(column * share, share), share)
        here = slice(row, row + slab.shape[0])
        h, l = split(slab[...])
        high[here, lanes] = h
        low[here, lanes] = l
        row += slab.shape[0] if i % 2 == 1 else 0

    def take(start, width):
        lanes = pl.ds(pl.multiple_of(start, HALF), width)
        return high[:, lanes], low[:, lanes]

    contract = ((0,), (0,))
    own = take(quarter * PIECE, PIECE)
    block = dot3(own, own, contract)
    flat[0:HALF, :] = block[0:HALF, :]
    flat[HALF : HALF + HALF // 2, 0:HALF] = block[HALF : HALF + HALF // 2, HALF:]
    flat[HALF : HALF + HALF // 2, HALF:] = block[HALF + HALF // 2 :, HALF:]
    for k in range(1, 4):
        bit = lax.rem(lax.div(quarter, 1 if k == 1 else 2), 2)
        other = lax.bitwise_xor(quarter, k)
        left = jnp.where(bit == 0, quarter * PIECE, other * PIECE + HALF)
        right = jnp.where(bit == 0, other * PIECE, quarter * PIECE)
        row = PACKED + (k - 4) * HALF
        flat[row : row + HALF, :] = dot3(take(left, HALF), take(right, PIECE), contract)
    part = out.shape[1]
    for slot in range(8):
        z = lax.bitwise_xor(zed, ORDER[slot % 4])
        x = lax.bitwise_xor(ex, slot // 4)
        base = pl.multiple_of((z * 2 + x) * part, 8)
        out[slot] = flat[pl.ds(base, part), :]


def gram_share(at, slabs):
    rows = sum(slab.shape[0] for slab in slabs) // 2
    width = 2 * slabs[0].shape[1]
    return pl.pallas_call(
        functools.partial(gram_kernel, len(slabs) // 4),
        in_specs=[SCALARS] + [WHOLE] * len(slabs),
        out_specs=WHOLE,
        out_shape=jax.ShapeDtypeStruct((8, PACKED // 8, PIECE), F32),
        scratch_shapes=[pltpu.VMEM((rows, width), BF16)] * 2 + [pltpu.VMEM((PACKED, PIECE), F32)],
        compiler_params=params(),
        name="gram_share",
    )(at, *slabs)


def update_kernel(scale, places, count, at, *refs):
    pieces, refs = refs[: len(places)], refs[len(places) :]
    owns, acrosses, refs = refs[:count], refs[count : 2 * count], refs[2 * count :]
    out, packed, gram, high, low = refs
    zed, ex, core, half = at[0], at[1], at[2], at[3]
    part = pieces[0].shape[1]
    for ref, slots in zip(pieces, places):
        for n, (kz, kx, kc, kf) in enumerate(slots):
            quarter = 2 * lax.bitwise_xor(half, kf) + lax.bitwise_xor(core, kc)
            chip = 2 * lax.bitwise_xor(zed, kz) + lax.bitwise_xor(ex, kx)
            row = pl.multiple_of(quarter * PACKED + chip * part, 8)
            packed[pl.ds(row, part), :] = ref[n]
    trace = jnp.zeros((1, 1), F32)
    rows = lax.broadcasted_iota(jnp.int32, (HALF, HALF), 0)
    columns = lax.broadcasted_iota(jnp.int32, (HALF, HALF), 1)

    def put(block, row, column):
        h, l = split(block)
        here = (slice(row, row + block.shape[0]), slice(column, column + block.shape[1]))
        high[here] = h
        low[here] = l

    for q in range(4):
        base, edge = q * PACKED, q * PIECE
        top = packed[base : base + HALF, :]
        bottom = packed[base + HALF : base + HALF + HALF // 2, :]
        bottom = jnp.concatenate([bottom[:, :HALF], bottom[:, HALF:]], 0)
        for block in (top[:, :HALF], bottom):
            trace += jnp.sum(jnp.where(rows == columns, block, 0.0), keepdims=True)
        put(top, edge, edge)
        put(top[:, HALF:].T, edge + HALF, edge)
        put(bottom, edge + HALF, edge + HALF)
        for k in range(1, 4):
            other = q ^ k
            if q > other:
                continue
            row = PACKED + (k - 4) * HALF
            for first, owner in ((0, q), (HALF, other)):
                block = packed[owner * PACKED + row : owner * PACKED + row + HALF, :]
                put(block, edge + first, other * PIECE)
                put(block.T, other * PIECE, edge + first)
    inv = 1.0 / (jnp.sqrt(trace) + 1e-07)
    share = owns[0].shape[1]
    contract = ((1,), (0,))

    def mine(which):
        return pl.ds(pl.multiple_of(which * share, share), share)

    unit = jnp.concatenate([own[...] for own in owns], 0) * inv
    far = jnp.concatenate([across[...] for across in acrosses], 0) * inv
    first = dot3(split(unit), (high[mine(half), :], low[mine(half), :]), contract)
    first += dot3(split(far), (high[mine(1 - half), :], low[mine(1 - half), :]), contract)
    first = first * (inv * inv)
    gram[...] = first
    second = dot3(split(first), (high[:, mine(half)], low[:, mine(half)]), contract)
    second = second * (inv * inv)
    result = 3.4445 * unit + (-4.775 * gram[:, mine(half)] + 2.0315 * second)
    out[...] = (scale * result).astype(out.dtype)


def update(at, pieces, places, owns, acrosses, scale):
    rows = sum(own.shape[0] for own in owns)
    share = owns[0].shape[1]
    width = 2 * share
    return pl.pallas_call(
        functools.partial(update_kernel, scale, places, len(owns)),
        in_specs=[SCALARS] + [WHOLE] * (len(pieces) + 2 * len(owns)),
        out_specs=WHOLE,
        out_shape=jax.ShapeDtypeStruct((rows, share), BF16),
        scratch_shapes=[
            pltpu.VMEM((4 * PACKED, PIECE), F32),
            pltpu.VMEM((rows, width), F32),
            pltpu.VMEM((width, width), BF16),
            pltpu.VMEM((width, width), BF16),
        ],
        compiler_params=params(),
        name="update",
    )(at, *pieces, *owns, *acrosses)


AXIS_BITS = {"f": 1, "c": 2, "x": 4, "z1": 8, "z2": 16}


def flip(value, *names):
    mask = sum(AXIS_BITS[name] for name in names)
    count = lax.axis_size(("dp", "fsdp"))
    return lax.ppermute(value, ("dp", "fsdp"), [(i, i ^ mask) for i in range(count)])


SIDES = (("x",), ("c", "x"))


def fast_body(partials, scales):
    values, scales = partials[0], scales[0]
    features, share = values.shape
    own_rows = features // lax.axis_size("dp")
    rank = lax.axis_index("dp")
    at = jnp.stack([rank // 4, rank // 2 % 2, rank % 2, lax.axis_index("fsdp")])
    unit = own_rows // sum(CHUNKS)
    spans, start = [], 0
    for size in CHUNKS:
        spans.append((start, size * unit))
        start += size * unit

    own, core_raw, *outs = pack(values, scales, at, own_rows, spans)
    core_raw = flip(core_raw, "c")
    raws = [flip(out, *SIDES[n % 2]) for n, out in enumerate(outs)]
    heads = raws[:2]
    owns, acrosses, slabs = [], [], []
    after, before = [], []
    for n, (start, rows) in enumerate(spans):
        pair = raws[2 * n : 2 * n + 2]
        keep, *go = dequant(
            at, scales, own, core_raw, heads, pair, own_rows, start, rows, after
        )
        got = [flip(part, "z1") for part in go]
        sent = add([keep[1], got[1]], owns[-1:])
        half = keep[0] + got[0]
        after = [sent]
        grad = add([half, flip(sent, "z2")], before)
        across = flip(grad, "f")
        owns.append(grad)
        acrosses.append(across)
        before = [across, flip(grad, "c"), flip(grad, "c", "f")]
        slabs += [grad] + before

    shared = gram_share(at, slabs)
    got = shared[:4] + flip(shared[4:], "x")
    got = got[:2] + flip(got[2:], "z1")
    piece = got[:1] + flip(got[1:], "z2")

    pair = jnp.concatenate([piece, flip(piece, "z2")])
    other = flip(pair, "z1")
    a, b = pair, other
    ax, bf = flip(a, "x"), flip(b, "f")
    near = jnp.concatenate([a, ax])
    far = jnp.concatenate([b, bf])
    near_f, far_x = flip(near, "f"), flip(far, "x")
    parts = [near, far, near_f, far_x]
    z_pair, z_other = ((0, 0), (2, 0)), ((1, 0), (3, 0))

    def places(zeds, first, second):
        return [(z, x, 0, f) for x, f in (first, second) for z, _ in zeds]

    slots = [
        places(z_pair, (0, 0), (1, 0)),
        places(z_other, (0, 0), (0, 1)),
        places(z_pair, (0, 1), (1, 1)),
        places(z_other, (1, 0), (1, 1)),
    ]
    parts += [flip(part, "c") for part in parts]
    slots += [[(z, x, 1, f) for z, x, _, f in group] for group in slots]
    scale = float(0.25 * np.sqrt(np.float32(features * 2 * share)))
    return update(at, parts, slots, owns, acrosses, scale)


def plain_body(partials, scales):
    values, scales = partials[0], scales[0]
    features, share = values.shape
    dp = lax.axis_size("dp")
    rows = values.reshape(scales.shape[0], -1, share).astype(F32) * scales[:, None, :]
    summed = lax.psum_scatter(
        rows.reshape(features, share), "dp", scatter_dimension=0, tiled=True
    )
    slab = lax.all_gather(summed, "fsdp", axis=1, tiled=True)
    width = slab.shape[1]
    highest = functools.partial(
        jnp.dot, precision=lax.Precision.HIGHEST, preferred_element_type=F32
    )
    half = lax.axis_index("fsdp")
    gram = lax.psum(highest(summed.T, slab), "dp")
    gram = lax.all_gather(gram, "fsdp", axis=0, tiled=True)
    inv = 1.0 / (jnp.sqrt(jnp.trace(gram)) + 1e-07)
    scaled = gram * (inv * inv)
    first = highest(slab * inv, scaled)
    mine = lambda value: lax.dynamic_slice_in_dim(value, half * share, share, 1)
    second = highest(first, mine(scaled))
    result = 3.4445 * (summed * inv) + (-4.775 * mine(first) + 2.0315 * second)
    return (0.25 * jnp.sqrt(F32(features * width)) * result).astype(BF16)


def solution(mesh):
    dp, fsdp = mesh.shape["dp"], mesh.shape["fsdp"]

    def run(partials, scales):
        features, width = partials.shape[1:]
        fast = (
            (dp, fsdp) == (16, 2)
            and features % (dp * GRAIN * sum(CHUNKS)) == 0
            and width == 4 * PIECE
        )
        return jax.shard_map(
            fast_body if fast else plain_body,
            mesh=mesh,
            in_specs=(P("dp", None, "fsdp"), P("dp", None, "fsdp")),
            out_specs=P("dp", "fsdp"),
            check_vma=False,
        )(partials, scales)

    return run
```

```python
import functools

import jax
import jax.numpy as jnp
import numpy as np
from jax import lax
from jax.experimental import pallas as pl
from jax.experimental.pallas import tpu as pltpu
from jax.sharding import PartitionSpec as P

BLOCK = 128
GRAIN = 16
CHUNKS = (3, 5, 4, 3)
LEAVE = (1, 2, 3)
ORDER = (0, 2, 1, 3)
PIECE = 256
HALF = PIECE // 2
PACKED = HALF + HALF // 2 + 3 * HALF
F32 = jnp.float32
BF16 = jnp.bfloat16
VMEM = 48 * 1024 * 1024
WHOLE = pl.BlockSpec(memory_space=pltpu.VMEM)
SCALARS = pl.BlockSpec(memory_space=pltpu.SMEM)
ANYWHERE = pl.BlockSpec(memory_space=pl.ANY)


def params():
    return pltpu.CompilerParams(vmem_limit_bytes=VMEM)


def split(value):
    high = value.astype(BF16)
    return high, (value - high.astype(F32)).astype(BF16)


def dot3(a, b, contract):
    dims = (contract, ((), ()))

    def one(u, v):
        return lax.dot_general(u, v, dims, preferred_element_type=F32)

    return one(a[0], b[0]) + (one(a[0], b[1]) + one(a[1], b[0]))


def slot_row(at, side, slot, own_rows):
    zed, ex, core = at[0], at[1], at[2]
    z = lax.bitwise_xor(zed, ORDER[slot])
    c = lax.bitwise_xor(core, side % 2)
    x = lax.bitwise_xor(ex, side // 2)
    return ((z * 2 + x) * 2 + c) * own_rows


SLOTS = len(ORDER)
SPAN = 4
TAIL = 3 * SLOTS * SPAN


def pack_kernel(own_rows, spans, at, values, scales, own, *refs):
    outs, gathered = refs[:-1], refs[-1]
    blocks = scales.shape[0]

    def copy(side, start, rows, out):
        for slot in range(SLOTS):
            base = pl.multiple_of(slot_row(at, side, slot, own_rows) + start, GRAIN)
            out[slot * rows : (slot + 1) * rows, :] = values[pl.ds(base, rows), :]

    def tail(side, out):
        for slot in range(SLOTS):
            first = slot_row(at, side, slot, own_rows) // BLOCK
            for n in range(SPAN):
                row = pl.ds(jnp.minimum(first + n, blocks - 1), 1)
                gathered[slot * SPAN + n : slot * SPAN + n + 1, :] = scales[row, :]
        left = gathered[...]
        for n in range(3):
            part = left.astype(BF16)
            row = out.shape[0] - TAIL + n * SLOTS * SPAN
            out[row : row + SLOTS * SPAN, :] = part
            left = left - part.astype(F32)

    copy(0, 0, own_rows, own)
    copy(1, 0, own_rows, outs[0])
    tail(1, outs[0])
    for n, (start, rows) in enumerate(spans):
        for side in (2, 3):
            out = outs[2 * n + side - 1]
            copy(side, start, rows, out)
            if n == 0:
                tail(side, out)


def pack(values, scales, at, own_rows, spans):
    width = values.shape[1]
    lengths = [SLOTS * own_rows, SLOTS * own_rows + TAIL]
    for n, (_, rows) in enumerate(spans):
        lengths += [SLOTS * rows + (TAIL if n == 0 else 0)] * 2
    return pl.pallas_call(
        functools.partial(pack_kernel, own_rows, spans),
        in_specs=[SCALARS, WHOLE, WHOLE],
        out_specs=[WHOLE] * len(lengths),
        out_shape=[jax.ShapeDtypeStruct((rows, width), BF16) for rows in lengths],
        scratch_shapes=[pltpu.VMEM((SLOTS * SPAN, width), F32)],
        compiler_params=params(),
        name="pack_rows",
    )(at, values, scales)


def dequant_kernel(own_rows, start, rows, at, scales, own, core_raw, *refs):
    heads, raws, refs = refs[:2], refs[2:4], refs[4:]
    outs, packed = refs[-4:-1], refs[-1]
    size = SLOTS * SPAN
    for n, ref in enumerate((core_raw, *heads)):
        row = ref.shape[0] - TAIL
        parts = [
            ref[row + k * size : row + (k + 1) * size, :].astype(F32) for k in range(3)
        ]
        packed[n * size : (n + 1) * size, :] = parts[0] + parts[1] + parts[2]
    for slot in range(SLOTS):
        base = slot_row(at, 0, slot, own_rows)
        for g in range(rows // GRAIN):
            block = (base + (start + g * GRAIN)) // BLOCK
            span = slot * SPAN + block - base // BLOCK
            here = slice(g * GRAIN, (g + 1) * GRAIN)
            row = slot * own_rows + start + g * GRAIN
            there = slice(row, row + GRAIN)
            row = slot * rows + g * GRAIN
            total = own[there, :].astype(F32) * scales[pl.ds(block, 1), :]
            total += core_raw[there, :].astype(F32) * packed[pl.ds(span, 1), :]
            for n, raw in enumerate(raws):
                part = raw[row : row + GRAIN, :].astype(F32)
                total += part * packed[pl.ds((n + 1) * size + span, 1), :]
            if slot < 2:
                outs[0][slot, here, :] = total
            else:
                outs[slot - 1][here, :] = total


def dequant(at, scales, own, core_raw, heads, raws, own_rows, start, rows, after, carry):
    width = own.shape[1]
    part = jax.ShapeDtypeStruct((rows, width), F32)
    shapes = [jax.ShapeDtypeStruct((2, rows, width), F32), part, part]
    first, count = 8 + len(after), len(carry)

    def kernel(*refs):
        kept = refs[:8] + refs[first + count : first + count + 3] + refs[-1:]
        dequant_kernel(own_rows, start, rows, *kept)

    outs = pl.pallas_call(
        kernel,
        in_specs=[SCALARS] + [WHOLE] * 7 + [ANYWHERE] * (len(after) + count),
        out_specs=[WHOLE] * 3 + [ANYWHERE] * count,
        out_shape=shapes + [jax.ShapeDtypeStruct(x.shape, x.dtype) for x in carry],
        scratch_shapes=[pltpu.VMEM((3 * SLOTS * SPAN, width), F32)],
        input_output_aliases={first + n: 3 + n for n in range(count)},
        compiler_params=params(),
        name="dequant_sum",
    )(at, scales, own, core_raw, *heads, *raws, *after, *carry)
    return outs[:3], outs[3:]


def add(terms, after):
    def kernel(*refs):
        total = refs[0][...]
        for ref in refs[1 : len(terms)]:
            total = total + ref[...]
        refs[-1][...] = total

    return pl.pallas_call(
        kernel,
        in_specs=[WHOLE] * len(terms) + [ANYWHERE] * len(after),
        out_specs=WHOLE,
        out_shape=jax.ShapeDtypeStruct(terms[0].shape, F32),
        compiler_params=params(),
        name="add_rows",
    )(*terms, *after)


def gram_kernel(count, at, *refs):
    slabs, (out, high, low, flat) = refs[: 2 * count], refs[2 * count :]
    zed, ex, half = at[0], at[1], at[3]
    share = slabs[0].shape[1]
    row = 0
    for i, slab in enumerate(slabs):
        column = half if i % 2 == 0 else 1 - half
        lanes = pl.ds(pl.multiple_of(column * share, share), share)
        here = slice(row, row + slab.shape[0])
        h, l = split(slab[...])
        high[here, lanes] = h
        low[here, lanes] = l
        row += slab.shape[0] if i % 2 == 1 else 0

    def take(start, width):
        lanes = pl.ds(pl.multiple_of(start, HALF), width)
        return high[:, lanes], low[:, lanes]

    contract = ((0,), (0,))
    part = out.shape[1]
    for side in range(2):
        quarter = 2 * half + lax.bitwise_xor(at[2], side)
        own = take(quarter * PIECE, PIECE)
        block = dot3(own, own, contract)
        flat[0:HALF, :] = block[0:HALF, :]
        flat[HALF : HALF + HALF // 2, 0:HALF] = block[HALF : HALF + HALF // 2, HALF:]
        flat[HALF : HALF + HALF // 2, HALF:] = block[HALF + HALF // 2 :, HALF:]
        for k in range(1, 4):
            bit = lax.rem(lax.div(quarter, 1 if k == 1 else 2), 2)
            other = lax.bitwise_xor(quarter, k)
            left = jnp.where(bit == 0, quarter * PIECE, other * PIECE + HALF)
            right = jnp.where(bit == 0, other * PIECE, quarter * PIECE)
            row = PACKED + (k - 4) * HALF
            flat[row : row + HALF, :] = dot3(take(left, HALF), take(right, PIECE), contract)
        for slot in range(8):
            z = lax.bitwise_xor(zed, ORDER[slot % 4])
            x = lax.bitwise_xor(ex, slot // 4)
            base = pl.multiple_of((z * 2 + x) * part, 8)
            out[side * 8 + slot] = flat[pl.ds(base, part), :]


def gram_share(at, slabs):
    rows = sum(slab.shape[0] for slab in slabs) // 2
    width = 2 * slabs[0].shape[1]
    return pl.pallas_call(
        functools.partial(gram_kernel, len(slabs) // 2),
        in_specs=[SCALARS] + [WHOLE] * len(slabs),
        out_specs=WHOLE,
        out_shape=jax.ShapeDtypeStruct((16, PACKED // 8, PIECE), F32),
        scratch_shapes=[pltpu.VMEM((rows, width), BF16)] * 2 + [pltpu.VMEM((PACKED, PIECE), F32)],
        compiler_params=params(),
        name="gram_share",
    )(at, *slabs)


def update_kernel(scale, places, count, at, *refs):
    pieces, refs = refs[: len(places)], refs[len(places) :]
    owns, acrosses, refs = refs[:count], refs[count : 2 * count], refs[2 * count :]
    out, packed, gram, high, low = refs
    zed, ex, core, half = at[0], at[1], at[2], at[3]
    part = pieces[0].shape[1]
    for ref, slots in zip(pieces, places):
        for n, (kz, kx, kc, kf) in enumerate(slots):
            quarter = 2 * lax.bitwise_xor(half, kf) + lax.bitwise_xor(core, kc)
            chip = 2 * lax.bitwise_xor(zed, kz) + lax.bitwise_xor(ex, kx)
            row = pl.multiple_of(quarter * PACKED + chip * part, 8)
            packed[pl.ds(row, part), :] = ref[n]
    trace = jnp.zeros((1, 1), F32)
    rows = lax.broadcasted_iota(jnp.int32, (HALF, HALF), 0)
    columns = lax.broadcasted_iota(jnp.int32, (HALF, HALF), 1)

    def put(block, row, column):
        h, l = split(block)
        here = (slice(row, row + block.shape[0]), slice(column, column + block.shape[1]))
        high[here] = h
        low[here] = l

    for q in range(4):
        base, edge = q * PACKED, q * PIECE
        top = packed[base : base + HALF, :]
        bottom = packed[base + HALF : base + HALF + HALF // 2, :]
        bottom = jnp.concatenate([bottom[:, :HALF], bottom[:, HALF:]], 0)
        for block in (top[:, :HALF], bottom):
            trace += jnp.sum(jnp.where(rows == columns, block, 0.0), keepdims=True)
        put(top, edge, edge)
        put(top[:, HALF:].T, edge + HALF, edge)
        put(bottom, edge + HALF, edge + HALF)
        for k in range(1, 4):
            other = q ^ k
            if q > other:
                continue
            row = PACKED + (k - 4) * HALF
            for first, owner in ((0, q), (HALF, other)):
                block = packed[owner * PACKED + row : owner * PACKED + row + HALF, :]
                put(block, edge + first, other * PIECE)
                put(block.T, other * PIECE, edge + first)
    inv = 1.0 / (jnp.sqrt(trace) + 1e-07)
    share = owns[0].shape[1]
    contract = ((1,), (0,))

    def mine(which):
        return pl.ds(pl.multiple_of(which * share, share), share)

    unit = jnp.concatenate([own[...] for own in owns], 0) * inv
    far = jnp.concatenate([across[...] for across in acrosses], 0) * inv
    first = dot3(split(unit), (high[mine(half), :], low[mine(half), :]), contract)
    first += dot3(split(far), (high[mine(1 - half), :], low[mine(1 - half), :]), contract)
    first = first * (inv * inv)
    gram[...] = first
    second = dot3(split(first), (high[:, mine(half)], low[:, mine(half)]), contract)
    second = second * (inv * inv)
    result = 3.4445 * unit + (-4.775 * gram[:, mine(half)] + 2.0315 * second)
    out[...] = (scale * result).astype(out.dtype)


def update(at, pieces, places, owns, acrosses, scale):
    rows = sum(own.shape[0] for own in owns)
    share = owns[0].shape[1]
    width = 2 * share
    return pl.pallas_call(
        functools.partial(update_kernel, scale, places, len(owns)),
        in_specs=[SCALARS] + [WHOLE] * (len(pieces) + 2 * len(owns)),
        out_specs=WHOLE,
        out_shape=jax.ShapeDtypeStruct((rows, share), BF16),
        scratch_shapes=[
            pltpu.VMEM((4 * PACKED, PIECE), F32),
            pltpu.VMEM((rows, width), F32),
            pltpu.VMEM((width, width), BF16),
            pltpu.VMEM((width, width), BF16),
        ],
        compiler_params=params(),
        name="update",
    )(at, *pieces, *owns, *acrosses)


AXIS_BITS = {"f": 1, "c": 2, "x": 4, "z1": 8, "z2": 16}


def flip(value, *names):
    mask = sum(AXIS_BITS[name] for name in names)
    count = lax.axis_size(("dp", "fsdp"))
    return lax.ppermute(value, ("dp", "fsdp"), [(i, i ^ mask) for i in range(count)])


SIDES = (("x",), ("c", "x"))


def fast_body(partials, scales):
    values, scales = partials[0], scales[0]
    features, share = values.shape
    own_rows = features // lax.axis_size("dp")
    rank = lax.axis_index("dp")
    at = jnp.stack([rank // 4, rank // 2 % 2, rank % 2, lax.axis_index("fsdp")])
    unit = own_rows // sum(CHUNKS)
    spans, start = [], 0
    for size in CHUNKS:
        spans.append((start, size * unit))
        start += size * unit

    own, core_raw, *outs = pack(values, scales, at, own_rows, spans)
    core_raw = flip(core_raw, "c")

    def cross(pair):
        return [flip(out, *side) for out, side in zip(pair, SIDES)]

    outs = [outs[2 * n : 2 * n + 2] for n in range(len(spans))]
    raws = [cross(pair) for pair in outs[:2]]
    heads = raws[0]
    owns, acrosses, slabs = [], [], []
    after, before, grads, held = [], [], [], []
    for n, (start, rows) in enumerate(spans):
        carry = outs[n + 2] if n + 2 < len(spans) else []
        (keep, *go), carry = dequant(
            at, scales, own, core_raw, heads, raws[n], own_rows, start, rows, after, carry
        )
        if carry:
            raws.append(cross(carry))
        got = [flip(part, "z1") for part in go]
        sent = add([keep[1], got[1]], grads[-1:])
        half = keep[0] + got[0]
        after = [sent, half]
        grad = add([half, flip(sent, "z2")], before)
        grads.append(grad)
        held.append(grad)
        before = []
        if n in LEAVE:
            group = jnp.concatenate(held) if len(held) > 1 else grad
            across = flip(group, "f")
            owns.append(group)
            acrosses.append(across)
            slabs += [group, across]
            before, held = [across], []

    shared = gram_share(at, slabs)
    core = flip(shared[8:], "c")
    got = (shared[:4] + core[:4]) + flip(shared[4:8] + core[4:], "x")
    got = got[:2] + flip(got[2:], "z1")
    piece = got[:1] + flip(got[1:], "z2")

    pair = jnp.concatenate([piece, flip(piece, "z2")])
    other = flip(pair, "z1")
    a, b = pair, other
    ax, bf = flip(a, "x"), flip(b, "f")
    near = jnp.concatenate([a, ax])
    far = jnp.concatenate([b, bf])
    near_f, far_x = flip(near, "f"), flip(far, "x")
    parts = [near, far, near_f, far_x]
    z_pair, z_other = ((0, 0), (2, 0)), ((1, 0), (3, 0))

    def places(zeds, first, second):
        return [(z, x, 0, f) for x, f in (first, second) for z, _ in zeds]

    slots = [
        places(z_pair, (0, 0), (1, 0)),
        places(z_other, (0, 0), (0, 1)),
        places(z_pair, (0, 1), (1, 1)),
        places(z_other, (1, 0), (1, 1)),
    ]
    parts += [flip(part, "c") for part in parts]
    slots += [[(z, x, 1, f) for z, x, _, f in group] for group in slots]
    scale = float(0.25 * np.sqrt(np.float32(features * 2 * share)))
    return update(at, parts, slots, owns, acrosses, scale)


def plain_body(partials, scales):
    values, scales = partials[0], scales[0]
    features, share = values.shape
    dp = lax.axis_size("dp")
    rows = values.reshape(scales.shape[0], -1, share).astype(F32) * scales[:, None, :]
    summed = lax.psum_scatter(
        rows.reshape(features, share), "dp", scatter_dimension=0, tiled=True
    )
    slab = lax.all_gather(summed, "fsdp", axis=1, tiled=True)
    width = slab.shape[1]
    highest = functools.partial(
        jnp.dot, precision=lax.Precision.HIGHEST, preferred_element_type=F32
    )
    half = lax.axis_index("fsdp")
    gram = lax.psum(highest(summed.T, slab), "dp")
    gram = lax.all_gather(gram, "fsdp", axis=0, tiled=True)
    inv = 1.0 / (jnp.sqrt(jnp.trace(gram)) + 1e-07)
    scaled = gram * (inv * inv)
    first = highest(slab * inv, scaled)
    mine = lambda value: lax.dynamic_slice_in_dim(value, half * share, share, 1)
    second = highest(first, mine(scaled))
    result = 3.4445 * (summed * inv) + (-4.775 * mine(first) + 2.0315 * second)
    return (0.25 * jnp.sqrt(F32(features * width)) * result).astype(BF16)


def solution(mesh):
    dp, fsdp = mesh.shape["dp"], mesh.shape["fsdp"]

    def run(partials, scales):
        features, width = partials.shape[1:]
        fast = (
            (dp, fsdp) == (16, 2)
            and features % (dp * GRAIN * sum(CHUNKS)) == 0
            and width == 4 * PIECE
        )
        return jax.shard_map(
            fast_body if fast else plain_body,
            mesh=mesh,
            in_specs=(P("dp", None, "fsdp"), P("dp", None, "fsdp")),
            out_specs=P("dp", "fsdp"),
            check_vma=False,
        )(partials, scales)

    return run
```

```python
import functools

import jax
import jax.numpy as jnp
import numpy as np
from jax import lax
from jax.experimental import pallas as pl
from jax.experimental.pallas import tpu as pltpu
from jax.sharding import PartitionSpec as P

BLOCK = 128
GRAIN = 16
CHUNKS = (5, 6, 4)
LEAVE = (0, 1, 2)
ORDER = (0, 2, 1, 3)
PIECE = 256
HALF = PIECE // 2
PACKED = HALF + HALF // 2 + 3 * HALF
F32 = jnp.float32
BF16 = jnp.bfloat16
VMEM = 48 * 1024 * 1024
WHOLE = pl.BlockSpec(memory_space=pltpu.VMEM)
SCALARS = pl.BlockSpec(memory_space=pltpu.SMEM)
ANYWHERE = pl.BlockSpec(memory_space=pl.ANY)


def params():
    return pltpu.CompilerParams(vmem_limit_bytes=VMEM)


def split(value):
    high = value.astype(BF16)
    return high, (value - high.astype(F32)).astype(BF16)


def dot3(a, b, contract):
    dims = (contract, ((), ()))

    def one(u, v):
        return lax.dot_general(u, v, dims, preferred_element_type=F32)

    return one(a[0], b[0]) + (one(a[0], b[1]) + one(a[1], b[0]))


def slot_row(at, side, slot, own_rows):
    zed, ex, core = at[0], at[1], at[2]
    z = lax.bitwise_xor(zed, ORDER[slot])
    c = lax.bitwise_xor(core, side % 2)
    x = lax.bitwise_xor(ex, side // 2)
    return ((z * 2 + x) * 2 + c) * own_rows


SLOTS = len(ORDER)
SPAN = 4
TAIL = 3 * SLOTS * SPAN


def pack_kernel(own_rows, spans, at, values, scales, own, *refs):
    outs, gathered = refs[:-1], refs[-1]
    blocks = scales.shape[0]

    def copy(side, start, rows, out):
        for slot in range(SLOTS):
            base = pl.multiple_of(slot_row(at, side, slot, own_rows) + start, GRAIN)
            out[slot * rows : (slot + 1) * rows, :] = values[pl.ds(base, rows), :]

    def tail(side, out):
        for slot in range(SLOTS):
            first = slot_row(at, side, slot, own_rows) // BLOCK
            for n in range(SPAN):
                row = jnp.minimum(first + n, blocks - 1)
                gathered[slot * SPAN + n : slot * SPAN + n + 1, :] = scales[row]
        left = gathered[...]
        for n in range(3):
            part = left.astype(BF16)
            row = out.shape[0] - TAIL + n * SLOTS * SPAN
            out[row : row + SLOTS * SPAN, :] = part
            left = left - part.astype(F32)

    copy(0, 0, own_rows, own)
    copy(1, 0, own_rows, outs[0])
    tail(1, outs[0])
    for n, (start, rows) in enumerate(spans):
        for side in (2, 3):
            out = outs[2 * n + side - 1]
            copy(side, start, rows, out)
            if n == 0:
                tail(side, out)


def pack(values, scales, at, own_rows, spans):
    width = values.shape[1]
    lengths = [SLOTS * own_rows, SLOTS * own_rows + TAIL]
    for n, (_, rows) in enumerate(spans):
        lengths += [SLOTS * rows + (TAIL if n == 0 else 0)] * 2
    return pl.pallas_call(
        functools.partial(pack_kernel, own_rows, spans),
        in_specs=[SCALARS, WHOLE, WHOLE],
        out_specs=[WHOLE] * len(lengths),
        out_shape=[jax.ShapeDtypeStruct((rows, width), BF16) for rows in lengths],
        scratch_shapes=[pltpu.VMEM((SLOTS * SPAN, width), F32)],
        compiler_params=params(),
        name="pack_rows",
    )(at, values, scales)


def dequant_kernel(own_rows, start, rows, at, scales, own, core_raw, *refs):
    heads, raws, refs = refs[:2], refs[2:4], refs[4:]
    outs, packed = refs[-4:-1], refs[-1]
    size = SLOTS * SPAN
    for n, ref in enumerate((core_raw, *heads)):
        row = ref.shape[0] - TAIL
        parts = [
            ref[row + k * size : row + (k + 1) * size, :].astype(F32) for k in range(3)
        ]
        packed[n * size : (n + 1) * size, :] = parts[0] + parts[1] + parts[2]
    for slot in range(SLOTS):
        base = slot_row(at, 0, slot, own_rows)
        for g in range(rows // GRAIN):
            block = (base + (start + g * GRAIN)) // BLOCK
            span = slot * SPAN + block - base // BLOCK
            here = slice(g * GRAIN, (g + 1) * GRAIN)
            row = slot * own_rows + start + g * GRAIN
            there = slice(row, row + GRAIN)
            row = slot * rows + g * GRAIN
            total = own[there, :].astype(F32) * scales[block]
            total += core_raw[there, :].astype(F32) * packed[pl.ds(span, 1), :]
            for n, raw in enumerate(raws):
                part = raw[row : row + GRAIN, :].astype(F32)
                total += part * packed[pl.ds((n + 1) * size + span, 1), :]
            if slot < 2:
                outs[0][slot, here, :] = total
            else:
                outs[slot - 1][here, :] = total


def dequant(at, scales, own, core_raw, heads, raws, own_rows, start, rows, after, carry):
    width = own.shape[1]
    part = jax.ShapeDtypeStruct((rows, width), F32)
    shapes = [jax.ShapeDtypeStruct((2, rows, width), F32), part, part]
    first, count = 8 + len(after), len(carry)

    def kernel(*refs):
        kept = refs[:8] + refs[first + count : first + count + 3] + refs[-1:]
        dequant_kernel(own_rows, start, rows, *kept)

    outs = pl.pallas_call(
        kernel,
        in_specs=[SCALARS] + [WHOLE] * 7 + [ANYWHERE] * (len(after) + count),
        out_specs=[WHOLE] * 3 + [ANYWHERE] * count,
        out_shape=shapes + [jax.ShapeDtypeStruct(x.shape, x.dtype) for x in carry],
        scratch_shapes=[pltpu.VMEM((3 * SLOTS * SPAN, width), F32)],
        input_output_aliases={first + n: 3 + n for n in range(count)},
        compiler_params=params(),
        name="dequant_sum",
    )(at, scales, own, core_raw, *heads, *raws, *after, *carry)
    return outs[:3], outs[3:]


def add(terms, after):
    def kernel(*refs):
        total = refs[0][...]
        for ref in refs[1 : len(terms)]:
            total = total + ref[...]
        refs[-1][...] = total

    return pl.pallas_call(
        kernel,
        in_specs=[WHOLE] * len(terms) + [ANYWHERE] * len(after),
        out_specs=WHOLE,
        out_shape=jax.ShapeDtypeStruct(terms[0].shape, F32),
        compiler_params=params(),
        name="add_rows",
    )(*terms, *after)


def gram_kernel(count, at, *refs):
    slabs, (out, high, low, flat) = refs[: 2 * count], refs[2 * count :]
    zed, ex, half = at[0], at[1], at[3]
    share = slabs[0].shape[1]
    row = 0
    for i, slab in enumerate(slabs):
        column = half if i % 2 == 0 else 1 - half
        lanes = pl.ds(pl.multiple_of(column * share, share), share)
        here = slice(row, row + slab.shape[0])
        h, l = split(slab[...])
        high[here, lanes] = h
        low[here, lanes] = l
        row += slab.shape[0] if i % 2 == 1 else 0

    def take(start, width):
        lanes = pl.ds(pl.multiple_of(start, HALF), width)
        return high[:, lanes], low[:, lanes]

    contract = ((0,), (0,))
    part = out.shape[1]
    for side in range(2):
        quarter = 2 * half + lax.bitwise_xor(at[2], side)
        own = take(quarter * PIECE, PIECE)
        block = dot3(own, own, contract)
        flat[0:HALF, :] = block[0:HALF, :]
        flat[HALF : HALF + HALF // 2, 0:HALF] = block[HALF : HALF + HALF // 2, HALF:]
        flat[HALF : HALF + HALF // 2, HALF:] = block[HALF + HALF // 2 :, HALF:]
        for k in range(1, 4):
            bit = lax.rem(lax.div(quarter, 1 if k == 1 else 2), 2)
            other = lax.bitwise_xor(quarter, k)
            left = jnp.where(bit == 0, quarter * PIECE, other * PIECE + HALF)
            right = jnp.where(bit == 0, other * PIECE, quarter * PIECE)
            row = PACKED + (k - 4) * HALF
            flat[row : row + HALF, :] = dot3(take(left, HALF), take(right, PIECE), contract)
        for slot in range(8):
            z = lax.bitwise_xor(zed, ORDER[slot % 4])
            x = lax.bitwise_xor(ex, slot // 4)
            base = pl.multiple_of((z * 2 + x) * part, 8)
            out[side * 8 + slot] = flat[pl.ds(base, part), :]


def gram_share(at, slabs):
    rows = sum(slab.shape[0] for slab in slabs) // 2
    width = 2 * slabs[0].shape[1]
    return pl.pallas_call(
        functools.partial(gram_kernel, len(slabs) // 2),
        in_specs=[SCALARS] + [WHOLE] * len(slabs),
        out_specs=WHOLE,
        out_shape=jax.ShapeDtypeStruct((16, PACKED // 8, PIECE), F32),
        scratch_shapes=[pltpu.VMEM((rows, width), BF16)] * 2 + [pltpu.VMEM((PACKED, PIECE), F32)],
        compiler_params=params(),
        name="gram_share",
    )(at, *slabs)


def update_kernel(scale, places, count, at, *refs):
    pieces, refs = refs[: len(places)], refs[len(places) :]
    owns, acrosses, refs = refs[:count], refs[count : 2 * count], refs[2 * count :]
    out, packed, gram, high, low = refs
    zed, ex, core, half = at[0], at[1], at[2], at[3]
    part = pieces[0].shape[1]
    for ref, slots in zip(pieces, places):
        for n, (kz, kx, kc, kf) in enumerate(slots):
            quarter = 2 * lax.bitwise_xor(half, kf) + lax.bitwise_xor(core, kc)
            chip = 2 * lax.bitwise_xor(zed, kz) + lax.bitwise_xor(ex, kx)
            row = pl.multiple_of(quarter * PACKED + chip * part, 8)
            packed[pl.ds(row, part), :] = ref[n]
    trace = jnp.zeros((1, 1), F32)
    rows = lax.broadcasted_iota(jnp.int32, (HALF, HALF), 0)
    columns = lax.broadcasted_iota(jnp.int32, (HALF, HALF), 1)

    def put(block, row, column):
        h, l = split(block)
        here = (slice(row, row + block.shape[0]), slice(column, column + block.shape[1]))
        high[here] = h
        low[here] = l

    for q in range(4):
        base, edge = q * PACKED, q * PIECE
        top = packed[base : base + HALF, :]
        bottom = packed[base + HALF : base + HALF + HALF // 2, :]
        bottom = jnp.concatenate([bottom[:, :HALF], bottom[:, HALF:]], 0)
        for block in (top[:, :HALF], bottom):
            trace += jnp.sum(jnp.where(rows == columns, block, 0.0), keepdims=True)
        put(top, edge, edge)
        put(top[:, HALF:].T, edge + HALF, edge)
        put(bottom, edge + HALF, edge + HALF)
        for k in range(1, 4):
            other = q ^ k
            if q > other:
                continue
            row = PACKED + (k - 4) * HALF
            for first, owner in ((0, q), (HALF, other)):
                block = packed[owner * PACKED + row : owner * PACKED + row + HALF, :]
                put(block, edge + first, other * PIECE)
                put(block.T, other * PIECE, edge + first)
    inv = 1.0 / (jnp.sqrt(trace) + 1e-07)
    share = owns[0].shape[1]
    contract = ((1,), (0,))

    def mine(which):
        return pl.ds(pl.multiple_of(which * share, share), share)

    unit = jnp.concatenate([own[...] for own in owns], 0) * inv
    far = jnp.concatenate([across[...] for across in acrosses], 0) * inv
    first = dot3(split(unit), (high[mine(half), :], low[mine(half), :]), contract)
    first += dot3(split(far), (high[mine(1 - half), :], low[mine(1 - half), :]), contract)
    first = first * (inv * inv)
    gram[...] = first
    second = dot3(split(first), (high[:, mine(half)], low[:, mine(half)]), contract)
    second = second * (inv * inv)
    result = 3.4445 * unit + (-4.775 * gram[:, mine(half)] + 2.0315 * second)
    out[...] = (scale * result).astype(out.dtype)


def update(at, pieces, places, owns, acrosses, scale):
    rows = sum(own.shape[0] for own in owns)
    share = owns[0].shape[1]
    width = 2 * share
    return pl.pallas_call(
        functools.partial(update_kernel, scale, places, len(owns)),
        in_specs=[SCALARS] + [WHOLE] * (len(pieces) + 2 * len(owns)),
        out_specs=WHOLE,
        out_shape=jax.ShapeDtypeStruct((rows, share), BF16),
        scratch_shapes=[
            pltpu.VMEM((4 * PACKED, PIECE), F32),
            pltpu.VMEM((rows, width), F32),
            pltpu.VMEM((width, width), BF16),
            pltpu.VMEM((width, width), BF16),
        ],
        compiler_params=params(),
        name="update",
    )(at, *pieces, *owns, *acrosses)


AXIS_BITS = {"f": 1, "c": 2, "x": 4, "z1": 8, "z2": 16}


def flip(value, *names):
    mask = sum(AXIS_BITS[name] for name in names)
    count = lax.axis_size(("dp", "fsdp"))
    return lax.ppermute(value, ("dp", "fsdp"), [(i, i ^ mask) for i in range(count)])


SIDES = (("x",), ("c", "x"))


def fast_body(partials, scales):
    values, scales = partials[0], scales.transpose(1, 0, 2)
    features, share = values.shape
    own_rows = features // lax.axis_size("dp")
    rank = lax.axis_index("dp")
    at = jnp.stack([rank // 4, rank // 2 % 2, rank % 2, lax.axis_index("fsdp")])
    unit = own_rows // sum(CHUNKS)
    spans, start = [], 0
    for size in CHUNKS:
        spans.append((start, size * unit))
        start += size * unit

    own, core_raw, *outs = pack(values, scales, at, own_rows, spans)
    core_raw = flip(core_raw, "c")

    def cross(pair):
        return [flip(out, *side) for out, side in zip(pair, SIDES)]

    outs = [outs[2 * n : 2 * n + 2] for n in range(len(spans))]
    raws = [cross(pair) for pair in outs[:2]]
    heads = raws[0]
    owns, acrosses, slabs = [], [], []
    after, before, grads, held = [], [], [], []
    for n, (start, rows) in enumerate(spans):
        carry = outs[n + 2] if n + 2 < len(spans) else []
        (keep, *go), carry = dequant(
            at, scales, own, core_raw, heads, raws[n], own_rows, start, rows, after, carry
        )
        if carry:
            raws.append(cross(carry))
        got = [flip(part, "z1") for part in go]
        sent = add([keep[1], got[1]], grads[-1:])
        half = keep[0] + got[0]
        after = [sent, half]
        grad = add([half, flip(sent, "z2")], before)
        grads.append(grad)
        held.append(grad)
        before = []
        if n in LEAVE:
            group = jnp.concatenate(held) if len(held) > 1 else grad
            across = flip(group, "f")
            owns.append(group)
            acrosses.append(across)
            slabs += [group, across]
            before, held = [across], []

    shared = gram_share(at, slabs)
    core = flip(shared[8:], "c")
    got = (shared[:4] + core[:4]) + flip(shared[4:8] + core[4:], "x")
    got = got[:2] + flip(got[2:], "z1")
    piece = got[:1] + flip(got[1:], "z2")

    pair = jnp.concatenate([piece, flip(piece, "z2")])
    other = flip(pair, "z1")
    a, b = pair, other
    ax, bf = flip(a, "x"), flip(b, "f")
    near = jnp.concatenate([a, ax])
    far = jnp.concatenate([b, bf])
    near_f, far_x = flip(near, "f"), flip(far, "x")
    parts = [near, far, near_f, far_x]
    z_pair, z_other = ((0, 0), (2, 0)), ((1, 0), (3, 0))

    def places(zeds, first, second):
        return [(z, x, 0, f) for x, f in (first, second) for z, _ in zeds]

    slots = [
        places(z_pair, (0, 0), (1, 0)),
        places(z_other, (0, 0), (0, 1)),
        places(z_pair, (0, 1), (1, 1)),
        places(z_other, (1, 0), (1, 1)),
    ]
    parts += [flip(part, "c") for part in parts]
    slots += [[(z, x, 1, f) for z, x, _, f in group] for group in slots]
    scale = float(0.25 * np.sqrt(np.float32(features * 2 * share)))
    return update(at, parts, slots, owns, acrosses, scale)


def plain_body(partials, scales):
    values, scales = partials[0], scales[0]
    features, share = values.shape
    dp = lax.axis_size("dp")
    rows = values.reshape(scales.shape[0], -1, share).astype(F32) * scales[:, None, :]
    summed = lax.psum_scatter(
        rows.reshape(features, share), "dp", scatter_dimension=0, tiled=True
    )
    slab = lax.all_gather(summed, "fsdp", axis=1, tiled=True)
    width = slab.shape[1]
    highest = functools.partial(
        jnp.dot, precision=lax.Precision.HIGHEST, preferred_element_type=F32
    )
    half = lax.axis_index("fsdp")
    gram = lax.psum(highest(summed.T, slab), "dp")
    gram = lax.all_gather(gram, "fsdp", axis=0, tiled=True)
    inv = 1.0 / (jnp.sqrt(jnp.trace(gram)) + 1e-07)
    scaled = gram * (inv * inv)
    first = highest(slab * inv, scaled)
    mine = lambda value: lax.dynamic_slice_in_dim(value, half * share, share, 1)
    second = highest(first, mine(scaled))
    result = 3.4445 * (summed * inv) + (-4.775 * mine(first) + 2.0315 * second)
    return (0.25 * jnp.sqrt(F32(features * width)) * result).astype(BF16)


def solution(mesh):
    dp, fsdp = mesh.shape["dp"], mesh.shape["fsdp"]

    def run(partials, scales):
        features, width = partials.shape[1:]
        fast = (
            (dp, fsdp) == (16, 2)
            and features % (dp * GRAIN * sum(CHUNKS)) == 0
            and width == 4 * PIECE
        )
        return jax.shard_map(
            fast_body if fast else plain_body,
            mesh=mesh,
            in_specs=(P("dp", None, "fsdp"), P("dp", None, "fsdp")),
            out_specs=P("dp", "fsdp"),
            check_vma=False,
        )(partials, scales)

    return run
```

```python
import functools

import jax
import jax.numpy as jnp
import numpy as np
from jax import lax
from jax.experimental import pallas as pl
from jax.experimental.pallas import tpu as pltpu
from jax.sharding import PartitionSpec as P

BLOCK = 128
GRAIN = 16
CHUNKS = (3, 5, 4, 3)
LEAVE = (1, 2, 3)
ORDER = (0, 2, 1, 3)
PIECE = 256
HALF = PIECE // 2
PACKED = HALF + HALF // 2 + 3 * HALF
F32 = jnp.float32
BF16 = jnp.bfloat16
VMEM = 48 * 1024 * 1024
WHOLE = pl.BlockSpec(memory_space=pltpu.VMEM)
SCALARS = pl.BlockSpec(memory_space=pltpu.SMEM)
ANYWHERE = pl.BlockSpec(memory_space=pl.ANY)


def params():
    return pltpu.CompilerParams(vmem_limit_bytes=VMEM)


def split(value):
    high = value.astype(BF16)
    return high, (value - high.astype(F32)).astype(BF16)


def dot3(a, b, contract):
    dims = (contract, ((), ()))

    def one(u, v):
        return lax.dot_general(u, v, dims, preferred_element_type=F32)

    return one(a[0], b[0]) + (one(a[0], b[1]) + one(a[1], b[0]))


def slot_row(at, side, slot, own_rows):
    zed, ex, core = at[0], at[1], at[2]
    z = lax.bitwise_xor(zed, ORDER[slot])
    c = lax.bitwise_xor(core, side % 2)
    x = lax.bitwise_xor(ex, side // 2)
    return ((z * 2 + x) * 2 + c) * own_rows


SLOTS = len(ORDER)
SPAN = 4
TAIL = 3 * SLOTS * SPAN


def pack_kernel(own_rows, spans, at, values, scales, own, *refs):
    outs, gathered = refs[:-1], refs[-1]
    blocks = scales.shape[0]

    def copy(side, start, rows, out):
        for slot in range(SLOTS):
            base = pl.multiple_of(slot_row(at, side, slot, own_rows) + start, GRAIN)
            out[slot * rows : (slot + 1) * rows, :] = values[pl.ds(base, rows), :]

    def tail(side, out):
        for slot in range(SLOTS):
            first = slot_row(at, side, slot, own_rows) // BLOCK
            for n in range(SPAN):
                row = jnp.minimum(first + n, blocks - 1)
                gathered[slot * SPAN + n : slot * SPAN + n + 1, :] = scales[row]
        left = gathered[...]
        for n in range(3):
            part = left.astype(BF16)
            row = out.shape[0] - TAIL + n * SLOTS * SPAN
            out[row : row + SLOTS * SPAN, :] = part
            left = left - part.astype(F32)

    copy(0, 0, own_rows, own)
    copy(1, 0, own_rows, outs[0])
    tail(1, outs[0])
    for n, (start, rows) in enumerate(spans):
        for side in (2, 3):
            out = outs[2 * n + side - 1]
            copy(side, start, rows, out)
            if n == 0:
                tail(side, out)


def pack(values, scales, at, own_rows, spans):
    width = values.shape[1]
    lengths = [SLOTS * own_rows, SLOTS * own_rows + TAIL]
    for n, (_, rows) in enumerate(spans):
        lengths += [SLOTS * rows + (TAIL if n == 0 else 0)] * 2
    return pl.pallas_call(
        functools.partial(pack_kernel, own_rows, spans),
        in_specs=[SCALARS, WHOLE, WHOLE],
        out_specs=[WHOLE] * len(lengths),
        out_shape=[jax.ShapeDtypeStruct((rows, width), BF16) for rows in lengths],
        scratch_shapes=[pltpu.VMEM((SLOTS * SPAN, width), F32)],
        compiler_params=params(),
        name="pack_rows",
    )(at, values, scales)


def dequant_kernel(own_rows, start, rows, at, scales, own, core_raw, *refs):
    heads, raws, refs = refs[:2], refs[2:4], refs[4:]
    outs, packed = refs[-4:-1], refs[-1]
    size = SLOTS * SPAN
    for n, ref in enumerate((core_raw, *heads)):
        row = ref.shape[0] - TAIL
        parts = [
            ref[row + k * size : row + (k + 1) * size, :].astype(F32) for k in range(3)
        ]
        packed[n * size : (n + 1) * size, :] = parts[0] + parts[1] + parts[2]
    for slot in range(SLOTS):
        base = slot_row(at, 0, slot, own_rows)
        for g in range(rows // GRAIN):
            block = (base + (start + g * GRAIN)) // BLOCK
            span = slot * SPAN + block - base // BLOCK
            here = slice(g * GRAIN, (g + 1) * GRAIN)
            row = slot * own_rows + start + g * GRAIN
            there = slice(row, row + GRAIN)
            row = slot * rows + g * GRAIN
            total = own[there, :].astype(F32) * scales[block]
            total += core_raw[there, :].astype(F32) * packed[pl.ds(span, 1), :]
            for n, raw in enumerate(raws):
                part = raw[row : row + GRAIN, :].astype(F32)
                total += part * packed[pl.ds((n + 1) * size + span, 1), :]
            if slot < 2:
                outs[0][slot, here, :] = total
            else:
                outs[slot - 1][here, :] = total


def dequant(at, scales, own, core_raw, heads, raws, own_rows, start, rows, after, carry):
    width = own.shape[1]
    part = jax.ShapeDtypeStruct((rows, width), F32)
    shapes = [jax.ShapeDtypeStruct((2, rows, width), F32), part, part]
    first, count = 8 + len(after), len(carry)

    def kernel(*refs):
        kept = refs[:8] + refs[first + count : first + count + 3] + refs[-1:]
        dequant_kernel(own_rows, start, rows, *kept)

    outs = pl.pallas_call(
        kernel,
        in_specs=[SCALARS] + [WHOLE] * 7 + [ANYWHERE] * (len(after) + count),
        out_specs=[WHOLE] * 3 + [ANYWHERE] * count,
        out_shape=shapes + [jax.ShapeDtypeStruct(x.shape, x.dtype) for x in carry],
        scratch_shapes=[pltpu.VMEM((3 * SLOTS * SPAN, width), F32)],
        input_output_aliases={first + n: 3 + n for n in range(count)},
        compiler_params=params(),
        name="dequant_sum",
    )(at, scales, own, core_raw, *heads, *raws, *after, *carry)
    return outs[:3], outs[3:]


def add(terms, after):
    def kernel(*refs):
        total = refs[0][...]
        for ref in refs[1 : len(terms)]:
            total = total + ref[...]
        refs[-1][...] = total

    return pl.pallas_call(
        kernel,
        in_specs=[WHOLE] * len(terms) + [ANYWHERE] * len(after),
        out_specs=WHOLE,
        out_shape=jax.ShapeDtypeStruct(terms[0].shape, F32),
        compiler_params=params(),
        name="add_rows",
    )(*terms, *after)


def gram_kernel(count, at, *refs):
    slabs, (out, high, low, flat) = refs[: 2 * count], refs[2 * count :]
    zed, ex, half = at[0], at[1], at[3]
    share = slabs[0].shape[1]
    row = 0
    for i, slab in enumerate(slabs):
        column = half if i % 2 == 0 else 1 - half
        lanes = pl.ds(pl.multiple_of(column * share, share), share)
        here = slice(row, row + slab.shape[0])
        h, l = split(slab[...])
        high[here, lanes] = h
        low[here, lanes] = l
        row += slab.shape[0] if i % 2 == 1 else 0

    def take(start, width):
        lanes = pl.ds(pl.multiple_of(start, HALF), width)
        return high[:, lanes], low[:, lanes]

    contract = ((0,), (0,))
    part = out.shape[1]
    for side in range(2):
        quarter = 2 * half + lax.bitwise_xor(at[2], side)
        own = take(quarter * PIECE, PIECE)
        block = dot3(own, own, contract)
        flat[0:HALF, :] = block[0:HALF, :]
        flat[HALF : HALF + HALF // 2, 0:HALF] = block[HALF : HALF + HALF // 2, HALF:]
        flat[HALF : HALF + HALF // 2, HALF:] = block[HALF + HALF // 2 :, HALF:]
        for k in range(1, 4):
            bit = lax.rem(lax.div(quarter, 1 if k == 1 else 2), 2)
            other = lax.bitwise_xor(quarter, k)
            left = jnp.where(bit == 0, quarter * PIECE, other * PIECE + HALF)
            right = jnp.where(bit == 0, other * PIECE, quarter * PIECE)
            row = PACKED + (k - 4) * HALF
            flat[row : row + HALF, :] = dot3(take(left, HALF), take(right, PIECE), contract)
        for slot in range(8):
            z = lax.bitwise_xor(zed, ORDER[slot % 4])
            x = lax.bitwise_xor(ex, slot // 4)
            base = pl.multiple_of((z * 2 + x) * part, 8)
            out[side * 8 + slot] = flat[pl.ds(base, part), :]


def gram_share(at, slabs):
    rows = sum(slab.shape[0] for slab in slabs) // 2
    width = 2 * slabs[0].shape[1]
    return pl.pallas_call(
        functools.partial(gram_kernel, len(slabs) // 2),
        in_specs=[SCALARS] + [WHOLE] * len(slabs),
        out_specs=WHOLE,
        out_shape=jax.ShapeDtypeStruct((16, PACKED // 8, PIECE), F32),
        scratch_shapes=[pltpu.VMEM((rows, width), BF16)] * 2 + [pltpu.VMEM((PACKED, PIECE), F32)],
        compiler_params=params(),
        name="gram_share",
    )(at, *slabs)


def update_kernel(scale, places, count, at, *refs):
    pieces, refs = refs[: len(places)], refs[len(places) :]
    owns, acrosses, refs = refs[:count], refs[count : 2 * count], refs[2 * count :]
    out, packed, gram, high, low = refs
    zed, ex, core, half = at[0], at[1], at[2], at[3]
    part = pieces[0].shape[1]
    for ref, slots in zip(pieces, places):
        for n, (kz, kx, kc, kf) in enumerate(slots):
            quarter = 2 * lax.bitwise_xor(half, kf) + lax.bitwise_xor(core, kc)
            chip = 2 * lax.bitwise_xor(zed, kz) + lax.bitwise_xor(ex, kx)
            row = pl.multiple_of(quarter * PACKED + chip * part, 8)
            packed[pl.ds(row, part), :] = ref[n]
    trace = jnp.zeros((1, 1), F32)
    rows = lax.broadcasted_iota(jnp.int32, (HALF, HALF), 0)
    columns = lax.broadcasted_iota(jnp.int32, (HALF, HALF), 1)

    def put(block, row, column):
        h, l = split(block)
        here = (slice(row, row + block.shape[0]), slice(column, column + block.shape[1]))
        high[here] = h
        low[here] = l

    for q in range(4):
        base, edge = q * PACKED, q * PIECE
        top = packed[base : base + HALF, :]
        bottom = packed[base + HALF : base + HALF + HALF // 2, :]
        bottom = jnp.concatenate([bottom[:, :HALF], bottom[:, HALF:]], 0)
        for block in (top[:, :HALF], bottom):
            trace += jnp.sum(jnp.where(rows == columns, block, 0.0), keepdims=True)
        put(top, edge, edge)
        put(top[:, HALF:].T, edge + HALF, edge)
        put(bottom, edge + HALF, edge + HALF)
        for k in range(1, 4):
            other = q ^ k
            if q > other:
                continue
            row = PACKED + (k - 4) * HALF
            for first, owner in ((0, q), (HALF, other)):
                block = packed[owner * PACKED + row : owner * PACKED + row + HALF, :]
                put(block, edge + first, other * PIECE)
                put(block.T, other * PIECE, edge + first)
    inv = 1.0 / (jnp.sqrt(trace) + 1e-07)
    share = owns[0].shape[1]
    contract = ((1,), (0,))

    def mine(which):
        return pl.ds(pl.multiple_of(which * share, share), share)

    unit = jnp.concatenate([own[...] for own in owns], 0) * inv
    far = jnp.concatenate([across[...] for across in acrosses], 0) * inv
    first = dot3(split(unit), (high[mine(half), :], low[mine(half), :]), contract)
    first += dot3(split(far), (high[mine(1 - half), :], low[mine(1 - half), :]), contract)
    first = first * (inv * inv)
    gram[...] = first
    second = dot3(split(first), (high[:, mine(half)], low[:, mine(half)]), contract)
    second = second * (inv * inv)
    result = 3.4445 * unit + (-4.775 * gram[:, mine(half)] + 2.0315 * second)
    out[...] = (scale * result).astype(out.dtype)


def update(at, pieces, places, owns, acrosses, scale):
    rows = sum(own.shape[0] for own in owns)
    share = owns[0].shape[1]
    width = 2 * share
    return pl.pallas_call(
        functools.partial(update_kernel, scale, places, len(owns)),
        in_specs=[SCALARS] + [WHOLE] * (len(pieces) + 2 * len(owns)),
        out_specs=WHOLE,
        out_shape=jax.ShapeDtypeStruct((rows, share), BF16),
        scratch_shapes=[
            pltpu.VMEM((4 * PACKED, PIECE), F32),
            pltpu.VMEM((rows, width), F32),
            pltpu.VMEM((width, width), BF16),
            pltpu.VMEM((width, width), BF16),
        ],
        compiler_params=params(),
        name="update",
    )(at, *pieces, *owns, *acrosses)


AXIS_BITS = {"f": 1, "c": 2, "x": 4, "z1": 8, "z2": 16}


def flip(value, *names):
    mask = sum(AXIS_BITS[name] for name in names)
    count = lax.axis_size(("dp", "fsdp"))
    return lax.ppermute(value, ("dp", "fsdp"), [(i, i ^ mask) for i in range(count)])


SIDES = (("x",), ("c", "x"))


def fast_body(partials, scales):
    values, scales = partials[0], scales.transpose(1, 0, 2)
    features, share = values.shape
    own_rows = features // lax.axis_size("dp")
    rank = lax.axis_index("dp")
    at = jnp.stack([rank // 4, rank // 2 % 2, rank % 2, lax.axis_index("fsdp")])
    unit = own_rows // sum(CHUNKS)
    spans, start = [], 0
    for size in CHUNKS:
        spans.append((start, size * unit))
        start += size * unit

    own, core_raw, *outs = pack(values, scales, at, own_rows, spans)
    core_raw = flip(core_raw, "c")

    def cross(pair):
        return [flip(out, *side) for out, side in zip(pair, SIDES)]

    outs = [outs[2 * n : 2 * n + 2] for n in range(len(spans))]
    raws = [cross(pair) for pair in outs[:2]]
    heads = raws[0]
    owns, acrosses, slabs = [], [], []
    after, before, grads, held = [], [], [], []
    for n, (start, rows) in enumerate(spans):
        carry = outs[n + 2] if n + 2 < len(spans) else []
        (keep, *go), carry = dequant(
            at, scales, own, core_raw, heads, raws[n], own_rows, start, rows, after, carry
        )
        if carry:
            raws.append(cross(carry))
        got = [flip(part, "z1") for part in go]
        sent = add([keep[1], got[1]], grads[-1:])
        half = keep[0] + got[0]
        after = [sent, half] if n < len(spans) - 2 else after
        grad = add([half, flip(sent, "z2")], before)
        grads.append(grad)
        held.append(grad)
        before = []
        if n in LEAVE:
            group = jnp.concatenate(held) if len(held) > 1 else grad
            across = flip(group, "f")
            owns.append(group)
            acrosses.append(across)
            slabs += [group, across]
            before, held = [across], []

    shared = gram_share(at, slabs)
    core = flip(shared[8:], "c")
    got = (shared[:4] + core[:4]) + flip(shared[4:8] + core[4:], "x")
    got = got[:2] + flip(got[2:], "z1")
    piece = got[:1] + flip(got[1:], "z2")

    pair = jnp.concatenate([piece, flip(piece, "z2")])
    other = flip(pair, "z1")
    a, b = pair, other
    ax, bf = flip(a, "x"), flip(b, "f")
    near = jnp.concatenate([a, ax])
    far = jnp.concatenate([b, bf])
    near_f, far_x = flip(near, "f"), flip(far, "x")
    parts = [near, far, near_f, far_x]
    z_pair, z_other = ((0, 0), (2, 0)), ((1, 0), (3, 0))

    def places(zeds, first, second):
        return [(z, x, 0, f) for x, f in (first, second) for z, _ in zeds]

    slots = [
        places(z_pair, (0, 0), (1, 0)),
        places(z_other, (0, 0), (0, 1)),
        places(z_pair, (0, 1), (1, 1)),
        places(z_other, (1, 0), (1, 1)),
    ]
    parts += [flip(part, "c") for part in parts]
    slots += [[(z, x, 1, f) for z, x, _, f in group] for group in slots]
    scale = float(0.25 * np.sqrt(np.float32(features * 2 * share)))
    return update(at, parts, slots, owns, acrosses, scale)


def plain_body(partials, scales):
    values, scales = partials[0], scales[0]
    features, share = values.shape
    dp = lax.axis_size("dp")
    rows = values.reshape(scales.shape[0], -1, share).astype(F32) * scales[:, None, :]
    summed = lax.psum_scatter(
        rows.reshape(features, share), "dp", scatter_dimension=0, tiled=True
    )
    slab = lax.all_gather(summed, "fsdp", axis=1, tiled=True)
    width = slab.shape[1]
    highest = functools.partial(
        jnp.dot, precision=lax.Precision.HIGHEST, preferred_element_type=F32
    )
    half = lax.axis_index("fsdp")
    gram = lax.psum(highest(summed.T, slab), "dp")
    gram = lax.all_gather(gram, "fsdp", axis=0, tiled=True)
    inv = 1.0 / (jnp.sqrt(jnp.trace(gram)) + 1e-07)
    scaled = gram * (inv * inv)
    first = highest(slab * inv, scaled)
    mine = lambda value: lax.dynamic_slice_in_dim(value, half * share, share, 1)
    second = highest(first, mine(scaled))
    result = 3.4445 * (summed * inv) + (-4.775 * mine(first) + 2.0315 * second)
    return (0.25 * jnp.sqrt(F32(features * width)) * result).astype(BF16)


def solution(mesh):
    dp, fsdp = mesh.shape["dp"], mesh.shape["fsdp"]

    def run(partials, scales):
        features, width = partials.shape[1:]
        fast = (
            (dp, fsdp) == (16, 2)
            and features % (dp * GRAIN * sum(CHUNKS)) == 0
            and width == 4 * PIECE
        )
        return jax.shard_map(
            fast_body if fast else plain_body,
            mesh=mesh,
            in_specs=(P("dp", None, "fsdp"), P("dp", None, "fsdp")),
            out_specs=P("dp", "fsdp"),
            check_vma=False,
        )(partials, scales)

    return run
```

```python
import functools

import jax
import jax.numpy as jnp
import numpy as np
from jax import lax
from jax.experimental import pallas as pl
from jax.experimental.pallas import tpu as pltpu
from jax.sharding import PartitionSpec as P

BLOCK = 128
GRAIN = 16
CHUNKS = (3, 5, 4, 3)
LEAVE = (0, 1, 3)
SUM_AFTER = ((), ("sent0", "half0"), ("sent1", "half1", "grad0"), ("keep2",))
SENT_AFTER = ((), (), (), ("grad1",))
GRAD_AFTER = ((), ("sent2", "across0"), ("sent3",), ("across1",))
ORDER = (0, 2, 1, 3)
PIECE = 256
HALF = PIECE // 2
PACKED = HALF + HALF // 2 + 3 * HALF
F32 = jnp.float32
BF16 = jnp.bfloat16
VMEM = 48 * 1024 * 1024
WHOLE = pl.BlockSpec(memory_space=pltpu.VMEM)
SCALARS = pl.BlockSpec(memory_space=pltpu.SMEM)
ANYWHERE = pl.BlockSpec(memory_space=pl.ANY)


def params():
    return pltpu.CompilerParams(vmem_limit_bytes=VMEM)


def split(value):
    high = value.astype(BF16)
    return high, (value - high.astype(F32)).astype(BF16)


def dot3(a, b, contract):
    dims = (contract, ((), ()))

    def one(u, v):
        return lax.dot_general(u, v, dims, preferred_element_type=F32)

    return one(a[0], b[0]) + (one(a[0], b[1]) + one(a[1], b[0]))


def slot_row(at, side, slot, own_rows):
    zed, ex, core = at[0], at[1], at[2]
    z = lax.bitwise_xor(zed, ORDER[slot])
    c = lax.bitwise_xor(core, side % 2)
    x = lax.bitwise_xor(ex, side // 2)
    return ((z * 2 + x) * 2 + c) * own_rows


SLOTS = len(ORDER)
SPAN = 4
TAIL = 3 * SLOTS * SPAN


def pack_kernel(own_rows, spans, at, values, scales, own, *refs):
    outs, gathered = refs[:-1], refs[-1]
    blocks = scales.shape[0]

    def copy(side, start, rows, out):
        for slot in range(SLOTS):
            base = pl.multiple_of(slot_row(at, side, slot, own_rows) + start, GRAIN)
            out[slot * rows : (slot + 1) * rows, :] = values[pl.ds(base, rows), :]

    def tail(side, out):
        for slot in range(SLOTS):
            first = slot_row(at, side, slot, own_rows) // BLOCK
            for n in range(SPAN):
                row = jnp.minimum(first + n, blocks - 1)
                gathered[slot * SPAN + n : slot * SPAN + n + 1, :] = scales[row]
        left = gathered[...]
        for n in range(3):
            part = left.astype(BF16)
            row = out.shape[0] - TAIL + n * SLOTS * SPAN
            out[row : row + SLOTS * SPAN, :] = part
            left = left - part.astype(F32)

    copy(0, 0, own_rows, own)
    copy(1, 0, own_rows, outs[0])
    tail(1, outs[0])
    for n, (start, rows) in enumerate(spans):
        for side in (2, 3):
            out = outs[2 * n + side - 1]
            copy(side, start, rows, out)
            if n == 0:
                tail(side, out)


def pack(values, scales, at, own_rows, spans):
    width = values.shape[1]
    lengths = [SLOTS * own_rows, SLOTS * own_rows + TAIL]
    for n, (_, rows) in enumerate(spans):
        lengths += [SLOTS * rows + (TAIL if n == 0 else 0)] * 2
    return pl.pallas_call(
        functools.partial(pack_kernel, own_rows, spans),
        in_specs=[SCALARS, WHOLE, WHOLE],
        out_specs=[WHOLE] * len(lengths),
        out_shape=[jax.ShapeDtypeStruct((rows, width), BF16) for rows in lengths],
        scratch_shapes=[pltpu.VMEM((SLOTS * SPAN, width), F32)],
        compiler_params=params(),
        name="pack_rows",
    )(at, values, scales)


def dequant_kernel(own_rows, start, rows, at, scales, own, core_raw, *refs):
    heads, raws, refs = refs[:2], refs[2:4], refs[4:]
    outs, packed = refs[-4:-1], refs[-1]
    size = SLOTS * SPAN
    for n, ref in enumerate((core_raw, *heads)):
        row = ref.shape[0] - TAIL
        parts = [
            ref[row + k * size : row + (k + 1) * size, :].astype(F32) for k in range(3)
        ]
        packed[n * size : (n + 1) * size, :] = parts[0] + parts[1] + parts[2]
    for slot in range(SLOTS):
        base = slot_row(at, 0, slot, own_rows)
        for g in range(rows // GRAIN):
            block = (base + (start + g * GRAIN)) // BLOCK
            span = slot * SPAN + block - base // BLOCK
            here = slice(g * GRAIN, (g + 1) * GRAIN)
            row = slot * own_rows + start + g * GRAIN
            there = slice(row, row + GRAIN)
            row = slot * rows + g * GRAIN
            total = own[there, :].astype(F32) * scales[block]
            total += core_raw[there, :].astype(F32) * packed[pl.ds(span, 1), :]
            for n, raw in enumerate(raws):
                part = raw[row : row + GRAIN, :].astype(F32)
                total += part * packed[pl.ds((n + 1) * size + span, 1), :]
            if slot < 2:
                outs[0][slot, here, :] = total
            else:
                outs[slot - 1][here, :] = total


def dequant(at, scales, own, core_raw, heads, raws, own_rows, start, rows, after, carry):
    width = own.shape[1]
    part = jax.ShapeDtypeStruct((rows, width), F32)
    shapes = [jax.ShapeDtypeStruct((2, rows, width), F32), part, part]
    first, count = 8 + len(after), len(carry)

    def kernel(*refs):
        kept = refs[:8] + refs[first + count : first + count + 3] + refs[-1:]
        dequant_kernel(own_rows, start, rows, *kept)

    outs = pl.pallas_call(
        kernel,
        in_specs=[SCALARS] + [WHOLE] * 7 + [ANYWHERE] * (len(after) + count),
        out_specs=[WHOLE] * 3 + [ANYWHERE] * count,
        out_shape=shapes + [jax.ShapeDtypeStruct(x.shape, x.dtype) for x in carry],
        scratch_shapes=[pltpu.VMEM((3 * SLOTS * SPAN, width), F32)],
        input_output_aliases={first + n: 3 + n for n in range(count)},
        compiler_params=params(),
        name="dequant_sum",
    )(at, scales, own, core_raw, *heads, *raws, *after, *carry)
    return outs[:3], outs[3:]


def add(terms, after):
    def kernel(*refs):
        total = refs[0][...]
        for ref in refs[1 : len(terms)]:
            total = total + ref[...]
        refs[-1][...] = total

    return pl.pallas_call(
        kernel,
        in_specs=[WHOLE] * len(terms) + [ANYWHERE] * len(after),
        out_specs=WHOLE,
        out_shape=jax.ShapeDtypeStruct(terms[0].shape, F32),
        compiler_params=params(),
        name="add_rows",
    )(*terms, *after)


def gram_kernel(count, at, *refs):
    slabs, (out, high, low, flat) = refs[: 2 * count], refs[2 * count :]
    zed, ex, half = at[0], at[1], at[3]
    share = slabs[0].shape[1]
    row = 0
    for i, slab in enumerate(slabs):
        column = half if i % 2 == 0 else 1 - half
        lanes = pl.ds(pl.multiple_of(column * share, share), share)
        here = slice(row, row + slab.shape[0])
        h, l = split(slab[...])
        high[here, lanes] = h
        low[here, lanes] = l
        row += slab.shape[0] if i % 2 == 1 else 0

    def take(start, width):
        lanes = pl.ds(pl.multiple_of(start, HALF), width)
        return high[:, lanes], low[:, lanes]

    contract = ((0,), (0,))
    part = out.shape[1]
    for side in range(2):
        quarter = 2 * half + lax.bitwise_xor(at[2], side)
        own = take(quarter * PIECE, PIECE)
        block = dot3(own, own, contract)
        flat[0:HALF, :] = block[0:HALF, :]
        flat[HALF : HALF + HALF // 2, 0:HALF] = block[HALF : HALF + HALF // 2, HALF:]
        flat[HALF : HALF + HALF // 2, HALF:] = block[HALF + HALF // 2 :, HALF:]
        for k in range(1, 4):
            bit = lax.rem(lax.div(quarter, 1 if k == 1 else 2), 2)
            other = lax.bitwise_xor(quarter, k)
            left = jnp.where(bit == 0, quarter * PIECE, other * PIECE + HALF)
            right = jnp.where(bit == 0, other * PIECE, quarter * PIECE)
            row = PACKED + (k - 4) * HALF
            flat[row : row + HALF, :] = dot3(take(left, HALF), take(right, PIECE), contract)
        for slot in range(8):
            z = lax.bitwise_xor(zed, ORDER[slot % 4])
            x = lax.bitwise_xor(ex, slot // 4)
            base = pl.multiple_of((z * 2 + x) * part, 8)
            out[side * 8 + slot] = flat[pl.ds(base, part), :]


def gram_share(at, slabs):
    rows = sum(slab.shape[0] for slab in slabs) // 2
    width = 2 * slabs[0].shape[1]
    return pl.pallas_call(
        functools.partial(gram_kernel, len(slabs) // 2),
        in_specs=[SCALARS] + [WHOLE] * len(slabs),
        out_specs=WHOLE,
        out_shape=jax.ShapeDtypeStruct((16, PACKED // 8, PIECE), F32),
        scratch_shapes=[pltpu.VMEM((rows, width), BF16)] * 2 + [pltpu.VMEM((PACKED, PIECE), F32)],
        compiler_params=params(),
        name="gram_share",
    )(at, *slabs)


def update_kernel(scale, places, count, at, *refs):
    pieces, refs = refs[: len(places)], refs[len(places) :]
    owns, acrosses, refs = refs[:count], refs[count : 2 * count], refs[2 * count :]
    out, packed, gram, high, low = refs
    zed, ex, core, half = at[0], at[1], at[2], at[3]
    part = pieces[0].shape[1]
    for ref, slots in zip(pieces, places):
        for n, (kz, kx, kc, kf) in enumerate(slots):
            quarter = 2 * lax.bitwise_xor(half, kf) + lax.bitwise_xor(core, kc)
            chip = 2 * lax.bitwise_xor(zed, kz) + lax.bitwise_xor(ex, kx)
            row = pl.multiple_of(quarter * PACKED + chip * part, 8)
            packed[pl.ds(row, part), :] = ref[n]
    trace = jnp.zeros((1, 1), F32)
    rows = lax.broadcasted_iota(jnp.int32, (HALF, HALF), 0)
    columns = lax.broadcasted_iota(jnp.int32, (HALF, HALF), 1)

    def put(block, row, column):
        h, l = split(block)
        here = (slice(row, row + block.shape[0]), slice(column, column + block.shape[1]))
        high[here] = h
        low[here] = l

    for q in range(4):
        base, edge = q * PACKED, q * PIECE
        top = packed[base : base + HALF, :]
        bottom = packed[base + HALF : base + HALF + HALF // 2, :]
        bottom = jnp.concatenate([bottom[:, :HALF], bottom[:, HALF:]], 0)
        for block in (top[:, :HALF], bottom):
            trace += jnp.sum(jnp.where(rows == columns, block, 0.0), keepdims=True)
        put(top, edge, edge)
        put(top[:, HALF:].T, edge + HALF, edge)
        put(bottom, edge + HALF, edge + HALF)
        for k in range(1, 4):
            other = q ^ k
            if q > other:
                continue
            row = PACKED + (k - 4) * HALF
            for first, owner in ((0, q), (HALF, other)):
                block = packed[owner * PACKED + row : owner * PACKED + row + HALF, :]
                put(block, edge + first, other * PIECE)
                put(block.T, other * PIECE, edge + first)
    inv = 1.0 / (jnp.sqrt(trace) + 1e-07)
    share = owns[0].shape[1]
    contract = ((1,), (0,))

    def mine(which):
        return pl.ds(pl.multiple_of(which * share, share), share)

    unit = jnp.concatenate([own[...] for own in owns], 0) * inv
    far = jnp.concatenate([across[...] for across in acrosses], 0) * inv
    first = dot3(split(unit), (high[mine(half), :], low[mine(half), :]), contract)
    first += dot3(split(far), (high[mine(1 - half), :], low[mine(1 - half), :]), contract)
    first = first * (inv * inv)
    gram[...] = first
    second = dot3(split(first), (high[:, mine(half)], low[:, mine(half)]), contract)
    second = second * (inv * inv)
    result = 3.4445 * unit + (-4.775 * gram[:, mine(half)] + 2.0315 * second)
    out[...] = (scale * result).astype(out.dtype)


def update(at, pieces, places, owns, acrosses, scale):
    rows = sum(own.shape[0] for own in owns)
    share = owns[0].shape[1]
    width = 2 * share
    return pl.pallas_call(
        functools.partial(update_kernel, scale, places, len(owns)),
        in_specs=[SCALARS] + [WHOLE] * (len(pieces) + 2 * len(owns)),
        out_specs=WHOLE,
        out_shape=jax.ShapeDtypeStruct((rows, share), BF16),
        scratch_shapes=[
            pltpu.VMEM((4 * PACKED, PIECE), F32),
            pltpu.VMEM((rows, width), F32),
            pltpu.VMEM((width, width), BF16),
            pltpu.VMEM((width, width), BF16),
        ],
        compiler_params=params(),
        name="update",
    )(at, *pieces, *owns, *acrosses)


AXIS_BITS = {"f": 1, "c": 2, "x": 4, "z1": 8, "z2": 16}


def flip(value, *names):
    mask = sum(AXIS_BITS[name] for name in names)
    count = lax.axis_size(("dp", "fsdp"))
    return lax.ppermute(value, ("dp", "fsdp"), [(i, i ^ mask) for i in range(count)])


SIDES = (("x",), ("c", "x"))


def fast_body(partials, scales):
    values, scales = partials[0], scales.transpose(1, 0, 2)
    features, share = values.shape
    own_rows = features // lax.axis_size("dp")
    rank = lax.axis_index("dp")
    at = jnp.stack([rank // 4, rank // 2 % 2, rank % 2, lax.axis_index("fsdp")])
    unit = own_rows // sum(CHUNKS)
    spans, start = [], 0
    for size in CHUNKS:
        spans.append((start, size * unit))
        start += size * unit

    own, core_raw, *outs = pack(values, scales, at, own_rows, spans)
    core_raw = flip(core_raw, "c")

    def cross(pair):
        return [flip(out, *side) for out, side in zip(pair, SIDES)]

    outs = [outs[2 * n : 2 * n + 2] for n in range(len(spans))]
    raws = [cross(pair) for pair in outs[:2]]
    heads = raws[0]
    owns, acrosses, slabs = [], [], []
    keeps, sents, halves, grads, held = [], [], [], [], []

    def finish(n):
        grads.append(add([halves[n], flip(sents[n], "z2")], there(*GRAD_AFTER[n])))
        held.append(grads[n])
        if n in LEAVE:
            group = jnp.concatenate(held) if len(held) > 1 else grads[n]
            across = flip(group, "f")
            owns.append(group)
            acrosses.append(across)
            slabs.extend([group, across])
            held.clear()

    def there(*names):
        kinds = {"keep": keeps, "sent": sents, "half": halves, "grad": grads, "across": acrosses}
        return [kinds[name[:-1]][int(name[-1])] for name in names]

    for n, (start, rows) in enumerate(spans):
        carry = outs[n + 2] if n + 2 < len(spans) else []
        (keep, *go), carry = dequant(
            at, scales, own, core_raw, heads, raws[n], own_rows, start, rows,
            there(*SUM_AFTER[n]), carry,
        )
        if carry:
            raws.append(cross(carry))
        keeps.append(keep)
        got = [flip(part, "z1") for part in go]
        sents.append(add([keep[1], got[1]], there(*SENT_AFTER[n])))
        halves.append(keep[0] + got[0])
        if n > 0:
            finish(n - 1)
    finish(len(spans) - 1)
    shared = gram_share(at, slabs)
    core = flip(shared[8:], "c")
    got = (shared[:4] + core[:4]) + flip(shared[4:8] + core[4:], "x")
    got = got[:2] + flip(got[2:], "z1")
    piece = got[:1] + flip(got[1:], "z2")

    pair = jnp.concatenate([piece, flip(piece, "z2")])
    other = flip(pair, "z1")
    a, b = pair, other
    ax, bf = flip(a, "x"), flip(b, "f")
    near = jnp.concatenate([a, ax])
    far = jnp.concatenate([b, bf])
    near_f, far_x = flip(near, "f"), flip(far, "x")
    parts = [near, far, near_f, far_x]
    z_pair, z_other = ((0, 0), (2, 0)), ((1, 0), (3, 0))

    def places(zeds, first, second):
        return [(z, x, 0, f) for x, f in (first, second) for z, _ in zeds]

    slots = [
        places(z_pair, (0, 0), (1, 0)),
        places(z_other, (0, 0), (0, 1)),
        places(z_pair, (0, 1), (1, 1)),
        places(z_other, (1, 0), (1, 1)),
    ]
    parts += [flip(part, "c") for part in parts]
    slots += [[(z, x, 1, f) for z, x, _, f in group] for group in slots]
    scale = float(0.25 * np.sqrt(np.float32(features * 2 * share)))
    return update(at, parts, slots, owns, acrosses, scale)


def plain_body(partials, scales):
    values, scales = partials[0], scales[0]
    features, share = values.shape
    dp = lax.axis_size("dp")
    rows = values.reshape(scales.shape[0], -1, share).astype(F32) * scales[:, None, :]
    summed = lax.psum_scatter(
        rows.reshape(features, share), "dp", scatter_dimension=0, tiled=True
    )
    slab = lax.all_gather(summed, "fsdp", axis=1, tiled=True)
    width = slab.shape[1]
    highest = functools.partial(
        jnp.dot, precision=lax.Precision.HIGHEST, preferred_element_type=F32
    )
    half = lax.axis_index("fsdp")
    gram = lax.psum(highest(summed.T, slab), "dp")
    gram = lax.all_gather(gram, "fsdp", axis=0, tiled=True)
    inv = 1.0 / (jnp.sqrt(jnp.trace(gram)) + 1e-07)
    scaled = gram * (inv * inv)
    first = highest(slab * inv, scaled)
    mine = lambda value: lax.dynamic_slice_in_dim(value, half * share, share, 1)
    second = highest(first, mine(scaled))
    result = 3.4445 * (summed * inv) + (-4.775 * mine(first) + 2.0315 * second)
    return (0.25 * jnp.sqrt(F32(features * width)) * result).astype(BF16)


def solution(mesh):
    dp, fsdp = mesh.shape["dp"], mesh.shape["fsdp"]

    def run(partials, scales):
        features, width = partials.shape[1:]
        fast = (
            (dp, fsdp) == (16, 2)
            and features % (dp * GRAIN * sum(CHUNKS)) == 0
            and width == 4 * PIECE
        )
        return jax.shard_map(
            fast_body if fast else plain_body,
            mesh=mesh,
            in_specs=(P("dp", None, "fsdp"), P("dp", None, "fsdp")),
            out_specs=P("dp", "fsdp"),
            check_vma=False,
        )(partials, scales)

    return run
```

```python
import functools

import jax
import jax.numpy as jnp
import numpy as np
from jax import lax
from jax.experimental import pallas as pl
from jax.experimental.pallas import tpu as pltpu
from jax.sharding import PartitionSpec as P

BLOCK = 128
GRAIN = 16
CHUNKS = (3, 5, 4, 3)
LEAVE = (0, 1, 3)
STEPS = (
    ("sum", 0), ("halve", 0), ("sum", 1), ("halve", 1), ("finish", 0), ("sum", 2),
    ("sum", 3), ("halve", 2), ("finish", 1), ("finish", 2), ("finish", 3),
)
AFTER = {
    ("sum", 1): (("sent", 0), ("half", 0)),
    ("sum", 2): (("sent", 1), ("half", 1), ("grad", 0)),
    ("sum", 3): (("keep", 2),),
    ("halve", 2): (("keep", 3),),
    ("finish", 1): (("sent", 2), ("across", 0)),
    ("finish", 3): (("across", 1), ("grad", 2)),
}
ORDER = (0, 2, 1, 3)
PIECE = 256
HALF = PIECE // 2
PACKED = HALF + HALF // 2 + 3 * HALF
F32 = jnp.float32
BF16 = jnp.bfloat16
VMEM = 48 * 1024 * 1024
WHOLE = pl.BlockSpec(memory_space=pltpu.VMEM)
SCALARS = pl.BlockSpec(memory_space=pltpu.SMEM)
ANYWHERE = pl.BlockSpec(memory_space=pl.ANY)


def params():
    return pltpu.CompilerParams(vmem_limit_bytes=VMEM)


def split(value):
    high = value.astype(BF16)
    return high, (value - high.astype(F32)).astype(BF16)


def dot3(a, b, contract):
    dims = (contract, ((), ()))

    def one(u, v):
        return lax.dot_general(u, v, dims, preferred_element_type=F32)

    return one(a[0], b[0]) + (one(a[0], b[1]) + one(a[1], b[0]))


def slot_row(at, side, slot, own_rows):
    zed, ex, core = at[0], at[1], at[2]
    z = lax.bitwise_xor(zed, ORDER[slot])
    c = lax.bitwise_xor(core, side % 2)
    x = lax.bitwise_xor(ex, side // 2)
    return ((z * 2 + x) * 2 + c) * own_rows


SLOTS = len(ORDER)
GROUPS = {
    "halves": ((0, 1), (2,), (3,)),
    "pair": ((0, 1), (2, 3)),
    "direct": ((0,), (1,), (2,), (3,)),
}
ROUTES = ("halves", "halves", "halves", "direct")
SPAN = 4
TAIL = 3 * SLOTS * SPAN


def pack_kernel(own_rows, spans, at, values, scales, own, *refs):
    outs, gathered = refs[:-1], refs[-1]
    blocks = scales.shape[0]

    def copy(side, start, rows, out):
        for slot in range(SLOTS):
            base = pl.multiple_of(slot_row(at, side, slot, own_rows) + start, GRAIN)
            out[slot * rows : (slot + 1) * rows, :] = values[pl.ds(base, rows), :]

    def tail(side, out):
        for slot in range(SLOTS):
            first = slot_row(at, side, slot, own_rows) // BLOCK
            for n in range(SPAN):
                row = jnp.minimum(first + n, blocks - 1)
                gathered[slot * SPAN + n : slot * SPAN + n + 1, :] = scales[row]
        left = gathered[...]
        for n in range(3):
            part = left.astype(BF16)
            row = out.shape[0] - TAIL + n * SLOTS * SPAN
            out[row : row + SLOTS * SPAN, :] = part
            left = left - part.astype(F32)

    copy(0, 0, own_rows, own)
    copy(1, 0, own_rows, outs[0])
    tail(1, outs[0])
    for n, (start, rows) in enumerate(spans):
        for side in (2, 3):
            out = outs[2 * n + side - 1]
            copy(side, start, rows, out)
            if n == 0:
                tail(side, out)


def pack(values, scales, at, own_rows, spans):
    width = values.shape[1]
    lengths = [SLOTS * own_rows, SLOTS * own_rows + TAIL]
    for n, (_, rows) in enumerate(spans):
        lengths += [SLOTS * rows + (TAIL if n == 0 else 0)] * 2
    return pl.pallas_call(
        functools.partial(pack_kernel, own_rows, spans),
        in_specs=[SCALARS, WHOLE, WHOLE],
        out_specs=[WHOLE] * len(lengths),
        out_shape=[jax.ShapeDtypeStruct((rows, width), BF16) for rows in lengths],
        scratch_shapes=[pltpu.VMEM((SLOTS * SPAN, width), F32)],
        compiler_params=params(),
        name="pack_rows",
    )(at, values, scales)


def dequant_kernel(own_rows, start, rows, groups, at, scales, own, core_raw, *refs):
    heads, raws, refs = refs[:2], refs[2:4], refs[4:]
    outs, packed = refs[-1 - len(groups) : -1], refs[-1]
    size = SLOTS * SPAN
    for n, ref in enumerate((core_raw, *heads)):
        row = ref.shape[0] - TAIL
        parts = [
            ref[row + k * size : row + (k + 1) * size, :].astype(F32) for k in range(3)
        ]
        packed[n * size : (n + 1) * size, :] = parts[0] + parts[1] + parts[2]
    for slot in range(SLOTS):
        base = slot_row(at, 0, slot, own_rows)
        for g in range(rows // GRAIN):
            block = (base + (start + g * GRAIN)) // BLOCK
            span = slot * SPAN + block - base // BLOCK
            here = slice(g * GRAIN, (g + 1) * GRAIN)
            row = slot * own_rows + start + g * GRAIN
            there = slice(row, row + GRAIN)
            row = slot * rows + g * GRAIN
            total = own[there, :].astype(F32) * scales[block]
            total += core_raw[there, :].astype(F32) * packed[pl.ds(span, 1), :]
            for n, raw in enumerate(raws):
                part = raw[row : row + GRAIN, :].astype(F32)
                total += part * packed[pl.ds((n + 1) * size + span, 1), :]
            for out, group in zip(outs, groups):
                if slot in group and len(group) > 1:
                    out[group.index(slot), here, :] = total
                elif slot in group:
                    out[here, :] = total


def dequant(
    at, scales, own, core_raw, heads, raws, own_rows, start, rows, groups, after, carry
):
    width = own.shape[1]
    shapes = [
        jax.ShapeDtypeStruct((len(group), rows, width)[len(group) == 1 :], F32)
        for group in groups
    ]
    first, count, made = 8 + len(after), len(carry), len(groups)

    def kernel(*refs):
        kept = refs[:8] + refs[first + count : first + count + made] + refs[-1:]
        dequant_kernel(own_rows, start, rows, groups, *kept)

    outs = pl.pallas_call(
        kernel,
        in_specs=[SCALARS] + [WHOLE] * 7 + [ANYWHERE] * (len(after) + count),
        out_specs=[WHOLE] * made + [ANYWHERE] * count,
        out_shape=shapes + [jax.ShapeDtypeStruct(x.shape, x.dtype) for x in carry],
        scratch_shapes=[pltpu.VMEM((3 * SLOTS * SPAN, width), F32)],
        input_output_aliases={first + n: made + n for n in range(count)},
        compiler_params=params(),
        name="dequant_sum",
    )(at, scales, own, core_raw, *heads, *raws, *after, *carry)
    return outs[:made], outs[made:]


def add(terms, after):
    def kernel(*refs):
        total = refs[0][...]
        for ref in refs[1 : len(terms)]:
            total = total + ref[...]
        refs[-1][...] = total

    return pl.pallas_call(
        kernel,
        in_specs=[WHOLE] * len(terms) + [ANYWHERE] * len(after),
        out_specs=WHOLE,
        out_shape=jax.ShapeDtypeStruct(terms[0].shape, F32),
        compiler_params=params(),
        name="add_rows",
    )(*terms, *after)


def gram_kernel(count, at, *refs):
    slabs, (out, high, low, flat) = refs[: 2 * count], refs[2 * count :]
    zed, ex, half = at[0], at[1], at[3]
    share = slabs[0].shape[1]
    row = 0
    for i, slab in enumerate(slabs):
        column = half if i % 2 == 0 else 1 - half
        lanes = pl.ds(pl.multiple_of(column * share, share), share)
        here = slice(row, row + slab.shape[0])
        h, l = split(slab[...])
        high[here, lanes] = h
        low[here, lanes] = l
        row += slab.shape[0] if i % 2 == 1 else 0

    def take(start, width):
        lanes = pl.ds(pl.multiple_of(start, HALF), width)
        return high[:, lanes], low[:, lanes]

    contract = ((0,), (0,))
    part = out.shape[1]
    for side in range(2):
        quarter = 2 * half + lax.bitwise_xor(at[2], side)
        own = take(quarter * PIECE, PIECE)
        block = dot3(own, own, contract)
        flat[0:HALF, :] = block[0:HALF, :]
        flat[HALF : HALF + HALF // 2, 0:HALF] = block[HALF : HALF + HALF // 2, HALF:]
        flat[HALF : HALF + HALF // 2, HALF:] = block[HALF + HALF // 2 :, HALF:]
        for k in range(1, 4):
            bit = lax.rem(lax.div(quarter, 1 if k == 1 else 2), 2)
            other = lax.bitwise_xor(quarter, k)
            left = jnp.where(bit == 0, quarter * PIECE, other * PIECE + HALF)
            right = jnp.where(bit == 0, other * PIECE, quarter * PIECE)
            row = PACKED + (k - 4) * HALF
            flat[row : row + HALF, :] = dot3(take(left, HALF), take(right, PIECE), contract)
        for slot in range(8):
            z = lax.bitwise_xor(zed, ORDER[slot % 4])
            x = lax.bitwise_xor(ex, slot // 4)
            base = pl.multiple_of((z * 2 + x) * part, 8)
            out[side * 8 + slot] = flat[pl.ds(base, part), :]


def gram_share(at, slabs):
    rows = sum(slab.shape[0] for slab in slabs) // 2
    width = 2 * slabs[0].shape[1]
    return pl.pallas_call(
        functools.partial(gram_kernel, len(slabs) // 2),
        in_specs=[SCALARS] + [WHOLE] * len(slabs),
        out_specs=WHOLE,
        out_shape=jax.ShapeDtypeStruct((16, PACKED // 8, PIECE), F32),
        scratch_shapes=[pltpu.VMEM((rows, width), BF16)] * 2 + [pltpu.VMEM((PACKED, PIECE), F32)],
        compiler_params=params(),
        name="gram_share",
    )(at, *slabs)


def update_kernel(scale, places, count, at, *refs):
    pieces, refs = refs[: len(places)], refs[len(places) :]
    owns, acrosses, refs = refs[:count], refs[count : 2 * count], refs[2 * count :]
    out, packed, gram, high, low = refs
    zed, ex, core, half = at[0], at[1], at[2], at[3]
    part = pieces[0].shape[1]
    for ref, slots in zip(pieces, places):
        for n, (kz, kx, kc, kf) in enumerate(slots):
            quarter = 2 * lax.bitwise_xor(half, kf) + lax.bitwise_xor(core, kc)
            chip = 2 * lax.bitwise_xor(zed, kz) + lax.bitwise_xor(ex, kx)
            row = pl.multiple_of(quarter * PACKED + chip * part, 8)
            packed[pl.ds(row, part), :] = ref[n]
    trace = jnp.zeros((1, 1), F32)
    rows = lax.broadcasted_iota(jnp.int32, (HALF, HALF), 0)
    columns = lax.broadcasted_iota(jnp.int32, (HALF, HALF), 1)

    def put(block, row, column):
        h, l = split(block)
        here = (slice(row, row + block.shape[0]), slice(column, column + block.shape[1]))
        high[here] = h
        low[here] = l

    for q in range(4):
        base, edge = q * PACKED, q * PIECE
        top = packed[base : base + HALF, :]
        bottom = packed[base + HALF : base + HALF + HALF // 2, :]
        bottom = jnp.concatenate([bottom[:, :HALF], bottom[:, HALF:]], 0)
        for block in (top[:, :HALF], bottom):
            trace += jnp.sum(jnp.where(rows == columns, block, 0.0), keepdims=True)
        put(top, edge, edge)
        put(top[:, HALF:].T, edge + HALF, edge)
        put(bottom, edge + HALF, edge + HALF)
        for k in range(1, 4):
            other = q ^ k
            if q > other:
                continue
            row = PACKED + (k - 4) * HALF
            for first, owner in ((0, q), (HALF, other)):
                block = packed[owner * PACKED + row : owner * PACKED + row + HALF, :]
                put(block, edge + first, other * PIECE)
                put(block.T, other * PIECE, edge + first)
    inv = 1.0 / (jnp.sqrt(trace) + 1e-07)
    share = owns[0].shape[1]
    contract = ((1,), (0,))

    def mine(which):
        return pl.ds(pl.multiple_of(which * share, share), share)

    unit = jnp.concatenate([own[...] for own in owns], 0) * inv
    far = jnp.concatenate([across[...] for across in acrosses], 0) * inv
    first = dot3(split(unit), (high[mine(half), :], low[mine(half), :]), contract)
    first += dot3(split(far), (high[mine(1 - half), :], low[mine(1 - half), :]), contract)
    first = first * (inv * inv)
    gram[...] = first
    second = dot3(split(first), (high[:, mine(half)], low[:, mine(half)]), contract)
    second = second * (inv * inv)
    result = 3.4445 * unit + (-4.775 * gram[:, mine(half)] + 2.0315 * second)
    out[...] = (scale * result).astype(out.dtype)


def update(at, pieces, places, owns, acrosses, scale):
    rows = sum(own.shape[0] for own in owns)
    share = owns[0].shape[1]
    width = 2 * share
    return pl.pallas_call(
        functools.partial(update_kernel, scale, places, len(owns)),
        in_specs=[SCALARS] + [WHOLE] * (len(pieces) + 2 * len(owns)),
        out_specs=WHOLE,
        out_shape=jax.ShapeDtypeStruct((rows, share), BF16),
        scratch_shapes=[
            pltpu.VMEM((4 * PACKED, PIECE), F32),
            pltpu.VMEM((rows, width), F32),
            pltpu.VMEM((width, width), BF16),
            pltpu.VMEM((width, width), BF16),
        ],
        compiler_params=params(),
        name="update",
    )(at, *pieces, *owns, *acrosses)


AXIS_BITS = {"f": 1, "c": 2, "x": 4, "z1": 8, "z2": 16}


def flip(value, *names):
    mask = sum(AXIS_BITS[name] for name in names)
    count = lax.axis_size(("dp", "fsdp"))
    return lax.ppermute(value, ("dp", "fsdp"), [(i, i ^ mask) for i in range(count)])


ZEDS = (("z2",), ("z1",), ("z1", "z2"))
SIDES = (("x",), ("c", "x"))


def fast_body(partials, scales):
    values, scales = partials[0], scales.transpose(1, 0, 2)
    features, share = values.shape
    own_rows = features // lax.axis_size("dp")
    rank = lax.axis_index("dp")
    at = jnp.stack([rank // 4, rank // 2 % 2, rank % 2, lax.axis_index("fsdp")])
    unit = own_rows // sum(CHUNKS)
    spans, start = [], 0
    for size in CHUNKS:
        spans.append((start, size * unit))
        start += size * unit

    own, core_raw, *outs = pack(values, scales, at, own_rows, spans)
    core_raw = flip(core_raw, "c")

    def cross(pair):
        return [flip(out, *side) for out, side in zip(pair, SIDES)]

    outs = [outs[2 * n : 2 * n + 2] for n in range(len(spans))]
    raws = [cross(pair) for pair in outs[:2]]
    heads = raws[0]
    owns, acrosses, slabs, held = [], [], [], []
    made = {}

    def there(step, n):
        return [made[name] for name in AFTER.get((step, n), ())]

    def add_partials(n):
        start, rows = spans[n]
        carry = outs[n + 2] if n + 2 < len(spans) else []
        (keep, *go), carry = dequant(
            at, scales, own, core_raw, heads, raws[n], own_rows, start, rows,
            GROUPS[ROUTES[n]], there("sum", n), carry,
        )
        if carry:
            raws.append(cross(carry))
        made["keep", n] = keep
        if ROUTES[n] == "direct":
            made["got", n] = [flip(part, *names) for part, names in zip(go, ZEDS)]
        elif ROUTES[n] == "halves":
            made["got", n] = [flip(part, "z1") for part in go]
        else:
            made["got", n] = flip(go[0], "z1")

    def halve(n):
        keep, got = made["keep", n], made["got", n]
        made["sent", n] = add([keep[1], got[1]], there("halve", n))
        made["half", n] = keep[0] + got[0]

    def finish(n):
        if ROUTES[n] == "direct":
            terms = [made["keep", n], *made["got", n]]
        else:
            terms = [made["half", n], flip(made["sent", n], "z2")]
        made["grad", n] = add(terms, there("finish", n))
        held.append(made["grad", n])
        if n in LEAVE:
            group = jnp.concatenate(held) if len(held) > 1 else held[0]
            across = flip(group, "f")
            made["across", n] = across
            owns.append(group)
            acrosses.append(across)
            slabs.extend([group, across])
            held.clear()

    for step, n in STEPS:
        {"sum": add_partials, "halve": halve, "finish": finish}[step](n)

    shared = gram_share(at, slabs)
    core = flip(shared[8:], "c")
    got = (shared[:4] + core[:4]) + flip(shared[4:8] + core[4:], "x")
    got = got[:2] + flip(got[2:], "z1")
    piece = got[:1] + flip(got[1:], "z2")

    pair = jnp.concatenate([piece, flip(piece, "z2")])
    other = flip(pair, "z1")
    a, b = pair, other
    ax, bf = flip(a, "x"), flip(b, "f")
    near = jnp.concatenate([a, ax])
    far = jnp.concatenate([b, bf])
    near_f, far_x = flip(near, "f"), flip(far, "x")
    parts = [near, far, near_f, far_x]
    z_pair, z_other = ((0, 0), (2, 0)), ((1, 0), (3, 0))

    def places(zeds, first, second):
        return [(z, x, 0, f) for x, f in (first, second) for z, _ in zeds]

    slots = [
        places(z_pair, (0, 0), (1, 0)),
        places(z_other, (0, 0), (0, 1)),
        places(z_pair, (0, 1), (1, 1)),
        places(z_other, (1, 0), (1, 1)),
    ]
    parts += [flip(part, "c") for part in parts]
    slots += [[(z, x, 1, f) for z, x, _, f in group] for group in slots]
    scale = float(0.25 * np.sqrt(np.float32(features * 2 * share)))
    return update(at, parts, slots, owns, acrosses, scale)


def plain_body(partials, scales):
    values, scales = partials[0], scales[0]
    features, share = values.shape
    dp = lax.axis_size("dp")
    rows = values.reshape(scales.shape[0], -1, share).astype(F32) * scales[:, None, :]
    summed = lax.psum_scatter(
        rows.reshape(features, share), "dp", scatter_dimension=0, tiled=True
    )
    slab = lax.all_gather(summed, "fsdp", axis=1, tiled=True)
    width = slab.shape[1]
    highest = functools.partial(
        jnp.dot, precision=lax.Precision.HIGHEST, preferred_element_type=F32
    )
    half = lax.axis_index("fsdp")
    gram = lax.psum(highest(summed.T, slab), "dp")
    gram = lax.all_gather(gram, "fsdp", axis=0, tiled=True)
    inv = 1.0 / (jnp.sqrt(jnp.trace(gram)) + 1e-07)
    scaled = gram * (inv * inv)
    first = highest(slab * inv, scaled)
    mine = lambda value: lax.dynamic_slice_in_dim(value, half * share, share, 1)
    second = highest(first, mine(scaled))
    result = 3.4445 * (summed * inv) + (-4.775 * mine(first) + 2.0315 * second)
    return (0.25 * jnp.sqrt(F32(features * width)) * result).astype(BF16)


def solution(mesh):
    dp, fsdp = mesh.shape["dp"], mesh.shape["fsdp"]

    def run(partials, scales):
        features, width = partials.shape[1:]
        fast = (
            (dp, fsdp) == (16, 2)
            and features % (dp * GRAIN * sum(CHUNKS)) == 0
            and width == 4 * PIECE
        )
        return jax.shard_map(
            fast_body if fast else plain_body,
            mesh=mesh,
            in_specs=(P("dp", None, "fsdp"), P("dp", None, "fsdp")),
            out_specs=P("dp", "fsdp"),
            check_vma=False,
        )(partials, scales)

    return run
```

```python
import functools

import jax
import jax.numpy as jnp
import numpy as np
from jax import lax
from jax.experimental import pallas as pl
from jax.experimental.pallas import tpu as pltpu
from jax.sharding import PartitionSpec as P

BLOCK = 128
GRAIN = 16
CHUNKS = (3, 5, 4, 3)
LEAVE = (0, 1, 3)
STEPS = (
    ("sum", 0), ("halve", 0), ("sum", 1), ("halve", 1), ("finish", 0), ("sum", 2),
    ("sum", 3), ("halve", 2), ("finish", 1), ("finish", 2), ("finish", 3),
)
AFTER = {
    ("sum", 1): (("sent", 0), ("half", 0)),
    ("sum", 2): (("sent", 1), ("half", 1), ("grad", 0)),
    ("sum", 3): (("keep", 2),),
    ("halve", 2): (("keep", 3),),
    ("finish", 1): (("sent", 2), ("across", 0)),
    ("finish", 3): (("across", 1), ("grad", 2)),
}
ORDER = (0, 2, 1, 3)
PIECE = 256
HALF = PIECE // 2
PACKED = HALF + HALF // 2 + 3 * HALF
F32 = jnp.float32
BF16 = jnp.bfloat16
VMEM = 48 * 1024 * 1024
WHOLE = pl.BlockSpec(memory_space=pltpu.VMEM)
SCALARS = pl.BlockSpec(memory_space=pltpu.SMEM)
ANYWHERE = pl.BlockSpec(memory_space=pl.ANY)


def params():
    return pltpu.CompilerParams(vmem_limit_bytes=VMEM)


def split(value):
    high = value.astype(BF16)
    return high, (value - high.astype(F32)).astype(BF16)


def dot3(a, b, contract):
    dims = (contract, ((), ()))

    def one(u, v):
        return lax.dot_general(u, v, dims, preferred_element_type=F32)

    return one(a[0], b[0]) + (one(a[0], b[1]) + one(a[1], b[0]))


def slot_row(at, side, slot, own_rows):
    zed, ex, core = at[0], at[1], at[2]
    z = lax.bitwise_xor(zed, ORDER[slot])
    c = lax.bitwise_xor(core, side % 2)
    x = lax.bitwise_xor(ex, side // 2)
    return ((z * 2 + x) * 2 + c) * own_rows


SLOTS = len(ORDER)
GROUPS = {
    "halves": ((0, 1), (2,), (3,)),
    "pair": ((0, 1), (2, 3)),
    "direct": ((0,), (1,), (2,), (3,)),
}
ROUTES = ("halves", "halves", "halves", "direct")
SPAN = 4
TAIL = 3 * SLOTS * SPAN


def pack_kernel(own_rows, spans, at, values, scales, own, *refs):
    outs, (table, gathered, sem, table_sem) = refs[:-4], refs[-4:]
    blocks = table.shape[0]
    copies = []

    def copy(side, start, rows, out):
        for slot in range(SLOTS):
            base = pl.multiple_of(slot_row(at, side, slot, own_rows) + start, GRAIN)
            copies.append(
                pltpu.make_async_copy(
                    values.at[pl.ds(base, rows), :],
                    out.at[pl.ds(slot * rows, rows), :],
                    sem.at[len(copies)],
                )
            )
            copies[-1].start()

    def tail(side, out):
        for slot in range(SLOTS):
            first = slot_row(at, side, slot, own_rows) // BLOCK
            for n in range(SPAN):
                row = jnp.minimum(first + n, blocks - 1)
                gathered[slot * SPAN + n : slot * SPAN + n + 1, :] = table[row]
        left = gathered[...]
        for n in range(3):
            part = left.astype(BF16)
            row = out.shape[0] - TAIL + n * SLOTS * SPAN
            out[row : row + SLOTS * SPAN, :] = part
            left = left - part.astype(F32)

    table_copy = pltpu.make_async_copy(scales, table, table_sem)
    table_copy.start()
    for n, (start, rows) in enumerate(spans):
        for side in (2, 3):
            copy(side, start, rows, outs[2 * n + side - 1])
        if n == 0:
            copy(1, 0, own_rows, outs[0])
    copy(0, 0, own_rows, own)
    table_copy.wait()
    for side in range(1, 4):
        tail(side, outs[side - 1])
    for each in copies:
        each.wait()


def pack(values, scales, at, own_rows, spans):
    width = values.shape[1]
    lengths = [SLOTS * own_rows, SLOTS * own_rows + TAIL]
    for n, (_, rows) in enumerate(spans):
        lengths += [SLOTS * rows + (TAIL if n == 0 else 0)] * 2
    return pl.pallas_call(
        functools.partial(pack_kernel, own_rows, spans),
        in_specs=[SCALARS] + [pl.BlockSpec(memory_space=pltpu.HBM)] * 2,
        out_specs=[WHOLE] * len(lengths),
        out_shape=[jax.ShapeDtypeStruct((rows, width), BF16) for rows in lengths],
        scratch_shapes=[
            pltpu.VMEM(scales.shape, F32),
            pltpu.VMEM((SLOTS * SPAN, width), F32),
            pltpu.SemaphoreType.DMA((2 * SLOTS * (1 + len(spans)),)),
            pltpu.SemaphoreType.DMA,
        ],
        compiler_params=params(),
        name="pack_rows",
    )(at, values, scales)


def dequant_kernel(own_rows, start, rows, groups, at, scales, own, core_raw, *refs):
    heads, raws, refs = refs[:2], refs[2:4], refs[4:]
    outs, packed = refs[-1 - len(groups) : -1], refs[-1]
    size = SLOTS * SPAN
    for n, ref in enumerate((core_raw, *heads)):
        row = ref.shape[0] - TAIL
        parts = [
            ref[row + k * size : row + (k + 1) * size, :].astype(F32) for k in range(3)
        ]
        packed[n * size : (n + 1) * size, :] = parts[0] + parts[1] + parts[2]
    for slot in range(SLOTS):
        base = slot_row(at, 0, slot, own_rows)
        for g in range(rows // GRAIN):
            block = (base + (start + g * GRAIN)) // BLOCK
            span = slot * SPAN + block - base // BLOCK
            here = slice(g * GRAIN, (g + 1) * GRAIN)
            row = slot * own_rows + start + g * GRAIN
            there = slice(row, row + GRAIN)
            row = slot * rows + g * GRAIN
            total = own[there, :].astype(F32) * scales[block]
            total += core_raw[there, :].astype(F32) * packed[pl.ds(span, 1), :]
            for n, raw in enumerate(raws):
                part = raw[row : row + GRAIN, :].astype(F32)
                total += part * packed[pl.ds((n + 1) * size + span, 1), :]
            for out, group in zip(outs, groups):
                if slot in group and len(group) > 1:
                    out[group.index(slot), here, :] = total
                elif slot in group:
                    out[here, :] = total


def dequant(
    at, scales, own, core_raw, heads, raws, own_rows, start, rows, groups, after, carry
):
    width = own.shape[1]
    shapes = [
        jax.ShapeDtypeStruct((len(group), rows, width)[len(group) == 1 :], F32)
        for group in groups
    ]
    first, count, made = 8 + len(after), len(carry), len(groups)

    def kernel(*refs):
        kept = refs[:8] + refs[first + count : first + count + made] + refs[-1:]
        dequant_kernel(own_rows, start, rows, groups, *kept)

    outs = pl.pallas_call(
        kernel,
        in_specs=[SCALARS] + [WHOLE] * 7 + [ANYWHERE] * (len(after) + count),
        out_specs=[WHOLE] * made + [ANYWHERE] * count,
        out_shape=shapes + [jax.ShapeDtypeStruct(x.shape, x.dtype) for x in carry],
        scratch_shapes=[pltpu.VMEM((3 * SLOTS * SPAN, width), F32)],
        input_output_aliases={first + n: made + n for n in range(count)},
        compiler_params=params(),
        name="dequant_sum",
    )(at, scales, own, core_raw, *heads, *raws, *after, *carry)
    return outs[:made], outs[made:]


def add(terms, after):
    def kernel(*refs):
        total = refs[0][...]
        for ref in refs[1 : len(terms)]:
            total = total + ref[...]
        refs[-1][...] = total

    return pl.pallas_call(
        kernel,
        in_specs=[WHOLE] * len(terms) + [ANYWHERE] * len(after),
        out_specs=WHOLE,
        out_shape=jax.ShapeDtypeStruct(terms[0].shape, F32),
        compiler_params=params(),
        name="add_rows",
    )(*terms, *after)


def gram_kernel(count, at, *refs):
    slabs, (out, high, low, flat) = refs[: 2 * count], refs[2 * count :]
    zed, ex, half = at[0], at[1], at[3]
    share = slabs[0].shape[1]
    row = 0
    for i, slab in enumerate(slabs):
        column = half if i % 2 == 0 else 1 - half
        lanes = pl.ds(pl.multiple_of(column * share, share), share)
        here = slice(row, row + slab.shape[0])
        h, l = split(slab[...])
        high[here, lanes] = h
        low[here, lanes] = l
        row += slab.shape[0] if i % 2 == 1 else 0

    def take(start, width):
        lanes = pl.ds(pl.multiple_of(start, HALF), width)
        return high[:, lanes], low[:, lanes]

    contract = ((0,), (0,))
    part = out.shape[1]
    for side in range(2):
        quarter = 2 * half + lax.bitwise_xor(at[2], side)
        own = take(quarter * PIECE, PIECE)
        block = dot3(own, own, contract)
        flat[0:HALF, :] = block[0:HALF, :]
        flat[HALF : HALF + HALF // 2, 0:HALF] = block[HALF : HALF + HALF // 2, HALF:]
        flat[HALF : HALF + HALF // 2, HALF:] = block[HALF + HALF // 2 :, HALF:]
        for k in range(1, 4):
            bit = lax.rem(lax.div(quarter, 1 if k == 1 else 2), 2)
            other = lax.bitwise_xor(quarter, k)
            left = jnp.where(bit == 0, quarter * PIECE, other * PIECE + HALF)
            right = jnp.where(bit == 0, other * PIECE, quarter * PIECE)
            row = PACKED + (k - 4) * HALF
            flat[row : row + HALF, :] = dot3(take(left, HALF), take(right, PIECE), contract)
        for slot in range(8):
            z = lax.bitwise_xor(zed, ORDER[slot % 4])
            x = lax.bitwise_xor(ex, slot // 4)
            base = pl.multiple_of((z * 2 + x) * part, 8)
            out[side * 8 + slot] = flat[pl.ds(base, part), :]


def gram_share(at, slabs):
    rows = sum(slab.shape[0] for slab in slabs) // 2
    width = 2 * slabs[0].shape[1]
    return pl.pallas_call(
        functools.partial(gram_kernel, len(slabs) // 2),
        in_specs=[SCALARS] + [WHOLE] * len(slabs),
        out_specs=WHOLE,
        out_shape=jax.ShapeDtypeStruct((16, PACKED // 8, PIECE), F32),
        scratch_shapes=[pltpu.VMEM((rows, width), BF16)] * 2 + [pltpu.VMEM((PACKED, PIECE), F32)],
        compiler_params=params(),
        name="gram_share",
    )(at, *slabs)


def update_kernel(scale, places, count, at, *refs):
    pieces, refs = refs[: len(places)], refs[len(places) :]
    owns, acrosses, refs = refs[:count], refs[count : 2 * count], refs[2 * count :]
    out, packed, gram, high, low = refs
    zed, ex, core, half = at[0], at[1], at[2], at[3]
    part = pieces[0].shape[1]
    for ref, slots in zip(pieces, places):
        for n, (kz, kx, kc, kf) in enumerate(slots):
            quarter = 2 * lax.bitwise_xor(half, kf) + lax.bitwise_xor(core, kc)
            chip = 2 * lax.bitwise_xor(zed, kz) + lax.bitwise_xor(ex, kx)
            row = pl.multiple_of(quarter * PACKED + chip * part, 8)
            packed[pl.ds(row, part), :] = ref[n]
    trace = jnp.zeros((1, 1), F32)
    rows = lax.broadcasted_iota(jnp.int32, (HALF, HALF), 0)
    columns = lax.broadcasted_iota(jnp.int32, (HALF, HALF), 1)

    def put(block, row, column):
        h, l = split(block)
        here = (slice(row, row + block.shape[0]), slice(column, column + block.shape[1]))
        high[here] = h
        low[here] = l

    for q in range(4):
        base, edge = q * PACKED, q * PIECE
        top = packed[base : base + HALF, :]
        bottom = packed[base + HALF : base + HALF + HALF // 2, :]
        bottom = jnp.concatenate([bottom[:, :HALF], bottom[:, HALF:]], 0)
        for block in (top[:, :HALF], bottom):
            trace += jnp.sum(jnp.where(rows == columns, block, 0.0), keepdims=True)
        put(top, edge, edge)
        put(top[:, HALF:].T, edge + HALF, edge)
        put(bottom, edge + HALF, edge + HALF)
        for k in range(1, 4):
            other = q ^ k
            if q > other:
                continue
            row = PACKED + (k - 4) * HALF
            for first, owner in ((0, q), (HALF, other)):
                block = packed[owner * PACKED + row : owner * PACKED + row + HALF, :]
                put(block, edge + first, other * PIECE)
                put(block.T, other * PIECE, edge + first)
    inv = 1.0 / (jnp.sqrt(trace) + 1e-07)
    share = owns[0].shape[1]
    contract = ((1,), (0,))

    def mine(which):
        return pl.ds(pl.multiple_of(which * share, share), share)

    unit = jnp.concatenate([own[...] for own in owns], 0) * inv
    far = jnp.concatenate([across[...] for across in acrosses], 0) * inv
    first = dot3(split(unit), (high[mine(half), :], low[mine(half), :]), contract)
    first += dot3(split(far), (high[mine(1 - half), :], low[mine(1 - half), :]), contract)
    first = first * (inv * inv)
    gram[...] = first
    second = dot3(split(first), (high[:, mine(half)], low[:, mine(half)]), contract)
    second = second * (inv * inv)
    result = 3.4445 * unit + (-4.775 * gram[:, mine(half)] + 2.0315 * second)
    out[...] = (scale * result).astype(out.dtype)


def update(at, pieces, places, owns, acrosses, scale):
    rows = sum(own.shape[0] for own in owns)
    share = owns[0].shape[1]
    width = 2 * share
    return pl.pallas_call(
        functools.partial(update_kernel, scale, places, len(owns)),
        in_specs=[SCALARS] + [WHOLE] * (len(pieces) + 2 * len(owns)),
        out_specs=WHOLE,
        out_shape=jax.ShapeDtypeStruct((rows, share), BF16),
        scratch_shapes=[
            pltpu.VMEM((4 * PACKED, PIECE), F32),
            pltpu.VMEM((rows, width), F32),
            pltpu.VMEM((width, width), BF16),
            pltpu.VMEM((width, width), BF16),
        ],
        compiler_params=params(),
        name="update",
    )(at, *pieces, *owns, *acrosses)


AXIS_BITS = {"f": 1, "c": 2, "x": 4, "z1": 8, "z2": 16}


def flip(value, *names):
    mask = sum(AXIS_BITS[name] for name in names)
    count = lax.axis_size(("dp", "fsdp"))
    return lax.ppermute(value, ("dp", "fsdp"), [(i, i ^ mask) for i in range(count)])


ZEDS = (("z2",), ("z1",), ("z1", "z2"))
SIDES = (("x",), ("c", "x"))


def fast_body(partials, scales):
    values, scales = partials[0], scales.transpose(1, 0, 2)
    features, share = values.shape
    own_rows = features // lax.axis_size("dp")
    rank = lax.axis_index("dp")
    at = jnp.stack([rank // 4, rank // 2 % 2, rank % 2, lax.axis_index("fsdp")])
    unit = own_rows // sum(CHUNKS)
    spans, start = [], 0
    for size in CHUNKS:
        spans.append((start, size * unit))
        start += size * unit

    own, core_raw, *outs = pack(values, scales, at, own_rows, spans)
    core_raw = flip(core_raw, "c")

    def cross(pair):
        return [flip(out, *side) for out, side in zip(pair, SIDES)]

    outs = [outs[2 * n : 2 * n + 2] for n in range(len(spans))]
    raws = [cross(pair) for pair in outs[:2]]
    heads = raws[0]
    owns, acrosses, slabs, held = [], [], [], []
    made = {}

    def there(step, n):
        return [made[name] for name in AFTER.get((step, n), ())]

    def add_partials(n):
        start, rows = spans[n]
        carry = outs[n + 2] if n + 2 < len(spans) else []
        (keep, *go), carry = dequant(
            at, scales, own, core_raw, heads, raws[n], own_rows, start, rows,
            GROUPS[ROUTES[n]], there("sum", n), carry,
        )
        if carry:
            raws.append(cross(carry))
        made["keep", n] = keep
        if ROUTES[n] == "direct":
            made["got", n] = [flip(part, *names) for part, names in zip(go, ZEDS)]
            made["next", n] = made["got", n][1]
        elif ROUTES[n] == "halves":
            made["got", n] = [flip(part, "z1") for part in go]
        else:
            made["got", n] = flip(go[0], "z1")

    def halve(n):
        keep, got = made["keep", n], made["got", n]
        made["sent", n] = add([keep[1], got[1]], there("halve", n))
        made["half", n] = keep[0] + got[0]

    def finish(n):
        if ROUTES[n] == "direct":
            terms = [made["keep", n], *made["got", n]]
        else:
            terms = [made["half", n], flip(made["sent", n], "z2")]
        made["grad", n] = add(terms, there("finish", n))
        held.append(made["grad", n])
        if n in LEAVE:
            group = jnp.concatenate(held) if len(held) > 1 else held[0]
            across = flip(group, "f")
            made["across", n] = across
            owns.append(group)
            acrosses.append(across)
            slabs.extend([group, across])
            held.clear()

    for step, n in STEPS:
        {"sum": add_partials, "halve": halve, "finish": finish}[step](n)

    shared = gram_share(at, slabs)
    core = flip(shared[8:], "c")
    got = (shared[:4] + core[:4]) + flip(shared[4:8] + core[4:], "x")
    got = got[:2] + flip(got[2:], "z1")
    piece = got[:1] + flip(got[1:], "z2")

    pair = jnp.concatenate([piece, flip(piece, "z2")])
    other = flip(pair, "z1")
    a, b = pair, other
    ax, bf = flip(a, "x"), flip(b, "f")
    near = jnp.concatenate([a, ax])
    far = jnp.concatenate([b, bf])
    near_f, far_x = flip(near, "f"), flip(far, "x")
    parts = [near, far, near_f, far_x]
    z_pair, z_other = ((0, 0), (2, 0)), ((1, 0), (3, 0))

    def places(zeds, first, second):
        return [(z, x, 0, f) for x, f in (first, second) for z, _ in zeds]

    slots = [
        places(z_pair, (0, 0), (1, 0)),
        places(z_other, (0, 0), (0, 1)),
        places(z_pair, (0, 1), (1, 1)),
        places(z_other, (1, 0), (1, 1)),
    ]
    parts += [flip(part, "c") for part in parts]
    slots += [[(z, x, 1, f) for z, x, _, f in group] for group in slots]
    scale = float(0.25 * np.sqrt(np.float32(features * 2 * share)))
    return update(at, parts, slots, owns, acrosses, scale)


def plain_body(partials, scales):
    values, scales = partials[0], scales[0]
    features, share = values.shape
    dp = lax.axis_size("dp")
    rows = values.reshape(scales.shape[0], -1, share).astype(F32) * scales[:, None, :]
    summed = lax.psum_scatter(
        rows.reshape(features, share), "dp", scatter_dimension=0, tiled=True
    )
    slab = lax.all_gather(summed, "fsdp", axis=1, tiled=True)
    width = slab.shape[1]
    highest = functools.partial(
        jnp.dot, precision=lax.Precision.HIGHEST, preferred_element_type=F32
    )
    half = lax.axis_index("fsdp")
    gram = lax.psum(highest(summed.T, slab), "dp")
    gram = lax.all_gather(gram, "fsdp", axis=0, tiled=True)
    inv = 1.0 / (jnp.sqrt(jnp.trace(gram)) + 1e-07)
    scaled = gram * (inv * inv)
    first = highest(slab * inv, scaled)
    mine = lambda value: lax.dynamic_slice_in_dim(value, half * share, share, 1)
    second = highest(first, mine(scaled))
    result = 3.4445 * (summed * inv) + (-4.775 * mine(first) + 2.0315 * second)
    return (0.25 * jnp.sqrt(F32(features * width)) * result).astype(BF16)


def solution(mesh):
    dp, fsdp = mesh.shape["dp"], mesh.shape["fsdp"]

    def run(partials, scales):
        features, width = partials.shape[1:]
        fast = (
            (dp, fsdp) == (16, 2)
            and features % (dp * GRAIN * sum(CHUNKS)) == 0
            and width == 4 * PIECE
        )
        return jax.shard_map(
            fast_body if fast else plain_body,
            mesh=mesh,
            in_specs=(P("dp", None, "fsdp"), P("dp", None, "fsdp")),
            out_specs=P("dp", "fsdp"),
            check_vma=False,
        )(partials, scales)

    return run
```

```python
import functools

import jax
import jax.numpy as jnp
import numpy as np
from jax import lax
from jax.experimental import pallas as pl
from jax.experimental.pallas import tpu as pltpu
from jax.sharding import PartitionSpec as P

BLOCK = 128
GRAIN = 16
CHUNKS = (3, 5, 4, 3)
LEAVE = (0, 3)
STEPS = (
    ("sum", 0), ("halve", 0), ("sum", 1), ("halve", 1), ("sum", 2), ("sum", 3), ("halve", 2),
    ("finish", 0, 1), ("halve", 3), ("finish", 2), ("finish", 3),
)
AFTER = {
    ("sum", 1): (("sent", 0), ("half", 0)),
    ("sum", 2): (("sent", 1), ("half", 1)),
    ("sum", 3): (("keep", 2),),
    ("halve", 2): (("keep", 3),),
    ("finish", 0): (("sent", 2), ("next", 3)),
    ("finish", 2): (("sent", 3),),
    ("finish", 3): (("across", 0),),
}
ORDER = (0, 2, 1, 3)
PIECE = 256
HALF = PIECE // 2
PACKED = HALF + HALF // 2 + 3 * HALF
F32 = jnp.float32
BF16 = jnp.bfloat16
VMEM = 48 * 1024 * 1024
WHOLE = pl.BlockSpec(memory_space=pltpu.VMEM)
SCALARS = pl.BlockSpec(memory_space=pltpu.SMEM)
ANYWHERE = pl.BlockSpec(memory_space=pl.ANY)


def params():
    return pltpu.CompilerParams(vmem_limit_bytes=VMEM)


def split(value):
    high = value.astype(BF16)
    return high, (value - high.astype(F32)).astype(BF16)


def dot3(a, b, contract):
    dims = (contract, ((), ()))

    def one(u, v):
        return lax.dot_general(u, v, dims, preferred_element_type=F32)

    return one(a[0], b[0]) + (one(a[0], b[1]) + one(a[1], b[0]))


def slot_row(at, side, slot, own_rows):
    zed, ex, core = at[0], at[1], at[2]
    z = lax.bitwise_xor(zed, ORDER[slot])
    c = lax.bitwise_xor(core, side % 2)
    x = lax.bitwise_xor(ex, side // 2)
    return ((z * 2 + x) * 2 + c) * own_rows


SLOTS = len(ORDER)
GROUPS = {
    "halves": ((0, 1), (2,), (3,)),
    "pair": ((0, 1), (2, 3)),
    "direct": ((0,), (1,), (2,), (3,)),
}
ROUTES = ("halves", "halves", "halves", "halves")
SPAN = 4
TAIL = 3 * SLOTS * SPAN


def pack_kernel(own_rows, spans, at, values, scales, own, *refs):
    outs, gathered = refs[:-1], refs[-1]
    blocks = scales.shape[0]

    def copy(side, start, rows, out):
        for slot in range(SLOTS):
            base = pl.multiple_of(slot_row(at, side, slot, own_rows) + start, GRAIN)
            out[slot * rows : (slot + 1) * rows, :] = values[pl.ds(base, rows), :]

    def tail(side, out):
        for slot in range(SLOTS):
            first = slot_row(at, side, slot, own_rows) // BLOCK
            for n in range(SPAN):
                row = jnp.minimum(first + n, blocks - 1)
                gathered[slot * SPAN + n : slot * SPAN + n + 1, :] = scales[row]
        left = gathered[...]
        for n in range(3):
            part = left.astype(BF16)
            row = out.shape[0] - TAIL + n * SLOTS * SPAN
            out[row : row + SLOTS * SPAN, :] = part
            left = left - part.astype(F32)

    copy(0, 0, own_rows, own)
    copy(1, 0, own_rows, outs[0])
    tail(1, outs[0])
    for n, (start, rows) in enumerate(spans):
        for side in (2, 3):
            out = outs[2 * n + side - 1]
            copy(side, start, rows, out)
            if n == 0:
                tail(side, out)


def pack(values, scales, at, own_rows, spans):
    width = values.shape[1]
    lengths = [SLOTS * own_rows, SLOTS * own_rows + TAIL]
    for n, (_, rows) in enumerate(spans):
        lengths += [SLOTS * rows + (TAIL if n == 0 else 0)] * 2
    return pl.pallas_call(
        functools.partial(pack_kernel, own_rows, spans),
        in_specs=[SCALARS, WHOLE, WHOLE],
        out_specs=[WHOLE] * len(lengths),
        out_shape=[jax.ShapeDtypeStruct((rows, width), BF16) for rows in lengths],
        scratch_shapes=[pltpu.VMEM((SLOTS * SPAN, width), F32)],
        compiler_params=params(),
        name="pack_rows",
    )(at, values, scales)


def dequant_kernel(own_rows, start, rows, groups, at, scales, own, core_raw, *refs):
    heads, raws, refs = refs[:2], refs[2:4], refs[4:]
    outs, packed = refs[-1 - len(groups) : -1], refs[-1]
    size = SLOTS * SPAN
    for n, ref in enumerate((core_raw, *heads)):
        row = ref.shape[0] - TAIL
        parts = [
            ref[row + k * size : row + (k + 1) * size, :].astype(F32) for k in range(3)
        ]
        packed[n * size : (n + 1) * size, :] = parts[0] + parts[1] + parts[2]
    for slot in range(SLOTS):
        base = slot_row(at, 0, slot, own_rows)
        for g in range(rows // GRAIN):
            block = (base + (start + g * GRAIN)) // BLOCK
            span = slot * SPAN + block - base // BLOCK
            here = slice(g * GRAIN, (g + 1) * GRAIN)
            row = slot * own_rows + start + g * GRAIN
            there = slice(row, row + GRAIN)
            row = slot * rows + g * GRAIN
            total = own[there, :].astype(F32) * scales[block]
            total += core_raw[there, :].astype(F32) * packed[pl.ds(span, 1), :]
            for n, raw in enumerate(raws):
                part = raw[row : row + GRAIN, :].astype(F32)
                total += part * packed[pl.ds((n + 1) * size + span, 1), :]
            for out, group in zip(outs, groups):
                if slot in group and len(group) > 1:
                    out[group.index(slot), here, :] = total
                elif slot in group:
                    out[here, :] = total


def dequant(
    at, scales, own, core_raw, heads, raws, own_rows, start, rows, groups, after, carry
):
    width = own.shape[1]
    shapes = [
        jax.ShapeDtypeStruct((len(group), rows, width)[len(group) == 1 :], F32)
        for group in groups
    ]
    first, count, made = 8 + len(after), len(carry), len(groups)

    def kernel(*refs):
        kept = refs[:8] + refs[first + count : first + count + made] + refs[-1:]
        dequant_kernel(own_rows, start, rows, groups, *kept)

    outs = pl.pallas_call(
        kernel,
        in_specs=[SCALARS] + [WHOLE] * 7 + [ANYWHERE] * (len(after) + count),
        out_specs=[WHOLE] * made + [ANYWHERE] * count,
        out_shape=shapes + [jax.ShapeDtypeStruct(x.shape, x.dtype) for x in carry],
        scratch_shapes=[pltpu.VMEM((3 * SLOTS * SPAN, width), F32)],
        input_output_aliases={first + n: made + n for n in range(count)},
        compiler_params=params(),
        name="dequant_sum",
    )(at, scales, own, core_raw, *heads, *raws, *after, *carry)
    return outs[:made], outs[made:]


def add(terms, after):
    def kernel(*refs):
        total = refs[0][...]
        for ref in refs[1 : len(terms)]:
            total = total + ref[...]
        refs[-1][...] = total

    return pl.pallas_call(
        kernel,
        in_specs=[WHOLE] * len(terms) + [ANYWHERE] * len(after),
        out_specs=WHOLE,
        out_shape=jax.ShapeDtypeStruct(terms[0].shape, F32),
        compiler_params=params(),
        name="add_rows",
    )(*terms, *after)


def gram_kernel(count, at, *refs):
    slabs, (out, high, low, flat) = refs[: 2 * count], refs[2 * count :]
    zed, ex, half = at[0], at[1], at[3]
    share = slabs[0].shape[1]
    row = 0
    for i, slab in enumerate(slabs):
        column = half if i % 2 == 0 else 1 - half
        lanes = pl.ds(pl.multiple_of(column * share, share), share)
        here = slice(row, row + slab.shape[0])
        h, l = split(slab[...])
        high[here, lanes] = h
        low[here, lanes] = l
        row += slab.shape[0] if i % 2 == 1 else 0

    def take(start, width):
        lanes = pl.ds(pl.multiple_of(start, HALF), width)
        return high[:, lanes], low[:, lanes]

    contract = ((0,), (0,))
    part = out.shape[1]
    for side in range(2):
        quarter = 2 * half + lax.bitwise_xor(at[2], side)
        own = take(quarter * PIECE, PIECE)
        block = dot3(own, own, contract)
        flat[0:HALF, :] = block[0:HALF, :]
        flat[HALF : HALF + HALF // 2, 0:HALF] = block[HALF : HALF + HALF // 2, HALF:]
        flat[HALF : HALF + HALF // 2, HALF:] = block[HALF + HALF // 2 :, HALF:]
        for k in range(1, 4):
            bit = lax.rem(lax.div(quarter, 1 if k == 1 else 2), 2)
            other = lax.bitwise_xor(quarter, k)
            left = jnp.where(bit == 0, quarter * PIECE, other * PIECE + HALF)
            right = jnp.where(bit == 0, other * PIECE, quarter * PIECE)
            row = PACKED + (k - 4) * HALF
            flat[row : row + HALF, :] = dot3(take(left, HALF), take(right, PIECE), contract)
        for slot in range(8):
            z = lax.bitwise_xor(zed, ORDER[slot % 4])
            x = lax.bitwise_xor(ex, slot // 4)
            base = pl.multiple_of((z * 2 + x) * part, 8)
            out[side * 8 + slot] = flat[pl.ds(base, part), :]


def gram_share(at, slabs):
    rows = sum(slab.shape[0] for slab in slabs) // 2
    width = 2 * slabs[0].shape[1]
    return pl.pallas_call(
        functools.partial(gram_kernel, len(slabs) // 2),
        in_specs=[SCALARS] + [WHOLE] * len(slabs),
        out_specs=WHOLE,
        out_shape=jax.ShapeDtypeStruct((16, PACKED // 8, PIECE), F32),
        scratch_shapes=[pltpu.VMEM((rows, width), BF16)] * 2 + [pltpu.VMEM((PACKED, PIECE), F32)],
        compiler_params=params(),
        name="gram_share",
    )(at, *slabs)


def update_kernel(scale, places, count, at, *refs):
    pieces, refs = refs[: len(places)], refs[len(places) :]
    owns, acrosses, refs = refs[:count], refs[count : 2 * count], refs[2 * count :]
    out, packed, gram, high, low = refs
    zed, ex, core, half = at[0], at[1], at[2], at[3]
    part = pieces[0].shape[1]
    for ref, slots in zip(pieces, places):
        for n, (kz, kx, kc, kf) in enumerate(slots):
            quarter = 2 * lax.bitwise_xor(half, kf) + lax.bitwise_xor(core, kc)
            chip = 2 * lax.bitwise_xor(zed, kz) + lax.bitwise_xor(ex, kx)
            row = pl.multiple_of(quarter * PACKED + chip * part, 8)
            packed[pl.ds(row, part), :] = ref[n]
    trace = jnp.zeros((1, 1), F32)
    rows = lax.broadcasted_iota(jnp.int32, (HALF, HALF), 0)
    columns = lax.broadcasted_iota(jnp.int32, (HALF, HALF), 1)

    def put(block, row, column):
        h, l = split(block)
        here = (slice(row, row + block.shape[0]), slice(column, column + block.shape[1]))
        high[here] = h
        low[here] = l

    for q in range(4):
        base, edge = q * PACKED, q * PIECE
        top = packed[base : base + HALF, :]
        bottom = packed[base + HALF : base + HALF + HALF // 2, :]
        bottom = jnp.concatenate([bottom[:, :HALF], bottom[:, HALF:]], 0)
        for block in (top[:, :HALF], bottom):
            trace += jnp.sum(jnp.where(rows == columns, block, 0.0), keepdims=True)
        put(top, edge, edge)
        put(top[:, HALF:].T, edge + HALF, edge)
        put(bottom, edge + HALF, edge + HALF)
        for k in range(1, 4):
            other = q ^ k
            if q > other:
                continue
            row = PACKED + (k - 4) * HALF
            for first, owner in ((0, q), (HALF, other)):
                block = packed[owner * PACKED + row : owner * PACKED + row + HALF, :]
                put(block, edge + first, other * PIECE)
                put(block.T, other * PIECE, edge + first)
    inv = 1.0 / (jnp.sqrt(trace) + 1e-07)
    share = owns[0].shape[1]
    contract = ((1,), (0,))

    def mine(which):
        return pl.ds(pl.multiple_of(which * share, share), share)

    unit = jnp.concatenate([own[...] for own in owns], 0) * inv
    far = jnp.concatenate([across[...] for across in acrosses], 0) * inv
    first = dot3(split(unit), (high[mine(half), :], low[mine(half), :]), contract)
    first += dot3(split(far), (high[mine(1 - half), :], low[mine(1 - half), :]), contract)
    first = first * (inv * inv)
    gram[...] = first
    second = dot3(split(first), (high[:, mine(half)], low[:, mine(half)]), contract)
    second = second * (inv * inv)
    result = 3.4445 * unit + (-4.775 * gram[:, mine(half)] + 2.0315 * second)
    out[...] = (scale * result).astype(out.dtype)


def update(at, pieces, places, owns, acrosses, scale):
    rows = sum(own.shape[0] for own in owns)
    share = owns[0].shape[1]
    width = 2 * share
    return pl.pallas_call(
        functools.partial(update_kernel, scale, places, len(owns)),
        in_specs=[SCALARS] + [WHOLE] * (len(pieces) + 2 * len(owns)),
        out_specs=WHOLE,
        out_shape=jax.ShapeDtypeStruct((rows, share), BF16),
        scratch_shapes=[
            pltpu.VMEM((4 * PACKED, PIECE), F32),
            pltpu.VMEM((rows, width), F32),
            pltpu.VMEM((width, width), BF16),
            pltpu.VMEM((width, width), BF16),
        ],
        compiler_params=params(),
        name="update",
    )(at, *pieces, *owns, *acrosses)


AXIS_BITS = {"f": 1, "c": 2, "x": 4, "z1": 8, "z2": 16}


def flip(value, *names):
    mask = sum(AXIS_BITS[name] for name in names)
    count = lax.axis_size(("dp", "fsdp"))
    return lax.ppermute(value, ("dp", "fsdp"), [(i, i ^ mask) for i in range(count)])


ZEDS = (("z2",), ("z1",), ("z1", "z2"))
SIDES = (("x",), ("c", "x"))


def fast_body(partials, scales):
    values, scales = partials[0], scales.transpose(1, 0, 2)
    features, share = values.shape
    own_rows = features // lax.axis_size("dp")
    rank = lax.axis_index("dp")
    at = jnp.stack([rank // 4, rank // 2 % 2, rank % 2, lax.axis_index("fsdp")])
    unit = own_rows // sum(CHUNKS)
    spans, start = [], 0
    for size in CHUNKS:
        spans.append((start, size * unit))
        start += size * unit

    own, core_raw, *outs = pack(values, scales, at, own_rows, spans)
    core_raw = flip(core_raw, "c")

    def cross(pair):
        return [flip(out, *side) for out, side in zip(pair, SIDES)]

    outs = [outs[2 * n : 2 * n + 2] for n in range(len(spans))]
    raws = [cross(pair) for pair in outs[:2]]
    heads = raws[0]
    owns, acrosses, slabs, held = [], [], [], []
    made = {}

    def there(step, n):
        return [made[name] for name in AFTER.get((step, n), ())]

    def add_partials(n):
        start, rows = spans[n]
        carry = outs[n + 2] if n + 2 < len(spans) else []
        (keep, *go), carry = dequant(
            at, scales, own, core_raw, heads, raws[n], own_rows, start, rows,
            GROUPS[ROUTES[n]], there("sum", n), carry,
        )
        if carry:
            raws.append(cross(carry))
        made["keep", n] = keep
        if ROUTES[n] == "direct":
            made["got", n] = [flip(part, *names) for part, names in zip(go, ZEDS)]
            made["next", n] = made["got", n][1]
        elif ROUTES[n] == "halves":
            made["got", n] = [flip(part, "z1") for part in go]
            made["next", n] = made["got", n][1]
        else:
            made["got", n] = flip(go[0], "z1")

    def halve(n):
        keep, got = made["keep", n], made["got", n]
        made["sent", n] = add([keep[1], got[1]], there("halve", n))
        made["half", n] = keep[0] + got[0]

    def finish(*chunks):
        if ROUTES[chunks[0]] == "direct":
            terms = [made["keep", chunks[0]], *made["got", chunks[0]]]
        else:
            halves, sent = (
                jnp.concatenate([made[kind, n] for n in chunks]) for kind in ("half", "sent")
            )
            terms = [halves, flip(sent, "z2")]
        made["grad", chunks[0]] = add(terms, there("finish", chunks[0]))
        held.append(made["grad", chunks[0]])
        if chunks[0] in LEAVE:
            group = jnp.concatenate(held)
            across = flip(group, "f")
            made["across", chunks[0]] = across
            owns.append(group)
            acrosses.append(across)
            slabs.extend([group, across])
            held.clear()

    for step, *chunks in STEPS:
        {"sum": add_partials, "halve": halve, "finish": finish}[step](*chunks)

    shared = gram_share(at, slabs)
    core = flip(shared[8:], "c")
    got = (shared[:4] + core[:4]) + flip(shared[4:8] + core[4:], "x")
    got = got[:2] + flip(got[2:], "z1")
    piece = got[:1] + flip(got[1:], "z2")

    pair = jnp.concatenate([piece, flip(piece, "z2")])
    other = flip(pair, "z1")
    a, b = pair, other
    ax, bf = flip(a, "x"), flip(b, "f")
    near = jnp.concatenate([a, ax])
    far = jnp.concatenate([b, bf])
    near_f, far_x = flip(near, "f"), flip(far, "x")
    parts = [near, far, near_f, far_x]
    z_pair, z_other = ((0, 0), (2, 0)), ((1, 0), (3, 0))

    def places(zeds, first, second):
        return [(z, x, 0, f) for x, f in (first, second) for z, _ in zeds]

    slots = [
        places(z_pair, (0, 0), (1, 0)),
        places(z_other, (0, 0), (0, 1)),
        places(z_pair, (0, 1), (1, 1)),
        places(z_other, (1, 0), (1, 1)),
    ]
    parts += [flip(part, "c") for part in parts]
    slots += [[(z, x, 1, f) for z, x, _, f in group] for group in slots]
    scale = float(0.25 * np.sqrt(np.float32(features * 2 * share)))
    return update(at, parts, slots, owns, acrosses, scale)


def plain_body(partials, scales):
    values, scales = partials[0], scales[0]
    features, share = values.shape
    dp = lax.axis_size("dp")
    rows = values.reshape(scales.shape[0], -1, share).astype(F32) * scales[:, None, :]
    summed = lax.psum_scatter(
        rows.reshape(features, share), "dp", scatter_dimension=0, tiled=True
    )
    slab = lax.all_gather(summed, "fsdp", axis=1, tiled=True)
    width = slab.shape[1]
    highest = functools.partial(
        jnp.dot, precision=lax.Precision.HIGHEST, preferred_element_type=F32
    )
    half = lax.axis_index("fsdp")
    gram = lax.psum(highest(summed.T, slab), "dp")
    gram = lax.all_gather(gram, "fsdp", axis=0, tiled=True)
    inv = 1.0 / (jnp.sqrt(jnp.trace(gram)) + 1e-07)
    scaled = gram * (inv * inv)
    first = highest(slab * inv, scaled)
    mine = lambda value: lax.dynamic_slice_in_dim(value, half * share, share, 1)
    second = highest(first, mine(scaled))
    result = 3.4445 * (summed * inv) + (-4.775 * mine(first) + 2.0315 * second)
    return (0.25 * jnp.sqrt(F32(features * width)) * result).astype(BF16)


def solution(mesh):
    dp, fsdp = mesh.shape["dp"], mesh.shape["fsdp"]

    def run(partials, scales):
        features, width = partials.shape[1:]
        fast = (
            (dp, fsdp) == (16, 2)
            and features % (dp * GRAIN * sum(CHUNKS)) == 0
            and width == 4 * PIECE
        )
        return jax.shard_map(
            fast_body if fast else plain_body,
            mesh=mesh,
            in_specs=(P("dp", None, "fsdp"), P("dp", None, "fsdp")),
            out_specs=P("dp", "fsdp"),
            check_vma=False,
        )(partials, scales)

    return run
```

```python
import functools

import jax
import jax.numpy as jnp
import numpy as np
from jax import lax
from jax.experimental import pallas as pl
from jax.experimental.pallas import tpu as pltpu
from jax.sharding import PartitionSpec as P

BLOCK = 128
GRAIN = 16
CHUNKS = (3, 5, 4, 3)
LEAVE = (0, 1, 3)
STEPS = (
    ("sum", 0), ("halve", 0), ("sum", 1), ("halve", 1), ("finish", 0), ("sum", 2),
    ("sum", 3), ("halve", 2), ("finish", 1), ("finish", 2), ("finish", 3),
)
AFTER = {
    ("sum", 1): (("sent", 0), ("half", 0)),
    ("sum", 2): (("sent", 1), ("half", 1), ("grad", 0)),
    ("sum", 3): (("keep", 2),),
    ("halve", 2): (("keep", 3),),
    ("finish", 1): (("sent", 2), ("across", 0)),
    ("finish", 3): (("across", 1), ("grad", 2)),
}
ORDER = (0, 2, 1, 3)
PIECE = 256
HALF = PIECE // 2
PACKED = HALF + HALF // 2 + 3 * HALF
F32 = jnp.float32
BF16 = jnp.bfloat16
VMEM = 48 * 1024 * 1024
WHOLE = pl.BlockSpec(memory_space=pltpu.VMEM)
SCALARS = pl.BlockSpec(memory_space=pltpu.SMEM)
ANYWHERE = pl.BlockSpec(memory_space=pl.ANY)


def params():
    return pltpu.CompilerParams(vmem_limit_bytes=VMEM)


def split(value):
    high = value.astype(BF16)
    return high, (value - high.astype(F32)).astype(BF16)


def dot3(a, b, contract):
    dims = (contract, ((), ()))

    def one(u, v):
        return lax.dot_general(u, v, dims, preferred_element_type=F32)

    return one(a[0], b[0]) + (one(a[0], b[1]) + one(a[1], b[0]))


def slot_row(at, side, slot, own_rows):
    zed, ex, core = at[0], at[1], at[2]
    z = lax.bitwise_xor(zed, ORDER[slot])
    c = lax.bitwise_xor(core, side % 2)
    x = lax.bitwise_xor(ex, side // 2)
    return ((z * 2 + x) * 2 + c) * own_rows


SLOTS = len(ORDER)
GROUPS = {
    "halves": ((0, 1), (2,), (3,)),
    "pair": ((0, 1), (2, 3)),
    "direct": ((0,), (1,), (2,), (3,)),
}
ROUTES = ("halves", "halves", "halves", "direct")
SPAN = 4
TAIL = 3 * SLOTS * SPAN


def pack_kernel(own_rows, spans, at, values, scales, own, *refs):
    outs, gathered = refs[:-1], refs[-1]
    blocks = scales.shape[0]

    def copy(side, start, rows, out):
        for slot in range(SLOTS):
            base = pl.multiple_of(slot_row(at, side, slot, own_rows) + start, GRAIN)
            out[slot * rows : (slot + 1) * rows, :] = values[pl.ds(base, rows), :]

    def tail(side, out):
        for slot in range(SLOTS):
            first = slot_row(at, side, slot, own_rows) // BLOCK
            for n in range(SPAN):
                row = jnp.minimum(first + n, blocks - 1)
                gathered[slot * SPAN + n : slot * SPAN + n + 1, :] = scales[row]
        left = gathered[...]
        for n in range(3):
            part = left.astype(BF16)
            row = out.shape[0] - TAIL + n * SLOTS * SPAN
            out[row : row + SLOTS * SPAN, :] = part
            left = left - part.astype(F32)

    copy(0, 0, own_rows, own)
    copy(1, 0, own_rows, outs[0])
    tail(1, outs[0])
    for n, (start, rows) in enumerate(spans):
        for side in (2, 3):
            out = outs[2 * n + side - 1]
            copy(side, start, rows, out)
            if n == 0:
                tail(side, out)


def pack(values, scales, at, own_rows, spans):
    width = values.shape[1]
    lengths = [SLOTS * own_rows, SLOTS * own_rows + TAIL]
    for n, (_, rows) in enumerate(spans):
        lengths += [SLOTS * rows + (TAIL if n == 0 else 0)] * 2
    return pl.pallas_call(
        functools.partial(pack_kernel, own_rows, spans),
        in_specs=[SCALARS, WHOLE, WHOLE],
        out_specs=[WHOLE] * len(lengths),
        out_shape=[jax.ShapeDtypeStruct((rows, width), BF16) for rows in lengths],
        scratch_shapes=[pltpu.VMEM((SLOTS * SPAN, width), F32)],
        compiler_params=params(),
        name="pack_rows",
    )(at, values, scales)


def dequant_kernel(own_rows, start, rows, groups, at, scales, own, core_raw, *refs):
    heads, raws, refs = refs[:2], refs[2:4], refs[4:]
    outs, packed = refs[-1 - len(groups) : -1], refs[-1]
    size = SLOTS * SPAN
    for n, ref in enumerate((core_raw, *heads)):
        row = ref.shape[0] - TAIL
        parts = [
            ref[row + k * size : row + (k + 1) * size, :].astype(F32) for k in range(3)
        ]
        packed[n * size : (n + 1) * size, :] = parts[0] + parts[1] + parts[2]
    for slot in range(SLOTS):
        base = slot_row(at, 0, slot, own_rows)
        for g in range(rows // GRAIN):
            block = (base + (start + g * GRAIN)) // BLOCK
            span = slot * SPAN + block - base // BLOCK
            here = slice(g * GRAIN, (g + 1) * GRAIN)
            row = slot * own_rows + start + g * GRAIN
            there = slice(row, row + GRAIN)
            row = slot * rows + g * GRAIN
            total = own[there, :].astype(F32) * scales[block]
            total += core_raw[there, :].astype(F32) * packed[pl.ds(span, 1), :]
            for n, raw in enumerate(raws):
                part = raw[row : row + GRAIN, :].astype(F32)
                total += part * packed[pl.ds((n + 1) * size + span, 1), :]
            for out, group in zip(outs, groups):
                if slot in group and len(group) > 1:
                    out[group.index(slot), here, :] = total
                elif slot in group:
                    out[here, :] = total


def dequant(
    at, scales, own, core_raw, heads, raws, own_rows, start, rows, groups, after, carry
):
    width = own.shape[1]
    shapes = [
        jax.ShapeDtypeStruct((len(group), rows, width)[len(group) == 1 :], F32)
        for group in groups
    ]
    first, count, made = 8 + len(after), len(carry), len(groups)

    def kernel(*refs):
        kept = refs[:8] + refs[first + count : first + count + made] + refs[-1:]
        dequant_kernel(own_rows, start, rows, groups, *kept)

    outs = pl.pallas_call(
        kernel,
        in_specs=[SCALARS] + [WHOLE] * 7 + [ANYWHERE] * (len(after) + count),
        out_specs=[WHOLE] * made + [ANYWHERE] * count,
        out_shape=shapes + [jax.ShapeDtypeStruct(x.shape, x.dtype) for x in carry],
        scratch_shapes=[pltpu.VMEM((3 * SLOTS * SPAN, width), F32)],
        input_output_aliases={first + n: made + n for n in range(count)},
        compiler_params=params(),
        name="dequant_sum",
    )(at, scales, own, core_raw, *heads, *raws, *after, *carry)
    return outs[:made], outs[made:]


def add(terms, after):
    def kernel(*refs):
        total = refs[0][...]
        for ref in refs[1 : len(terms)]:
            total = total + ref[...]
        refs[-1][...] = total

    return pl.pallas_call(
        kernel,
        in_specs=[WHOLE] * len(terms) + [ANYWHERE] * len(after),
        out_specs=WHOLE,
        out_shape=jax.ShapeDtypeStruct(terms[0].shape, F32),
        compiler_params=params(),
        name="add_rows",
    )(*terms, *after)


def gram_kernel(side, count, at, *refs):
    slabs, (out, high, low, flat) = refs[: 2 * count], refs[-4:]
    zed, ex, half = at[0], at[1], at[3]
    share = slabs[0].shape[1]
    row = 0
    for i, slab in enumerate(slabs):
        column = half if i % 2 == 0 else 1 - half
        lanes = pl.ds(pl.multiple_of(column * share, share), share)
        here = slice(row, row + slab.shape[0])
        h, l = split(slab[...])
        high[here, lanes] = h
        low[here, lanes] = l
        row += slab.shape[0] if i % 2 == 1 else 0

    def take(start, width):
        lanes = pl.ds(pl.multiple_of(start, HALF), width)
        return high[:, lanes], low[:, lanes]

    contract = ((0,), (0,))
    part = out.shape[1]
    quarter = 2 * half + lax.bitwise_xor(at[2], side)
    own = take(quarter * PIECE, PIECE)
    block = dot3(own, own, contract)
    flat[0:HALF, :] = block[0:HALF, :]
    flat[HALF : HALF + HALF // 2, 0:HALF] = block[HALF : HALF + HALF // 2, HALF:]
    flat[HALF : HALF + HALF // 2, HALF:] = block[HALF + HALF // 2 :, HALF:]
    for k in range(1, 4):
        bit = lax.rem(lax.div(quarter, 1 if k == 1 else 2), 2)
        other = lax.bitwise_xor(quarter, k)
        left = jnp.where(bit == 0, quarter * PIECE, other * PIECE + HALF)
        right = jnp.where(bit == 0, other * PIECE, quarter * PIECE)
        row = PACKED + (k - 4) * HALF
        flat[row : row + HALF, :] = dot3(take(left, HALF), take(right, PIECE), contract)
    for slot in range(8):
        z = lax.bitwise_xor(zed, ORDER[slot % 4])
        x = lax.bitwise_xor(ex, slot // 4)
        base = pl.multiple_of((z * 2 + x) * part, 8)
        out[slot] = flat[pl.ds(base, part), :]


def gram_share(at, side, slabs, after):
    rows = sum(slab.shape[0] for slab in slabs) // 2
    width = 2 * slabs[0].shape[1]
    return pl.pallas_call(
        functools.partial(gram_kernel, side, len(slabs) // 2),
        in_specs=[SCALARS] + [WHOLE] * len(slabs) + [ANYWHERE] * len(after),
        out_specs=WHOLE,
        out_shape=jax.ShapeDtypeStruct((8, PACKED // 8, PIECE), F32),
        scratch_shapes=[pltpu.VMEM((rows, width), BF16)] * 2 + [pltpu.VMEM((PACKED, PIECE), F32)],
        compiler_params=params(),
        name="gram_share",
    )(at, *slabs, *after)


def update_kernel(scale, places, count, at, *refs):
    pieces, refs = refs[: len(places)], refs[len(places) :]
    owns, acrosses, refs = refs[:count], refs[count : 2 * count], refs[2 * count :]
    out, packed, gram, high, low = refs
    zed, ex, core, half = at[0], at[1], at[2], at[3]
    part = pieces[0].shape[1]
    for ref, slots in zip(pieces, places):
        for n, (kz, kx, kc, kf) in enumerate(slots):
            quarter = 2 * lax.bitwise_xor(half, kf) + lax.bitwise_xor(core, kc)
            chip = 2 * lax.bitwise_xor(zed, kz) + lax.bitwise_xor(ex, kx)
            row = pl.multiple_of(quarter * PACKED + chip * part, 8)
            packed[pl.ds(row, part), :] = ref[n]
    trace = jnp.zeros((1, 1), F32)
    rows = lax.broadcasted_iota(jnp.int32, (HALF, HALF), 0)
    columns = lax.broadcasted_iota(jnp.int32, (HALF, HALF), 1)

    def put(block, row, column):
        h, l = split(block)
        here = (slice(row, row + block.shape[0]), slice(column, column + block.shape[1]))
        high[here] = h
        low[here] = l

    for q in range(4):
        base, edge = q * PACKED, q * PIECE
        top = packed[base : base + HALF, :]
        bottom = packed[base + HALF : base + HALF + HALF // 2, :]
        bottom = jnp.concatenate([bottom[:, :HALF], bottom[:, HALF:]], 0)
        for block in (top[:, :HALF], bottom):
            trace += jnp.sum(jnp.where(rows == columns, block, 0.0), keepdims=True)
        put(top, edge, edge)
        put(top[:, HALF:].T, edge + HALF, edge)
        put(bottom, edge + HALF, edge + HALF)
        for k in range(1, 4):
            other = q ^ k
            if q > other:
                continue
            row = PACKED + (k - 4) * HALF
            for first, owner in ((0, q), (HALF, other)):
                block = packed[owner * PACKED + row : owner * PACKED + row + HALF, :]
                put(block, edge + first, other * PIECE)
                put(block.T, other * PIECE, edge + first)
    inv = 1.0 / (jnp.sqrt(trace) + 1e-07)
    share = owns[0].shape[1]
    contract = ((1,), (0,))

    def mine(which):
        return pl.ds(pl.multiple_of(which * share, share), share)

    unit = jnp.concatenate([own[...] for own in owns], 0) * inv
    far = jnp.concatenate([across[...] for across in acrosses], 0) * inv
    first = dot3(split(unit), (high[mine(half), :], low[mine(half), :]), contract)
    first += dot3(split(far), (high[mine(1 - half), :], low[mine(1 - half), :]), contract)
    first = first * (inv * inv)
    gram[...] = first
    second = dot3(split(first), (high[:, mine(half)], low[:, mine(half)]), contract)
    second = second * (inv * inv)
    result = 3.4445 * unit + (-4.775 * gram[:, mine(half)] + 2.0315 * second)
    out[...] = (scale * result).astype(out.dtype)


def update(at, pieces, places, owns, acrosses, scale):
    rows = sum(own.shape[0] for own in owns)
    share = owns[0].shape[1]
    width = 2 * share
    return pl.pallas_call(
        functools.partial(update_kernel, scale, places, len(owns)),
        in_specs=[SCALARS] + [WHOLE] * (len(pieces) + 2 * len(owns)),
        out_specs=WHOLE,
        out_shape=jax.ShapeDtypeStruct((rows, share), BF16),
        scratch_shapes=[
            pltpu.VMEM((4 * PACKED, PIECE), F32),
            pltpu.VMEM((rows, width), F32),
            pltpu.VMEM((width, width), BF16),
            pltpu.VMEM((width, width), BF16),
        ],
        compiler_params=params(),
        name="update",
    )(at, *pieces, *owns, *acrosses)


AXIS_BITS = {"f": 1, "c": 2, "x": 4, "z1": 8, "z2": 16}


def flip(value, *names):
    mask = sum(AXIS_BITS[name] for name in names)
    count = lax.axis_size(("dp", "fsdp"))
    return lax.ppermute(value, ("dp", "fsdp"), [(i, i ^ mask) for i in range(count)])


ZEDS = (("z2",), ("z1",), ("z1", "z2"))
SIDES = (("x",), ("c", "x"))


def fast_body(partials, scales):
    values, scales = partials[0], scales.transpose(1, 0, 2)
    features, share = values.shape
    own_rows = features // lax.axis_size("dp")
    rank = lax.axis_index("dp")
    at = jnp.stack([rank // 4, rank // 2 % 2, rank % 2, lax.axis_index("fsdp")])
    unit = own_rows // sum(CHUNKS)
    spans, start = [], 0
    for size in CHUNKS:
        spans.append((start, size * unit))
        start += size * unit

    own, core_raw, *outs = pack(values, scales, at, own_rows, spans)
    core_raw = flip(core_raw, "c")

    def cross(pair):
        return [flip(out, *side) for out, side in zip(pair, SIDES)]

    outs = [outs[2 * n : 2 * n + 2] for n in range(len(spans))]
    raws = [cross(pair) for pair in outs[:2]]
    heads = raws[0]
    owns, acrosses, slabs, held = [], [], [], []
    made = {}

    def there(step, n):
        return [made[name] for name in AFTER.get((step, n), ())]

    def add_partials(n):
        start, rows = spans[n]
        carry = outs[n + 2] if n + 2 < len(spans) else []
        (keep, *go), carry = dequant(
            at, scales, own, core_raw, heads, raws[n], own_rows, start, rows,
            GROUPS[ROUTES[n]], there("sum", n), carry,
        )
        if carry:
            raws.append(cross(carry))
        made["keep", n] = keep
        if ROUTES[n] == "direct":
            made["got", n] = [flip(part, *names) for part, names in zip(go, ZEDS)]
        elif ROUTES[n] == "halves":
            made["got", n] = [flip(part, "z1") for part in go]
        else:
            made["got", n] = flip(go[0], "z1")

    def halve(n):
        keep, got = made["keep", n], made["got", n]
        made["sent", n] = add([keep[1], got[1]], there("halve", n))
        made["half", n] = keep[0] + got[0]

    def finish(n):
        if ROUTES[n] == "direct":
            terms = [made["keep", n], *made["got", n]]
        else:
            terms = [made["half", n], flip(made["sent", n], "z2")]
        made["grad", n] = add(terms, there("finish", n))
        held.append(made["grad", n])
        if n in LEAVE:
            group = jnp.concatenate(held) if len(held) > 1 else held[0]
            across = flip(group, "f")
            made["across", n] = across
            owns.append(group)
            acrosses.append(across)
            slabs.extend([group, across])
            held.clear()

    for step, n in STEPS:
        {"sum": add_partials, "halve": halve, "finish": finish}[step](n)

    far_core = gram_share(at, 1, slabs, [])
    core = flip(far_core, "c")
    shared = gram_share(at, 0, slabs, [far_core])
    got = (shared[:4] + core[:4]) + flip(shared[4:] + core[4:], "x")
    got = got[:2] + flip(got[2:], "z1")
    pair = got + flip(got, "z2")[::-1]
    other = flip(pair, "z1")
    a, b = pair, other
    ax, bf = flip(a, "x"), flip(b, "f")
    near = jnp.concatenate([a, ax])
    far = jnp.concatenate([b, bf])
    near_f, far_x = flip(near, "f"), flip(far, "x")
    parts = [near, far, near_f, far_x]
    z_pair, z_other = ((0, 0), (2, 0)), ((1, 0), (3, 0))

    def places(zeds, first, second):
        return [(z, x, 0, f) for x, f in (first, second) for z, _ in zeds]

    slots = [
        places(z_pair, (0, 0), (1, 0)),
        places(z_other, (0, 0), (0, 1)),
        places(z_pair, (0, 1), (1, 1)),
        places(z_other, (1, 0), (1, 1)),
    ]
    parts += [flip(part, "c") for part in parts]
    slots += [[(z, x, 1, f) for z, x, _, f in group] for group in slots]
    scale = float(0.25 * np.sqrt(np.float32(features * 2 * share)))
    return update(at, parts, slots, owns, acrosses, scale)


def plain_body(partials, scales):
    values, scales = partials[0], scales[0]
    features, share = values.shape
    dp = lax.axis_size("dp")
    rows = values.reshape(scales.shape[0], -1, share).astype(F32) * scales[:, None, :]
    summed = lax.psum_scatter(
        rows.reshape(features, share), "dp", scatter_dimension=0, tiled=True
    )
    slab = lax.all_gather(summed, "fsdp", axis=1, tiled=True)
    width = slab.shape[1]
    highest = functools.partial(
        jnp.dot, precision=lax.Precision.HIGHEST, preferred_element_type=F32
    )
    half = lax.axis_index("fsdp")
    gram = lax.psum(highest(summed.T, slab), "dp")
    gram = lax.all_gather(gram, "fsdp", axis=0, tiled=True)
    inv = 1.0 / (jnp.sqrt(jnp.trace(gram)) + 1e-07)
    scaled = gram * (inv * inv)
    first = highest(slab * inv, scaled)
    mine = lambda value: lax.dynamic_slice_in_dim(value, half * share, share, 1)
    second = highest(first, mine(scaled))
    result = 3.4445 * (summed * inv) + (-4.775 * mine(first) + 2.0315 * second)
    return (0.25 * jnp.sqrt(F32(features * width)) * result).astype(BF16)


def solution(mesh):
    dp, fsdp = mesh.shape["dp"], mesh.shape["fsdp"]

    def run(partials, scales):
        features, width = partials.shape[1:]
        fast = (
            (dp, fsdp) == (16, 2)
            and features % (dp * GRAIN * sum(CHUNKS)) == 0
            and width == 4 * PIECE
        )
        return jax.shard_map(
            fast_body if fast else plain_body,
            mesh=mesh,
            in_specs=(P("dp", None, "fsdp"), P("dp", None, "fsdp")),
            out_specs=P("dp", "fsdp"),
            check_vma=False,
        )(partials, scales)

    return run
```

```python
import functools

import jax
import jax.numpy as jnp
import numpy as np
from jax import lax
from jax.experimental import pallas as pl
from jax.experimental.pallas import tpu as pltpu
from jax.sharding import PartitionSpec as P

BLOCK = 128
GRAIN = 16
CHUNKS = (3, 5, 4, 3)
LEAVE = (0, 1, 3)
STEPS = (
    ("sum", 0), ("halve", 0), ("sum", 1), ("halve", 1), ("finish", 0), ("sum", 2),
    ("sum", 3), ("halve", 2), ("finish", 1), ("finish", 2), ("finish", 3),
)
AFTER = {
    ("sum", 1): (("sent", 0), ("half", 0)),
    ("sum", 2): (("sent", 1), ("half", 1), ("grad", 0)),
    ("sum", 3): (("keep", 2),),
    ("halve", 2): (("keep", 3),),
    ("finish", 1): (("sent", 2), ("across", 0)),
    ("finish", 3): (("across", 1), ("grad", 2)),
}
ORDER = (0, 2, 1, 3)
PIECE = 256
HALF = PIECE // 2
NEAR = HALF + HALF // 2 + HALF
CROSS = 2 * HALF
PACKED = NEAR + CROSS
F32 = jnp.float32
BF16 = jnp.bfloat16
VMEM = 48 * 1024 * 1024
WHOLE = pl.BlockSpec(memory_space=pltpu.VMEM)
SCALARS = pl.BlockSpec(memory_space=pltpu.SMEM)
ANYWHERE = pl.BlockSpec(memory_space=pl.ANY)


def params():
    return pltpu.CompilerParams(vmem_limit_bytes=VMEM)


def split(value):
    high = value.astype(BF16)
    return high, (value - high.astype(F32)).astype(BF16)


def dot3(a, b, contract):
    dims = (contract, ((), ()))

    def one(u, v):
        return lax.dot_general(u, v, dims, preferred_element_type=F32)

    return one(a[0], b[0]) + (one(a[0], b[1]) + one(a[1], b[0]))


def slot_row(at, side, slot, own_rows):
    zed, ex, core = at[0], at[1], at[2]
    z = lax.bitwise_xor(zed, ORDER[slot])
    c = lax.bitwise_xor(core, side % 2)
    x = lax.bitwise_xor(ex, side // 2)
    return ((z * 2 + x) * 2 + c) * own_rows


SLOTS = len(ORDER)
GROUPS = {
    "halves": ((0, 1), (2,), (3,)),
    "pair": ((0, 1), (2, 3)),
    "direct": ((0,), (1,), (2,), (3,)),
}
ROUTES = ("halves", "halves", "halves", "direct")
SPAN = 4
TAIL = 3 * SLOTS * SPAN


def pack_kernel(own_rows, spans, at, values, scales, own, *refs):
    outs, gathered = refs[:-1], refs[-1]
    blocks = scales.shape[0]

    def copy(side, start, rows, out):
        for slot in range(SLOTS):
            base = pl.multiple_of(slot_row(at, side, slot, own_rows) + start, GRAIN)
            out[slot * rows : (slot + 1) * rows, :] = values[pl.ds(base, rows), :]

    def tail(side, out):
        for slot in range(SLOTS):
            first = slot_row(at, side, slot, own_rows) // BLOCK
            for n in range(SPAN):
                row = jnp.minimum(first + n, blocks - 1)
                gathered[slot * SPAN + n : slot * SPAN + n + 1, :] = scales[row]
        left = gathered[...]
        for n in range(3):
            part = left.astype(BF16)
            row = out.shape[0] - TAIL + n * SLOTS * SPAN
            out[row : row + SLOTS * SPAN, :] = part
            left = left - part.astype(F32)

    copy(0, 0, own_rows, own)
    copy(1, 0, own_rows, outs[0])
    tail(1, outs[0])
    for n, (start, rows) in enumerate(spans):
        for side in (2, 3):
            out = outs[2 * n + side - 1]
            copy(side, start, rows, out)
            if n == 0:
                tail(side, out)


def pack(values, scales, at, own_rows, spans):
    width = values.shape[1]
    lengths = [SLOTS * own_rows, SLOTS * own_rows + TAIL]
    for n, (_, rows) in enumerate(spans):
        lengths += [SLOTS * rows + (TAIL if n == 0 else 0)] * 2
    return pl.pallas_call(
        functools.partial(pack_kernel, own_rows, spans),
        in_specs=[SCALARS, WHOLE, WHOLE],
        out_specs=[WHOLE] * len(lengths),
        out_shape=[jax.ShapeDtypeStruct((rows, width), BF16) for rows in lengths],
        scratch_shapes=[pltpu.VMEM((SLOTS * SPAN, width), F32)],
        compiler_params=params(),
        name="pack_rows",
    )(at, values, scales)


def dequant_kernel(own_rows, start, rows, groups, at, scales, own, core_raw, *refs):
    heads, raws, refs = refs[:2], refs[2:4], refs[4:]
    outs, packed = refs[-1 - len(groups) : -1], refs[-1]
    size = SLOTS * SPAN
    for n, ref in enumerate((core_raw, *heads)):
        row = ref.shape[0] - TAIL
        parts = [
            ref[row + k * size : row + (k + 1) * size, :].astype(F32) for k in range(3)
        ]
        packed[n * size : (n + 1) * size, :] = parts[0] + parts[1] + parts[2]
    for slot in range(SLOTS):
        base = slot_row(at, 0, slot, own_rows)
        for g in range(rows // GRAIN):
            block = (base + (start + g * GRAIN)) // BLOCK
            span = slot * SPAN + block - base // BLOCK
            here = slice(g * GRAIN, (g + 1) * GRAIN)
            row = slot * own_rows + start + g * GRAIN
            there = slice(row, row + GRAIN)
            row = slot * rows + g * GRAIN
            total = own[there, :].astype(F32) * scales[block]
            total += core_raw[there, :].astype(F32) * packed[pl.ds(span, 1), :]
            for n, raw in enumerate(raws):
                part = raw[row : row + GRAIN, :].astype(F32)
                total += part * packed[pl.ds((n + 1) * size + span, 1), :]
            for out, group in zip(outs, groups):
                if slot in group and len(group) > 1:
                    out[group.index(slot), here, :] = total
                elif slot in group:
                    out[here, :] = total


def dequant(
    at, scales, own, core_raw, heads, raws, own_rows, start, rows, groups, after, carry
):
    width = own.shape[1]
    shapes = [
        jax.ShapeDtypeStruct((len(group), rows, width)[len(group) == 1 :], F32)
        for group in groups
    ]
    first, count, made = 8 + len(after), len(carry), len(groups)

    def kernel(*refs):
        kept = refs[:8] + refs[first + count : first + count + made] + refs[-1:]
        dequant_kernel(own_rows, start, rows, groups, *kept)

    outs = pl.pallas_call(
        kernel,
        in_specs=[SCALARS] + [WHOLE] * 7 + [ANYWHERE] * (len(after) + count),
        out_specs=[WHOLE] * made + [ANYWHERE] * count,
        out_shape=shapes + [jax.ShapeDtypeStruct(x.shape, x.dtype) for x in carry],
        scratch_shapes=[pltpu.VMEM((3 * SLOTS * SPAN, width), F32)],
        input_output_aliases={first + n: made + n for n in range(count)},
        compiler_params=params(),
        name="dequant_sum",
    )(at, scales, own, core_raw, *heads, *raws, *after, *carry)
    return outs[:made], outs[made:]


def add(terms, after):
    def kernel(*refs):
        total = refs[0][...]
        for ref in refs[1 : len(terms)]:
            total = total + ref[...]
        refs[-1][...] = total

    return pl.pallas_call(
        kernel,
        in_specs=[WHOLE] * len(terms) + [ANYWHERE] * len(after),
        out_specs=WHOLE,
        out_shape=jax.ShapeDtypeStruct(terms[0].shape, F32),
        compiler_params=params(),
        name="add_rows",
    )(*terms, *after)


def put_rows(slabs, high, low, column):
    row = 0
    for slab in slabs:
        here, share = slice(row, row + slab.shape[0]), slab.shape[1]
        high[here, column : column + share], low[here, column : column + share] = split(slab[...])
        row += slab.shape[0]


def put_slots(at, flat, out):
    part = out.shape[1]
    for slot in range(8):
        z = lax.bitwise_xor(at[0], ORDER[slot % 4])
        x = lax.bitwise_xor(at[1], slot // 4)
        out[slot] = flat[pl.ds(pl.multiple_of((z * 2 + x) * part, 8), part), :]


def near_kernel(count, at, *refs):
    slabs, outs, (high, low, flat) = refs[:count], refs[count : count + 2], refs[-3:]
    put_rows(slabs, high, low, 0)

    def take(start, width):
        lanes = pl.ds(pl.multiple_of(start, HALF), width)
        return high[:, lanes], low[:, lanes]

    contract = ((0,), (0,))
    for side, out in enumerate(outs):
        core = lax.bitwise_xor(at[2], side)
        own = take(core * PIECE, PIECE)
        block = dot3(own, own, contract)
        flat[0:HALF, :] = block[0:HALF, :]
        flat[HALF : HALF + HALF // 2, 0:HALF] = block[HALF : HALF + HALF // 2, HALF:]
        flat[HALF : HALF + HALF // 2, HALF:] = block[HALF + HALF // 2 :, HALF:]
        left = take(core * HALF, HALF)
        flat[NEAR - HALF :, :] = dot3(left, take(PIECE, PIECE), contract)
        put_slots(at, flat, out)


def cross_kernel(count, at, *refs):
    slabs, outs, (high, low, flat) = refs[: 2 * count], refs[-5:-3], refs[-3:]
    share = slabs[0].shape[1]
    put_rows(slabs[:count], high, low, 0)
    put_rows(slabs[count:], high, low, share)

    def take(start, width):
        lanes = pl.ds(pl.multiple_of(start, HALF), width)
        return high[:, lanes], low[:, lanes]

    contract = ((0,), (0,))
    half = at[3]
    for side, out in enumerate(outs):
        core = lax.bitwise_xor(at[2], side)
        for k in range(2):
            mine = core * PIECE
            other = share + lax.bitwise_xor(core, k) * PIECE
            left = jnp.where(half == 0, mine, other + HALF)
            right = jnp.where(half == 0, other, mine)
            flat[k * HALF : (k + 1) * HALF, :] = dot3(
                take(left, HALF), take(right, PIECE), contract
            )
        put_slots(at, flat, out)


def gram_part(kernel, at, slabs, count, packed, name, after):
    rows = sum(slab.shape[0] for slab in slabs[:count])
    width = slabs[0].shape[1] * (len(slabs) // count)
    return pl.pallas_call(
        functools.partial(kernel, count),
        in_specs=[SCALARS] + [WHOLE] * len(slabs) + [ANYWHERE] * len(after),
        out_specs=[WHOLE] * 2,
        out_shape=[jax.ShapeDtypeStruct((8, packed // 8, PIECE), F32)] * 2,
        scratch_shapes=[pltpu.VMEM((rows, width), BF16)] * 2 + [pltpu.VMEM((packed, PIECE), F32)],
        compiler_params=params(),
        name=name,
    )(at, *slabs, *after)


def update_kernel(scale, places, count, at, *refs):
    pieces, refs = refs[: len(places)], refs[len(places) :]
    owns, acrosses, refs = refs[:count], refs[count : 2 * count], refs[2 * count :]
    out, packed, gram, high, low = refs
    zed, ex, core, half = at[0], at[1], at[2], at[3]
    part, near = pieces[0].shape[1], NEAR // 8
    for ref, slots in zip(pieces, places):
        for n, (kz, kx, kc, kf) in enumerate(slots):
            quarter = 2 * lax.bitwise_xor(half, kf) + lax.bitwise_xor(core, kc)
            chip = 2 * lax.bitwise_xor(zed, kz) + lax.bitwise_xor(ex, kx)
            base = quarter * PACKED
            for start, size, first in ((0, near, 0), (near, part - near, NEAR)):
                row = pl.multiple_of(base + first + chip * size, 8)
                packed[pl.ds(row, size), :] = ref[n, start : start + size, :]
    trace = jnp.zeros((1, 1), F32)
    rows = lax.broadcasted_iota(jnp.int32, (HALF, HALF), 0)
    columns = lax.broadcasted_iota(jnp.int32, (HALF, HALF), 1)

    def put(block, row, column):
        h, l = split(block)
        here = (slice(row, row + block.shape[0]), slice(column, column + block.shape[1]))
        high[here] = h
        low[here] = l

    for q in range(4):
        base, edge = q * PACKED, q * PIECE
        top = packed[base : base + HALF, :]
        bottom = packed[base + HALF : base + HALF + HALF // 2, :]
        bottom = jnp.concatenate([bottom[:, :HALF], bottom[:, HALF:]], 0)
        for block in (top[:, :HALF], bottom):
            trace += jnp.sum(jnp.where(rows == columns, block, 0.0), keepdims=True)
        put(top, edge, edge)
        put(top[:, HALF:].T, edge + HALF, edge)
        put(bottom, edge + HALF, edge + HALF)
        for k in range(1, 4):
            other = q ^ k
            if q > other:
                continue
            row = PACKED + (k - 4) * HALF
            for first, owner in ((0, q), (HALF, other)):
                block = packed[owner * PACKED + row : owner * PACKED + row + HALF, :]
                put(block, edge + first, other * PIECE)
                put(block.T, other * PIECE, edge + first)
    inv = 1.0 / (jnp.sqrt(trace) + 1e-07)
    share = owns[0].shape[1]
    contract = ((1,), (0,))

    def mine(which):
        return pl.ds(pl.multiple_of(which * share, share), share)

    unit = jnp.concatenate([own[...] for own in owns], 0) * inv
    far = jnp.concatenate([across[...] for across in acrosses], 0) * inv
    first = dot3(split(unit), (high[mine(half), :], low[mine(half), :]), contract)
    first += dot3(split(far), (high[mine(1 - half), :], low[mine(1 - half), :]), contract)
    first = first * (inv * inv)
    gram[...] = first
    second = dot3(split(first), (high[:, mine(half)], low[:, mine(half)]), contract)
    second = second * (inv * inv)
    result = 3.4445 * unit + (-4.775 * gram[:, mine(half)] + 2.0315 * second)
    out[...] = (scale * result).astype(out.dtype)


def update(at, pieces, places, owns, acrosses, scale):
    rows = sum(own.shape[0] for own in owns)
    share = owns[0].shape[1]
    width = 2 * share
    return pl.pallas_call(
        functools.partial(update_kernel, scale, places, len(owns)),
        in_specs=[SCALARS] + [WHOLE] * (len(pieces) + 2 * len(owns)),
        out_specs=WHOLE,
        out_shape=jax.ShapeDtypeStruct((rows, share), BF16),
        scratch_shapes=[
            pltpu.VMEM((4 * PACKED, PIECE), F32),
            pltpu.VMEM((rows, width), F32),
            pltpu.VMEM((width, width), BF16),
            pltpu.VMEM((width, width), BF16),
        ],
        compiler_params=params(),
        name="update",
    )(at, *pieces, *owns, *acrosses)


AXIS_BITS = {"f": 1, "c": 2, "x": 4, "z1": 8, "z2": 16}


def flip(value, *names):
    mask = sum(AXIS_BITS[name] for name in names)
    count = lax.axis_size(("dp", "fsdp"))
    return lax.ppermute(value, ("dp", "fsdp"), [(i, i ^ mask) for i in range(count)])


ZEDS = (("z2",), ("z1",), ("z1", "z2"))
SIDES = (("x",), ("c", "x"))


def fast_body(partials, scales):
    values, scales = partials[0], scales.transpose(1, 0, 2)
    features, share = values.shape
    own_rows = features // lax.axis_size("dp")
    rank = lax.axis_index("dp")
    at = jnp.stack([rank // 4, rank // 2 % 2, rank % 2, lax.axis_index("fsdp")])
    unit = own_rows // sum(CHUNKS)
    spans, start = [], 0
    for size in CHUNKS:
        spans.append((start, size * unit))
        start += size * unit

    own, core_raw, *outs = pack(values, scales, at, own_rows, spans)
    core_raw = flip(core_raw, "c")

    def cross(pair):
        return [flip(out, *side) for out, side in zip(pair, SIDES)]

    outs = [outs[2 * n : 2 * n + 2] for n in range(len(spans))]
    raws = [cross(pair) for pair in outs[:2]]
    heads = raws[0]
    owns, acrosses, held = [], [], []
    made = {}

    def there(step, n):
        return [made[name] for name in AFTER.get((step, n), ())]

    def add_partials(n):
        start, rows = spans[n]
        carry = outs[n + 2] if n + 2 < len(spans) else []
        (keep, *go), carry = dequant(
            at, scales, own, core_raw, heads, raws[n], own_rows, start, rows,
            GROUPS[ROUTES[n]], there("sum", n), carry,
        )
        if carry:
            raws.append(cross(carry))
        made["keep", n] = keep
        if ROUTES[n] == "direct":
            made["got", n] = [flip(part, *names) for part, names in zip(go, ZEDS)]
        elif ROUTES[n] == "halves":
            made["got", n] = [flip(part, "z1") for part in go]
        else:
            made["got", n] = flip(go[0], "z1")

    def halve(n):
        keep, got = made["keep", n], made["got", n]
        made["sent", n] = add([keep[1], got[1]], there("halve", n))
        made["half", n] = keep[0] + got[0]

    def finish(n):
        if ROUTES[n] == "direct":
            terms = [made["keep", n], *made["got", n]]
        else:
            terms = [made["half", n], flip(made["sent", n], "z2")]
        made["grad", n] = add(terms, there("finish", n))
        held.append(made["grad", n])
        if n in LEAVE:
            group = jnp.concatenate(held) if len(held) > 1 else held[0]
            across = flip(group, "f")
            made["across", n] = across
            owns.append(group)
            acrosses.append(across)
            held.clear()

    for step, n in STEPS:
        {"sum": add_partials, "halve": halve, "finish": finish}[step](n)

    count = len(owns)
    near, far_near = gram_part(near_kernel, at, owns, count, NEAR, "gram_near", [])
    core = flip(far_near, "c")
    near_sent = add([near[4:], core[4:]], [])
    near_got = flip(near_sent, "x")
    cross_own, far_cross = gram_part(
        cross_kernel, at, owns + acrosses, count, CROSS, "gram_cross", [near_sent]
    )
    cross_core = [flip(far_cross[4:], "c"), flip(far_cross[:4], "c")]
    cross_got = flip(add([cross_own[4:], cross_core[0]], [near_got]), "x")
    got = jnp.concatenate(
        [near[:4] + core[:4] + near_got, cross_own[:4] + cross_core[1] + cross_got], 1
    )
    got = got[:2] + flip(got[2:], "z1")
    pair = got + flip(got, "z2")[::-1]
    other = flip(pair, "z1")
    a, b = pair, other
    ax, bf = flip(a, "x"), flip(b, "f")
    near = jnp.concatenate([a, ax])
    far = jnp.concatenate([b, bf])
    near_f, far_x = flip(near, "f"), flip(far, "x")
    parts = [near, far, near_f, far_x]
    z_pair, z_other = ((0, 0), (2, 0)), ((1, 0), (3, 0))

    def places(zeds, first, second):
        return [(z, x, 0, f) for x, f in (first, second) for z, _ in zeds]

    slots = [
        places(z_pair, (0, 0), (1, 0)),
        places(z_other, (0, 0), (0, 1)),
        places(z_pair, (0, 1), (1, 1)),
        places(z_other, (1, 0), (1, 1)),
    ]
    parts += [flip(part, "c") for part in parts]
    slots += [[(z, x, 1, f) for z, x, _, f in group] for group in slots]
    scale = float(0.25 * np.sqrt(np.float32(features * 2 * share)))
    return update(at, parts, slots, owns, acrosses, scale)


def plain_body(partials, scales):
    values, scales = partials[0], scales[0]
    features, share = values.shape
    dp = lax.axis_size("dp")
    rows = values.reshape(scales.shape[0], -1, share).astype(F32) * scales[:, None, :]
    summed = lax.psum_scatter(
        rows.reshape(features, share), "dp", scatter_dimension=0, tiled=True
    )
    slab = lax.all_gather(summed, "fsdp", axis=1, tiled=True)
    width = slab.shape[1]
    highest = functools.partial(
        jnp.dot, precision=lax.Precision.HIGHEST, preferred_element_type=F32
    )
    half = lax.axis_index("fsdp")
    gram = lax.psum(highest(summed.T, slab), "dp")
    gram = lax.all_gather(gram, "fsdp", axis=0, tiled=True)
    inv = 1.0 / (jnp.sqrt(jnp.trace(gram)) + 1e-07)
    scaled = gram * (inv * inv)
    first = highest(slab * inv, scaled)
    mine = lambda value: lax.dynamic_slice_in_dim(value, half * share, share, 1)
    second = highest(first, mine(scaled))
    result = 3.4445 * (summed * inv) + (-4.775 * mine(first) + 2.0315 * second)
    return (0.25 * jnp.sqrt(F32(features * width)) * result).astype(BF16)


def solution(mesh):
    dp, fsdp = mesh.shape["dp"], mesh.shape["fsdp"]

    def run(partials, scales):
        features, width = partials.shape[1:]
        fast = (
            (dp, fsdp) == (16, 2)
            and features % (dp * GRAIN * sum(CHUNKS)) == 0
            and width == 4 * PIECE
        )
        return jax.shard_map(
            fast_body if fast else plain_body,
            mesh=mesh,
            in_specs=(P("dp", None, "fsdp"), P("dp", None, "fsdp")),
            out_specs=P("dp", "fsdp"),
            check_vma=False,
        )(partials, scales)

    return run
```

```python
import functools

import jax
import jax.numpy as jnp
import numpy as np
from jax import lax
from jax.experimental import pallas as pl
from jax.experimental.pallas import tpu as pltpu
from jax.sharding import PartitionSpec as P

BLOCK = 128
GRAIN = 16
CHUNKS = (3, 5, 4, 3)
LEAVE = (0, 1, 3)
STEPS = (
    ("sum", 0), ("halve", 0), ("sum", 1), ("halve", 1), ("finish", 0), ("sum", 2),
    ("sum", 3), ("halve", 2), ("finish", 1), ("finish", 2), ("finish", 3),
)
AFTER = {
    ("sum", 1): (("sent", 0), ("half", 0)),
    ("sum", 2): (("sent", 1), ("half", 1), ("grad", 0)),
    ("sum", 3): (("keep", 2),),
    ("halve", 2): (("keep", 3),),
    ("finish", 1): (("sent", 2), ("across", 0)),
    ("finish", 3): (("across", 1), ("grad", 2)),
}
ORDER = (0, 2, 1, 3)
PIECE = 256
HALF = PIECE // 2
NEAR = HALF + HALF // 2 + HALF
CROSS = 2 * HALF
PACKED = NEAR + CROSS
F32 = jnp.float32
BF16 = jnp.bfloat16
VMEM = 48 * 1024 * 1024
WHOLE = pl.BlockSpec(memory_space=pltpu.VMEM)
SCALARS = pl.BlockSpec(memory_space=pltpu.SMEM)
ANYWHERE = pl.BlockSpec(memory_space=pl.ANY)


def params():
    return pltpu.CompilerParams(vmem_limit_bytes=VMEM)


def split(value):
    high = value.astype(BF16)
    return high, (value - high.astype(F32)).astype(BF16)


def dot3(a, b, contract):
    dims = (contract, ((), ()))

    def one(u, v):
        return lax.dot_general(u, v, dims, preferred_element_type=F32)

    return one(a[0], b[0]) + (one(a[0], b[1]) + one(a[1], b[0]))


def slot_row(at, side, slot, own_rows):
    zed, ex, core = at[0], at[1], at[2]
    z = lax.bitwise_xor(zed, ORDER[slot])
    c = lax.bitwise_xor(core, side % 2)
    x = lax.bitwise_xor(ex, side // 2)
    return ((z * 2 + x) * 2 + c) * own_rows


SLOTS = len(ORDER)
GROUPS = {
    "halves": ((0, 1), (2,), (3,)),
    "pair": ((0, 1), (2, 3)),
    "direct": ((0,), (1,), (2,), (3,)),
}
ROUTES = ("halves", "halves", "halves", "direct")
SPAN = 4
TAIL = 3 * SLOTS * SPAN


def pack_kernel(own_rows, spans, at, values, scales, own, *refs):
    outs, gathered = refs[:-1], refs[-1]
    blocks = scales.shape[0]

    def copy(side, start, rows, out):
        for slot in range(SLOTS):
            base = pl.multiple_of(slot_row(at, side, slot, own_rows) + start, GRAIN)
            out[slot * rows : (slot + 1) * rows, :] = values[pl.ds(base, rows), :]

    def tail(side, out):
        for slot in range(SLOTS):
            first = slot_row(at, side, slot, own_rows) // BLOCK
            for n in range(SPAN):
                row = jnp.minimum(first + n, blocks - 1)
                gathered[slot * SPAN + n : slot * SPAN + n + 1, :] = scales[row]
        left = gathered[...]
        for n in range(3):
            part = left.astype(BF16)
            row = out.shape[0] - TAIL + n * SLOTS * SPAN
            out[row : row + SLOTS * SPAN, :] = part
            left = left - part.astype(F32)

    copy(0, 0, own_rows, own)
    copy(1, 0, own_rows, outs[0])
    tail(1, outs[0])
    for n, (start, rows) in enumerate(spans):
        for side in (2, 3):
            out = outs[2 * n + side - 1]
            copy(side, start, rows, out)
            if n == 0:
                tail(side, out)


def pack(values, scales, at, own_rows, spans):
    width = values.shape[1]
    lengths = [SLOTS * own_rows, SLOTS * own_rows + TAIL]
    for n, (_, rows) in enumerate(spans):
        lengths += [SLOTS * rows + (TAIL if n == 0 else 0)] * 2
    return pl.pallas_call(
        functools.partial(pack_kernel, own_rows, spans),
        in_specs=[SCALARS, WHOLE, WHOLE],
        out_specs=[WHOLE] * len(lengths),
        out_shape=[jax.ShapeDtypeStruct((rows, width), BF16) for rows in lengths],
        scratch_shapes=[pltpu.VMEM((SLOTS * SPAN, width), F32)],
        compiler_params=params(),
        name="pack_rows",
    )(at, values, scales)


def dequant_kernel(own_rows, start, rows, groups, at, scales, own, core_raw, *refs):
    heads, raws, refs = refs[:2], refs[2:4], refs[4:]
    outs, packed = refs[-1 - len(groups) : -1], refs[-1]
    size = SLOTS * SPAN
    for n, ref in enumerate((core_raw, *heads)):
        row = ref.shape[0] - TAIL
        parts = [
            ref[row + k * size : row + (k + 1) * size, :].astype(F32) for k in range(3)
        ]
        packed[n * size : (n + 1) * size, :] = parts[0] + parts[1] + parts[2]
    for slot in range(SLOTS):
        base = slot_row(at, 0, slot, own_rows)
        for g in range(rows // GRAIN):
            block = (base + (start + g * GRAIN)) // BLOCK
            span = slot * SPAN + block - base // BLOCK
            here = slice(g * GRAIN, (g + 1) * GRAIN)
            row = slot * own_rows + start + g * GRAIN
            there = slice(row, row + GRAIN)
            row = slot * rows + g * GRAIN
            total = own[there, :].astype(F32) * scales[block]
            total += core_raw[there, :].astype(F32) * packed[pl.ds(span, 1), :]
            for n, raw in enumerate(raws):
                part = raw[row : row + GRAIN, :].astype(F32)
                total += part * packed[pl.ds((n + 1) * size + span, 1), :]
            for out, group in zip(outs, groups):
                if slot in group and len(group) > 1:
                    out[group.index(slot), here, :] = total
                elif slot in group:
                    out[here, :] = total


def dequant(
    at, scales, own, core_raw, heads, raws, own_rows, start, rows, groups, after, carry
):
    width = own.shape[1]
    shapes = [
        jax.ShapeDtypeStruct((len(group), rows, width)[len(group) == 1 :], F32)
        for group in groups
    ]
    first, count, made = 8 + len(after), len(carry), len(groups)

    def kernel(*refs):
        kept = refs[:8] + refs[first + count : first + count + made] + refs[-1:]
        dequant_kernel(own_rows, start, rows, groups, *kept)

    outs = pl.pallas_call(
        kernel,
        in_specs=[SCALARS] + [WHOLE] * 7 + [ANYWHERE] * (len(after) + count),
        out_specs=[WHOLE] * made + [ANYWHERE] * count,
        out_shape=shapes + [jax.ShapeDtypeStruct(x.shape, x.dtype) for x in carry],
        scratch_shapes=[pltpu.VMEM((3 * SLOTS * SPAN, width), F32)],
        input_output_aliases={first + n: made + n for n in range(count)},
        compiler_params=params(),
        name="dequant_sum",
    )(at, scales, own, core_raw, *heads, *raws, *after, *carry)
    return outs[:made], outs[made:]


def add(terms, after, swap=False):
    def kernel(*refs):
        total = refs[0][...]
        for ref in refs[1 : len(terms) - swap]:
            total = total + ref[...]
        if swap:
            last = refs[len(terms) - 1]
            refs[-1][0] = total[0] + last[1]
            refs[-1][1] = total[1] + last[0]
        else:
            refs[-1][...] = total

    return pl.pallas_call(
        kernel,
        in_specs=[WHOLE] * len(terms) + [ANYWHERE] * len(after),
        out_specs=WHOLE,
        out_shape=jax.ShapeDtypeStruct(terms[0].shape, F32),
        compiler_params=params(),
        name="add_rows",
    )(*terms, *after)


def put_rows(slabs, high, low, column):
    row = 0
    for slab in slabs:
        here, share = slice(row, row + slab.shape[0]), slab.shape[1]
        high[here, column : column + share], low[here, column : column + share] = split(slab[...])
        row += slab.shape[0]


def put_slots(at, flat, out):
    part = out.shape[1]
    for slot in range(8):
        z = lax.bitwise_xor(at[0], ORDER[slot % 4])
        x = lax.bitwise_xor(at[1], slot // 4)
        out[slot] = flat[pl.ds(pl.multiple_of((z * 2 + x) * part, 8), part), :]


def near_kernel(count, at, *refs):
    slabs, outs, (high, low, flat) = refs[:count], refs[count : count + 2], refs[-3:]
    put_rows(slabs, high, low, 0)

    def take(start, width):
        lanes = pl.ds(pl.multiple_of(start, HALF), width)
        return high[:, lanes], low[:, lanes]

    contract = ((0,), (0,))
    for side, out in enumerate(outs):
        core = lax.bitwise_xor(at[2], side)
        own = take(core * PIECE, PIECE)
        block = dot3(own, own, contract)
        flat[0:HALF, :] = block[0:HALF, :]
        flat[HALF : HALF + HALF // 2, 0:HALF] = block[HALF : HALF + HALF // 2, HALF:]
        flat[HALF : HALF + HALF // 2, HALF:] = block[HALF + HALF // 2 :, HALF:]
        left = take(core * HALF, HALF)
        flat[NEAR - HALF :, :] = dot3(left, take(PIECE, PIECE), contract)
        put_slots(at, flat, out)


def cross_kernel(count, at, *refs):
    slabs, outs, (high, low, flat) = refs[: 2 * count], refs[-5:-3], refs[-3:]
    share = slabs[0].shape[1]
    put_rows(slabs[:count], high, low, 0)
    put_rows(slabs[count:], high, low, share)

    def take(start, width):
        lanes = pl.ds(pl.multiple_of(start, HALF), width)
        return high[:, lanes], low[:, lanes]

    contract = ((0,), (0,))
    half = at[3]
    for side, out in enumerate(outs):
        core = lax.bitwise_xor(at[2], side)
        for k in range(2):
            mine = core * PIECE
            other = share + lax.bitwise_xor(core, k) * PIECE
            left = jnp.where(half == 0, mine, other + HALF)
            right = jnp.where(half == 0, other, mine)
            flat[k * HALF : (k + 1) * HALF, :] = dot3(
                take(left, HALF), take(right, PIECE), contract
            )
        put_slots(at, flat, out)


def gram_part(kernel, at, slabs, count, packed, name, after):
    rows = sum(slab.shape[0] for slab in slabs[:count])
    width = slabs[0].shape[1] * (len(slabs) // count)
    return pl.pallas_call(
        functools.partial(kernel, count),
        in_specs=[SCALARS] + [WHOLE] * len(slabs) + [ANYWHERE] * len(after),
        out_specs=[WHOLE] * 2,
        out_shape=[jax.ShapeDtypeStruct((8, packed // 8, PIECE), F32)] * 2,
        scratch_shapes=[pltpu.VMEM((rows, width), BF16)] * 2 + [pltpu.VMEM((packed, PIECE), F32)],
        compiler_params=params(),
        name=name,
    )(at, *slabs, *after)


def update_kernel(scale, places, count, at, *refs):
    pieces, refs = refs[: len(places)], refs[len(places) :]
    owns, acrosses, refs = refs[:count], refs[count : 2 * count], refs[2 * count :]
    out, packed, gram, high, low = refs
    zed, ex, core, half = at[0], at[1], at[2], at[3]
    for ref, (first, slots) in zip(pieces, places):
        part = ref.shape[1]
        for n, (kz, kx, kc, kf) in enumerate(slots):
            quarter = 2 * lax.bitwise_xor(half, kf) + lax.bitwise_xor(core, kc)
            chip = 2 * lax.bitwise_xor(zed, kz) + lax.bitwise_xor(ex, kx)
            row = pl.multiple_of(quarter * PACKED + first + chip * part, 8)
            packed[pl.ds(row, part), :] = ref[n]
    trace = jnp.zeros((1, 1), F32)
    rows = lax.broadcasted_iota(jnp.int32, (HALF, HALF), 0)
    columns = lax.broadcasted_iota(jnp.int32, (HALF, HALF), 1)

    def put(block, row, column):
        h, l = split(block)
        here = (slice(row, row + block.shape[0]), slice(column, column + block.shape[1]))
        high[here] = h
        low[here] = l

    for q in range(4):
        base, edge = q * PACKED, q * PIECE
        top = packed[base : base + HALF, :]
        bottom = packed[base + HALF : base + HALF + HALF // 2, :]
        bottom = jnp.concatenate([bottom[:, :HALF], bottom[:, HALF:]], 0)
        for block in (top[:, :HALF], bottom):
            trace += jnp.sum(jnp.where(rows == columns, block, 0.0), keepdims=True)
        put(top, edge, edge)
        put(top[:, HALF:].T, edge + HALF, edge)
        put(bottom, edge + HALF, edge + HALF)
        for k in range(1, 4):
            other = q ^ k
            if q > other:
                continue
            row = PACKED + (k - 4) * HALF
            for first, owner in ((0, q), (HALF, other)):
                block = packed[owner * PACKED + row : owner * PACKED + row + HALF, :]
                put(block, edge + first, other * PIECE)
                put(block.T, other * PIECE, edge + first)
    inv = 1.0 / (jnp.sqrt(trace) + 1e-07)
    share = owns[0].shape[1]
    contract = ((1,), (0,))

    def mine(which):
        return pl.ds(pl.multiple_of(which * share, share), share)

    unit = jnp.concatenate([own[...] for own in owns], 0) * inv
    far = jnp.concatenate([across[...] for across in acrosses], 0) * inv
    first = dot3(split(unit), (high[mine(half), :], low[mine(half), :]), contract)
    first += dot3(split(far), (high[mine(1 - half), :], low[mine(1 - half), :]), contract)
    first = first * (inv * inv)
    gram[...] = first
    second = dot3(split(first), (high[:, mine(half)], low[:, mine(half)]), contract)
    second = second * (inv * inv)
    result = 3.4445 * unit + (-4.775 * gram[:, mine(half)] + 2.0315 * second)
    out[...] = (scale * result).astype(out.dtype)


def update(at, pieces, places, owns, acrosses, scale):
    rows = sum(own.shape[0] for own in owns)
    share = owns[0].shape[1]
    width = 2 * share
    return pl.pallas_call(
        functools.partial(update_kernel, scale, places, len(owns)),
        in_specs=[SCALARS] + [WHOLE] * (len(pieces) + 2 * len(owns)),
        out_specs=WHOLE,
        out_shape=jax.ShapeDtypeStruct((rows, share), BF16),
        scratch_shapes=[
            pltpu.VMEM((4 * PACKED, PIECE), F32),
            pltpu.VMEM((rows, width), F32),
            pltpu.VMEM((width, width), BF16),
            pltpu.VMEM((width, width), BF16),
        ],
        compiler_params=params(),
        name="update",
    )(at, *pieces, *owns, *acrosses)


AXIS_BITS = {"f": 1, "c": 2, "x": 4, "z1": 8, "z2": 16}


def flip(value, *names):
    mask = sum(AXIS_BITS[name] for name in names)
    count = lax.axis_size(("dp", "fsdp"))
    return lax.ppermute(value, ("dp", "fsdp"), [(i, i ^ mask) for i in range(count)])


ZEDS = (("z2",), ("z1",), ("z1", "z2"))
SIDES = (("x",), ("c", "x"))


def fast_body(partials, scales):
    values, scales = partials[0], scales.transpose(1, 0, 2)
    features, share = values.shape
    own_rows = features // lax.axis_size("dp")
    rank = lax.axis_index("dp")
    at = jnp.stack([rank // 4, rank // 2 % 2, rank % 2, lax.axis_index("fsdp")])
    unit = own_rows // sum(CHUNKS)
    spans, start = [], 0
    for size in CHUNKS:
        spans.append((start, size * unit))
        start += size * unit

    own, core_raw, *outs = pack(values, scales, at, own_rows, spans)
    core_raw = flip(core_raw, "c")

    def cross(pair):
        return [flip(out, *side) for out, side in zip(pair, SIDES)]

    outs = [outs[2 * n : 2 * n + 2] for n in range(len(spans))]
    raws = [cross(pair) for pair in outs[:2]]
    heads = raws[0]
    owns, acrosses, held = [], [], []
    made = {}

    def there(step, n):
        return [made[name] for name in AFTER.get((step, n), ())]

    def add_partials(n):
        start, rows = spans[n]
        carry = outs[n + 2] if n + 2 < len(spans) else []
        (keep, *go), carry = dequant(
            at, scales, own, core_raw, heads, raws[n], own_rows, start, rows,
            GROUPS[ROUTES[n]], there("sum", n), carry,
        )
        if carry:
            raws.append(cross(carry))
        made["keep", n] = keep
        if ROUTES[n] == "direct":
            made["got", n] = [flip(part, *names) for part, names in zip(go, ZEDS)]
        elif ROUTES[n] == "halves":
            made["got", n] = [flip(part, "z1") for part in go]
        else:
            made["got", n] = flip(go[0], "z1")

    def halve(n):
        keep, got = made["keep", n], made["got", n]
        made["sent", n] = add([keep[1], got[1]], there("halve", n))
        made["half", n] = keep[0] + got[0]

    def finish(n):
        if ROUTES[n] == "direct":
            terms = [made["keep", n], *made["got", n]]
        else:
            terms = [made["half", n], flip(made["sent", n], "z2")]
        made["grad", n] = add(terms, there("finish", n))
        held.append(made["grad", n])
        if n in LEAVE:
            group = jnp.concatenate(held) if len(held) > 1 else held[0]
            across = flip(group, "f")
            made["across", n] = across
            owns.append(group)
            acrosses.append(across)
            held.clear()

    for step, n in STEPS:
        {"sum": add_partials, "halve": halve, "finish": finish}[step](n)

    count = len(owns)
    own, far = gram_part(near_kernel, at, owns, count, NEAR, "gram_near", [])
    core = flip(far, "c")
    near_sent = add([own[4:], core[4:]], [])
    near_x = flip(near_sent, "x")
    cross_own, far = gram_part(
        cross_kernel, at, owns + acrosses, count, CROSS, "gram_cross", [near_sent]
    )
    cross_core = [flip(far[4:], "c"), flip(far[:4], "c")]
    cross_x = flip(add([cross_own[4:], cross_core[0]], [near_x]), "x")

    near = own[:4] + core[:4] + near_x
    near_z1 = flip(near[2:], "z1")
    near = near[:2] + near_z1
    near_z2 = flip(near, "z2")
    near = add([near, near_z2], [], swap=True)
    near_other = flip(near, "z1")

    cross = add([cross_own[:4], cross_core[1], cross_x], [near_z1])
    cross = add([cross[:2], flip(cross[2:], "z1")], [near_z2])
    cross = add([cross, flip(cross, "z2")], [near_other], swap=True)
    cross_other = flip(cross, "z1")

    near = jnp.concatenate([near, near_other])
    near = jnp.concatenate([near, flip(near, "x")])
    cross = jnp.concatenate([cross, cross_other])
    cross = jnp.concatenate([cross, flip(cross, "f")])
    parts = [near, flip(near, "f"), cross, flip(cross, "x")]
    parts += [flip(part, "c") for part in parts]
    near_slots = [(z, x, 0, 0) for x in range(2) for z in ORDER]
    cross_slots = [(z, 0, 0, f) for f in range(2) for z in ORDER]
    slots = [
        near_slots,
        [(z, x, c, 1) for z, x, c, _ in near_slots],
        cross_slots,
        [(z, 1, c, f) for z, _, c, f in cross_slots],
    ]
    slots += [[(z, x, 1, f) for z, x, _, f in group] for group in slots]
    firsts = [0, 0, NEAR, NEAR] * 2
    places = list(zip(firsts, slots))
    scale = float(0.25 * np.sqrt(np.float32(features * 2 * share)))
    return update(at, parts, places, owns, acrosses, scale)


def plain_body(partials, scales):
    values, scales = partials[0], scales[0]
    features, share = values.shape
    dp = lax.axis_size("dp")
    rows = values.reshape(scales.shape[0], -1, share).astype(F32) * scales[:, None, :]
    summed = lax.psum_scatter(
        rows.reshape(features, share), "dp", scatter_dimension=0, tiled=True
    )
    slab = lax.all_gather(summed, "fsdp", axis=1, tiled=True)
    width = slab.shape[1]
    highest = functools.partial(
        jnp.dot, precision=lax.Precision.HIGHEST, preferred_element_type=F32
    )
    half = lax.axis_index("fsdp")
    gram = lax.psum(highest(summed.T, slab), "dp")
    gram = lax.all_gather(gram, "fsdp", axis=0, tiled=True)
    inv = 1.0 / (jnp.sqrt(jnp.trace(gram)) + 1e-07)
    scaled = gram * (inv * inv)
    first = highest(slab * inv, scaled)
    mine = lambda value: lax.dynamic_slice_in_dim(value, half * share, share, 1)
    second = highest(first, mine(scaled))
    result = 3.4445 * (summed * inv) + (-4.775 * mine(first) + 2.0315 * second)
    return (0.25 * jnp.sqrt(F32(features * width)) * result).astype(BF16)


def solution(mesh):
    dp, fsdp = mesh.shape["dp"], mesh.shape["fsdp"]

    def run(partials, scales):
        features, width = partials.shape[1:]
        fast = (
            (dp, fsdp) == (16, 2)
            and features % (dp * GRAIN * sum(CHUNKS)) == 0
            and width == 4 * PIECE
        )
        return jax.shard_map(
            fast_body if fast else plain_body,
            mesh=mesh,
            in_specs=(P("dp", None, "fsdp"), P("dp", None, "fsdp")),
            out_specs=P("dp", "fsdp"),
            check_vma=False,
        )(partials, scales)

    return run
```

```python
import functools

import jax
import jax.numpy as jnp
import numpy as np
from jax import lax
from jax.experimental import pallas as pl
from jax.experimental.pallas import tpu as pltpu
from jax.sharding import PartitionSpec as P

BLOCK = 128
GRAIN = 16
CHUNKS = (3, 5, 4, 3)
LEAVE = (0, 1, 3)
STEPS = (
    ("sum", 0), ("halve", 0), ("sum", 1), ("sum", 2), ("halve", 1), ("finish", 0), ("sum", 3),
    ("halve", 2), ("finish", 1), ("halve", 3), ("finish", 2), ("finish", 3),
)
AFTER = {
    ("sum", 1): (("sent", 0), ("half", 0)),
    ("sum", 2): (("near", 1), ("last", 1)),
    ("halve", 1): (("keep", 2),),
    ("finish", 0): (("keep", 2),),
    ("sum", 3): (("sent", 1), ("grad", 0)),
    ("halve", 2): (("keep", 3),),
    ("finish", 1): (("sent", 2), ("last", 3), ("across", 0)),
    ("finish", 2): (("sent", 3),),
    ("finish", 3): (("across", 1),),
}
ORDER = (0, 2, 1, 3)
PIECE = 256
HALF = PIECE // 2
NEAR = HALF + HALF // 2 + HALF
CROSS = 2 * HALF
PACKED = NEAR + CROSS
F32 = jnp.float32
BF16 = jnp.bfloat16
VMEM = 48 * 1024 * 1024
WHOLE = pl.BlockSpec(memory_space=pltpu.VMEM)
SCALARS = pl.BlockSpec(memory_space=pltpu.SMEM)
ANYWHERE = pl.BlockSpec(memory_space=pl.ANY)


def params():
    return pltpu.CompilerParams(vmem_limit_bytes=VMEM)


def split(value):
    high = value.astype(BF16)
    return high, (value - high.astype(F32)).astype(BF16)


def dot3(a, b, contract):
    dims = (contract, ((), ()))

    def one(u, v):
        return lax.dot_general(u, v, dims, preferred_element_type=F32)

    return one(a[0], b[0]) + (one(a[0], b[1]) + one(a[1], b[0]))


def slot_row(at, side, slot, own_rows):
    zed, ex, core = at[0], at[1], at[2]
    z = lax.bitwise_xor(zed, ORDER[slot])
    c = lax.bitwise_xor(core, side % 2)
    x = lax.bitwise_xor(ex, side // 2)
    return ((z * 2 + x) * 2 + c) * own_rows


SLOTS = len(ORDER)
GROUPS = {
    "halves": ((0, 1), (2,), (3,)),
    "pair": ((0, 1), (2, 3)),
    "direct": ((0,), (1,), (2,), (3,)),
}
ROUTES = ("halves", "halves", "halves", "halves")
SPAN = 4
TAIL = 3 * SLOTS * SPAN


def pack_kernel(own_rows, spans, at, values, scales, own, *refs):
    outs, gathered = refs[:-1], refs[-1]
    blocks = scales.shape[0]

    def copy(side, start, rows, out):
        for slot in range(SLOTS):
            base = pl.multiple_of(slot_row(at, side, slot, own_rows) + start, GRAIN)
            out[slot * rows : (slot + 1) * rows, :] = values[pl.ds(base, rows), :]

    def tail(side, out):
        for slot in range(SLOTS):
            first = slot_row(at, side, slot, own_rows) // BLOCK
            for n in range(SPAN):
                row = jnp.minimum(first + n, blocks - 1)
                gathered[slot * SPAN + n : slot * SPAN + n + 1, :] = scales[row]
        left = gathered[...]
        for n in range(3):
            part = left.astype(BF16)
            row = out.shape[0] - TAIL + n * SLOTS * SPAN
            out[row : row + SLOTS * SPAN, :] = part
            left = left - part.astype(F32)

    copy(0, 0, own_rows, own)
    copy(1, 0, own_rows, outs[0])
    tail(1, outs[0])
    for n, (start, rows) in enumerate(spans):
        for side in (2, 3):
            out = outs[2 * n + side - 1]
            copy(side, start, rows, out)
            if n == 0:
                tail(side, out)


def pack(values, scales, at, own_rows, spans):
    width = values.shape[1]
    lengths = [SLOTS * own_rows, SLOTS * own_rows + TAIL]
    for n, (_, rows) in enumerate(spans):
        lengths += [SLOTS * rows + (TAIL if n == 0 else 0)] * 2
    return pl.pallas_call(
        functools.partial(pack_kernel, own_rows, spans),
        in_specs=[SCALARS, WHOLE, WHOLE],
        out_specs=[WHOLE] * len(lengths),
        out_shape=[jax.ShapeDtypeStruct((rows, width), BF16) for rows in lengths],
        scratch_shapes=[pltpu.VMEM((SLOTS * SPAN, width), F32)],
        compiler_params=params(),
        name="pack_rows",
    )(at, values, scales)


def dequant_kernel(own_rows, start, rows, groups, at, scales, own, core_raw, *refs):
    heads, raws, refs = refs[:2], refs[2:4], refs[4:]
    outs, packed = refs[-1 - len(groups) : -1], refs[-1]
    size = SLOTS * SPAN
    for n, ref in enumerate((core_raw, *heads)):
        row = ref.shape[0] - TAIL
        parts = [
            ref[row + k * size : row + (k + 1) * size, :].astype(F32) for k in range(3)
        ]
        packed[n * size : (n + 1) * size, :] = parts[0] + parts[1] + parts[2]
    for slot in range(SLOTS):
        base = slot_row(at, 0, slot, own_rows)
        for g in range(rows // GRAIN):
            block = (base + (start + g * GRAIN)) // BLOCK
            span = slot * SPAN + block - base // BLOCK
            here = slice(g * GRAIN, (g + 1) * GRAIN)
            row = slot * own_rows + start + g * GRAIN
            there = slice(row, row + GRAIN)
            row = slot * rows + g * GRAIN
            total = own[there, :].astype(F32) * scales[block]
            total += core_raw[there, :].astype(F32) * packed[pl.ds(span, 1), :]
            for n, raw in enumerate(raws):
                part = raw[row : row + GRAIN, :].astype(F32)
                total += part * packed[pl.ds((n + 1) * size + span, 1), :]
            for out, group in zip(outs, groups):
                if slot in group and len(group) > 1:
                    out[group.index(slot), here, :] = total
                elif slot in group:
                    out[here, :] = total


def dequant(
    at, scales, own, core_raw, heads, raws, own_rows, start, rows, groups, after, carry
):
    width = own.shape[1]
    shapes = [
        jax.ShapeDtypeStruct((len(group), rows, width)[len(group) == 1 :], F32)
        for group in groups
    ]
    first, count, made = 8 + len(after), len(carry), len(groups)

    def kernel(*refs):
        kept = refs[:8] + refs[first + count : first + count + made] + refs[-1:]
        dequant_kernel(own_rows, start, rows, groups, *kept)

    outs = pl.pallas_call(
        kernel,
        in_specs=[SCALARS] + [WHOLE] * 7 + [ANYWHERE] * (len(after) + count),
        out_specs=[WHOLE] * made + [ANYWHERE] * count,
        out_shape=shapes + [jax.ShapeDtypeStruct(x.shape, x.dtype) for x in carry],
        scratch_shapes=[pltpu.VMEM((3 * SLOTS * SPAN, width), F32)],
        input_output_aliases={first + n: made + n for n in range(count)},
        compiler_params=params(),
        name="dequant_sum",
    )(at, scales, own, core_raw, *heads, *raws, *after, *carry)
    return outs[:made], outs[made:]


def add(terms, after, swap=False):
    def kernel(*refs):
        total = refs[0][...]
        for ref in refs[1 : len(terms) - swap]:
            total = total + ref[...]
        if swap:
            last = refs[len(terms) - 1]
            refs[-1][0] = total[0] + last[1]
            refs[-1][1] = total[1] + last[0]
        else:
            refs[-1][...] = total

    return pl.pallas_call(
        kernel,
        in_specs=[WHOLE] * len(terms) + [ANYWHERE] * len(after),
        out_specs=WHOLE,
        out_shape=jax.ShapeDtypeStruct(terms[0].shape, F32),
        compiler_params=params(),
        name="add_rows",
    )(*terms, *after)


def put_rows(slabs, high, low, column):
    row = 0
    for slab in slabs:
        here, share = slice(row, row + slab.shape[0]), slab.shape[1]
        high[here, column : column + share], low[here, column : column + share] = split(slab[...])
        row += slab.shape[0]


def put_slots(at, flat, out):
    part = out.shape[1]
    for slot in range(8):
        z = lax.bitwise_xor(at[0], ORDER[slot % 4])
        x = lax.bitwise_xor(at[1], slot // 4)
        out[slot] = flat[pl.ds(pl.multiple_of((z * 2 + x) * part, 8), part), :]


def near_kernel(count, at, *refs):
    slabs, outs, (high, low, flat) = refs[:count], refs[count : count + 2], refs[-3:]
    put_rows(slabs, high, low, 0)

    def take(start, width):
        lanes = pl.ds(pl.multiple_of(start, HALF), width)
        return high[:, lanes], low[:, lanes]

    contract = ((0,), (0,))
    for side, out in enumerate(outs):
        core = lax.bitwise_xor(at[2], side)
        own = take(core * PIECE, PIECE)
        block = dot3(own, own, contract)
        flat[0:HALF, :] = block[0:HALF, :]
        flat[HALF : HALF + HALF // 2, 0:HALF] = block[HALF : HALF + HALF // 2, HALF:]
        flat[HALF : HALF + HALF // 2, HALF:] = block[HALF + HALF // 2 :, HALF:]
        left = take(core * HALF, HALF)
        flat[NEAR - HALF :, :] = dot3(left, take(PIECE, PIECE), contract)
        put_slots(at, flat, out)


def cross_kernel(count, at, *refs):
    slabs, outs, (high, low, flat) = refs[: 2 * count], refs[-5:-3], refs[-3:]
    share = slabs[0].shape[1]
    put_rows(slabs[:count], high, low, 0)
    put_rows(slabs[count:], high, low, share)

    def take(start, width):
        lanes = pl.ds(pl.multiple_of(start, HALF), width)
        return high[:, lanes], low[:, lanes]

    contract = ((0,), (0,))
    half = at[3]
    for side, out in enumerate(outs):
        core = lax.bitwise_xor(at[2], side)
        for k in range(2):
            mine = core * PIECE
            other = share + lax.bitwise_xor(core, k) * PIECE
            left = jnp.where(half == 0, mine, other + HALF)
            right = jnp.where(half == 0, other, mine)
            flat[k * HALF : (k + 1) * HALF, :] = dot3(
                take(left, HALF), take(right, PIECE), contract
            )
        put_slots(at, flat, out)


def gram_part(kernel, at, slabs, count, packed, name, after):
    rows = sum(slab.shape[0] for slab in slabs[:count])
    width = slabs[0].shape[1] * (len(slabs) // count)
    return pl.pallas_call(
        functools.partial(kernel, count),
        in_specs=[SCALARS] + [WHOLE] * len(slabs) + [ANYWHERE] * len(after),
        out_specs=[WHOLE] * 2,
        out_shape=[jax.ShapeDtypeStruct((8, packed // 8, PIECE), F32)] * 2,
        scratch_shapes=[pltpu.VMEM((rows, width), BF16)] * 2 + [pltpu.VMEM((packed, PIECE), F32)],
        compiler_params=params(),
        name=name,
    )(at, *slabs, *after)


def update_kernel(scale, places, count, at, *refs):
    pieces, refs = refs[: len(places)], refs[len(places) :]
    owns, acrosses, refs = refs[:count], refs[count : 2 * count], refs[2 * count :]
    out, packed, gram, high, low = refs
    zed, ex, core, half = at[0], at[1], at[2], at[3]
    for ref, (first, slots) in zip(pieces, places):
        part = ref.shape[1]
        for n, (kz, kx, kc, kf) in enumerate(slots):
            quarter = 2 * lax.bitwise_xor(half, kf) + lax.bitwise_xor(core, kc)
            chip = 2 * lax.bitwise_xor(zed, kz) + lax.bitwise_xor(ex, kx)
            row = pl.multiple_of(quarter * PACKED + first + chip * part, 8)
            packed[pl.ds(row, part), :] = ref[n]
    trace = jnp.zeros((1, 1), F32)
    rows = lax.broadcasted_iota(jnp.int32, (HALF, HALF), 0)
    columns = lax.broadcasted_iota(jnp.int32, (HALF, HALF), 1)

    def put(block, row, column):
        h, l = split(block)
        here = (slice(row, row + block.shape[0]), slice(column, column + block.shape[1]))
        high[here] = h
        low[here] = l

    for q in range(4):
        base, edge = q * PACKED, q * PIECE
        top = packed[base : base + HALF, :]
        bottom = packed[base + HALF : base + HALF + HALF // 2, :]
        bottom = jnp.concatenate([bottom[:, :HALF], bottom[:, HALF:]], 0)
        for block in (top[:, :HALF], bottom):
            trace += jnp.sum(jnp.where(rows == columns, block, 0.0), keepdims=True)
        put(top, edge, edge)
        put(top[:, HALF:].T, edge + HALF, edge)
        put(bottom, edge + HALF, edge + HALF)
        for k in range(1, 4):
            other = q ^ k
            if q > other:
                continue
            row = PACKED + (k - 4) * HALF
            for first, owner in ((0, q), (HALF, other)):
                block = packed[owner * PACKED + row : owner * PACKED + row + HALF, :]
                put(block, edge + first, other * PIECE)
                put(block.T, other * PIECE, edge + first)
    inv = 1.0 / (jnp.sqrt(trace) + 1e-07)
    share = owns[0].shape[1]
    contract = ((1,), (0,))

    def mine(which):
        return pl.ds(pl.multiple_of(which * share, share), share)

    unit = jnp.concatenate([own[...] for own in owns], 0) * inv
    far = jnp.concatenate([across[...] for across in acrosses], 0) * inv
    first = dot3(split(unit), (high[mine(half), :], low[mine(half), :]), contract)
    first += dot3(split(far), (high[mine(1 - half), :], low[mine(1 - half), :]), contract)
    first = first * (inv * inv)
    gram[...] = first
    second = dot3(split(first), (high[:, mine(half)], low[:, mine(half)]), contract)
    second = second * (inv * inv)
    result = 3.4445 * unit + (-4.775 * gram[:, mine(half)] + 2.0315 * second)
    out[...] = (scale * result).astype(out.dtype)


def update(at, pieces, places, owns, acrosses, scale):
    rows = sum(own.shape[0] for own in owns)
    share = owns[0].shape[1]
    width = 2 * share
    return pl.pallas_call(
        functools.partial(update_kernel, scale, places, len(owns)),
        in_specs=[SCALARS] + [WHOLE] * (len(pieces) + 2 * len(owns)),
        out_specs=WHOLE,
        out_shape=jax.ShapeDtypeStruct((rows, share), BF16),
        scratch_shapes=[
            pltpu.VMEM((4 * PACKED, PIECE), F32),
            pltpu.VMEM((rows, width), F32),
            pltpu.VMEM((width, width), BF16),
            pltpu.VMEM((width, width), BF16),
        ],
        compiler_params=params(),
        name="update",
    )(at, *pieces, *owns, *acrosses)


AXIS_BITS = {"f": 1, "c": 2, "x": 4, "z1": 8, "z2": 16}


def flip(value, *names):
    mask = sum(AXIS_BITS[name] for name in names)
    count = lax.axis_size(("dp", "fsdp"))
    return lax.ppermute(value, ("dp", "fsdp"), [(i, i ^ mask) for i in range(count)])


ZEDS = (("z2",), ("z1",), ("z1", "z2"))
SIDES = (("x",), ("c", "x"))


def fast_body(partials, scales):
    values, scales = partials[0], scales.transpose(1, 0, 2)
    features, share = values.shape
    own_rows = features // lax.axis_size("dp")
    rank = lax.axis_index("dp")
    at = jnp.stack([rank // 4, rank // 2 % 2, rank % 2, lax.axis_index("fsdp")])
    unit = own_rows // sum(CHUNKS)
    spans, start = [], 0
    for size in CHUNKS:
        spans.append((start, size * unit))
        start += size * unit

    own, core_raw, *outs = pack(values, scales, at, own_rows, spans)
    core_raw = flip(core_raw, "c")

    def cross(pair):
        return [flip(out, *side) for out, side in zip(pair, SIDES)]

    outs = [outs[2 * n : 2 * n + 2] for n in range(len(spans))]
    raws = [cross(pair) for pair in outs[:2]]
    heads = raws[0]
    owns, acrosses, held = [], [], []
    made = {}

    def there(step, n):
        return [made[name] for name in AFTER.get((step, n), ())]

    def add_partials(n):
        start, rows = spans[n]
        carry = outs[n + 2] if n + 2 < len(spans) else []
        (keep, *go), carry = dequant(
            at, scales, own, core_raw, heads, raws[n], own_rows, start, rows,
            GROUPS[ROUTES[n]], there("sum", n), carry,
        )
        if carry:
            raws.append(cross(carry))
        made["keep", n] = keep
        if ROUTES[n] == "direct":
            made["got", n] = [flip(part, *names) for part, names in zip(go, ZEDS)]
        elif ROUTES[n] == "halves":
            made["got", n] = [flip(part, "z1") for part in go]
            made["near", n], made["last", n] = made["got", n]
        else:
            made["got", n] = flip(go[0], "z1")

    def halve(n):
        keep, got = made["keep", n], made["got", n]
        made["sent", n] = add([keep[1], got[1]], there("halve", n))
        made["half", n] = keep[0] + got[0]

    def finish(n):
        if ROUTES[n] == "direct":
            terms = [made["keep", n], *made["got", n]]
        else:
            terms = [made["half", n], flip(made["sent", n], "z2")]
        made["grad", n] = add(terms, there("finish", n))
        held.append(made["grad", n])
        if n in LEAVE:
            group = jnp.concatenate(held) if len(held) > 1 else held[0]
            across = flip(group, "f")
            made["across", n] = across
            owns.append(group)
            acrosses.append(across)
            held.clear()

    for step, n in STEPS:
        {"sum": add_partials, "halve": halve, "finish": finish}[step](n)

    count = len(owns)
    own, far = gram_part(near_kernel, at, owns, count, NEAR, "gram_near", [])
    core = flip(far, "c")
    near_sent = add([own[4:], core[4:]], [])
    near_x = flip(near_sent, "x")
    cross_own, far = gram_part(
        cross_kernel, at, owns + acrosses, count, CROSS, "gram_cross", [near_sent]
    )
    cross_core = [flip(far[4:], "c"), flip(far[:4], "c")]
    cross_x = flip(add([cross_own[4:], cross_core[0]], [near_x]), "x")

    near = own[:4] + core[:4] + near_x
    near_z1 = flip(near[2:], "z1")
    near = near[:2] + near_z1
    near_z2 = flip(near, "z2")
    near = add([near, near_z2], [], swap=True)
    near_other = flip(near, "z1")

    cross = add([cross_own[:4], cross_core[1], cross_x], [near_z1])
    cross = add([cross[:2], flip(cross[2:], "z1")], [near_z2])
    cross = add([cross, flip(cross, "z2")], [near_other], swap=True)
    cross_other = flip(cross, "z1")

    near = jnp.concatenate([near, near_other])
    near = jnp.concatenate([near, flip(near, "x")])
    cross = jnp.concatenate([cross, cross_other])
    cross = jnp.concatenate([cross, flip(cross, "f")])
    parts = [near, flip(near, "f"), cross, flip(cross, "x")]
    parts += [flip(part, "c") for part in parts]
    near_slots = [(z, x, 0, 0) for x in range(2) for z in ORDER]
    cross_slots = [(z, 0, 0, f) for f in range(2) for z in ORDER]
    slots = [
        near_slots,
        [(z, x, c, 1) for z, x, c, _ in near_slots],
        cross_slots,
        [(z, 1, c, f) for z, _, c, f in cross_slots],
    ]
    slots += [[(z, x, 1, f) for z, x, _, f in group] for group in slots]
    firsts = [0, 0, NEAR, NEAR] * 2
    places = list(zip(firsts, slots))
    scale = float(0.25 * np.sqrt(np.float32(features * 2 * share)))
    return update(at, parts, places, owns, acrosses, scale)


def plain_body(partials, scales):
    values, scales = partials[0], scales[0]
    features, share = values.shape
    dp = lax.axis_size("dp")
    rows = values.reshape(scales.shape[0], -1, share).astype(F32) * scales[:, None, :]
    summed = lax.psum_scatter(
        rows.reshape(features, share), "dp", scatter_dimension=0, tiled=True
    )
    slab = lax.all_gather(summed, "fsdp", axis=1, tiled=True)
    width = slab.shape[1]
    highest = functools.partial(
        jnp.dot, precision=lax.Precision.HIGHEST, preferred_element_type=F32
    )
    half = lax.axis_index("fsdp")
    gram = lax.psum(highest(summed.T, slab), "dp")
    gram = lax.all_gather(gram, "fsdp", axis=0, tiled=True)
    inv = 1.0 / (jnp.sqrt(jnp.trace(gram)) + 1e-07)
    scaled = gram * (inv * inv)
    first = highest(slab * inv, scaled)
    mine = lambda value: lax.dynamic_slice_in_dim(value, half * share, share, 1)
    second = highest(first, mine(scaled))
    result = 3.4445 * (summed * inv) + (-4.775 * mine(first) + 2.0315 * second)
    return (0.25 * jnp.sqrt(F32(features * width)) * result).astype(BF16)


def solution(mesh):
    dp, fsdp = mesh.shape["dp"], mesh.shape["fsdp"]

    def run(partials, scales):
        features, width = partials.shape[1:]
        fast = (
            (dp, fsdp) == (16, 2)
            and features % (dp * GRAIN * sum(CHUNKS)) == 0
            and width == 4 * PIECE
        )
        return jax.shard_map(
            fast_body if fast else plain_body,
            mesh=mesh,
            in_specs=(P("dp", None, "fsdp"), P("dp", None, "fsdp")),
            out_specs=P("dp", "fsdp"),
            check_vma=False,
        )(partials, scales)

    return run
```

```python
import functools

import jax
import jax.numpy as jnp
import numpy as np
from jax import lax
from jax.experimental import pallas as pl
from jax.experimental.pallas import tpu as pltpu
from jax.sharding import PartitionSpec as P

BLOCK = 128
GRAIN = 16
CHUNKS = (3, 4, 5, 3)
LEAVE = (0, 1, 3)
STEPS = (
    ("sum", 0), ("halve", 0), ("sum", 1), ("sum", 2), ("halve", 1), ("finish", 0), ("sum", 3),
    ("halve", 2), ("finish", 1), ("halve", 3), ("finish", 2), ("finish", 3),
)
AFTER = {
    ("sum", 1): (("sent", 0), ("half", 0)),
    ("sum", 2): (("near", 1), ("last", 1)),
    ("halve", 1): (("keep", 2),),
    ("finish", 0): (("keep", 2),),
    ("sum", 3): (("sent", 1), ("grad", 0)),
    ("halve", 2): (("keep", 3),),
    ("halve", 3): (("sent", 2),),
    ("finish", 1): (("sent", 2), ("last", 3), ("across", 0)),
    ("finish", 2): (("sent", 3),),
    ("finish", 3): (("across", 1),),
}
ORDER = (0, 2, 1, 3)
PIECE = 256
HALF = PIECE // 2
NEAR = HALF + HALF // 2 + HALF
CROSS = 2 * HALF
PACKED = NEAR + CROSS
F32 = jnp.float32
BF16 = jnp.bfloat16
VMEM = 48 * 1024 * 1024
WHOLE = pl.BlockSpec(memory_space=pltpu.VMEM)
SCALARS = pl.BlockSpec(memory_space=pltpu.SMEM)
ANYWHERE = pl.BlockSpec(memory_space=pl.ANY)


def params():
    return pltpu.CompilerParams(vmem_limit_bytes=VMEM)


def split(value):
    high = value.astype(BF16)
    return high, (value - high.astype(F32)).astype(BF16)


def dot3(a, b, contract):
    dims = (contract, ((), ()))

    def one(u, v):
        return lax.dot_general(u, v, dims, preferred_element_type=F32)

    return one(a[0], b[0]) + (one(a[0], b[1]) + one(a[1], b[0]))


def slot_row(at, side, slot, own_rows):
    zed, ex, core = at[0], at[1], at[2]
    z = lax.bitwise_xor(zed, ORDER[slot])
    c = lax.bitwise_xor(core, side % 2)
    x = lax.bitwise_xor(ex, side // 2)
    return ((z * 2 + x) * 2 + c) * own_rows


SLOTS = len(ORDER)
GROUPS = {
    "halves": ((0, 1), (2,), (3,)),
    "pair": ((0, 1), (2, 3)),
    "direct": ((0,), (1,), (2,), (3,)),
}
ROUTES = ("halves", "halves", "pair", "halves")
SPAN = 4
TAIL = 3 * SLOTS * SPAN


def pack_kernel(own_rows, spans, at, values, scales, own, *refs):
    outs, gathered = refs[:-1], refs[-1]
    blocks = scales.shape[0]

    def copy(side, start, rows, out):
        for slot in range(SLOTS):
            base = pl.multiple_of(slot_row(at, side, slot, own_rows) + start, GRAIN)
            out[slot * rows : (slot + 1) * rows, :] = values[pl.ds(base, rows), :]

    def tail(side, out):
        for slot in range(SLOTS):
            first = slot_row(at, side, slot, own_rows) // BLOCK
            for n in range(SPAN):
                row = jnp.minimum(first + n, blocks - 1)
                gathered[slot * SPAN + n : slot * SPAN + n + 1, :] = scales[row]
        left = gathered[...]
        for n in range(3):
            part = left.astype(BF16)
            row = out.shape[0] - TAIL + n * SLOTS * SPAN
            out[row : row + SLOTS * SPAN, :] = part
            left = left - part.astype(F32)

    copy(0, 0, own_rows, own)
    copy(1, 0, own_rows, outs[0])
    tail(1, outs[0])
    for n, (start, rows) in enumerate(spans):
        for side in (2, 3):
            out = outs[2 * n + side - 1]
            copy(side, start, rows, out)
            if n == 0:
                tail(side, out)


def pack(values, scales, at, own_rows, spans):
    width = values.shape[1]
    lengths = [SLOTS * own_rows, SLOTS * own_rows + TAIL]
    for n, (_, rows) in enumerate(spans):
        lengths += [SLOTS * rows + (TAIL if n == 0 else 0)] * 2
    return pl.pallas_call(
        functools.partial(pack_kernel, own_rows, spans),
        in_specs=[SCALARS, WHOLE, WHOLE],
        out_specs=[WHOLE] * len(lengths),
        out_shape=[jax.ShapeDtypeStruct((rows, width), BF16) for rows in lengths],
        scratch_shapes=[pltpu.VMEM((SLOTS * SPAN, width), F32)],
        compiler_params=params(),
        name="pack_rows",
    )(at, values, scales)


def dequant_kernel(own_rows, start, rows, groups, at, scales, own, core_raw, *refs):
    heads, raws, refs = refs[:2], refs[2:4], refs[4:]
    outs, packed = refs[-1 - len(groups) : -1], refs[-1]
    size = SLOTS * SPAN
    for n, ref in enumerate((core_raw, *heads)):
        row = ref.shape[0] - TAIL
        parts = [
            ref[row + k * size : row + (k + 1) * size, :].astype(F32) for k in range(3)
        ]
        packed[n * size : (n + 1) * size, :] = parts[0] + parts[1] + parts[2]
    for slot in range(SLOTS):
        base = slot_row(at, 0, slot, own_rows)
        for g in range(rows // GRAIN):
            block = (base + (start + g * GRAIN)) // BLOCK
            span = slot * SPAN + block - base // BLOCK
            here = slice(g * GRAIN, (g + 1) * GRAIN)
            row = slot * own_rows + start + g * GRAIN
            there = slice(row, row + GRAIN)
            row = slot * rows + g * GRAIN
            total = own[there, :].astype(F32) * scales[block]
            total += core_raw[there, :].astype(F32) * packed[pl.ds(span, 1), :]
            for n, raw in enumerate(raws):
                part = raw[row : row + GRAIN, :].astype(F32)
                total += part * packed[pl.ds((n + 1) * size + span, 1), :]
            for out, group in zip(outs, groups):
                if slot in group and len(group) > 1:
                    out[group.index(slot), here, :] = total
                elif slot in group:
                    out[here, :] = total


def dequant(
    at, scales, own, core_raw, heads, raws, own_rows, start, rows, groups, after, carry
):
    width = own.shape[1]
    shapes = [
        jax.ShapeDtypeStruct((len(group), rows, width)[len(group) == 1 :], F32)
        for group in groups
    ]
    first, count, made = 8 + len(after), len(carry), len(groups)

    def kernel(*refs):
        kept = refs[:8] + refs[first + count : first + count + made] + refs[-1:]
        dequant_kernel(own_rows, start, rows, groups, *kept)

    outs = pl.pallas_call(
        kernel,
        in_specs=[SCALARS] + [WHOLE] * 7 + [ANYWHERE] * (len(after) + count),
        out_specs=[WHOLE] * made + [ANYWHERE] * count,
        out_shape=shapes + [jax.ShapeDtypeStruct(x.shape, x.dtype) for x in carry],
        scratch_shapes=[pltpu.VMEM((3 * SLOTS * SPAN, width), F32)],
        input_output_aliases={first + n: made + n for n in range(count)},
        compiler_params=params(),
        name="dequant_sum",
    )(at, scales, own, core_raw, *heads, *raws, *after, *carry)
    return outs[:made], outs[made:]


def add(terms, after, swap=False):
    def kernel(*refs):
        total = refs[0][...]
        for ref in refs[1 : len(terms) - swap]:
            total = total + ref[...]
        if swap:
            last = refs[len(terms) - 1]
            refs[-1][0] = total[0] + last[1]
            refs[-1][1] = total[1] + last[0]
        else:
            refs[-1][...] = total

    return pl.pallas_call(
        kernel,
        in_specs=[WHOLE] * len(terms) + [ANYWHERE] * len(after),
        out_specs=WHOLE,
        out_shape=jax.ShapeDtypeStruct(terms[0].shape, F32),
        compiler_params=params(),
        name="add_rows",
    )(*terms, *after)


def put_rows(slabs, high, low, column):
    row = 0
    for slab in slabs:
        here, share = slice(row, row + slab.shape[0]), slab.shape[1]
        high[here, column : column + share], low[here, column : column + share] = split(slab[...])
        row += slab.shape[0]


def put_slots(at, flat, out):
    part = out.shape[1]
    for slot in range(8):
        z = lax.bitwise_xor(at[0], ORDER[slot % 4])
        x = lax.bitwise_xor(at[1], slot // 4)
        out[slot] = flat[pl.ds(pl.multiple_of((z * 2 + x) * part, 8), part), :]


def near_kernel(count, at, *refs):
    slabs, outs, (high, low, flat) = refs[:count], refs[count : count + 2], refs[-3:]
    put_rows(slabs, high, low, 0)

    def take(start, width):
        lanes = pl.ds(pl.multiple_of(start, HALF), width)
        return high[:, lanes], low[:, lanes]

    contract = ((0,), (0,))
    for side, out in enumerate(outs):
        core = lax.bitwise_xor(at[2], side)
        own = take(core * PIECE, PIECE)
        block = dot3(own, own, contract)
        flat[0:HALF, :] = block[0:HALF, :]
        flat[HALF : HALF + HALF // 2, 0:HALF] = block[HALF : HALF + HALF // 2, HALF:]
        flat[HALF : HALF + HALF // 2, HALF:] = block[HALF + HALF // 2 :, HALF:]
        left = take(core * HALF, HALF)
        flat[NEAR - HALF :, :] = dot3(left, take(PIECE, PIECE), contract)
        put_slots(at, flat, out)


def cross_kernel(count, at, *refs):
    slabs, outs, (high, low, flat) = refs[: 2 * count], refs[-5:-3], refs[-3:]
    share = slabs[0].shape[1]
    put_rows(slabs[:count], high, low, 0)
    put_rows(slabs[count:], high, low, share)

    def take(start, width):
        lanes = pl.ds(pl.multiple_of(start, HALF), width)
        return high[:, lanes], low[:, lanes]

    contract = ((0,), (0,))
    half = at[3]
    for side, out in enumerate(outs):
        core = lax.bitwise_xor(at[2], side)
        for k in range(2):
            mine = core * PIECE
            other = share + lax.bitwise_xor(core, k) * PIECE
            left = jnp.where(half == 0, mine, other + HALF)
            right = jnp.where(half == 0, other, mine)
            flat[k * HALF : (k + 1) * HALF, :] = dot3(
                take(left, HALF), take(right, PIECE), contract
            )
        put_slots(at, flat, out)


def gram_part(kernel, at, slabs, count, packed, name, after):
    rows = sum(slab.shape[0] for slab in slabs[:count])
    width = slabs[0].shape[1] * (len(slabs) // count)
    return pl.pallas_call(
        functools.partial(kernel, count),
        in_specs=[SCALARS] + [WHOLE] * len(slabs) + [ANYWHERE] * len(after),
        out_specs=[WHOLE] * 2,
        out_shape=[jax.ShapeDtypeStruct((8, packed // 8, PIECE), F32)] * 2,
        scratch_shapes=[pltpu.VMEM((rows, width), BF16)] * 2 + [pltpu.VMEM((packed, PIECE), F32)],
        compiler_params=params(),
        name=name,
    )(at, *slabs, *after)


def update_kernel(scale, places, count, at, *refs):
    pieces, refs = refs[: len(places)], refs[len(places) :]
    owns, acrosses, refs = refs[:count], refs[count : 2 * count], refs[2 * count :]
    out, packed, gram, high, low = refs
    zed, ex, core, half = at[0], at[1], at[2], at[3]
    for ref, (first, slots) in zip(pieces, places):
        part = ref.shape[1]
        for n, (kz, kx, kc, kf) in enumerate(slots):
            quarter = 2 * lax.bitwise_xor(half, kf) + lax.bitwise_xor(core, kc)
            chip = 2 * lax.bitwise_xor(zed, kz) + lax.bitwise_xor(ex, kx)
            row = pl.multiple_of(quarter * PACKED + first + chip * part, 8)
            packed[pl.ds(row, part), :] = ref[n]
    trace = jnp.zeros((1, 1), F32)
    rows = lax.broadcasted_iota(jnp.int32, (HALF, HALF), 0)
    columns = lax.broadcasted_iota(jnp.int32, (HALF, HALF), 1)

    def put(block, row, column):
        h, l = split(block)
        here = (slice(row, row + block.shape[0]), slice(column, column + block.shape[1]))
        high[here] = h
        low[here] = l

    for q in range(4):
        base, edge = q * PACKED, q * PIECE
        top = packed[base : base + HALF, :]
        bottom = packed[base + HALF : base + HALF + HALF // 2, :]
        bottom = jnp.concatenate([bottom[:, :HALF], bottom[:, HALF:]], 0)
        for block in (top[:, :HALF], bottom):
            trace += jnp.sum(jnp.where(rows == columns, block, 0.0), keepdims=True)
        put(top, edge, edge)
        put(top[:, HALF:].T, edge + HALF, edge)
        put(bottom, edge + HALF, edge + HALF)
        for k in range(1, 4):
            other = q ^ k
            if q > other:
                continue
            row = PACKED + (k - 4) * HALF
            for first, owner in ((0, q), (HALF, other)):
                block = packed[owner * PACKED + row : owner * PACKED + row + HALF, :]
                put(block, edge + first, other * PIECE)
                put(block.T, other * PIECE, edge + first)
    inv = 1.0 / (jnp.sqrt(trace) + 1e-07)
    share = owns[0].shape[1]
    contract = ((1,), (0,))

    def mine(which):
        return pl.ds(pl.multiple_of(which * share, share), share)

    unit = jnp.concatenate([own[...] for own in owns], 0) * inv
    far = jnp.concatenate([across[...] for across in acrosses], 0) * inv
    first = dot3(split(unit), (high[mine(half), :], low[mine(half), :]), contract)
    first += dot3(split(far), (high[mine(1 - half), :], low[mine(1 - half), :]), contract)
    first = first * (inv * inv)
    gram[...] = first
    second = dot3(split(first), (high[:, mine(half)], low[:, mine(half)]), contract)
    second = second * (inv * inv)
    result = 3.4445 * unit + (-4.775 * gram[:, mine(half)] + 2.0315 * second)
    out[...] = (scale * result).astype(out.dtype)


def update(at, pieces, places, owns, acrosses, scale):
    rows = sum(own.shape[0] for own in owns)
    share = owns[0].shape[1]
    width = 2 * share
    return pl.pallas_call(
        functools.partial(update_kernel, scale, places, len(owns)),
        in_specs=[SCALARS] + [WHOLE] * (len(pieces) + 2 * len(owns)),
        out_specs=WHOLE,
        out_shape=jax.ShapeDtypeStruct((rows, share), BF16),
        scratch_shapes=[
            pltpu.VMEM((4 * PACKED, PIECE), F32),
            pltpu.VMEM((rows, width), F32),
            pltpu.VMEM((width, width), BF16),
            pltpu.VMEM((width, width), BF16),
        ],
        compiler_params=params(),
        name="update",
    )(at, *pieces, *owns, *acrosses)


AXIS_BITS = {"f": 1, "c": 2, "x": 4, "z1": 8, "z2": 16}


def flip(value, *names):
    mask = sum(AXIS_BITS[name] for name in names)
    count = lax.axis_size(("dp", "fsdp"))
    return lax.ppermute(value, ("dp", "fsdp"), [(i, i ^ mask) for i in range(count)])


ZEDS = (("z2",), ("z1",), ("z1", "z2"))
SIDES = (("x",), ("c", "x"))


def fast_body(partials, scales):
    values, scales = partials[0], scales.transpose(1, 0, 2)
    features, share = values.shape
    own_rows = features // lax.axis_size("dp")
    rank = lax.axis_index("dp")
    at = jnp.stack([rank // 4, rank // 2 % 2, rank % 2, lax.axis_index("fsdp")])
    unit = own_rows // sum(CHUNKS)
    spans, start = [], 0
    for size in CHUNKS:
        spans.append((start, size * unit))
        start += size * unit

    own, core_raw, *outs = pack(values, scales, at, own_rows, spans)
    core_raw = flip(core_raw, "c")

    def cross(pair):
        return [flip(out, *side) for out, side in zip(pair, SIDES)]

    outs = [outs[2 * n : 2 * n + 2] for n in range(len(spans))]
    raws = [cross(pair) for pair in outs[:2]]
    heads = raws[0]
    owns, acrosses, held = [], [], []
    made = {}

    def there(step, n):
        return [made[name] for name in AFTER.get((step, n), ())]

    def add_partials(n):
        start, rows = spans[n]
        carry = outs[n + 2] if n + 2 < len(spans) else []
        (keep, *go), carry = dequant(
            at, scales, own, core_raw, heads, raws[n], own_rows, start, rows,
            GROUPS[ROUTES[n]], there("sum", n), carry,
        )
        if carry:
            raws.append(cross(carry))
        made["keep", n] = keep
        if ROUTES[n] == "direct":
            made["got", n] = [flip(part, *names) for part, names in zip(go, ZEDS)]
        elif ROUTES[n] == "halves":
            made["got", n] = [flip(part, "z1") for part in go]
            made["near", n], made["last", n] = made["got", n]
        else:
            made["got", n] = flip(go[0], "z1")

    def halve(n):
        keep, got = made["keep", n], made["got", n]
        made["sent", n] = add([keep[1], got[1]], there("halve", n))
        made["half", n] = keep[0] + got[0]

    def finish(n):
        if ROUTES[n] == "direct":
            terms = [made["keep", n], *made["got", n]]
        else:
            terms = [made["half", n], flip(made["sent", n], "z2")]
        made["grad", n] = add(terms, there("finish", n))
        held.append(made["grad", n])
        if n in LEAVE:
            group = jnp.concatenate(held) if len(held) > 1 else held[0]
            across = flip(group, "f")
            made["across", n] = across
            owns.append(group)
            acrosses.append(across)
            held.clear()

    for step, n in STEPS:
        {"sum": add_partials, "halve": halve, "finish": finish}[step](n)

    count = len(owns)
    own, far = gram_part(near_kernel, at, owns, count, NEAR, "gram_near", [])
    core = flip(far, "c")
    near_sent = add([own[4:], core[4:]], [])
    near_x = flip(near_sent, "x")
    cross_own, far = gram_part(
        cross_kernel, at, owns + acrosses, count, CROSS, "gram_cross", [near_sent]
    )
    cross_core = [flip(far[4:], "c"), flip(far[:4], "c")]
    cross_x = flip(add([cross_own[4:], cross_core[0]], [near_x]), "x")

    near = own[:4] + core[:4] + near_x
    near_z1 = flip(near[2:], "z1")
    near = near[:2] + near_z1
    near_z2 = flip(near, "z2")
    near = add([near, near_z2], [], swap=True)
    near_other = flip(near, "z1")

    cross = add([cross_own[:4], cross_core[1], cross_x], [near_z1])
    cross = add([cross[:2], flip(cross[2:], "z1")], [near_z2])
    cross = add([cross, flip(cross, "z2")], [near_other], swap=True)
    cross_other = flip(cross, "z1")

    near = jnp.concatenate([near, near_other])
    near = jnp.concatenate([near, flip(near, "x")])
    cross = jnp.concatenate([cross, cross_other])
    cross = jnp.concatenate([cross, flip(cross, "f")])
    parts = [near, flip(near, "f"), cross, flip(cross, "x")]
    parts += [flip(part, "c") for part in parts]
    near_slots = [(z, x, 0, 0) for x in range(2) for z in ORDER]
    cross_slots = [(z, 0, 0, f) for f in range(2) for z in ORDER]
    slots = [
        near_slots,
        [(z, x, c, 1) for z, x, c, _ in near_slots],
        cross_slots,
        [(z, 1, c, f) for z, _, c, f in cross_slots],
    ]
    slots += [[(z, x, 1, f) for z, x, _, f in group] for group in slots]
    firsts = [0, 0, NEAR, NEAR] * 2
    places = list(zip(firsts, slots))
    scale = float(0.25 * np.sqrt(np.float32(features * 2 * share)))
    return update(at, parts, places, owns, acrosses, scale)


def plain_body(partials, scales):
    values, scales = partials[0], scales[0]
    features, share = values.shape
    dp = lax.axis_size("dp")
    rows = values.reshape(scales.shape[0], -1, share).astype(F32) * scales[:, None, :]
    summed = lax.psum_scatter(
        rows.reshape(features, share), "dp", scatter_dimension=0, tiled=True
    )
    slab = lax.all_gather(summed, "fsdp", axis=1, tiled=True)
    width = slab.shape[1]
    highest = functools.partial(
        jnp.dot, precision=lax.Precision.HIGHEST, preferred_element_type=F32
    )
    half = lax.axis_index("fsdp")
    gram = lax.psum(highest(summed.T, slab), "dp")
    gram = lax.all_gather(gram, "fsdp", axis=0, tiled=True)
    inv = 1.0 / (jnp.sqrt(jnp.trace(gram)) + 1e-07)
    scaled = gram * (inv * inv)
    first = highest(slab * inv, scaled)
    mine = lambda value: lax.dynamic_slice_in_dim(value, half * share, share, 1)
    second = highest(first, mine(scaled))
    result = 3.4445 * (summed * inv) + (-4.775 * mine(first) + 2.0315 * second)
    return (0.25 * jnp.sqrt(F32(features * width)) * result).astype(BF16)


def solution(mesh):
    dp, fsdp = mesh.shape["dp"], mesh.shape["fsdp"]

    def run(partials, scales):
        features, width = partials.shape[1:]
        fast = (
            (dp, fsdp) == (16, 2)
            and features % (dp * GRAIN * sum(CHUNKS)) == 0
            and width == 4 * PIECE
        )
        return jax.shard_map(
            fast_body if fast else plain_body,
            mesh=mesh,
            in_specs=(P("dp", None, "fsdp"), P("dp", None, "fsdp")),
            out_specs=P("dp", "fsdp"),
            check_vma=False,
        )(partials, scales)

    return run
```

```python
import functools

import jax
import jax.numpy as jnp
import numpy as np
from jax import lax
from jax.experimental import pallas as pl
from jax.experimental.pallas import tpu as pltpu
from jax.sharding import PartitionSpec as P

BLOCK = 128
GRAIN = 16
CHUNKS = (3, 5, 4, 3)
LEAVE = (0, 1, 3)
STEPS = (
    ("sum", 0), ("halve", 0), ("sum", 1), ("halve", 1), ("finish", 0), ("sum", 2),
    ("sum", 3), ("halve", 2), ("finish", 1), ("finish", 2), ("finish", 3),
)
AFTER = {
    ("sum", 1): (("sent", 0), ("half", 0)),
    ("sum", 2): (("sent", 1), ("half", 1), ("grad", 0)),
    ("sum", 3): (("keep", 2),),
    ("halve", 2): (("keep", 3),),
    ("finish", 1): (("sent", 2), ("across", 0)),
    ("finish", 3): (("across", 1), ("grad", 2)),
}
ORDER = (0, 2, 1, 3)
PIECE = 256
HALF = PIECE // 2
NEAR = HALF + HALF // 2 + HALF
CROSS = 2 * HALF
PACKED = NEAR + CROSS
F32 = jnp.float32
BF16 = jnp.bfloat16
VMEM = 48 * 1024 * 1024
WHOLE = pl.BlockSpec(memory_space=pltpu.VMEM)
SCALARS = pl.BlockSpec(memory_space=pltpu.SMEM)
ANYWHERE = pl.BlockSpec(memory_space=pl.ANY)


def params():
    return pltpu.CompilerParams(vmem_limit_bytes=VMEM)


def split(value):
    high = value.astype(BF16)
    return high, (value - high.astype(F32)).astype(BF16)


def dot3(a, b, contract):
    dims = (contract, ((), ()))

    def one(u, v):
        return lax.dot_general(u, v, dims, preferred_element_type=F32)

    return one(a[0], b[0]) + (one(a[0], b[1]) + one(a[1], b[0]))


def dot_rows(a, high, low):
    rows = a.shape[0]
    upper, lower = split(a)
    stacked = jnp.concatenate([upper, lower], 0)
    both = jnp.dot(stacked, high, preferred_element_type=F32)
    return both[:rows] + (both[rows:] + jnp.dot(upper, low, preferred_element_type=F32))


def slot_row(at, side, slot, own_rows):
    zed, ex, core = at[0], at[1], at[2]
    z = lax.bitwise_xor(zed, ORDER[slot])
    c = lax.bitwise_xor(core, side % 2)
    x = lax.bitwise_xor(ex, side // 2)
    return ((z * 2 + x) * 2 + c) * own_rows


SLOTS = len(ORDER)
GROUPS = {
    "halves": ((0, 1), (2,), (3,)),
    "pair": ((0, 1), (2, 3)),
    "direct": ((0,), (1,), (2,), (3,)),
}
ROUTES = ("halves", "halves", "halves", "direct")
SPAN = 4
TAIL = 3 * SLOTS * SPAN


def pack_kernel(own_rows, spans, at, values, scales, own, *refs):
    outs, (gathered, staged, sem) = refs[:-3], refs[-3:]
    blocks = scales.shape[0]
    copies = []

    def copy(side, out):
        for slot in range(SLOTS):
            base = pl.multiple_of(slot_row(at, side, slot, own_rows), GRAIN)
            copies.append(
                pltpu.make_async_copy(
                    values.at[pl.ds(base, own_rows), :],
                    out.at[pl.ds((side // 3 * SLOTS + slot) * own_rows, own_rows), :],
                    sem.at[len(copies)],
                )
            )
            copies[-1].start()

    def tail(side, out):
        for slot in range(SLOTS):
            first = slot_row(at, side, slot, own_rows) // BLOCK
            for n in range(SPAN):
                row = jnp.minimum(first + n, blocks - 1)
                gathered[slot * SPAN + n : slot * SPAN + n + 1, :] = scales[row]
        left = gathered[...]
        for n in range(3):
            part = left.astype(BF16)
            row = out.shape[0] - TAIL + n * SLOTS * SPAN
            out[row : row + SLOTS * SPAN, :] = part
            left = left - part.astype(F32)

    for side, out in ((2, staged), (3, staged), (1, outs[0]), (0, own)):
        copy(side, out)
    for side in range(1, 4):
        tail(side, outs[side - 1])
    for n, each in enumerate(copies):
        each.wait()
        if n < 2 * SLOTS:
            side, slot = n // SLOTS, n % SLOTS
            for k, (start, rows) in enumerate(spans):
                row = n * own_rows + start
                outs[1 + 2 * k + side][slot * rows : (slot + 1) * rows, :] = staged[row : row + rows, :]


def pack(values, scales, at, own_rows, spans):
    width = values.shape[1]
    lengths = [SLOTS * own_rows, SLOTS * own_rows + TAIL]
    for n, (_, rows) in enumerate(spans):
        lengths += [SLOTS * rows + (TAIL if n == 0 else 0)] * 2
    return pl.pallas_call(
        functools.partial(pack_kernel, own_rows, spans),
        in_specs=[SCALARS, pl.BlockSpec(memory_space=pltpu.HBM), WHOLE],
        out_specs=[WHOLE] * len(lengths),
        out_shape=[jax.ShapeDtypeStruct((rows, width), BF16) for rows in lengths],
        scratch_shapes=[
            pltpu.VMEM((SLOTS * SPAN, width), F32),
            pltpu.VMEM((2 * SLOTS * own_rows, width), BF16),
            pltpu.SemaphoreType.DMA((4 * SLOTS,)),
        ],
        compiler_params=params(),
        name="pack_rows",
    )(at, values, scales)


def dequant_kernel(own_rows, start, rows, groups, at, scales, own, core_raw, *refs):
    heads, raws, refs = refs[:2], refs[2:4], refs[4:]
    outs, packed = refs[-1 - len(groups) : -1], refs[-1]
    size = SLOTS * SPAN
    for n, ref in enumerate((core_raw, *heads)):
        row = ref.shape[0] - TAIL
        parts = [
            ref[row + k * size : row + (k + 1) * size, :].astype(F32) for k in range(3)
        ]
        packed[n * size : (n + 1) * size, :] = parts[0] + parts[1] + parts[2]
    for slot in range(SLOTS):
        base = slot_row(at, 0, slot, own_rows)
        for g in range(rows // GRAIN):
            block = (base + (start + g * GRAIN)) // BLOCK
            span = slot * SPAN + block - base // BLOCK
            here = slice(g * GRAIN, (g + 1) * GRAIN)
            row = slot * own_rows + start + g * GRAIN
            there = slice(row, row + GRAIN)
            row = slot * rows + g * GRAIN
            total = own[there, :].astype(F32) * scales[block]
            total += core_raw[there, :].astype(F32) * packed[pl.ds(span, 1), :]
            for n, raw in enumerate(raws):
                part = raw[row : row + GRAIN, :].astype(F32)
                total += part * packed[pl.ds((n + 1) * size + span, 1), :]
            for out, group in zip(outs, groups):
                if slot in group and len(group) > 1:
                    out[group.index(slot), here, :] = total
                elif slot in group:
                    out[here, :] = total


def dequant(
    at, scales, own, core_raw, heads, raws, own_rows, start, rows, groups, after, carry
):
    width = own.shape[1]
    shapes = [
        jax.ShapeDtypeStruct((len(group), rows, width)[len(group) == 1 :], F32)
        for group in groups
    ]
    first, count, made = 8 + len(after), len(carry), len(groups)

    def kernel(*refs):
        kept = refs[:8] + refs[first + count : first + count + made] + refs[-1:]
        dequant_kernel(own_rows, start, rows, groups, *kept)

    outs = pl.pallas_call(
        kernel,
        in_specs=[SCALARS] + [WHOLE] * 7 + [ANYWHERE] * (len(after) + count),
        out_specs=[WHOLE] * made + [ANYWHERE] * count,
        out_shape=shapes + [jax.ShapeDtypeStruct(x.shape, x.dtype) for x in carry],
        scratch_shapes=[pltpu.VMEM((3 * SLOTS * SPAN, width), F32)],
        input_output_aliases={first + n: made + n for n in range(count)},
        compiler_params=params(),
        name="dequant_sum",
    )(at, scales, own, core_raw, *heads, *raws, *after, *carry)
    return outs[:made], outs[made:]


def add(terms, after, swap=False):
    def kernel(*refs):
        total = refs[0][...]
        for ref in refs[1 : len(terms) - swap]:
            total = total + ref[...]
        if swap:
            last = refs[len(terms) - 1]
            refs[-1][0] = total[0] + last[1]
            refs[-1][1] = total[1] + last[0]
        else:
            refs[-1][...] = total

    return pl.pallas_call(
        kernel,
        in_specs=[WHOLE] * len(terms) + [ANYWHERE] * len(after),
        out_specs=WHOLE,
        out_shape=jax.ShapeDtypeStruct(terms[0].shape, F32),
        compiler_params=params(),
        name="add_rows",
    )(*terms, *after)


def put_rows(slabs, high, low, column):
    row = 0
    for slab in slabs:
        here, share = slice(row, row + slab.shape[0]), slab.shape[1]
        high[here, column : column + share], low[here, column : column + share] = split(slab[...])
        row += slab.shape[0]


def put_slots(at, flat, out):
    part = out.shape[1]
    for slot in range(8):
        z = lax.bitwise_xor(at[0], ORDER[slot % 4])
        x = lax.bitwise_xor(at[1], slot // 4)
        out[slot] = flat[pl.ds(pl.multiple_of((z * 2 + x) * part, 8), part), :]


def near_kernel(count, at, *refs):
    slabs, outs, (high, low, flat) = refs[:count], refs[count : count + 2], refs[-3:]
    put_rows(slabs, high, low, 0)

    def take(start, width):
        lanes = pl.ds(pl.multiple_of(start, HALF), width)
        return high[:, lanes], low[:, lanes]

    contract = ((0,), (0,))
    for side, out in enumerate(outs):
        core = lax.bitwise_xor(at[2], side)
        own = take(core * PIECE, PIECE)
        block = dot3(own, own, contract)
        flat[0:HALF, :] = block[0:HALF, :]
        flat[HALF : HALF + HALF // 2, 0:HALF] = block[HALF : HALF + HALF // 2, HALF:]
        flat[HALF : HALF + HALF // 2, HALF:] = block[HALF + HALF // 2 :, HALF:]
        left = take(core * HALF, HALF)
        flat[NEAR - HALF :, :] = dot3(left, take(PIECE, PIECE), contract)
        put_slots(at, flat, out)


def cross_kernel(count, at, *refs):
    slabs, outs, (high, low, flat) = refs[: 2 * count], refs[-5:-3], refs[-3:]
    share = slabs[0].shape[1]
    put_rows(slabs[:count], high, low, 0)
    put_rows(slabs[count:], high, low, share)

    def take(start, width):
        lanes = pl.ds(pl.multiple_of(start, HALF), width)
        return high[:, lanes], low[:, lanes]

    contract = ((0,), (0,))
    half = at[3]
    for side, out in enumerate(outs):
        core = lax.bitwise_xor(at[2], side)
        for k in range(2):
            mine = core * PIECE
            other = share + lax.bitwise_xor(core, k) * PIECE
            left = jnp.where(half == 0, mine, other + HALF)
            right = jnp.where(half == 0, other, mine)
            flat[k * HALF : (k + 1) * HALF, :] = dot3(
                take(left, HALF), take(right, PIECE), contract
            )
        put_slots(at, flat, out)


def gram_part(kernel, at, slabs, count, packed, name, after):
    rows = sum(slab.shape[0] for slab in slabs[:count])
    width = slabs[0].shape[1] * (len(slabs) // count)
    return pl.pallas_call(
        functools.partial(kernel, count),
        in_specs=[SCALARS] + [WHOLE] * len(slabs) + [ANYWHERE] * len(after),
        out_specs=[WHOLE] * 2,
        out_shape=[jax.ShapeDtypeStruct((8, packed // 8, PIECE), F32)] * 2,
        scratch_shapes=[pltpu.VMEM((rows, width), BF16)] * 2 + [pltpu.VMEM((packed, PIECE), F32)],
        compiler_params=params(),
        name=name,
    )(at, *slabs, *after)


def update_kernel(scale, places, count, at, *refs):
    pieces, refs = refs[: len(places)], refs[len(places) :]
    owns, acrosses, refs = refs[:count], refs[count : 2 * count], refs[2 * count :]
    out, packed, gram, high, low = refs
    zed, ex, core, half = at[0], at[1], at[2], at[3]
    for ref, (first, slots) in zip(pieces, places):
        part = ref.shape[1]
        for n, (kz, kx, kc, kf) in enumerate(slots):
            quarter = 2 * lax.bitwise_xor(half, kf) + lax.bitwise_xor(core, kc)
            chip = 2 * lax.bitwise_xor(zed, kz) + lax.bitwise_xor(ex, kx)
            row = pl.multiple_of(quarter * PACKED + first + chip * part, 8)
            packed[pl.ds(row, part), :] = ref[n]
    trace = jnp.zeros((1, 1), F32)
    rows = lax.broadcasted_iota(jnp.int32, (HALF, HALF), 0)
    columns = lax.broadcasted_iota(jnp.int32, (HALF, HALF), 1)

    def put(block, row, column):
        h, l = split(block)
        here = (slice(row, row + block.shape[0]), slice(column, column + block.shape[1]))
        high[here] = h
        low[here] = l

    for q in range(4):
        base, edge = q * PACKED, q * PIECE
        top = packed[base : base + HALF, :]
        bottom = packed[base + HALF : base + HALF + HALF // 2, :]
        bottom = jnp.concatenate([bottom[:, :HALF], bottom[:, HALF:]], 0)
        for block in (top[:, :HALF], bottom):
            trace += jnp.sum(jnp.where(rows == columns, block, 0.0), keepdims=True)
        put(top, edge, edge)
        put(top[:, HALF:].T, edge + HALF, edge)
        put(bottom, edge + HALF, edge + HALF)
        for k in range(1, 4):
            other = q ^ k
            if q > other:
                continue
            row = PACKED + (k - 4) * HALF
            for first, owner in ((0, q), (HALF, other)):
                block = packed[owner * PACKED + row : owner * PACKED + row + HALF, :]
                put(block, edge + first, other * PIECE)
                put(block.T, other * PIECE, edge + first)
    inv = 1.0 / (jnp.sqrt(trace) + 1e-07)
    share = owns[0].shape[1]

    def mine(which):
        return pl.ds(pl.multiple_of(which * share, share), share)

    unit = jnp.concatenate([own[...] for own in owns], 0) * inv
    far = jnp.concatenate([across[...] for across in acrosses], 0) * inv
    first = dot_rows(unit, high[mine(half), :], low[mine(half), :])
    first += dot_rows(far, high[mine(1 - half), :], low[mine(1 - half), :])
    first = first * (inv * inv)
    gram[...] = first
    second = dot_rows(first, high[:, mine(half)], low[:, mine(half)])
    second = second * (inv * inv)
    result = 3.4445 * unit + (-4.775 * gram[:, mine(half)] + 2.0315 * second)
    out[...] = (scale * result).astype(out.dtype)


def update(at, pieces, places, owns, acrosses, scale):
    rows = sum(own.shape[0] for own in owns)
    share = owns[0].shape[1]
    width = 2 * share
    return pl.pallas_call(
        functools.partial(update_kernel, scale, places, len(owns)),
        in_specs=[SCALARS] + [WHOLE] * (len(pieces) + 2 * len(owns)),
        out_specs=WHOLE,
        out_shape=jax.ShapeDtypeStruct((rows, share), BF16),
        scratch_shapes=[
            pltpu.VMEM((4 * PACKED, PIECE), F32),
            pltpu.VMEM((rows, width), F32),
            pltpu.VMEM((width, width), BF16),
            pltpu.VMEM((width, width), BF16),
        ],
        compiler_params=params(),
        name="update",
    )(at, *pieces, *owns, *acrosses)


AXIS_BITS = {"f": 1, "c": 2, "x": 4, "z1": 8, "z2": 16}


def flip(value, *names):
    mask = sum(AXIS_BITS[name] for name in names)
    count = lax.axis_size(("dp", "fsdp"))
    return lax.ppermute(value, ("dp", "fsdp"), [(i, i ^ mask) for i in range(count)])


ZEDS = (("z2",), ("z1",), ("z1", "z2"))
SIDES = (("x",), ("c", "x"))


def fast_body(partials, scales):
    values, scales = partials[0], scales.transpose(1, 0, 2)
    features, share = values.shape
    own_rows = features // lax.axis_size("dp")
    rank = lax.axis_index("dp")
    at = jnp.stack([rank // 4, rank // 2 % 2, rank % 2, lax.axis_index("fsdp")])
    unit = own_rows // sum(CHUNKS)
    spans, start = [], 0
    for size in CHUNKS:
        spans.append((start, size * unit))
        start += size * unit

    own, core_raw, *outs = pack(values, scales, at, own_rows, spans)
    core_raw = flip(core_raw, "c")

    def cross(pair):
        return [flip(out, *side) for out, side in zip(pair, SIDES)]

    outs = [outs[2 * n : 2 * n + 2] for n in range(len(spans))]
    raws = [cross(pair) for pair in outs[:2]]
    heads = raws[0]
    owns, acrosses, held = [], [], []
    made = {}

    def there(step, n):
        return [made[name] for name in AFTER.get((step, n), ())]

    def add_partials(n):
        start, rows = spans[n]
        carry = outs[n + 2] if n + 2 < len(spans) else []
        (keep, *go), carry = dequant(
            at, scales, own, core_raw, heads, raws[n], own_rows, start, rows,
            GROUPS[ROUTES[n]], there("sum", n), carry,
        )
        if carry:
            raws.append(cross(carry))
        made["keep", n] = keep
        if ROUTES[n] == "direct":
            made["got", n] = [flip(part, *names) for part, names in zip(go, ZEDS)]
        elif ROUTES[n] == "halves":
            made["got", n] = [flip(part, "z1") for part in go]
        else:
            made["got", n] = flip(go[0], "z1")

    def halve(n):
        keep, got = made["keep", n], made["got", n]
        made["sent", n] = add([keep[1], got[1]], there("halve", n))
        made["half", n] = keep[0] + got[0]

    def finish(n):
        if ROUTES[n] == "direct":
            terms = [made["keep", n], *made["got", n]]
        else:
            terms = [made["half", n], flip(made["sent", n], "z2")]
        made["grad", n] = add(terms, there("finish", n))
        held.append(made["grad", n])
        if n in LEAVE:
            group = jnp.concatenate(held) if len(held) > 1 else held[0]
            across = flip(group, "f")
            made["across", n] = across
            owns.append(group)
            acrosses.append(across)
            held.clear()

    for step, n in STEPS:
        {"sum": add_partials, "halve": halve, "finish": finish}[step](n)

    count = len(owns)
    own, far = gram_part(near_kernel, at, owns, count, NEAR, "gram_near", [])
    core = [flip(far[4:], "c"), flip(far[:4], "c")]
    near_sent = add([own[4:], core[0]], [])
    near_x = flip(near_sent, "x")
    cross_own, far = gram_part(
        cross_kernel, at, owns + acrosses, count, CROSS, "gram_cross", [near_sent]
    )
    cross_core = [flip(far[4:], "c"), flip(far[:4], "c")]
    cross_x = flip(add([cross_own[4:], cross_core[0]], [near_x]), "x")

    near = own[:4] + core[1] + near_x
    near_z1 = flip(near[2:], "z1")
    near = near[:2] + near_z1
    near_z2 = flip(near, "z2")
    near = add([near, near_z2], [], swap=True)
    near_other = flip(near, "z1")

    cross = add([cross_own[:4], cross_core[1], cross_x], [near_z1])
    cross = add([cross[:2], flip(cross[2:], "z1")], [near_z2])
    cross = add([cross, flip(cross, "z2")], [near_other], swap=True)
    cross_other = flip(cross, "z1")

    near = jnp.concatenate([near, near_other])
    near = jnp.concatenate([near, flip(near, "x")])
    cross = jnp.concatenate([cross, cross_other])
    cross = jnp.concatenate([cross, flip(cross, "f")])
    parts = [near, flip(near, "f"), cross, flip(cross, "x")]
    parts += [flip(part, "c") for part in parts]
    near_slots = [(z, x, 0, 0) for x in range(2) for z in ORDER]
    cross_slots = [(z, 0, 0, f) for f in range(2) for z in ORDER]
    slots = [
        near_slots,
        [(z, x, c, 1) for z, x, c, _ in near_slots],
        cross_slots,
        [(z, 1, c, f) for z, _, c, f in cross_slots],
    ]
    slots += [[(z, x, 1, f) for z, x, _, f in group] for group in slots]
    firsts = [0, 0, NEAR, NEAR] * 2
    places = list(zip(firsts, slots))
    scale = float(0.25 * np.sqrt(np.float32(features * 2 * share)))
    return update(at, parts, places, owns, acrosses, scale)


def plain_body(partials, scales):
    values, scales = partials[0], scales[0]
    features, share = values.shape
    dp = lax.axis_size("dp")
    rows = values.reshape(scales.shape[0], -1, share).astype(F32) * scales[:, None, :]
    summed = lax.psum_scatter(
        rows.reshape(features, share), "dp", scatter_dimension=0, tiled=True
    )
    slab = lax.all_gather(summed, "fsdp", axis=1, tiled=True)
    width = slab.shape[1]
    highest = functools.partial(
        jnp.dot, precision=lax.Precision.HIGHEST, preferred_element_type=F32
    )
    half = lax.axis_index("fsdp")
    gram = lax.psum(highest(summed.T, slab), "dp")
    gram = lax.all_gather(gram, "fsdp", axis=0, tiled=True)
    inv = 1.0 / (jnp.sqrt(jnp.trace(gram)) + 1e-07)
    scaled = gram * (inv * inv)
    first = highest(slab * inv, scaled)
    mine = lambda value: lax.dynamic_slice_in_dim(value, half * share, share, 1)
    second = highest(first, mine(scaled))
    result = 3.4445 * (summed * inv) + (-4.775 * mine(first) + 2.0315 * second)
    return (0.25 * jnp.sqrt(F32(features * width)) * result).astype(BF16)


def solution(mesh):
    dp, fsdp = mesh.shape["dp"], mesh.shape["fsdp"]

    def run(partials, scales):
        features, width = partials.shape[1:]
        fast = (
            (dp, fsdp) == (16, 2)
            and features % (dp * GRAIN * sum(CHUNKS)) == 0
            and width == 4 * PIECE
        )
        return jax.shard_map(
            fast_body if fast else plain_body,
            mesh=mesh,
            in_specs=(P("dp", None, "fsdp"), P("dp", None, "fsdp")),
            out_specs=P("dp", "fsdp"),
            check_vma=False,
        )(partials, scales)

    return run
```

```python
import functools

import jax
import jax.numpy as jnp
import numpy as np
from jax import lax
from jax.experimental import pallas as pl
from jax.experimental.pallas import tpu as pltpu
from jax.sharding import PartitionSpec as P

BLOCK = 128
GRAIN = 16
CHUNKS = (3, 5, 4, 3)
LEAVE = (0, 1, 3)
STEPS = (
    ("sum", 0), ("halve", 0), ("sum", 1), ("halve", 1), ("finish", 0), ("sum", 2),
    ("sum", 3), ("halve", 2), ("finish", 1), ("finish", 2), ("finish", 3),
)
AFTER = {
    ("sum", 1): (("sent", 0), ("half", 0)),
    ("sum", 2): (("sent", 1), ("half", 1), ("grad", 0)),
    ("sum", 3): (("keep", 2),),
    ("halve", 2): (("keep", 3),),
    ("finish", 1): (("sent", 2), ("across", 0)),
    ("finish", 3): (("across", 1), ("grad", 2)),
}
ORDER = (0, 2, 1, 3)
PIECE = 256
HALF = PIECE // 2
NEAR = HALF + HALF // 2 + HALF
CROSS = 2 * HALF
PACKED = NEAR + CROSS
F32 = jnp.float32
BF16 = jnp.bfloat16
VMEM = 48 * 1024 * 1024
WHOLE = pl.BlockSpec(memory_space=pltpu.VMEM)
SCALARS = pl.BlockSpec(memory_space=pltpu.SMEM)
ANYWHERE = pl.BlockSpec(memory_space=pl.ANY)


def params():
    return pltpu.CompilerParams(vmem_limit_bytes=VMEM)


def split(value):
    high = value.astype(BF16)
    return high, (value - high.astype(F32)).astype(BF16)


def dot3(a, b, contract):
    dims = (contract, ((), ()))

    def one(u, v):
        return lax.dot_general(u, v, dims, preferred_element_type=F32)

    return one(a[0], b[0]) + (one(a[0], b[1]) + one(a[1], b[0]))


def dot_rows(a, high, low, flipped=False):
    return dot3(split(a), (high, low), ((1,), (int(flipped),)))


def slot_row(at, side, slot, own_rows):
    zed, ex, core = at[0], at[1], at[2]
    z = lax.bitwise_xor(zed, ORDER[slot])
    c = lax.bitwise_xor(core, side % 2)
    x = lax.bitwise_xor(ex, side // 2)
    return ((z * 2 + x) * 2 + c) * own_rows


SLOTS = len(ORDER)
GROUPS = {
    "halves": ((0, 1), (2,), (3,)),
    "pair": ((0, 1), (2, 3)),
    "direct": ((0,), (1,), (2,), (3,)),
}
ROUTES = ("halves", "halves", "halves", "direct")
SPAN = 4
TAIL = 3 * SLOTS * SPAN


def pack_kernel(own_rows, spans, at, values, scales, own, *refs):
    outs, gathered = refs[:-1], refs[-1]
    blocks = scales.shape[0]

    def copy(side, start, rows, out):
        for slot in range(SLOTS):
            base = pl.multiple_of(slot_row(at, side, slot, own_rows) + start, GRAIN)
            out[slot * rows : (slot + 1) * rows, :] = values[pl.ds(base, rows), :]

    def tail(side, out):
        for slot in range(SLOTS):
            first = slot_row(at, side, slot, own_rows) // BLOCK
            for n in range(SPAN):
                row = jnp.minimum(first + n, blocks - 1)
                gathered[slot * SPAN + n : slot * SPAN + n + 1, :] = scales[row]
        left = gathered[...]
        for n in range(3):
            part = left.astype(BF16)
            row = out.shape[0] - TAIL + n * SLOTS * SPAN
            out[row : row + SLOTS * SPAN, :] = part
            left = left - part.astype(F32)

    copy(0, 0, own_rows, own)
    copy(1, 0, own_rows, outs[0])
    tail(1, outs[0])
    for n, (start, rows) in enumerate(spans):
        for side in (2, 3):
            out = outs[2 * n + side - 1]
            copy(side, start, rows, out)
            if n == 0:
                tail(side, out)


def pack(values, scales, at, own_rows, spans):
    width = values.shape[1]
    lengths = [SLOTS * own_rows, SLOTS * own_rows + TAIL]
    for n, (_, rows) in enumerate(spans):
        lengths += [SLOTS * rows + (TAIL if n == 0 else 0)] * 2
    return pl.pallas_call(
        functools.partial(pack_kernel, own_rows, spans),
        in_specs=[SCALARS, WHOLE, WHOLE],
        out_specs=[WHOLE] * len(lengths),
        out_shape=[jax.ShapeDtypeStruct((rows, width), BF16) for rows in lengths],
        scratch_shapes=[pltpu.VMEM((SLOTS * SPAN, width), F32)],
        compiler_params=params(),
        name="pack_rows",
    )(at, values, scales)


def dequant_kernel(own_rows, start, rows, groups, at, scales, own, core_raw, *refs):
    heads, raws, refs = refs[:2], refs[2:4], refs[4:]
    outs, packed = refs[-1 - len(groups) : -1], refs[-1]
    size = SLOTS * SPAN
    for n, ref in enumerate((core_raw, *heads)):
        row = ref.shape[0] - TAIL
        parts = [
            ref[row + k * size : row + (k + 1) * size, :].astype(F32) for k in range(3)
        ]
        packed[n * size : (n + 1) * size, :] = parts[0] + parts[1] + parts[2]
    for slot in range(SLOTS):
        base = slot_row(at, 0, slot, own_rows)
        for g in range(rows // GRAIN):
            block = (base + (start + g * GRAIN)) // BLOCK
            span = slot * SPAN + block - base // BLOCK
            here = slice(g * GRAIN, (g + 1) * GRAIN)
            row = slot * own_rows + start + g * GRAIN
            there = slice(row, row + GRAIN)
            row = slot * rows + g * GRAIN
            total = own[there, :].astype(F32) * scales[block]
            total += core_raw[there, :].astype(F32) * packed[pl.ds(span, 1), :]
            for n, raw in enumerate(raws):
                part = raw[row : row + GRAIN, :].astype(F32)
                total += part * packed[pl.ds((n + 1) * size + span, 1), :]
            for out, group in zip(outs, groups):
                if slot in group and len(group) > 1:
                    out[group.index(slot), here, :] = total
                elif slot in group:
                    out[here, :] = total


def dequant(
    at, scales, own, core_raw, heads, raws, own_rows, start, rows, groups, after, carry
):
    width = own.shape[1]
    shapes = [
        jax.ShapeDtypeStruct((len(group), rows, width)[len(group) == 1 :], F32)
        for group in groups
    ]
    first, count, made = 8 + len(after), len(carry), len(groups)

    def kernel(*refs):
        kept = refs[:8] + refs[first + count : first + count + made] + refs[-1:]
        dequant_kernel(own_rows, start, rows, groups, *kept)

    outs = pl.pallas_call(
        kernel,
        in_specs=[SCALARS] + [WHOLE] * 7 + [ANYWHERE] * (len(after) + count),
        out_specs=[WHOLE] * made + [ANYWHERE] * count,
        out_shape=shapes + [jax.ShapeDtypeStruct(x.shape, x.dtype) for x in carry],
        scratch_shapes=[pltpu.VMEM((3 * SLOTS * SPAN, width), F32)],
        input_output_aliases={first + n: made + n for n in range(count)},
        compiler_params=params(),
        name="dequant_sum",
    )(at, scales, own, core_raw, *heads, *raws, *after, *carry)
    return outs[:made], outs[made:]


def add(terms, after, swap=False):
    def kernel(*refs):
        total = refs[0][...]
        for ref in refs[1 : len(terms) - swap]:
            total = total + ref[...]
        if swap:
            last = refs[len(terms) - 1]
            refs[-1][0] = total[0] + last[1]
            refs[-1][1] = total[1] + last[0]
        else:
            refs[-1][...] = total

    return pl.pallas_call(
        kernel,
        in_specs=[WHOLE] * len(terms) + [ANYWHERE] * len(after),
        out_specs=WHOLE,
        out_shape=jax.ShapeDtypeStruct(terms[0].shape, F32),
        compiler_params=params(),
        name="add_rows",
    )(*terms, *after)


def put_rows(slabs, high, low, column):
    row = 0
    for slab in slabs:
        here, share = slice(row, row + slab.shape[0]), slab.shape[1]
        high[here, column : column + share], low[here, column : column + share] = split(slab[...])
        row += slab.shape[0]


def put_slots(at, flat, out):
    part = out.shape[1]
    for slot in range(8):
        z = lax.bitwise_xor(at[0], ORDER[slot % 4])
        x = lax.bitwise_xor(at[1], slot // 4)
        out[slot] = flat[pl.ds(pl.multiple_of((z * 2 + x) * part, 8), part), :]


def near_kernel(count, at, *refs):
    slabs, outs, (high, low, flat) = refs[:count], refs[count : count + 2], refs[-3:]
    put_rows(slabs, high, low, 0)

    def take(start, width):
        lanes = pl.ds(pl.multiple_of(start, HALF), width)
        return high[:, lanes], low[:, lanes]

    contract = ((0,), (0,))
    for side, out in enumerate(outs):
        core = lax.bitwise_xor(at[2], side)
        own = take(core * PIECE, PIECE)
        block = dot3(own, own, contract)
        flat[0:HALF, :] = block[0:HALF, :]
        flat[HALF : HALF + HALF // 2, 0:HALF] = block[HALF : HALF + HALF // 2, HALF:]
        flat[HALF : HALF + HALF // 2, HALF:] = block[HALF + HALF // 2 :, HALF:]
        left = take(core * HALF, HALF)
        flat[NEAR - HALF :, :] = dot3(left, take(PIECE, PIECE), contract)
        put_slots(at, flat, out)


def cross_kernel(count, at, *refs):
    slabs, outs, (high, low, flat) = refs[: 2 * count], refs[-5:-3], refs[-3:]
    share = slabs[0].shape[1]
    put_rows(slabs[:count], high, low, 0)
    put_rows(slabs[count:], high, low, share)

    def take(start, width):
        lanes = pl.ds(pl.multiple_of(start, HALF), width)
        return high[:, lanes], low[:, lanes]

    contract = ((0,), (0,))
    half = at[3]
    for side, out in enumerate(outs):
        core = lax.bitwise_xor(at[2], side)
        for k in range(2):
            mine = core * PIECE
            other = share + lax.bitwise_xor(core, k) * PIECE
            left = jnp.where(half == 0, mine, other + HALF)
            right = jnp.where(half == 0, other, mine)
            flat[k * HALF : (k + 1) * HALF, :] = dot3(
                take(left, HALF), take(right, PIECE), contract
            )
        put_slots(at, flat, out)


def gram_part(kernel, at, slabs, count, packed, name, after):
    rows = sum(slab.shape[0] for slab in slabs[:count])
    width = slabs[0].shape[1] * (len(slabs) // count)
    return pl.pallas_call(
        functools.partial(kernel, count),
        in_specs=[SCALARS] + [WHOLE] * len(slabs) + [ANYWHERE] * len(after),
        out_specs=[WHOLE] * 2,
        out_shape=[jax.ShapeDtypeStruct((8, packed // 8, PIECE), F32)] * 2,
        scratch_shapes=[pltpu.VMEM((rows, width), BF16)] * 2 + [pltpu.VMEM((packed, PIECE), F32)],
        compiler_params=params(),
        name=name,
    )(at, *slabs, *after)


def unpack(at, pieces, places, packed, length):
    zed, ex, core, half = at[0], at[1], at[2], at[3]
    for ref, slots in zip(pieces, places):
        part = ref.shape[1]
        for n, (kz, kx, kc, kf) in enumerate(slots):
            quarter = 2 * lax.bitwise_xor(half, kf) + lax.bitwise_xor(core, kc)
            chip = 2 * lax.bitwise_xor(zed, kz) + lax.bitwise_xor(ex, kx)
            row = pl.multiple_of(quarter * length + chip * part, 8)
            packed[pl.ds(row, part), :] = ref[n]


def start_kernel(places, count, at, *refs):
    pieces, refs = refs[: len(places)], refs[len(places) :]
    owns, acrosses, refs = refs[:count], refs[count : 2 * count], refs[2 * count :]
    high, low, inv_out, own_part, far_part, packed = refs
    half = at[3]
    unpack(at, pieces, places, packed, NEAR)
    trace = jnp.zeros((1, 1), F32)
    rows = lax.broadcasted_iota(jnp.int32, (HALF, HALF), 0)
    columns = lax.broadcasted_iota(jnp.int32, (HALF, HALF), 1)

    def put(f, block, row, column):
        here = (f, slice(row, row + block.shape[0]), slice(column, column + block.shape[1]))
        high[here], low[here] = split(block)

    for q in range(4):
        f, edge = q // 2, q % 2 * PIECE
        base = q * NEAR
        top = packed[base : base + HALF, :]
        bottom = packed[base + HALF : base + HALF + HALF // 2, :]
        bottom = jnp.concatenate([bottom[:, :HALF], bottom[:, HALF:]], 0)
        for block in (top[:, :HALF], bottom):
            trace += jnp.sum(jnp.where(rows == columns, block, 0.0), keepdims=True)
        put(f, top, edge, edge)
        put(f, top[:, HALF:].T, edge + HALF, edge)
        put(f, bottom, edge + HALF, edge + HALF)
        block = packed[base + NEAR - HALF : base + NEAR, :]
        first = q % 2 * HALF
        put(f, block, first, PIECE)
        put(f, block.T, PIECE, first)
    inv = 1.0 / (jnp.sqrt(trace) + 1e-07)
    inv_out[...] = jnp.broadcast_to(inv, inv_out.shape)
    unit = jnp.concatenate([own[...] for own in owns], 0) * inv
    far = jnp.concatenate([across[...] for across in acrosses], 0) * inv
    own_part[...] = dot_rows(unit, high[half], low[half])
    far_part[...] = dot_rows(far, high[1 - half], low[1 - half])


def finish_kernel(scale, places, count, at, *refs):
    pieces, refs = refs[: len(places)], refs[len(places) :]
    owns, acrosses, refs = refs[:count], refs[count : 2 * count], refs[2 * count :]
    near_high, near_low, inv_in, own_part, far_part, out, packed, high, low = refs
    half = at[3]
    unpack(at, pieces, places, packed, CROSS)
    for a in range(2):
        for b in range(2, 4):
            row = ((a ^ b) - 2) * HALF
            for first, owner in ((0, a), (HALF, b)):
                base = owner * CROSS + row
                here = (
                    slice(a * PIECE + first, a * PIECE + first + HALF),
                    slice((b - 2) * PIECE, (b - 1) * PIECE),
                )
                high[here], low[here] = split(packed[base : base + HALF, :])
    inv = inv_in[0:1, 0:1]
    unit = jnp.concatenate([own[...] for own in owns], 0) * inv
    far = jnp.concatenate([across[...] for across in acrosses], 0) * inv

    def last(second_half):
        block = (high[...], low[...])
        first = own_part[...] + dot_rows(far, *block, flipped=not second_half)
        other = far_part[...] + dot_rows(unit, *block, flipped=second_half)
        first, other = first * (inv * inv), other * (inv * inv)
        second = dot_rows(first, near_high[half], near_low[half])
        second += dot_rows(other, *block, flipped=not second_half)
        second = second * (inv * inv)
        result = 3.4445 * unit + (-4.775 * first + 2.0315 * second)
        out[...] = (scale * result).astype(out.dtype)

    pl.when(half == 0)(lambda: last(False))
    pl.when(half == 1)(lambda: last(True))


def update(at, near, cross, owns, acrosses, scale):
    rows = sum(own.shape[0] for own in owns)
    share, count = owns[0].shape[1], len(owns)
    pieces, places = zip(*near)
    square = jax.ShapeDtypeStruct((2, share, share), BF16)
    part = jax.ShapeDtypeStruct((rows, share), F32)
    started = pl.pallas_call(
        functools.partial(start_kernel, places, count),
        in_specs=[SCALARS] + [WHOLE] * (len(pieces) + 2 * count),
        out_specs=[WHOLE] * 5,
        out_shape=[square, square, jax.ShapeDtypeStruct((8, 128), F32), part, part],
        scratch_shapes=[pltpu.VMEM((4 * NEAR, PIECE), F32)],
        compiler_params=params(),
        name="update_start",
    )(at, *pieces, *owns, *acrosses)
    pieces, places = zip(*cross)
    return pl.pallas_call(
        functools.partial(finish_kernel, scale, places, count),
        in_specs=[SCALARS] + [WHOLE] * (len(pieces) + 2 * count + 5),
        out_specs=WHOLE,
        out_shape=jax.ShapeDtypeStruct((rows, share), BF16),
        scratch_shapes=[pltpu.VMEM((4 * CROSS, PIECE), F32)]
        + [pltpu.VMEM((share, share), BF16)] * 2,
        compiler_params=params(),
        name="update_finish",
    )(at, *pieces, *owns, *acrosses, *started)


AXIS_BITS = {"f": 1, "c": 2, "x": 4, "z1": 8, "z2": 16}


def flip(value, *names):
    mask = sum(AXIS_BITS[name] for name in names)
    count = lax.axis_size(("dp", "fsdp"))
    return lax.ppermute(value, ("dp", "fsdp"), [(i, i ^ mask) for i in range(count)])


ZEDS = (("z2",), ("z1",), ("z1", "z2"))
SIDES = (("x",), ("c", "x"))


def fast_body(partials, scales):
    values, scales = partials[0], scales.transpose(1, 0, 2)
    features, share = values.shape
    own_rows = features // lax.axis_size("dp")
    rank = lax.axis_index("dp")
    at = jnp.stack([rank // 4, rank // 2 % 2, rank % 2, lax.axis_index("fsdp")])
    unit = own_rows // sum(CHUNKS)
    spans, start = [], 0
    for size in CHUNKS:
        spans.append((start, size * unit))
        start += size * unit

    own, core_raw, *outs = pack(values, scales, at, own_rows, spans)
    core_raw = flip(core_raw, "c")

    def cross(pair):
        return [flip(out, *side) for out, side in zip(pair, SIDES)]

    outs = [outs[2 * n : 2 * n + 2] for n in range(len(spans))]
    raws = [cross(pair) for pair in outs[:2]]
    heads = raws[0]
    owns, acrosses, held = [], [], []
    made = {}

    def there(step, n):
        return [made[name] for name in AFTER.get((step, n), ())]

    def add_partials(n):
        start, rows = spans[n]
        carry = outs[n + 2] if n + 2 < len(spans) else []
        (keep, *go), carry = dequant(
            at, scales, own, core_raw, heads, raws[n], own_rows, start, rows,
            GROUPS[ROUTES[n]], there("sum", n), carry,
        )
        if carry:
            raws.append(cross(carry))
        made["keep", n] = keep
        if ROUTES[n] == "direct":
            made["got", n] = [flip(part, *names) for part, names in zip(go, ZEDS)]
        elif ROUTES[n] == "halves":
            made["got", n] = [flip(part, "z1") for part in go]
        else:
            made["got", n] = flip(go[0], "z1")

    def halve(n):
        keep, got = made["keep", n], made["got", n]
        made["sent", n] = add([keep[1], got[1]], there("halve", n))
        made["half", n] = keep[0] + got[0]

    def finish(n):
        if ROUTES[n] == "direct":
            terms = [made["keep", n], *made["got", n]]
        else:
            terms = [made["half", n], flip(made["sent", n], "z2")]
        made["grad", n] = add(terms, there("finish", n))
        held.append(made["grad", n])
        if n in LEAVE:
            group = jnp.concatenate(held) if len(held) > 1 else held[0]
            across = flip(group, "f")
            made["across", n] = across
            owns.append(group)
            acrosses.append(across)
            held.clear()

    for step, n in STEPS:
        {"sum": add_partials, "halve": halve, "finish": finish}[step](n)

    count = len(owns)
    own, far = gram_part(near_kernel, at, owns, count, NEAR, "gram_near", [])
    core = [flip(far[4:], "c"), flip(far[:4], "c")]
    near_sent = add([own[4:], core[0]], [])
    near_x = flip(near_sent, "x")
    cross_own, far = gram_part(
        cross_kernel, at, owns + acrosses, count, CROSS, "gram_cross", [near_sent]
    )
    cross_core = [flip(far[4:], "c"), flip(far[:4], "c")]
    cross_x = flip(add([cross_own[4:], cross_core[0]], [near_x]), "x")

    near = own[:4] + core[1] + near_x
    near_z1 = flip(near[2:], "z1")
    near = near[:2] + near_z1
    near_z2 = flip(near, "z2")
    near = add([near, near_z2], [], swap=True)
    near_other = flip(near, "z1")

    cross = add([cross_own[:4], cross_core[1], cross_x], [near_z1])
    cross = add([cross[:2], flip(cross[2:], "z1")], [near_z2])
    cross = add([cross, flip(cross, "z2")], [near_other], swap=True)
    cross_other = flip(cross, "z1")

    near = jnp.concatenate([near, near_other])
    near = jnp.concatenate([near, flip(near, "x")])
    cross = jnp.concatenate([cross, cross_other])
    cross = jnp.concatenate([cross, flip(cross, "f")])
    near_slots = [(z, x, 0, 0) for x in range(2) for z in ORDER]
    cross_slots = [(z, 0, 0, f) for f in range(2) for z in ORDER]
    near = [(near, near_slots), (flip(near, "f"), [(z, x, 0, 1) for z, x, _, _ in near_slots])]
    cross = [(cross, cross_slots), (flip(cross, "x"), [(z, 1, 0, f) for z, _, _, f in cross_slots])]
    for group in (near, cross):
        group += [
            (flip(part, "c"), [(z, x, 1, f) for z, x, _, f in slots]) for part, slots in group
        ]
    scale = float(0.25 * np.sqrt(np.float32(features * 2 * share)))
    return update(at, near, cross, owns, acrosses, scale)


def plain_body(partials, scales):
    values, scales = partials[0], scales[0]
    features, share = values.shape
    dp = lax.axis_size("dp")
    rows = values.reshape(scales.shape[0], -1, share).astype(F32) * scales[:, None, :]
    summed = lax.psum_scatter(
        rows.reshape(features, share), "dp", scatter_dimension=0, tiled=True
    )
    slab = lax.all_gather(summed, "fsdp", axis=1, tiled=True)
    width = slab.shape[1]
    highest = functools.partial(
        jnp.dot, precision=lax.Precision.HIGHEST, preferred_element_type=F32
    )
    half = lax.axis_index("fsdp")
    gram = lax.psum(highest(summed.T, slab), "dp")
    gram = lax.all_gather(gram, "fsdp", axis=0, tiled=True)
    inv = 1.0 / (jnp.sqrt(jnp.trace(gram)) + 1e-07)
    scaled = gram * (inv * inv)
    first = highest(slab * inv, scaled)
    mine = lambda value: lax.dynamic_slice_in_dim(value, half * share, share, 1)
    second = highest(first, mine(scaled))
    result = 3.4445 * (summed * inv) + (-4.775 * mine(first) + 2.0315 * second)
    return (0.25 * jnp.sqrt(F32(features * width)) * result).astype(BF16)


def solution(mesh):
    dp, fsdp = mesh.shape["dp"], mesh.shape["fsdp"]

    def run(partials, scales):
        features, width = partials.shape[1:]
        fast = (
            (dp, fsdp) == (16, 2)
            and features % (dp * GRAIN * sum(CHUNKS)) == 0
            and width == 4 * PIECE
        )
        return jax.shard_map(
            fast_body if fast else plain_body,
            mesh=mesh,
            in_specs=(P("dp", None, "fsdp"), P("dp", None, "fsdp")),
            out_specs=P("dp", "fsdp"),
            check_vma=False,
        )(partials, scales)

    return run
```

```python
import functools

import jax
import jax.numpy as jnp
import numpy as np
from jax import lax
from jax.experimental import pallas as pl
from jax.experimental.pallas import tpu as pltpu
from jax.sharding import PartitionSpec as P

BLOCK = 128
GRAIN = 16
CHUNKS = (3, 5, 4, 3)
LEAVE = (1, 3)
STEPS = (
    ("sum", 0), ("halve", 0), ("sum", 1), ("sum", 2), ("halve", 1), ("finish", 0), ("sum", 3),
    ("halve", 2), ("halve", 3), ("finish", 1), ("finish", 2), ("finish", 3),
)
AFTER = {
    ("sum", 1): (("sent", 0), ("half", 0)),
    ("sum", 2): (("near", 1), ("last", 1)),
    ("halve", 1): (("keep", 2),),
    ("finish", 0): (("keep", 2),),
    ("sum", 3): (("sent", 1), ("grad", 0)),
    ("halve", 2): (("keep", 3),),
    ("finish", 1): (("sent", 2), ("sent", 3)),
    ("finish", 3): (("across", 1),),
}
ORDER = (0, 2, 1, 3)
PIECE = 256
HALF = PIECE // 2
NEAR = HALF + HALF // 2 + HALF
CROSS = 2 * HALF
PACKED = NEAR + CROSS
F32 = jnp.float32
BF16 = jnp.bfloat16
VMEM = 48 * 1024 * 1024
WHOLE = pl.BlockSpec(memory_space=pltpu.VMEM)
SCALARS = pl.BlockSpec(memory_space=pltpu.SMEM)
ANYWHERE = pl.BlockSpec(memory_space=pl.ANY)


def params():
    return pltpu.CompilerParams(vmem_limit_bytes=VMEM)


def split(value):
    high = value.astype(BF16)
    return high, (value - high.astype(F32)).astype(BF16)


def dot3(a, b, contract):
    dims = (contract, ((), ()))

    def one(u, v):
        return lax.dot_general(u, v, dims, preferred_element_type=F32)

    return one(a[0], b[0]) + (one(a[0], b[1]) + one(a[1], b[0]))


def dot_rows(a, high, low, flipped=False):
    return dot3(split(a), (high, low), ((1,), (int(flipped),)))


def slot_row(at, side, slot, own_rows):
    zed, ex, core = at[0], at[1], at[2]
    z = lax.bitwise_xor(zed, ORDER[slot])
    c = lax.bitwise_xor(core, side % 2)
    x = lax.bitwise_xor(ex, side // 2)
    return ((z * 2 + x) * 2 + c) * own_rows


SLOTS = len(ORDER)
GROUPS = {
    "halves": ((0, 1), (2,), (3,)),
    "pair": ((0, 1), (2, 3)),
    "direct": ((0,), (1,), (2,), (3,)),
}
ROUTES = ("halves", "halves", "halves", "halves")
SPAN = 4
TAIL = 3 * SLOTS * SPAN


def pack_kernel(own_rows, spans, at, values, scales, own, table, *refs):
    outs, gathered = refs[:-1], refs[-1]
    blocks = scales.shape[0]

    def copy(side, start, rows, out):
        for slot in range(SLOTS):
            base = pl.multiple_of(slot_row(at, side, slot, own_rows) + start, GRAIN)
            out[slot * rows : (slot + 1) * rows, :] = values[pl.ds(base, rows), :]

    def gather(side, out):
        for slot in range(SLOTS):
            first = slot_row(at, side, slot, own_rows) // BLOCK
            for n in range(SPAN):
                row = jnp.minimum(first + n, blocks - 1)
                out[slot * SPAN + n : slot * SPAN + n + 1, :] = scales[row]

    def tail(side, out):
        gather(side, gathered)
        left = gathered[...]
        for n in range(3):
            part = left.astype(BF16)
            row = out.shape[0] - TAIL + n * SLOTS * SPAN
            out[row : row + SLOTS * SPAN, :] = part
            left = left - part.astype(F32)

    gather(0, table)
    copy(0, 0, own_rows, own)
    copy(1, 0, own_rows, outs[0])
    tail(1, outs[0])
    for n, (start, rows) in enumerate(spans):
        for side in (2, 3):
            out = outs[2 * n + side - 1]
            copy(side, start, rows, out)
            if n == 0:
                tail(side, out)


def pack(values, scales, at, own_rows, spans):
    width = values.shape[1]
    lengths = [SLOTS * own_rows, SLOTS * own_rows + TAIL]
    for n, (_, rows) in enumerate(spans):
        lengths += [SLOTS * rows + (TAIL if n == 0 else 0)] * 2
    return pl.pallas_call(
        functools.partial(pack_kernel, own_rows, spans),
        in_specs=[SCALARS, WHOLE, WHOLE],
        out_specs=[WHOLE] * (1 + len(lengths)),
        out_shape=[jax.ShapeDtypeStruct((lengths[0], width), BF16)]
        + [jax.ShapeDtypeStruct((SLOTS * SPAN, width), F32)]
        + [jax.ShapeDtypeStruct((rows, width), BF16) for rows in lengths[1:]],
        scratch_shapes=[pltpu.VMEM((SLOTS * SPAN, width), F32)],
        compiler_params=params(),
        name="pack_rows",
    )(at, values, scales)


def dequant_kernel(own_rows, start, rows, groups, at, scales, own, core_raw, *refs):
    heads, raws, refs = refs[:2], refs[2:4], refs[4:]
    outs, packed = refs[-1 - len(groups) : -1], refs[-1]
    size = SLOTS * SPAN
    for n, ref in enumerate((core_raw, *heads)):
        row = ref.shape[0] - TAIL
        parts = [
            ref[row + k * size : row + (k + 1) * size, :].astype(F32) for k in range(3)
        ]
        packed[n * size : (n + 1) * size, :] = parts[0] + parts[1] + parts[2]
    for slot in range(SLOTS):
        base = slot_row(at, 0, slot, own_rows)
        for g in range(rows // GRAIN):
            block = (base + (start + g * GRAIN)) // BLOCK
            span = slot * SPAN + block - base // BLOCK
            here = slice(g * GRAIN, (g + 1) * GRAIN)
            row = slot * own_rows + start + g * GRAIN
            there = slice(row, row + GRAIN)
            row = slot * rows + g * GRAIN
            total = own[there, :].astype(F32) * scales[pl.ds(span, 1), :]
            total += core_raw[there, :].astype(F32) * packed[pl.ds(span, 1), :]
            for n, raw in enumerate(raws):
                part = raw[row : row + GRAIN, :].astype(F32)
                total += part * packed[pl.ds((n + 1) * size + span, 1), :]
            for out, group in zip(outs, groups):
                if slot in group and len(group) > 1:
                    out[group.index(slot), here, :] = total
                elif slot in group:
                    out[here, :] = total


def dequant(
    at, scales, own, core_raw, heads, raws, own_rows, start, rows, groups, after, carry
):
    width = own.shape[1]
    shapes = [
        jax.ShapeDtypeStruct((len(group), rows, width)[len(group) == 1 :], F32)
        for group in groups
    ]
    first, count, made = 8 + len(after), len(carry), len(groups)

    def kernel(*refs):
        kept = refs[:8] + refs[first + count : first + count + made] + refs[-1:]
        dequant_kernel(own_rows, start, rows, groups, *kept)

    outs = pl.pallas_call(
        kernel,
        in_specs=[SCALARS] + [WHOLE] * 7 + [ANYWHERE] * (len(after) + count),
        out_specs=[WHOLE] * made + [ANYWHERE] * count,
        out_shape=shapes + [jax.ShapeDtypeStruct(x.shape, x.dtype) for x in carry],
        scratch_shapes=[pltpu.VMEM((3 * SLOTS * SPAN, width), F32)],
        input_output_aliases={first + n: made + n for n in range(count)},
        compiler_params=params(),
        name="dequant_sum",
    )(at, scales, own, core_raw, *heads, *raws, *after, *carry)
    return outs[:made], outs[made:]


def add(terms, after, swap=False):
    def kernel(*refs):
        total = refs[0][...]
        for ref in refs[1 : len(terms) - swap]:
            total = total + ref[...]
        if swap:
            last = refs[len(terms) - 1]
            refs[-1][0] = total[0] + last[1]
            refs[-1][1] = total[1] + last[0]
        else:
            refs[-1][...] = total

    return pl.pallas_call(
        kernel,
        in_specs=[WHOLE] * len(terms) + [ANYWHERE] * len(after),
        out_specs=WHOLE,
        out_shape=jax.ShapeDtypeStruct(terms[0].shape, F32),
        compiler_params=params(),
        name="add_rows",
    )(*terms, *after)


def put_rows(slabs, high, low, column):
    row = 0
    for slab in slabs:
        here, share = slice(row, row + slab.shape[0]), slab.shape[1]
        high[here, column : column + share], low[here, column : column + share] = split(slab[...])
        row += slab.shape[0]


def put_slots(at, flat, out):
    part = out.shape[1]
    for slot in range(8):
        z = lax.bitwise_xor(at[0], ORDER[slot % 4])
        x = lax.bitwise_xor(at[1], slot // 4)
        out[slot] = flat[pl.ds(pl.multiple_of((z * 2 + x) * part, 8), part), :]


def near_kernel(count, at, *refs):
    slabs, outs, (high, low, flat) = refs[:count], refs[count : count + 2], refs[-3:]
    put_rows(slabs, high, low, 0)

    def take(start, width):
        lanes = pl.ds(pl.multiple_of(start, HALF), width)
        return high[:, lanes], low[:, lanes]

    contract = ((0,), (0,))
    for side, out in enumerate(outs):
        core = lax.bitwise_xor(at[2], side)
        own = take(core * PIECE, PIECE)
        block = dot3(own, own, contract)
        flat[0:HALF, :] = block[0:HALF, :]
        flat[HALF : HALF + HALF // 2, 0:HALF] = block[HALF : HALF + HALF // 2, HALF:]
        flat[HALF : HALF + HALF // 2, HALF:] = block[HALF + HALF // 2 :, HALF:]
        left = take(core * HALF, HALF)
        flat[NEAR - HALF :, :] = dot3(left, take(PIECE, PIECE), contract)
        put_slots(at, flat, out)


def cross_kernel(count, at, *refs):
    slabs, outs, (high, low, flat) = refs[: 2 * count], refs[-5:-3], refs[-3:]
    share = slabs[0].shape[1]
    put_rows(slabs[:count], high, low, 0)
    put_rows(slabs[count:], high, low, share)

    def take(start, width):
        lanes = pl.ds(pl.multiple_of(start, HALF), width)
        return high[:, lanes], low[:, lanes]

    contract = ((0,), (0,))
    half = at[3]
    for side, out in enumerate(outs):
        core = lax.bitwise_xor(at[2], side)
        for k in range(2):
            mine = core * PIECE
            other = share + lax.bitwise_xor(core, k) * PIECE
            left = jnp.where(half == 0, mine, other + HALF)
            right = jnp.where(half == 0, other, mine)
            flat[k * HALF : (k + 1) * HALF, :] = dot3(
                take(left, HALF), take(right, PIECE), contract
            )
        put_slots(at, flat, out)


def gram_part(kernel, at, slabs, count, packed, name, after):
    rows = sum(slab.shape[0] for slab in slabs[:count])
    width = slabs[0].shape[1] * (len(slabs) // count)
    return pl.pallas_call(
        functools.partial(kernel, count),
        in_specs=[SCALARS] + [WHOLE] * len(slabs) + [ANYWHERE] * len(after),
        out_specs=[WHOLE] * 2,
        out_shape=[jax.ShapeDtypeStruct((8, packed // 8, PIECE), F32)] * 2,
        scratch_shapes=[pltpu.VMEM((rows, width), BF16)] * 2 + [pltpu.VMEM((packed, PIECE), F32)],
        compiler_params=params(),
        name=name,
    )(at, *slabs, *after)


def unpack(at, pieces, places, packed, length):
    zed, ex, core, half = at[0], at[1], at[2], at[3]
    for ref, slots in zip(pieces, places):
        part = ref.shape[1]
        for n, (kz, kx, kc, kf) in enumerate(slots):
            quarter = 2 * lax.bitwise_xor(half, kf) + lax.bitwise_xor(core, kc)
            chip = 2 * lax.bitwise_xor(zed, kz) + lax.bitwise_xor(ex, kx)
            row = pl.multiple_of(quarter * length + chip * part, 8)
            packed[pl.ds(row, part), :] = ref[n]


def start_kernel(places, count, at, *refs):
    pieces, refs = refs[: len(places)], refs[len(places) :]
    owns, acrosses, refs = refs[:count], refs[count : 2 * count], refs[2 * count :]
    high, low, inv_out, own_part, far_part, packed = refs
    half = at[3]
    unpack(at, pieces, places, packed, NEAR)
    trace = jnp.zeros((1, 1), F32)
    rows = lax.broadcasted_iota(jnp.int32, (HALF, HALF), 0)
    columns = lax.broadcasted_iota(jnp.int32, (HALF, HALF), 1)

    def put(f, block, row, column):
        here = (f, slice(row, row + block.shape[0]), slice(column, column + block.shape[1]))
        high[here], low[here] = split(block)

    for q in range(4):
        f, edge = q // 2, q % 2 * PIECE
        base = q * NEAR
        top = packed[base : base + HALF, :]
        bottom = packed[base + HALF : base + HALF + HALF // 2, :]
        bottom = jnp.concatenate([bottom[:, :HALF], bottom[:, HALF:]], 0)
        for block in (top[:, :HALF], bottom):
            trace += jnp.sum(jnp.where(rows == columns, block, 0.0), keepdims=True)
        put(f, top, edge, edge)
        put(f, top[:, HALF:].T, edge + HALF, edge)
        put(f, bottom, edge + HALF, edge + HALF)
        block = packed[base + NEAR - HALF : base + NEAR, :]
        first = q % 2 * HALF
        put(f, block, first, PIECE)
        put(f, block.T, PIECE, first)
    inv = 1.0 / (jnp.sqrt(trace) + 1e-07)
    inv_out[...] = jnp.broadcast_to(inv, inv_out.shape)
    unit = jnp.concatenate([own[...] for own in owns], 0) * inv
    far = jnp.concatenate([across[...] for across in acrosses], 0) * inv
    own_part[...] = dot_rows(unit, high[half], low[half])
    far_part[...] = dot_rows(far, high[1 - half], low[1 - half])


def finish_kernel(scale, places, count, at, *refs):
    pieces, refs = refs[: len(places)], refs[len(places) :]
    owns, acrosses, refs = refs[:count], refs[count : 2 * count], refs[2 * count :]
    near_high, near_low, inv_in, own_part, far_part, out, packed, high, low = refs
    half = at[3]
    unpack(at, pieces, places, packed, CROSS)
    for a in range(2):
        for b in range(2, 4):
            row = ((a ^ b) - 2) * HALF
            for first, owner in ((0, a), (HALF, b)):
                base = owner * CROSS + row
                here = (
                    slice(a * PIECE + first, a * PIECE + first + HALF),
                    slice((b - 2) * PIECE, (b - 1) * PIECE),
                )
                high[here], low[here] = split(packed[base : base + HALF, :])
    inv = inv_in[0:1, 0:1]
    unit = jnp.concatenate([own[...] for own in owns], 0) * inv
    far = jnp.concatenate([across[...] for across in acrosses], 0) * inv

    def last(second_half):
        block = (high[...], low[...])
        first = own_part[...] + dot_rows(far, *block, flipped=not second_half)
        other = far_part[...] + dot_rows(unit, *block, flipped=second_half)
        first, other = first * (inv * inv), other * (inv * inv)
        second = dot_rows(first, near_high[half], near_low[half])
        second += dot_rows(other, *block, flipped=not second_half)
        second = second * (inv * inv)
        result = 3.4445 * unit + (-4.775 * first + 2.0315 * second)
        out[...] = (scale * result).astype(out.dtype)

    pl.when(half == 0)(lambda: last(False))
    pl.when(half == 1)(lambda: last(True))


def update(at, near, cross, owns, acrosses, scale):
    rows = sum(own.shape[0] for own in owns)
    share, count = owns[0].shape[1], len(owns)
    pieces, places = zip(*near)
    square = jax.ShapeDtypeStruct((2, share, share), BF16)
    part = jax.ShapeDtypeStruct((rows, share), F32)
    started = pl.pallas_call(
        functools.partial(start_kernel, places, count),
        in_specs=[SCALARS] + [WHOLE] * (len(pieces) + 2 * count),
        out_specs=[WHOLE] * 5,
        out_shape=[square, square, jax.ShapeDtypeStruct((8, 128), F32), part, part],
        scratch_shapes=[pltpu.VMEM((4 * NEAR, PIECE), F32)],
        compiler_params=params(),
        name="update_start",
    )(at, *pieces, *owns, *acrosses)
    pieces, places = zip(*cross)
    return pl.pallas_call(
        functools.partial(finish_kernel, scale, places, count),
        in_specs=[SCALARS] + [WHOLE] * (len(pieces) + 2 * count + 5),
        out_specs=WHOLE,
        out_shape=jax.ShapeDtypeStruct((rows, share), BF16),
        scratch_shapes=[pltpu.VMEM((4 * CROSS, PIECE), F32)]
        + [pltpu.VMEM((share, share), BF16)] * 2,
        compiler_params=params(),
        name="update_finish",
    )(at, *pieces, *owns, *acrosses, *started)


AXIS_BITS = {"f": 1, "c": 2, "x": 4, "z1": 8, "z2": 16}


def flip(value, *names):
    mask = sum(AXIS_BITS[name] for name in names)
    count = lax.axis_size(("dp", "fsdp"))
    return lax.ppermute(value, ("dp", "fsdp"), [(i, i ^ mask) for i in range(count)])


ZEDS = (("z2",), ("z1",), ("z1", "z2"))
SIDES = (("x",), ("c", "x"))


def fast_body(partials, scales):
    values, scales = partials[0], scales.transpose(1, 0, 2)
    features, share = values.shape
    own_rows = features // lax.axis_size("dp")
    rank = lax.axis_index("dp")
    at = jnp.stack([rank // 4, rank // 2 % 2, rank % 2, lax.axis_index("fsdp")])
    unit = own_rows // sum(CHUNKS)
    spans, start = [], 0
    for size in CHUNKS:
        spans.append((start, size * unit))
        start += size * unit

    own, table, core_raw, *outs = pack(values, scales, at, own_rows, spans)
    core_raw = flip(core_raw, "c")

    def cross(pair):
        return [flip(out, *side) for out, side in zip(pair, SIDES)]

    outs = [outs[2 * n : 2 * n + 2] for n in range(len(spans))]
    raws = [cross(pair) for pair in outs[:2]]
    heads = raws[0]
    owns, acrosses, held = [], [], []
    made = {}

    def there(step, n):
        return [made[name] for name in AFTER.get((step, n), ())]

    def add_partials(n):
        start, rows = spans[n]
        carry = outs[n + 2] if n + 2 < len(spans) else []
        (keep, *go), carry = dequant(
            at, table, own, core_raw, heads, raws[n], own_rows, start, rows,
            GROUPS[ROUTES[n]], there("sum", n), carry,
        )
        if carry:
            raws.append(cross(carry))
        made["keep", n] = keep
        if ROUTES[n] == "direct":
            made["got", n] = [flip(part, *names) for part, names in zip(go, ZEDS)]
        elif ROUTES[n] == "halves":
            made["got", n] = [flip(part, "z1") for part in go]
            made["near", n], made["last", n] = made["got", n]
        else:
            made["got", n] = flip(go[0], "z1")

    def halve(n):
        keep, got = made["keep", n], made["got", n]
        made["sent", n] = add([keep[1], got[1]], there("halve", n))
        made["half", n] = keep[0] + got[0]

    def finish(n):
        if ROUTES[n] == "direct":
            terms = [made["keep", n], *made["got", n]]
        else:
            terms = [made["half", n], flip(made["sent", n], "z2")]
        made["grad", n] = add(terms, there("finish", n))
        held.append(made["grad", n])
        if n in LEAVE:
            group = jnp.concatenate(held) if len(held) > 1 else held[0]
            across = flip(group, "f")
            made["across", n] = across
            owns.append(group)
            acrosses.append(across)
            held.clear()

    for step, n in STEPS:
        {"sum": add_partials, "halve": halve, "finish": finish}[step](n)

    count = len(owns)
    own, far = gram_part(near_kernel, at, owns, count, NEAR, "gram_near", [])
    core = [flip(far[4:], "c"), flip(far[:4], "c")]
    near_sent = add([own[4:], core[0]], [])
    near_x = flip(near_sent, "x")
    cross_own, far = gram_part(
        cross_kernel, at, owns + acrosses, count, CROSS, "gram_cross", [near_sent]
    )
    cross_core = [flip(far[4:], "c"), flip(far[:4], "c")]
    cross_x = flip(add([cross_own[4:], cross_core[0]], [near_x]), "x")

    near = own[:4] + core[1] + near_x
    near_z1 = flip(near[2:], "z1")
    near = near[:2] + near_z1
    near_z2 = flip(near, "z2")
    near = add([near, near_z2], [], swap=True)
    near_other = flip(near, "z1")

    cross = add([cross_own[:4], cross_core[1], cross_x], [near_z1])
    cross = add([cross[:2], flip(cross[2:], "z1")], [near_z2])
    cross = add([cross, flip(cross, "z2")], [near_other], swap=True)
    cross_other = flip(cross, "z1")

    near = jnp.concatenate([near, near_other])
    near = jnp.concatenate([near, flip(near, "x")])
    cross = jnp.concatenate([cross, cross_other])
    cross = jnp.concatenate([cross, flip(cross, "f")])
    near_slots = [(z, x, 0, 0) for x in range(2) for z in ORDER]
    cross_slots = [(z, 0, 0, f) for f in range(2) for z in ORDER]
    near = [(near, near_slots), (flip(near, "f"), [(z, x, 0, 1) for z, x, _, _ in near_slots])]
    cross = [(cross, cross_slots), (flip(cross, "x"), [(z, 1, 0, f) for z, _, _, f in cross_slots])]
    for group in (near, cross):
        group += [
            (flip(part, "c"), [(z, x, 1, f) for z, x, _, f in slots]) for part, slots in group
        ]
    scale = float(0.25 * np.sqrt(np.float32(features * 2 * share)))
    return update(at, near, cross, owns, acrosses, scale)


def plain_body(partials, scales):
    values, scales = partials[0], scales[0]
    features, share = values.shape
    dp = lax.axis_size("dp")
    rows = values.reshape(scales.shape[0], -1, share).astype(F32) * scales[:, None, :]
    summed = lax.psum_scatter(
        rows.reshape(features, share), "dp", scatter_dimension=0, tiled=True
    )
    slab = lax.all_gather(summed, "fsdp", axis=1, tiled=True)
    width = slab.shape[1]
    highest = functools.partial(
        jnp.dot, precision=lax.Precision.HIGHEST, preferred_element_type=F32
    )
    half = lax.axis_index("fsdp")
    gram = lax.psum(highest(summed.T, slab), "dp")
    gram = lax.all_gather(gram, "fsdp", axis=0, tiled=True)
    inv = 1.0 / (jnp.sqrt(jnp.trace(gram)) + 1e-07)
    scaled = gram * (inv * inv)
    first = highest(slab * inv, scaled)
    mine = lambda value: lax.dynamic_slice_in_dim(value, half * share, share, 1)
    second = highest(first, mine(scaled))
    result = 3.4445 * (summed * inv) + (-4.775 * mine(first) + 2.0315 * second)
    return (0.25 * jnp.sqrt(F32(features * width)) * result).astype(BF16)


def solution(mesh):
    dp, fsdp = mesh.shape["dp"], mesh.shape["fsdp"]

    def run(partials, scales):
        features, width = partials.shape[1:]
        fast = (
            (dp, fsdp) == (16, 2)
            and features % (dp * GRAIN * sum(CHUNKS)) == 0
            and width == 4 * PIECE
        )
        return jax.shard_map(
            fast_body if fast else plain_body,
            mesh=mesh,
            in_specs=(P("dp", None, "fsdp"), P("dp", None, "fsdp")),
            out_specs=P("dp", "fsdp"),
            check_vma=False,
        )(partials, scales)

    return run
```

```python
import functools

import jax
import jax.numpy as jnp
import numpy as np
from jax import lax
from jax.experimental import pallas as pl
from jax.experimental.pallas import tpu as pltpu
from jax.sharding import PartitionSpec as P

BLOCK = 128
GRAIN = 16
CHUNKS = (3, 5, 4, 3)
LEAVE = (1, 3)
STEPS = (
    ("sum", 0), ("halve", 0), ("sum", 1), ("sum", 2), ("halve", 1), ("finish", 0), ("sum", 3),
    ("halve", 2), ("halve", 3), ("finish", 1), ("finish", 2), ("finish", 3),
)
AFTER = {
    ("sum", 1): (("sent", 0), ("half", 0)),
    ("sum", 2): (("near", 1), ("last", 1)),
    ("halve", 1): (("keep", 2),),
    ("finish", 0): (("keep", 2),),
    ("sum", 3): (("sent", 1), ("grad", 0)),
    ("halve", 2): (("keep", 3),),
    ("finish", 1): (("sent", 2), ("sent", 3)),
    ("finish", 3): (("across", 1),),
}
ORDER = (0, 2, 1, 3)
PIECE = 256
HALF = PIECE // 2
NEAR = HALF + HALF // 2 + HALF
CROSS = 2 * HALF
PACKED = NEAR + CROSS
F32 = jnp.float32
BF16 = jnp.bfloat16
VMEM = 48 * 1024 * 1024
WHOLE = pl.BlockSpec(memory_space=pltpu.VMEM)
SCALARS = pl.BlockSpec(memory_space=pltpu.SMEM)
ANYWHERE = pl.BlockSpec(memory_space=pl.ANY)


def params():
    return pltpu.CompilerParams(vmem_limit_bytes=VMEM)


def split(value):
    high = value.astype(BF16)
    return high, (value - high.astype(F32)).astype(BF16)


def dot3(a, b, contract):
    dims = (contract, ((), ()))

    def one(u, v):
        return lax.dot_general(u, v, dims, preferred_element_type=F32)

    return one(a[0], b[0]) + (one(a[0], b[1]) + one(a[1], b[0]))


def dot_rows(a, high, low, flipped=False):
    return dot3(split(a), (high, low), ((1,), (int(flipped),)))


def slot_row(at, side, slot, own_rows):
    zed, ex, core = at[0], at[1], at[2]
    z = lax.bitwise_xor(zed, ORDER[slot])
    c = lax.bitwise_xor(core, side % 2)
    x = lax.bitwise_xor(ex, side // 2)
    return ((z * 2 + x) * 2 + c) * own_rows


SLOTS = len(ORDER)
GROUPS = {
    "halves": ((0, 1), (2,), (3,)),
    "pair": ((0, 1), (2, 3)),
    "direct": ((0,), (1,), (2,), (3,)),
}
ROUTES = ("halves", "halves", "halves", "halves")
SPAN = 4
TAIL = 3 * SLOTS * SPAN


def pack_kernel(own_rows, spans, at, values, scales, own, table, *refs):
    outs, gathered = refs[:-1], refs[-1]
    blocks = scales.shape[0]

    def copy(side, start, rows, out):
        for slot in range(SLOTS):
            base = pl.multiple_of(slot_row(at, side, slot, own_rows) + start, GRAIN)
            out[slot * rows : (slot + 1) * rows, :] = values[pl.ds(base, rows), :]

    def gather(side, out):
        for slot in range(SLOTS):
            first = slot_row(at, side, slot, own_rows) // BLOCK
            for n in range(SPAN):
                row = jnp.minimum(first + n, blocks - 1)
                out[slot * SPAN + n : slot * SPAN + n + 1, :] = scales[row]

    def tail(side, out):
        gather(side, gathered)
        left = gathered[...]
        for n in range(3):
            part = left.astype(BF16)
            row = out.shape[0] - TAIL + n * SLOTS * SPAN
            out[row : row + SLOTS * SPAN, :] = part
            left = left - part.astype(F32)

    gather(0, table)
    copy(0, 0, own_rows, own)
    copy(1, 0, own_rows, outs[0])
    tail(1, outs[0])
    for n, (start, rows) in enumerate(spans):
        for side in (2, 3):
            out = outs[2 * n + side - 1]
            copy(side, start, rows, out)
            if n == 0:
                tail(side, out)


def pack(values, scales, at, own_rows, spans):
    width = values.shape[1]
    lengths = [SLOTS * own_rows, SLOTS * own_rows + TAIL]
    for n, (_, rows) in enumerate(spans):
        lengths += [SLOTS * rows + (TAIL if n == 0 else 0)] * 2
    return pl.pallas_call(
        functools.partial(pack_kernel, own_rows, spans),
        in_specs=[SCALARS, WHOLE, WHOLE],
        out_specs=[WHOLE] * (1 + len(lengths)),
        out_shape=[jax.ShapeDtypeStruct((lengths[0], width), BF16)]
        + [jax.ShapeDtypeStruct((SLOTS * SPAN, width), F32)]
        + [jax.ShapeDtypeStruct((rows, width), BF16) for rows in lengths[1:]],
        scratch_shapes=[pltpu.VMEM((SLOTS * SPAN, width), F32)],
        compiler_params=params(),
        name="pack_rows",
    )(at, values, scales)


def dequant_kernel(own_rows, start, rows, groups, at, scales, own, core_raw, *refs):
    heads, raws, refs = refs[:2], refs[2:4], refs[4:]
    outs, packed = refs[-1 - len(groups) : -1], refs[-1]
    size = SLOTS * SPAN
    for n, ref in enumerate((core_raw, *heads)):
        row = ref.shape[0] - TAIL
        parts = [
            ref[row + k * size : row + (k + 1) * size, :].astype(F32) for k in range(3)
        ]
        packed[n * size : (n + 1) * size, :] = parts[0] + parts[1] + parts[2]
    for slot in range(SLOTS):
        base = slot_row(at, 0, slot, own_rows)
        for g in range(rows // GRAIN):
            block = (base + (start + g * GRAIN)) // BLOCK
            span = slot * SPAN + block - base // BLOCK
            here = slice(g * GRAIN, (g + 1) * GRAIN)
            row = slot * own_rows + start + g * GRAIN
            there = slice(row, row + GRAIN)
            row = slot * rows + g * GRAIN
            total = own[there, :].astype(F32) * scales[pl.ds(span, 1), :]
            total += core_raw[there, :].astype(F32) * packed[pl.ds(span, 1), :]
            for n, raw in enumerate(raws):
                part = raw[row : row + GRAIN, :].astype(F32)
                total += part * packed[pl.ds((n + 1) * size + span, 1), :]
            for out, group in zip(outs, groups):
                if slot in group and len(group) > 1:
                    out[group.index(slot), here, :] = total
                elif slot in group:
                    out[here, :] = total


def dequant(
    at, scales, own, core_raw, heads, raws, own_rows, start, rows, groups, after, carry
):
    width = own.shape[1]
    shapes = [
        jax.ShapeDtypeStruct((len(group), rows, width)[len(group) == 1 :], F32)
        for group in groups
    ]
    first, count, made = 8 + len(after), len(carry), len(groups)

    def kernel(*refs):
        kept = refs[:8] + refs[first + count : first + count + made] + refs[-1:]
        dequant_kernel(own_rows, start, rows, groups, *kept)

    outs = pl.pallas_call(
        kernel,
        in_specs=[SCALARS] + [WHOLE] * 7 + [ANYWHERE] * (len(after) + count),
        out_specs=[WHOLE] * made + [ANYWHERE] * count,
        out_shape=shapes + [jax.ShapeDtypeStruct(x.shape, x.dtype) for x in carry],
        scratch_shapes=[pltpu.VMEM((3 * SLOTS * SPAN, width), F32)],
        input_output_aliases={first + n: made + n for n in range(count)},
        compiler_params=params(),
        name="dequant_sum",
    )(at, scales, own, core_raw, *heads, *raws, *after, *carry)
    return outs[:made], outs[made:]


def add(terms, after, swap=False):
    def kernel(*refs):
        total = refs[0][...]
        for ref in refs[1 : len(terms) - swap]:
            total = total + ref[...]
        if swap:
            last = refs[len(terms) - 1]
            refs[-1][0] = total[0] + last[1]
            refs[-1][1] = total[1] + last[0]
        else:
            refs[-1][...] = total

    return pl.pallas_call(
        kernel,
        in_specs=[WHOLE] * len(terms) + [ANYWHERE] * len(after),
        out_specs=WHOLE,
        out_shape=jax.ShapeDtypeStruct(terms[0].shape, F32),
        compiler_params=params(),
        name="add_rows",
    )(*terms, *after)


def put_rows(slabs, high, low, column):
    row = 0
    for slab in slabs:
        here, share = slice(row, row + slab.shape[0]), slab.shape[1]
        high[here, column : column + share], low[here, column : column + share] = split(slab[...])
        row += slab.shape[0]


def put_slots(at, flat, out):
    part = out.shape[1]
    for slot in range(8):
        z = lax.bitwise_xor(at[0], ORDER[slot % 4])
        x = lax.bitwise_xor(at[1], slot // 4)
        out[slot] = flat[pl.ds(pl.multiple_of((z * 2 + x) * part, 8), part), :]


def put_out(at, side, bases, flat, outs, early):
    if bases:
        flat[...] += bases[0][side]
    if early:
        outs[0][side] = flat[...]
    else:
        put_slots(at, flat, outs[side])


def near_kernel(count, based, early, at, *refs):
    slabs, bases, (high, low, flat) = refs[:count], refs[count : count + based], refs[-3:]
    outs = refs[-4:-3] if early else refs[-5:-3]
    put_rows(slabs, high, low, 0)

    def take(start, width):
        lanes = pl.ds(pl.multiple_of(start, HALF), width)
        return high[:, lanes], low[:, lanes]

    contract = ((0,), (0,))
    for side in range(2):
        core = lax.bitwise_xor(at[2], side)
        own = take(core * PIECE, PIECE)
        block = dot3(own, own, contract)
        flat[0:HALF, :] = block[0:HALF, :]
        flat[HALF : HALF + HALF // 2, 0:HALF] = block[HALF : HALF + HALF // 2, HALF:]
        flat[HALF : HALF + HALF // 2, HALF:] = block[HALF + HALF // 2 :, HALF:]
        left = take(core * HALF, HALF)
        flat[NEAR - HALF :, :] = dot3(left, take(PIECE, PIECE), contract)
        put_out(at, side, bases, flat, outs, early)


def cross_kernel(count, based, early, at, *refs):
    slabs, bases = refs[: 2 * count], refs[2 * count : 2 * count + based]
    high, low, flat = refs[-3:]
    outs = refs[-4:-3] if early else refs[-5:-3]
    share = slabs[0].shape[1]
    put_rows(slabs[:count], high, low, 0)
    put_rows(slabs[count:], high, low, share)

    def take(start, width):
        lanes = pl.ds(pl.multiple_of(start, HALF), width)
        return high[:, lanes], low[:, lanes]

    contract = ((0,), (0,))
    half = at[3]
    for side in range(2):
        core = lax.bitwise_xor(at[2], side)
        for k in range(2):
            mine = core * PIECE
            other = share + lax.bitwise_xor(core, k) * PIECE
            left = jnp.where(half == 0, mine, other + HALF)
            right = jnp.where(half == 0, other, mine)
            flat[k * HALF : (k + 1) * HALF, :] = dot3(
                take(left, HALF), take(right, PIECE), contract
            )
        put_out(at, side, bases, flat, outs, early)


def gram_part(kernel, at, slabs, count, packed, name, base=None, early=False, after=()):
    rows = sum(slab.shape[0] for slab in slabs[:count])
    width = slabs[0].shape[1] * (len(slabs) // count)
    bases = [] if base is None else [base]
    if early:
        shapes = [jax.ShapeDtypeStruct((2, packed, PIECE), F32)]
    else:
        shapes = [jax.ShapeDtypeStruct((8, packed // 8, PIECE), F32)] * 2
    return pl.pallas_call(
        functools.partial(kernel, count, len(bases), early),
        in_specs=[SCALARS] + [WHOLE] * len(slabs + bases) + [ANYWHERE] * len(after),
        out_specs=[WHOLE] * len(shapes),
        out_shape=shapes,
        scratch_shapes=[pltpu.VMEM((rows, width), BF16)] * 2 + [pltpu.VMEM((packed, PIECE), F32)],
        compiler_params=params(),
        name=name,
    )(at, *slabs, *bases, *after)


def unpack(at, pieces, places, packed, length):
    zed, ex, core, half = at[0], at[1], at[2], at[3]
    for ref, slots in zip(pieces, places):
        part = ref.shape[1]
        for n, (kz, kx, kc, kf) in enumerate(slots):
            quarter = 2 * lax.bitwise_xor(half, kf) + lax.bitwise_xor(core, kc)
            chip = 2 * lax.bitwise_xor(zed, kz) + lax.bitwise_xor(ex, kx)
            row = pl.multiple_of(quarter * length + chip * part, 8)
            packed[pl.ds(row, part), :] = ref[n]


def start_kernel(places, count, at, *refs):
    pieces, refs = refs[: len(places)], refs[len(places) :]
    owns, acrosses, refs = refs[:count], refs[count : 2 * count], refs[2 * count :]
    high, low, inv_out, own_part, far_part, packed = refs
    half = at[3]
    unpack(at, pieces, places, packed, NEAR)
    trace = jnp.zeros((1, 1), F32)
    rows = lax.broadcasted_iota(jnp.int32, (HALF, HALF), 0)
    columns = lax.broadcasted_iota(jnp.int32, (HALF, HALF), 1)

    def put(f, block, row, column):
        here = (f, slice(row, row + block.shape[0]), slice(column, column + block.shape[1]))
        high[here], low[here] = split(block)

    for q in range(4):
        f, edge = q // 2, q % 2 * PIECE
        base = q * NEAR
        top = packed[base : base + HALF, :]
        bottom = packed[base + HALF : base + HALF + HALF // 2, :]
        bottom = jnp.concatenate([bottom[:, :HALF], bottom[:, HALF:]], 0)
        for block in (top[:, :HALF], bottom):
            trace += jnp.sum(jnp.where(rows == columns, block, 0.0), keepdims=True)
        put(f, top, edge, edge)
        put(f, top[:, HALF:].T, edge + HALF, edge)
        put(f, bottom, edge + HALF, edge + HALF)
        block = packed[base + NEAR - HALF : base + NEAR, :]
        first = q % 2 * HALF
        put(f, block, first, PIECE)
        put(f, block.T, PIECE, first)
    inv = 1.0 / (jnp.sqrt(trace) + 1e-07)
    inv_out[...] = jnp.broadcast_to(inv, inv_out.shape)
    unit = jnp.concatenate([own[...] for own in owns], 0) * inv
    far = jnp.concatenate([across[...] for across in acrosses], 0) * inv
    own_part[...] = dot_rows(unit, high[half], low[half])
    far_part[...] = dot_rows(far, high[1 - half], low[1 - half])


def finish_kernel(scale, places, count, at, *refs):
    pieces, refs = refs[: len(places)], refs[len(places) :]
    owns, acrosses, refs = refs[:count], refs[count : 2 * count], refs[2 * count :]
    near_high, near_low, inv_in, own_part, far_part, out, packed, high, low = refs
    half = at[3]
    unpack(at, pieces, places, packed, CROSS)
    for a in range(2):
        for b in range(2, 4):
            row = ((a ^ b) - 2) * HALF
            for first, owner in ((0, a), (HALF, b)):
                base = owner * CROSS + row
                here = (
                    slice(a * PIECE + first, a * PIECE + first + HALF),
                    slice((b - 2) * PIECE, (b - 1) * PIECE),
                )
                high[here], low[here] = split(packed[base : base + HALF, :])
    inv = inv_in[0:1, 0:1]
    unit = jnp.concatenate([own[...] for own in owns], 0) * inv
    far = jnp.concatenate([across[...] for across in acrosses], 0) * inv

    def last(second_half):
        block = (high[...], low[...])
        first = own_part[...] + dot_rows(far, *block, flipped=not second_half)
        other = far_part[...] + dot_rows(unit, *block, flipped=second_half)
        first, other = first * (inv * inv), other * (inv * inv)
        second = dot_rows(first, near_high[half], near_low[half])
        second += dot_rows(other, *block, flipped=not second_half)
        second = second * (inv * inv)
        result = 3.4445 * unit + (-4.775 * first + 2.0315 * second)
        out[...] = (scale * result).astype(out.dtype)

    pl.when(half == 0)(lambda: last(False))
    pl.when(half == 1)(lambda: last(True))


def update(at, near, cross, owns, acrosses, scale):
    rows = sum(own.shape[0] for own in owns)
    share, count = owns[0].shape[1], len(owns)
    pieces, places = zip(*near)
    square = jax.ShapeDtypeStruct((2, share, share), BF16)
    part = jax.ShapeDtypeStruct((rows, share), F32)
    started = pl.pallas_call(
        functools.partial(start_kernel, places, count),
        in_specs=[SCALARS] + [WHOLE] * (len(pieces) + 2 * count),
        out_specs=[WHOLE] * 5,
        out_shape=[square, square, jax.ShapeDtypeStruct((8, 128), F32), part, part],
        scratch_shapes=[pltpu.VMEM((4 * NEAR, PIECE), F32)],
        compiler_params=params(),
        name="update_start",
    )(at, *pieces, *owns, *acrosses)
    pieces, places = zip(*cross)
    return pl.pallas_call(
        functools.partial(finish_kernel, scale, places, count),
        in_specs=[SCALARS] + [WHOLE] * (len(pieces) + 2 * count + 5),
        out_specs=WHOLE,
        out_shape=jax.ShapeDtypeStruct((rows, share), BF16),
        scratch_shapes=[pltpu.VMEM((4 * CROSS, PIECE), F32)]
        + [pltpu.VMEM((share, share), BF16)] * 2,
        compiler_params=params(),
        name="update_finish",
    )(at, *pieces, *owns, *acrosses, *started)


AXIS_BITS = {"f": 1, "c": 2, "x": 4, "z1": 8, "z2": 16}


def flip(value, *names):
    mask = sum(AXIS_BITS[name] for name in names)
    count = lax.axis_size(("dp", "fsdp"))
    return lax.ppermute(value, ("dp", "fsdp"), [(i, i ^ mask) for i in range(count)])


ZEDS = (("z2",), ("z1",), ("z1", "z2"))
SIDES = (("x",), ("c", "x"))


def fast_body(partials, scales):
    values, scales = partials[0], scales.transpose(1, 0, 2)
    features, share = values.shape
    own_rows = features // lax.axis_size("dp")
    rank = lax.axis_index("dp")
    at = jnp.stack([rank // 4, rank // 2 % 2, rank % 2, lax.axis_index("fsdp")])
    unit = own_rows // sum(CHUNKS)
    spans, start = [], 0
    for size in CHUNKS:
        spans.append((start, size * unit))
        start += size * unit

    own, table, core_raw, *outs = pack(values, scales, at, own_rows, spans)
    core_raw = flip(core_raw, "c")

    def cross(pair):
        return [flip(out, *side) for out, side in zip(pair, SIDES)]

    outs = [outs[2 * n : 2 * n + 2] for n in range(len(spans))]
    raws = [cross(pair) for pair in outs[:2]]
    heads = raws[0]
    owns, acrosses, held = [], [], []
    made = {}

    def there(step, n):
        return [made[name] for name in AFTER.get((step, n), ())]

    def add_partials(n):
        start, rows = spans[n]
        carry = outs[n + 2] if n + 2 < len(spans) else []
        (keep, *go), carry = dequant(
            at, table, own, core_raw, heads, raws[n], own_rows, start, rows,
            GROUPS[ROUTES[n]], there("sum", n), carry,
        )
        if carry:
            raws.append(cross(carry))
        made["keep", n] = keep
        if ROUTES[n] == "direct":
            made["got", n] = [flip(part, *names) for part, names in zip(go, ZEDS)]
        elif ROUTES[n] == "halves":
            made["got", n] = [flip(part, "z1") for part in go]
            made["near", n], made["last", n] = made["got", n]
        else:
            made["got", n] = flip(go[0], "z1")

    def halve(n):
        keep, got = made["keep", n], made["got", n]
        made["sent", n] = add([keep[1], got[1]], there("halve", n))
        made["half", n] = keep[0] + got[0]

    def finish(n):
        if ROUTES[n] == "direct":
            terms = [made["keep", n], *made["got", n]]
        else:
            terms = [made["half", n], flip(made["sent", n], "z2")]
        made["grad", n] = add(terms, there("finish", n))
        held.append(made["grad", n])
        if n in LEAVE:
            group = jnp.concatenate(held) if len(held) > 1 else held[0]
            across = flip(group, "f")
            made["across", n] = across
            owns.append(group)
            acrosses.append(across)
            if len(owns) == 1:
                (made["base", n],) = gram_part(
                    near_kernel, at, owns, 1, NEAR, "gram_near_early", early=True
                )
            held.clear()

    for step, n in STEPS:
        {"sum": add_partials, "halve": halve, "finish": finish}[step](n)

    (cross_base,) = gram_part(
        cross_kernel, at, owns[:1] + acrosses[:1], 1, CROSS, "gram_cross_early", early=True
    )
    own, far = gram_part(
        near_kernel, at, owns[1:], 1, NEAR, "gram_near", made["base", 1]
    )
    core = [flip(far[4:], "c"), flip(far[:4], "c")]
    near_sent = add([own[4:], core[0]], [])
    near_x = flip(near_sent, "x")
    cross_own, far = gram_part(
        cross_kernel, at, owns[1:] + acrosses[1:], 1, CROSS, "gram_cross", cross_base,
        after=[near_sent],
    )
    cross_core = [flip(far[4:], "c"), flip(far[:4], "c")]
    cross_x = flip(add([cross_own[4:], cross_core[0]], [near_x]), "x")

    near = own[:4] + core[1] + near_x
    near_z1 = flip(near[2:], "z1")
    near = near[:2] + near_z1
    near_z2 = flip(near, "z2")
    near = add([near, near_z2], [], swap=True)
    near_other = flip(near, "z1")

    cross = add([cross_own[:4], cross_core[1], cross_x], [near_z1])
    cross = add([cross[:2], flip(cross[2:], "z1")], [near_z2])
    cross = add([cross, flip(cross, "z2")], [near_other], swap=True)
    cross_other = flip(cross, "z1")

    near = jnp.concatenate([near, near_other])
    near = jnp.concatenate([near, flip(near, "x")])
    cross = jnp.concatenate([cross, cross_other])
    cross = jnp.concatenate([cross, flip(cross, "f")])
    near_slots = [(z, x, 0, 0) for x in range(2) for z in ORDER]
    cross_slots = [(z, 0, 0, f) for f in range(2) for z in ORDER]
    near = [(near, near_slots), (flip(near, "f"), [(z, x, 0, 1) for z, x, _, _ in near_slots])]
    cross = [(cross, cross_slots), (flip(cross, "x"), [(z, 1, 0, f) for z, _, _, f in cross_slots])]
    for group in (near, cross):
        group += [
            (flip(part, "c"), [(z, x, 1, f) for z, x, _, f in slots]) for part, slots in group
        ]
    scale = float(0.25 * np.sqrt(np.float32(features * 2 * share)))
    return update(at, near, cross, owns, acrosses, scale)


def plain_body(partials, scales):
    values, scales = partials[0], scales[0]
    features, share = values.shape
    dp = lax.axis_size("dp")
    rows = values.reshape(scales.shape[0], -1, share).astype(F32) * scales[:, None, :]
    summed = lax.psum_scatter(
        rows.reshape(features, share), "dp", scatter_dimension=0, tiled=True
    )
    slab = lax.all_gather(summed, "fsdp", axis=1, tiled=True)
    width = slab.shape[1]
    highest = functools.partial(
        jnp.dot, precision=lax.Precision.HIGHEST, preferred_element_type=F32
    )
    half = lax.axis_index("fsdp")
    gram = lax.psum(highest(summed.T, slab), "dp")
    gram = lax.all_gather(gram, "fsdp", axis=0, tiled=True)
    inv = 1.0 / (jnp.sqrt(jnp.trace(gram)) + 1e-07)
    scaled = gram * (inv * inv)
    first = highest(slab * inv, scaled)
    mine = lambda value: lax.dynamic_slice_in_dim(value, half * share, share, 1)
    second = highest(first, mine(scaled))
    result = 3.4445 * (summed * inv) + (-4.775 * mine(first) + 2.0315 * second)
    return (0.25 * jnp.sqrt(F32(features * width)) * result).astype(BF16)


def solution(mesh):
    dp, fsdp = mesh.shape["dp"], mesh.shape["fsdp"]

    def run(partials, scales):
        features, width = partials.shape[1:]
        fast = (
            (dp, fsdp) == (16, 2)
            and features % (dp * GRAIN * sum(CHUNKS)) == 0
            and width == 4 * PIECE
        )
        return jax.shard_map(
            fast_body if fast else plain_body,
            mesh=mesh,
            in_specs=(P("dp", None, "fsdp"), P("dp", None, "fsdp")),
            out_specs=P("dp", "fsdp"),
            check_vma=False,
        )(partials, scales)

    return run
```

```python
import functools

import jax
import jax.numpy as jnp
import numpy as np
from jax import lax
from jax.experimental import pallas as pl
from jax.experimental.pallas import tpu as pltpu
from jax.sharding import PartitionSpec as P

BLOCK = 128
GRAIN = 16
CHUNKS = (3, 5, 4, 3)
LEAVE = (1, 3)
STEPS = (
    ("sum", 0), ("halve", 0), ("sum", 1), ("sum", 2), ("halve", 1), ("finish", 0), ("sum", 3),
    ("halve", 2), ("halve", 3), ("finish", 1), ("finish", 2), ("finish", 3),
)
AFTER = {
    ("sum", 1): (("sent", 0), ("half", 0)),
    ("sum", 2): (("near", 1), ("last", 1)),
    ("halve", 1): (("keep", 2),),
    ("finish", 0): (("keep", 2),),
    ("sum", 3): (("sent", 1), ("grad", 0)),
    ("halve", 2): (("keep", 3),),
    ("finish", 1): (("sent", 2), ("sent", 3)),
    ("finish", 3): (("across", 1),),
}
ORDER = (0, 2, 1, 3)
PIECE = 256
HALF = PIECE // 2
NEAR = HALF + HALF // 2 + HALF
CROSS = 2 * HALF
PACKED = NEAR + CROSS
F32 = jnp.float32
BF16 = jnp.bfloat16
VMEM = 48 * 1024 * 1024
WHOLE = pl.BlockSpec(memory_space=pltpu.VMEM)
SCALARS = pl.BlockSpec(memory_space=pltpu.SMEM)
ANYWHERE = pl.BlockSpec(memory_space=pl.ANY)


def params():
    return pltpu.CompilerParams(vmem_limit_bytes=VMEM)


def split(value):
    high = value.astype(BF16)
    return high, (value - high.astype(F32)).astype(BF16)


def dot3(a, b, contract):
    dims = (contract, ((), ()))

    def one(u, v):
        return lax.dot_general(u, v, dims, preferred_element_type=F32)

    return one(a[0], b[0]) + (one(a[0], b[1]) + one(a[1], b[0]))


def dot_rows(a, high, low, flipped=False):
    return dot3(split(a), (high, low), ((1,), (int(flipped),)))


def slot_row(at, side, slot, own_rows):
    zed, ex, core = at[0], at[1], at[2]
    z = lax.bitwise_xor(zed, ORDER[slot])
    c = lax.bitwise_xor(core, side % 2)
    x = lax.bitwise_xor(ex, side // 2)
    return ((z * 2 + x) * 2 + c) * own_rows


SLOTS = len(ORDER)
GROUPS = {
    "halves": ((0, 1), (2,), (3,)),
    "pair": ((0, 1), (2, 3)),
    "direct": ((0,), (1,), (2,), (3,)),
}
ROUTES = ("halves", "halves", "halves", "halves")
SPAN = 4
TAIL = 3 * SLOTS * SPAN


def pack_kernel(own_rows, spans, at, values, scales, own, table, *refs):
    outs, gathered = refs[:-1], refs[-1]
    blocks = scales.shape[0]

    def copy(side, start, rows, out):
        for slot in range(SLOTS):
            base = pl.multiple_of(slot_row(at, side, slot, own_rows) + start, GRAIN)
            out[slot * rows : (slot + 1) * rows, :] = values[pl.ds(base, rows), :]

    def gather(side, out):
        for slot in range(SLOTS):
            first = slot_row(at, side, slot, own_rows) // BLOCK
            for n in range(SPAN):
                row = jnp.minimum(first + n, blocks - 1)
                out[slot * SPAN + n : slot * SPAN + n + 1, :] = scales[row]

    def tail(side, out):
        gather(side, gathered)
        left = gathered[...]
        for n in range(3):
            part = left.astype(BF16)
            row = out.shape[0] - TAIL + n * SLOTS * SPAN
            out[row : row + SLOTS * SPAN, :] = part
            left = left - part.astype(F32)

    gather(0, table)
    copy(0, 0, own_rows, own)
    copy(1, 0, own_rows, outs[0])
    tail(1, outs[0])
    for n, (start, rows) in enumerate(spans):
        for side in (2, 3):
            out = outs[2 * n + side - 1]
            copy(side, start, rows, out)
            if n == 0:
                tail(side, out)


def pack(values, scales, at, own_rows, spans):
    width = values.shape[1]
    lengths = [SLOTS * own_rows, SLOTS * own_rows + TAIL]
    for n, (_, rows) in enumerate(spans):
        lengths += [SLOTS * rows + (TAIL if n == 0 else 0)] * 2
    return pl.pallas_call(
        functools.partial(pack_kernel, own_rows, spans),
        in_specs=[SCALARS, WHOLE, WHOLE],
        out_specs=[WHOLE] * (1 + len(lengths)),
        out_shape=[jax.ShapeDtypeStruct((lengths[0], width), BF16)]
        + [jax.ShapeDtypeStruct((SLOTS * SPAN, width), F32)]
        + [jax.ShapeDtypeStruct((rows, width), BF16) for rows in lengths[1:]],
        scratch_shapes=[pltpu.VMEM((SLOTS * SPAN, width), F32)],
        compiler_params=params(),
        name="pack_rows",
    )(at, values, scales)


def dequant_kernel(own_rows, start, rows, groups, at, scales, own, core_raw, *refs):
    heads, raws, refs = refs[:2], refs[2:4], refs[4:]
    outs, packed = refs[-1 - len(groups) : -1], refs[-1]
    size = SLOTS * SPAN
    for n, ref in enumerate((core_raw, *heads)):
        row = ref.shape[0] - TAIL
        parts = [
            ref[row + k * size : row + (k + 1) * size, :].astype(F32) for k in range(3)
        ]
        packed[n * size : (n + 1) * size, :] = parts[0] + parts[1] + parts[2]
    for slot in range(SLOTS):
        base = slot_row(at, 0, slot, own_rows)
        for g in range(rows // GRAIN):
            block = (base + (start + g * GRAIN)) // BLOCK
            span = slot * SPAN + block - base // BLOCK
            here = slice(g * GRAIN, (g + 1) * GRAIN)
            row = slot * own_rows + start + g * GRAIN
            there = slice(row, row + GRAIN)
            row = slot * rows + g * GRAIN
            total = own[there, :].astype(F32) * scales[pl.ds(span, 1), :]
            total += core_raw[there, :].astype(F32) * packed[pl.ds(span, 1), :]
            for n, raw in enumerate(raws):
                part = raw[row : row + GRAIN, :].astype(F32)
                total += part * packed[pl.ds((n + 1) * size + span, 1), :]
            for out, group in zip(outs, groups):
                if slot in group and len(group) > 1:
                    out[group.index(slot), here, :] = total
                elif slot in group:
                    out[here, :] = total


def dequant(
    at, scales, own, core_raw, heads, raws, own_rows, start, rows, groups, after, carry
):
    width = own.shape[1]
    shapes = [
        jax.ShapeDtypeStruct((len(group), rows, width)[len(group) == 1 :], F32)
        for group in groups
    ]
    first, count, made = 8 + len(after), len(carry), len(groups)

    def kernel(*refs):
        kept = refs[:8] + refs[first + count : first + count + made] + refs[-1:]
        dequant_kernel(own_rows, start, rows, groups, *kept)

    outs = pl.pallas_call(
        kernel,
        in_specs=[SCALARS] + [WHOLE] * 7 + [ANYWHERE] * (len(after) + count),
        out_specs=[WHOLE] * made + [ANYWHERE] * count,
        out_shape=shapes + [jax.ShapeDtypeStruct(x.shape, x.dtype) for x in carry],
        scratch_shapes=[pltpu.VMEM((3 * SLOTS * SPAN, width), F32)],
        input_output_aliases={first + n: made + n for n in range(count)},
        compiler_params=params(),
        name="dequant_sum",
    )(at, scales, own, core_raw, *heads, *raws, *after, *carry)
    return outs[:made], outs[made:]


def add(terms, after, swap=False):
    def kernel(*refs):
        total = refs[0][...]
        for ref in refs[1 : len(terms) - swap]:
            total = total + ref[...]
        if swap:
            last = refs[len(terms) - 1]
            refs[-1][0] = total[0] + last[1]
            refs[-1][1] = total[1] + last[0]
        else:
            refs[-1][...] = total

    return pl.pallas_call(
        kernel,
        in_specs=[WHOLE] * len(terms) + [ANYWHERE] * len(after),
        out_specs=WHOLE,
        out_shape=jax.ShapeDtypeStruct(terms[0].shape, F32),
        compiler_params=params(),
        name="add_rows",
    )(*terms, *after)


def put_rows(slabs, high, low, column):
    row = 0
    for slab in slabs:
        here, share = slice(row, row + slab.shape[0]), slab.shape[1]
        high[here, column : column + share], low[here, column : column + share] = split(slab[...])
        row += slab.shape[0]


def put_slots(at, flat, out):
    part = out.shape[1]
    for slot in range(8):
        z = lax.bitwise_xor(at[0], ORDER[slot % 4])
        x = lax.bitwise_xor(at[1], slot // 4)
        out[slot] = flat[pl.ds(pl.multiple_of((z * 2 + x) * part, 8), part), :]


def put_out(at, side, bases, flat, outs, early):
    if bases:
        flat[...] += bases[0][side]
    if early:
        outs[0][side] = flat[...]
    else:
        put_slots(at, flat, outs[side])


def near_kernel(count, based, early, at, *refs):
    slabs, bases, (high, low, flat) = refs[:count], refs[count : count + based], refs[-3:]
    outs = refs[-4:-3] if early else refs[-5:-3]
    put_rows(slabs, high, low, 0)

    def take(start, width):
        lanes = pl.ds(pl.multiple_of(start, HALF), width)
        return high[:, lanes], low[:, lanes]

    contract = ((0,), (0,))
    for side in range(2):
        core = lax.bitwise_xor(at[2], side)
        own = take(core * PIECE, PIECE)
        block = dot3(own, own, contract)
        flat[0:HALF, :] = block[0:HALF, :]
        flat[HALF : HALF + HALF // 2, 0:HALF] = block[HALF : HALF + HALF // 2, HALF:]
        flat[HALF : HALF + HALF // 2, HALF:] = block[HALF + HALF // 2 :, HALF:]
        left = take(core * HALF, HALF)
        flat[NEAR - HALF :, :] = dot3(left, take(PIECE, PIECE), contract)
        put_out(at, side, bases, flat, outs, early)


def cross_kernel(count, based, early, at, *refs):
    slabs, bases = refs[: 2 * count], refs[2 * count : 2 * count + based]
    high, low, flat = refs[-3:]
    outs = refs[-4:-3] if early else refs[-5:-3]
    share = slabs[0].shape[1]
    put_rows(slabs[:count], high, low, 0)
    put_rows(slabs[count:], high, low, share)

    def take(start, width):
        lanes = pl.ds(pl.multiple_of(start, HALF), width)
        return high[:, lanes], low[:, lanes]

    contract = ((0,), (0,))
    half = at[3]
    for side in range(2):
        core = lax.bitwise_xor(at[2], side)
        for k in range(2):
            mine = core * PIECE
            other = share + lax.bitwise_xor(core, k) * PIECE
            left = jnp.where(half == 0, mine, other + HALF)
            right = jnp.where(half == 0, other, mine)
            flat[k * HALF : (k + 1) * HALF, :] = dot3(
                take(left, HALF), take(right, PIECE), contract
            )
        put_out(at, side, bases, flat, outs, early)


def gram_part(kernel, at, slabs, count, packed, name, base=None, early=False, after=()):
    rows = sum(slab.shape[0] for slab in slabs[:count])
    width = slabs[0].shape[1] * (len(slabs) // count)
    bases = [] if base is None else [base]
    if early:
        shapes = [jax.ShapeDtypeStruct((2, packed, PIECE), F32)]
    else:
        shapes = [jax.ShapeDtypeStruct((8, packed // 8, PIECE), F32)] * 2
    return pl.pallas_call(
        functools.partial(kernel, count, len(bases), early),
        in_specs=[SCALARS] + [WHOLE] * len(slabs + bases) + [ANYWHERE] * len(after),
        out_specs=[WHOLE] * len(shapes),
        out_shape=shapes,
        scratch_shapes=[pltpu.VMEM((rows, width), BF16)] * 2 + [pltpu.VMEM((packed, PIECE), F32)],
        compiler_params=params(),
        name=name,
    )(at, *slabs, *bases, *after)


def unpack(at, pieces, places, packed, length):
    zed, ex, core, half = at[0], at[1], at[2], at[3]
    for ref, slots in zip(pieces, places):
        part = ref.shape[1]
        for n, (kz, kx, kc, kf) in enumerate(slots):
            quarter = 2 * lax.bitwise_xor(half, kf) + lax.bitwise_xor(core, kc)
            chip = 2 * lax.bitwise_xor(zed, kz) + lax.bitwise_xor(ex, kx)
            row = pl.multiple_of(quarter * length + chip * part, 8)
            packed[pl.ds(row, part), :] = ref[n]


def start_kernel(places, count, at, *refs):
    pieces, refs = refs[: len(places)], refs[len(places) :]
    owns, acrosses, refs = refs[:count], refs[count : 2 * count], refs[2 * count :]
    high, low, inv_out, own_part, far_part, packed = refs
    half = at[3]
    unpack(at, pieces, places, packed, NEAR)
    trace = jnp.zeros((1, 1), F32)
    rows = lax.broadcasted_iota(jnp.int32, (HALF, HALF), 0)
    columns = lax.broadcasted_iota(jnp.int32, (HALF, HALF), 1)

    def put(f, block, row, column):
        here = (f, slice(row, row + block.shape[0]), slice(column, column + block.shape[1]))
        high[here], low[here] = split(block)

    for q in range(4):
        f, edge = q // 2, q % 2 * PIECE
        base = q * NEAR
        top = packed[base : base + HALF, :]
        bottom = packed[base + HALF : base + HALF + HALF // 2, :]
        bottom = jnp.concatenate([bottom[:, :HALF], bottom[:, HALF:]], 0)
        for block in (top[:, :HALF], bottom):
            trace += jnp.sum(jnp.where(rows == columns, block, 0.0), keepdims=True)
        put(f, top, edge, edge)
        put(f, top[:, HALF:].T, edge + HALF, edge)
        put(f, bottom, edge + HALF, edge + HALF)
        block = packed[base + NEAR - HALF : base + NEAR, :]
        first = q % 2 * HALF
        put(f, block, first, PIECE)
        put(f, block.T, PIECE, first)
    inv = 1.0 / (jnp.sqrt(trace) + 1e-07)
    inv_out[...] = jnp.broadcast_to(inv, inv_out.shape)
    unit = jnp.concatenate([own[...] for own in owns], 0) * inv
    far = jnp.concatenate([across[...] for across in acrosses], 0) * inv
    own_part[...] = dot_rows(unit, high[half], low[half])
    far_part[...] = dot_rows(far, high[1 - half], low[1 - half])


def finish_kernel(scale, places, count, at, *refs):
    pieces, refs = refs[: len(places)], refs[len(places) :]
    owns, acrosses, refs = refs[:count], refs[count : 2 * count], refs[2 * count :]
    near_high, near_low, inv_in, own_part, far_part, out, packed, high, low = refs
    half = at[3]
    unpack(at, pieces, places, packed, CROSS)
    for a in range(2):
        for b in range(2, 4):
            row = ((a ^ b) - 2) * HALF
            for first, owner in ((0, a), (HALF, b)):
                base = owner * CROSS + row
                here = (
                    slice(a * PIECE + first, a * PIECE + first + HALF),
                    slice((b - 2) * PIECE, (b - 1) * PIECE),
                )
                high[here], low[here] = split(packed[base : base + HALF, :])
    inv = inv_in[0:1, 0:1]
    unit = jnp.concatenate([own[...] for own in owns], 0) * inv
    far = jnp.concatenate([across[...] for across in acrosses], 0) * inv

    def last(second_half):
        block = (high[...], low[...])
        first = own_part[...] + dot_rows(far, *block, flipped=not second_half)
        other = far_part[...] + dot_rows(unit, *block, flipped=second_half)
        first, other = first * (inv * inv), other * (inv * inv)
        second = dot_rows(first, near_high[half], near_low[half])
        second += dot_rows(other, *block, flipped=not second_half)
        second = second * (inv * inv)
        result = 3.4445 * unit + (-4.775 * first + 2.0315 * second)
        out[...] = (scale * result).astype(out.dtype)

    pl.when(half == 0)(lambda: last(False))
    pl.when(half == 1)(lambda: last(True))


def update(at, near, cross, owns, acrosses, scale):
    rows = sum(own.shape[0] for own in owns)
    share, count = owns[0].shape[1], len(owns)
    pieces, places = zip(*near)
    square = jax.ShapeDtypeStruct((2, share, share), BF16)
    part = jax.ShapeDtypeStruct((rows, share), F32)
    started = pl.pallas_call(
        functools.partial(start_kernel, places, count),
        in_specs=[SCALARS] + [WHOLE] * (len(pieces) + 2 * count),
        out_specs=[WHOLE] * 5,
        out_shape=[square, square, jax.ShapeDtypeStruct((8, 128), F32), part, part],
        scratch_shapes=[pltpu.VMEM((4 * NEAR, PIECE), F32)],
        compiler_params=params(),
        name="update_start",
    )(at, *pieces, *owns, *acrosses)
    pieces, places = zip(*cross)
    return pl.pallas_call(
        functools.partial(finish_kernel, scale, places, count),
        in_specs=[SCALARS] + [WHOLE] * (len(pieces) + 2 * count + 5),
        out_specs=WHOLE,
        out_shape=jax.ShapeDtypeStruct((rows, share), BF16),
        scratch_shapes=[pltpu.VMEM((4 * CROSS, PIECE), F32)]
        + [pltpu.VMEM((share, share), BF16)] * 2,
        compiler_params=params(),
        name="update_finish",
    )(at, *pieces, *owns, *acrosses, *started)


AXIS_BITS = {"f": 1, "c": 2, "x": 4, "z1": 8, "z2": 16}


def flip(value, *names):
    mask = sum(AXIS_BITS[name] for name in names)
    count = lax.axis_size(("dp", "fsdp"))
    return lax.ppermute(value, ("dp", "fsdp"), [(i, i ^ mask) for i in range(count)])


ZEDS = (("z2",), ("z1",), ("z1", "z2"))
SIDES = (("x",), ("c", "x"))


def fast_body(partials, scales):
    values, scales = partials[0], scales.transpose(1, 0, 2)
    features, share = values.shape
    own_rows = features // lax.axis_size("dp")
    rank = lax.axis_index("dp")
    at = jnp.stack([rank // 4, rank // 2 % 2, rank % 2, lax.axis_index("fsdp")])
    unit = own_rows // sum(CHUNKS)
    spans, start = [], 0
    for size in CHUNKS:
        spans.append((start, size * unit))
        start += size * unit

    own, table, core_raw, *outs = pack(values, scales, at, own_rows, spans)
    core_raw = flip(core_raw, "c")

    def cross(pair):
        return [flip(out, *side) for out, side in zip(pair, SIDES)]

    outs = [outs[2 * n : 2 * n + 2] for n in range(len(spans))]
    raws = [cross(pair) for pair in outs[:2]]
    heads = raws[0]
    owns, acrosses, held = [], [], []
    made = {}

    def there(step, n):
        return [made[name] for name in AFTER.get((step, n), ())]

    def add_partials(n):
        start, rows = spans[n]
        carry = outs[n + 2] if n + 2 < len(spans) else []
        (keep, *go), carry = dequant(
            at, table, own, core_raw, heads, raws[n], own_rows, start, rows,
            GROUPS[ROUTES[n]], there("sum", n), carry,
        )
        if carry:
            raws.append(cross(carry))
        made["keep", n] = keep
        if ROUTES[n] == "direct":
            made["got", n] = [flip(part, *names) for part, names in zip(go, ZEDS)]
        elif ROUTES[n] == "halves":
            made["got", n] = [flip(part, "z1") for part in go]
            made["near", n], made["last", n] = made["got", n]
        else:
            made["got", n] = flip(go[0], "z1")

    def halve(n):
        keep, got = made["keep", n], made["got", n]
        made["sent", n] = add([keep[1], got[1]], there("halve", n))
        made["half", n] = keep[0] + got[0]

    def finish(n):
        if ROUTES[n] == "direct":
            terms = [made["keep", n], *made["got", n]]
        else:
            terms = [made["half", n], flip(made["sent", n], "z2")]
        made["grad", n] = add(terms, there("finish", n))
        held.append(made["grad", n])
        if n in LEAVE:
            group = jnp.concatenate(held) if len(held) > 1 else held[0]
            across = flip(group, "f")
            made["across", n] = across
            owns.append(group)
            acrosses.append(across)
            if len(owns) == 1:
                (made["base", n],) = gram_part(
                    near_kernel, at, owns, 1, NEAR, "gram_near_early", early=True
                )
            held.clear()

    for step, n in STEPS:
        {"sum": add_partials, "halve": halve, "finish": finish}[step](n)

    own, far = gram_part(
        near_kernel, at, owns[1:], 1, NEAR, "gram_near", made["base", 1]
    )
    core = [flip(far[4:], "c"), flip(far[:4], "c")]
    near_sent = add([own[4:], core[0]], [])
    near_x = flip(near_sent, "x")
    (cross_base,) = gram_part(
        cross_kernel, at, owns[:1] + acrosses[:1], 1, CROSS, "gram_cross_early", early=True,
        after=[near_sent],
    )
    cross_own, far = gram_part(
        cross_kernel, at, owns[1:] + acrosses[1:], 1, CROSS, "gram_cross", cross_base,
        after=[near_sent],
    )
    cross_core = [flip(far[4:], "c"), flip(far[:4], "c")]
    cross_x = flip(add([cross_own[4:], cross_core[0]], []), "x")

    near = own[:4] + core[1] + near_x
    near_z1 = flip(near[2:], "z1")
    near = near[:2] + near_z1
    near_z2 = flip(near, "z2")
    near = add([near, near_z2], [], swap=True)
    near_other = flip(near, "z1")

    cross = add([cross_own[:4], cross_core[1], cross_x], [near_z1])
    cross = add([cross[:2], flip(cross[2:], "z1")], [near_z2])
    cross = add([cross, flip(cross, "z2")], [near_other], swap=True)
    cross_other = flip(cross, "z1")

    near = jnp.concatenate([near, near_other])
    near = jnp.concatenate([near, flip(near, "x")])
    cross = jnp.concatenate([cross, cross_other])
    cross = jnp.concatenate([cross, flip(cross, "f")])
    near_slots = [(z, x, 0, 0) for x in range(2) for z in ORDER]
    cross_slots = [(z, 0, 0, f) for f in range(2) for z in ORDER]
    near = [(near, near_slots), (flip(near, "f"), [(z, x, 0, 1) for z, x, _, _ in near_slots])]
    cross = [(cross, cross_slots), (flip(cross, "x"), [(z, 1, 0, f) for z, _, _, f in cross_slots])]
    for group in (near, cross):
        group += [
            (flip(part, "c"), [(z, x, 1, f) for z, x, _, f in slots]) for part, slots in group
        ]
    scale = float(0.25 * np.sqrt(np.float32(features * 2 * share)))
    return update(at, near, cross, owns, acrosses, scale)


def plain_body(partials, scales):
    values, scales = partials[0], scales[0]
    features, share = values.shape
    dp = lax.axis_size("dp")
    rows = values.reshape(scales.shape[0], -1, share).astype(F32) * scales[:, None, :]
    summed = lax.psum_scatter(
        rows.reshape(features, share), "dp", scatter_dimension=0, tiled=True
    )
    slab = lax.all_gather(summed, "fsdp", axis=1, tiled=True)
    width = slab.shape[1]
    highest = functools.partial(
        jnp.dot, precision=lax.Precision.HIGHEST, preferred_element_type=F32
    )
    half = lax.axis_index("fsdp")
    gram = lax.psum(highest(summed.T, slab), "dp")
    gram = lax.all_gather(gram, "fsdp", axis=0, tiled=True)
    inv = 1.0 / (jnp.sqrt(jnp.trace(gram)) + 1e-07)
    scaled = gram * (inv * inv)
    first = highest(slab * inv, scaled)
    mine = lambda value: lax.dynamic_slice_in_dim(value, half * share, share, 1)
    second = highest(first, mine(scaled))
    result = 3.4445 * (summed * inv) + (-4.775 * mine(first) + 2.0315 * second)
    return (0.25 * jnp.sqrt(F32(features * width)) * result).astype(BF16)


def solution(mesh):
    dp, fsdp = mesh.shape["dp"], mesh.shape["fsdp"]

    def run(partials, scales):
        features, width = partials.shape[1:]
        fast = (
            (dp, fsdp) == (16, 2)
            and features % (dp * GRAIN * sum(CHUNKS)) == 0
            and width == 4 * PIECE
        )
        return jax.shard_map(
            fast_body if fast else plain_body,
            mesh=mesh,
            in_specs=(P("dp", None, "fsdp"), P("dp", None, "fsdp")),
            out_specs=P("dp", "fsdp"),
            check_vma=False,
        )(partials, scales)

    return run
```

```python
import functools

import jax
import jax.numpy as jnp
import numpy as np
from jax import lax
from jax.experimental import pallas as pl
from jax.experimental.pallas import tpu as pltpu
from jax.sharding import PartitionSpec as P

BLOCK = 128
GRAIN = 16
CHUNKS = (4, 4, 4, 3)
LEAVE = (1, 3)
STEPS = (
    ("sum", 0), ("halve", 0), ("sum", 1), ("sum", 2), ("halve", 1), ("finish", 0), ("sum", 3),
    ("halve", 2), ("halve", 3), ("finish", 1), ("finish", 2), ("finish", 3),
)
AFTER = {
    ("sum", 1): (("sent", 0), ("half", 0)),
    ("sum", 2): (("near", 1), ("last", 1)),
    ("halve", 1): (("keep", 2),),
    ("finish", 0): (("keep", 2),),
    ("sum", 3): (("sent", 1), ("grad", 0)),
    ("halve", 2): (("keep", 3),),
    ("finish", 1): (("sent", 2), ("sent", 3)),
    ("finish", 3): (("across", 1),),
}
ORDER = (0, 2, 1, 3)
PIECE = 256
HALF = PIECE // 2
NEAR = HALF + HALF // 2 + HALF
CROSS = 2 * HALF
PACKED = NEAR + CROSS
F32 = jnp.float32
BF16 = jnp.bfloat16
VMEM = 48 * 1024 * 1024
WHOLE = pl.BlockSpec(memory_space=pltpu.VMEM)
SCALARS = pl.BlockSpec(memory_space=pltpu.SMEM)
ANYWHERE = pl.BlockSpec(memory_space=pl.ANY)


def params():
    return pltpu.CompilerParams(vmem_limit_bytes=VMEM)


def split(value):
    high = value.astype(BF16)
    return high, (value - high.astype(F32)).astype(BF16)


def dot3(a, b, contract):
    dims = (contract, ((), ()))

    def one(u, v):
        return lax.dot_general(u, v, dims, preferred_element_type=F32)

    return one(a[0], b[0]) + (one(a[0], b[1]) + one(a[1], b[0]))


def dot_rows(a, high, low, flipped=False):
    return dot3(split(a), (high, low), ((1,), (int(flipped),)))


def slot_row(at, side, slot, own_rows):
    zed, ex, core = at[0], at[1], at[2]
    z = lax.bitwise_xor(zed, ORDER[slot])
    c = lax.bitwise_xor(core, side % 2)
    x = lax.bitwise_xor(ex, side // 2)
    return ((z * 2 + x) * 2 + c) * own_rows


SLOTS = len(ORDER)
GROUPS = {
    "halves": ((0, 1), (2,), (3,)),
    "pair": ((0, 1), (2, 3)),
    "direct": ((0,), (1,), (2,), (3,)),
}
ROUTES = ("halves", "halves", "halves", "halves")
SPAN = 4
TAIL = 3 * SLOTS * SPAN


def pack_kernel(own_rows, spans, at, values, scales, own, table, *refs):
    outs, gathered = refs[:-1], refs[-1]
    blocks = scales.shape[0]

    def copy(side, start, rows, out):
        for slot in range(SLOTS):
            base = pl.multiple_of(slot_row(at, side, slot, own_rows) + start, GRAIN)
            out[slot * rows : (slot + 1) * rows, :] = values[pl.ds(base, rows), :]

    def gather(side, out):
        for slot in range(SLOTS):
            first = slot_row(at, side, slot, own_rows) // BLOCK
            for n in range(SPAN):
                row = jnp.minimum(first + n, blocks - 1)
                out[slot * SPAN + n : slot * SPAN + n + 1, :] = scales[row]

    def tail(side, out):
        gather(side, gathered)
        left = gathered[...]
        for n in range(3):
            part = left.astype(BF16)
            row = out.shape[0] - TAIL + n * SLOTS * SPAN
            out[row : row + SLOTS * SPAN, :] = part
            left = left - part.astype(F32)

    gather(0, table)
    copy(0, 0, own_rows, own)
    copy(1, 0, own_rows, outs[0])
    tail(1, outs[0])
    for n, (start, rows) in enumerate(spans):
        for side in (2, 3):
            out = outs[2 * n + side - 1]
            copy(side, start, rows, out)
            if n == 0:
                tail(side, out)


def pack(values, scales, at, own_rows, spans):
    width = values.shape[1]
    lengths = [SLOTS * own_rows, SLOTS * own_rows + TAIL]
    for n, (_, rows) in enumerate(spans):
        lengths += [SLOTS * rows + (TAIL if n == 0 else 0)] * 2
    return pl.pallas_call(
        functools.partial(pack_kernel, own_rows, spans),
        in_specs=[SCALARS, WHOLE, WHOLE],
        out_specs=[WHOLE] * (1 + len(lengths)),
        out_shape=[jax.ShapeDtypeStruct((lengths[0], width), BF16)]
        + [jax.ShapeDtypeStruct((SLOTS * SPAN, width), F32)]
        + [jax.ShapeDtypeStruct((rows, width), BF16) for rows in lengths[1:]],
        scratch_shapes=[pltpu.VMEM((SLOTS * SPAN, width), F32)],
        compiler_params=params(),
        name="pack_rows",
    )(at, values, scales)


def dequant_kernel(own_rows, start, rows, groups, at, scales, own, core_raw, *refs):
    heads, raws, refs = refs[:2], refs[2:4], refs[4:]
    outs, packed = refs[-1 - len(groups) : -1], refs[-1]
    size = SLOTS * SPAN
    for n, ref in enumerate((core_raw, *heads)):
        row = ref.shape[0] - TAIL
        parts = [
            ref[row + k * size : row + (k + 1) * size, :].astype(F32) for k in range(3)
        ]
        packed[n * size : (n + 1) * size, :] = parts[0] + parts[1] + parts[2]
    for slot in range(SLOTS):
        base = slot_row(at, 0, slot, own_rows)
        for g in range(rows // GRAIN):
            block = (base + (start + g * GRAIN)) // BLOCK
            span = slot * SPAN + block - base // BLOCK
            here = slice(g * GRAIN, (g + 1) * GRAIN)
            row = slot * own_rows + start + g * GRAIN
            there = slice(row, row + GRAIN)
            row = slot * rows + g * GRAIN
            total = own[there, :].astype(F32) * scales[pl.ds(span, 1), :]
            total += core_raw[there, :].astype(F32) * packed[pl.ds(span, 1), :]
            for n, raw in enumerate(raws):
                part = raw[row : row + GRAIN, :].astype(F32)
                total += part * packed[pl.ds((n + 1) * size + span, 1), :]
            for out, group in zip(outs, groups):
                if slot in group and len(group) > 1:
                    out[group.index(slot), here, :] = total
                elif slot in group:
                    out[here, :] = total


def dequant(
    at, scales, own, core_raw, heads, raws, own_rows, start, rows, groups, after, carry
):
    width = own.shape[1]
    shapes = [
        jax.ShapeDtypeStruct((len(group), rows, width)[len(group) == 1 :], F32)
        for group in groups
    ]
    first, count, made = 8 + len(after), len(carry), len(groups)

    def kernel(*refs):
        kept = refs[:8] + refs[first + count : first + count + made] + refs[-1:]
        dequant_kernel(own_rows, start, rows, groups, *kept)

    outs = pl.pallas_call(
        kernel,
        in_specs=[SCALARS] + [WHOLE] * 7 + [ANYWHERE] * (len(after) + count),
        out_specs=[WHOLE] * made + [ANYWHERE] * count,
        out_shape=shapes + [jax.ShapeDtypeStruct(x.shape, x.dtype) for x in carry],
        scratch_shapes=[pltpu.VMEM((3 * SLOTS * SPAN, width), F32)],
        input_output_aliases={first + n: made + n for n in range(count)},
        compiler_params=params(),
        name="dequant_sum",
    )(at, scales, own, core_raw, *heads, *raws, *after, *carry)
    return outs[:made], outs[made:]


def add(terms, after, swap=False):
    def kernel(*refs):
        total = refs[0][...]
        for ref in refs[1 : len(terms) - swap]:
            total = total + ref[...]
        if swap:
            last = refs[len(terms) - 1]
            refs[-1][0] = total[0] + last[1]
            refs[-1][1] = total[1] + last[0]
        else:
            refs[-1][...] = total

    return pl.pallas_call(
        kernel,
        in_specs=[WHOLE] * len(terms) + [ANYWHERE] * len(after),
        out_specs=WHOLE,
        out_shape=jax.ShapeDtypeStruct(terms[0].shape, F32),
        compiler_params=params(),
        name="add_rows",
    )(*terms, *after)


def put_rows(slabs, high, low, column):
    row = 0
    for slab in slabs:
        here, share = slice(row, row + slab.shape[0]), slab.shape[1]
        high[here, column : column + share], low[here, column : column + share] = split(slab[...])
        row += slab.shape[0]


def put_slots(at, flat, out):
    part = out.shape[1]
    for slot in range(8):
        z = lax.bitwise_xor(at[0], ORDER[slot % 4])
        x = lax.bitwise_xor(at[1], slot // 4)
        out[slot] = flat[pl.ds(pl.multiple_of((z * 2 + x) * part, 8), part), :]


def put_out(at, side, bases, flat, outs, early):
    if bases:
        flat[...] += bases[0][side]
    if early:
        outs[0][side] = flat[...]
    else:
        put_slots(at, flat, outs[side])


def near_kernel(count, based, early, at, *refs):
    slabs, bases, (high, low, flat) = refs[:count], refs[count : count + based], refs[-3:]
    outs = refs[-4:-3] if early else refs[-5:-3]
    put_rows(slabs, high, low, 0)

    def take(start, width):
        lanes = pl.ds(pl.multiple_of(start, HALF), width)
        return high[:, lanes], low[:, lanes]

    contract = ((0,), (0,))
    for side in range(2):
        core = lax.bitwise_xor(at[2], side)
        own = take(core * PIECE, PIECE)
        block = dot3(own, own, contract)
        flat[0:HALF, :] = block[0:HALF, :]
        flat[HALF : HALF + HALF // 2, 0:HALF] = block[HALF : HALF + HALF // 2, HALF:]
        flat[HALF : HALF + HALF // 2, HALF:] = block[HALF + HALF // 2 :, HALF:]
        left = take(core * HALF, HALF)
        flat[NEAR - HALF :, :] = dot3(left, take(PIECE, PIECE), contract)
        put_out(at, side, bases, flat, outs, early)


def cross_kernel(count, based, early, at, *refs):
    slabs, bases = refs[: 2 * count], refs[2 * count : 2 * count + based]
    high, low, flat = refs[-3:]
    outs = refs[-4:-3] if early else refs[-5:-3]
    share = slabs[0].shape[1]
    put_rows(slabs[:count], high, low, 0)
    put_rows(slabs[count:], high, low, share)

    def take(start, width):
        lanes = pl.ds(pl.multiple_of(start, HALF), width)
        return high[:, lanes], low[:, lanes]

    contract = ((0,), (0,))
    half = at[3]
    for side in range(2):
        core = lax.bitwise_xor(at[2], side)
        for k in range(2):
            mine = core * PIECE
            other = share + lax.bitwise_xor(core, k) * PIECE
            left = jnp.where(half == 0, mine, other + HALF)
            right = jnp.where(half == 0, other, mine)
            flat[k * HALF : (k + 1) * HALF, :] = dot3(
                take(left, HALF), take(right, PIECE), contract
            )
        put_out(at, side, bases, flat, outs, early)


def gram_part(kernel, at, slabs, count, packed, name, base=None, early=False, after=()):
    rows = sum(slab.shape[0] for slab in slabs[:count])
    width = slabs[0].shape[1] * (len(slabs) // count)
    bases = [] if base is None else [base]
    if early:
        shapes = [jax.ShapeDtypeStruct((2, packed, PIECE), F32)]
    else:
        shapes = [jax.ShapeDtypeStruct((8, packed // 8, PIECE), F32)] * 2
    return pl.pallas_call(
        functools.partial(kernel, count, len(bases), early),
        in_specs=[SCALARS] + [WHOLE] * len(slabs + bases) + [ANYWHERE] * len(after),
        out_specs=[WHOLE] * len(shapes),
        out_shape=shapes,
        scratch_shapes=[pltpu.VMEM((rows, width), BF16)] * 2 + [pltpu.VMEM((packed, PIECE), F32)],
        compiler_params=params(),
        name=name,
    )(at, *slabs, *bases, *after)


def unpack(at, pieces, places, packed, length):
    zed, ex, core, half = at[0], at[1], at[2], at[3]
    for ref, slots in zip(pieces, places):
        part = ref.shape[1]
        for n, (kz, kx, kc, kf) in enumerate(slots):
            quarter = 2 * lax.bitwise_xor(half, kf) + lax.bitwise_xor(core, kc)
            chip = 2 * lax.bitwise_xor(zed, kz) + lax.bitwise_xor(ex, kx)
            row = pl.multiple_of(quarter * length + chip * part, 8)
            packed[pl.ds(row, part), :] = ref[n]


def start_kernel(places, count, at, *refs):
    pieces, refs = refs[: len(places)], refs[len(places) :]
    owns, acrosses, refs = refs[:count], refs[count : 2 * count], refs[2 * count :]
    high, low, inv_out, own_part, far_part, packed = refs
    half = at[3]
    unpack(at, pieces, places, packed, NEAR)
    trace = jnp.zeros((1, 1), F32)
    rows = lax.broadcasted_iota(jnp.int32, (HALF, HALF), 0)
    columns = lax.broadcasted_iota(jnp.int32, (HALF, HALF), 1)

    def put(f, block, row, column):
        here = (f, slice(row, row + block.shape[0]), slice(column, column + block.shape[1]))
        high[here], low[here] = split(block)

    for q in range(4):
        f, edge = q // 2, q % 2 * PIECE
        base = q * NEAR
        top = packed[base : base + HALF, :]
        bottom = packed[base + HALF : base + HALF + HALF // 2, :]
        bottom = jnp.concatenate([bottom[:, :HALF], bottom[:, HALF:]], 0)
        for block in (top[:, :HALF], bottom):
            trace += jnp.sum(jnp.where(rows == columns, block, 0.0), keepdims=True)
        put(f, top, edge, edge)
        put(f, top[:, HALF:].T, edge + HALF, edge)
        put(f, bottom, edge + HALF, edge + HALF)
        block = packed[base + NEAR - HALF : base + NEAR, :]
        first = q % 2 * HALF
        put(f, block, first, PIECE)
        put(f, block.T, PIECE, first)
    inv = 1.0 / (jnp.sqrt(trace) + 1e-07)
    inv_out[...] = jnp.broadcast_to(inv, inv_out.shape)
    unit = jnp.concatenate([own[...] for own in owns], 0) * inv
    far = jnp.concatenate([across[...] for across in acrosses], 0) * inv
    own_part[...] = dot_rows(unit, high[half], low[half])
    far_part[...] = dot_rows(far, high[1 - half], low[1 - half])


def finish_kernel(scale, places, count, at, *refs):
    pieces, refs = refs[: len(places)], refs[len(places) :]
    owns, acrosses, refs = refs[:count], refs[count : 2 * count], refs[2 * count :]
    near_high, near_low, inv_in, own_part, far_part, out, packed, high, low = refs
    half = at[3]
    unpack(at, pieces, places, packed, CROSS)
    for a in range(2):
        for b in range(2, 4):
            row = ((a ^ b) - 2) * HALF
            for first, owner in ((0, a), (HALF, b)):
                base = owner * CROSS + row
                here = (
                    slice(a * PIECE + first, a * PIECE + first + HALF),
                    slice((b - 2) * PIECE, (b - 1) * PIECE),
                )
                high[here], low[here] = split(packed[base : base + HALF, :])
    inv = inv_in[0:1, 0:1]
    unit = jnp.concatenate([own[...] for own in owns], 0) * inv
    far = jnp.concatenate([across[...] for across in acrosses], 0) * inv

    def last(second_half):
        block = (high[...], low[...])
        first = own_part[...] + dot_rows(far, *block, flipped=not second_half)
        other = far_part[...] + dot_rows(unit, *block, flipped=second_half)
        first, other = first * (inv * inv), other * (inv * inv)
        second = dot_rows(first, near_high[half], near_low[half])
        second += dot_rows(other, *block, flipped=not second_half)
        second = second * (inv * inv)
        result = 3.4445 * unit + (-4.775 * first + 2.0315 * second)
        out[...] = (scale * result).astype(out.dtype)

    pl.when(half == 0)(lambda: last(False))
    pl.when(half == 1)(lambda: last(True))


def update(at, near, cross, owns, acrosses, scale):
    rows = sum(own.shape[0] for own in owns)
    share, count = owns[0].shape[1], len(owns)
    pieces, places = zip(*near)
    square = jax.ShapeDtypeStruct((2, share, share), BF16)
    part = jax.ShapeDtypeStruct((rows, share), F32)
    started = pl.pallas_call(
        functools.partial(start_kernel, places, count),
        in_specs=[SCALARS] + [WHOLE] * (len(pieces) + 2 * count),
        out_specs=[WHOLE] * 5,
        out_shape=[square, square, jax.ShapeDtypeStruct((8, 128), F32), part, part],
        scratch_shapes=[pltpu.VMEM((4 * NEAR, PIECE), F32)],
        compiler_params=params(),
        name="update_start",
    )(at, *pieces, *owns, *acrosses)
    pieces, places = zip(*cross)
    return pl.pallas_call(
        functools.partial(finish_kernel, scale, places, count),
        in_specs=[SCALARS] + [WHOLE] * (len(pieces) + 2 * count + 5),
        out_specs=WHOLE,
        out_shape=jax.ShapeDtypeStruct((rows, share), BF16),
        scratch_shapes=[pltpu.VMEM((4 * CROSS, PIECE), F32)]
        + [pltpu.VMEM((share, share), BF16)] * 2,
        compiler_params=params(),
        name="update_finish",
    )(at, *pieces, *owns, *acrosses, *started)


AXIS_BITS = {"f": 1, "c": 2, "x": 4, "z1": 8, "z2": 16}


def flip(value, *names):
    mask = sum(AXIS_BITS[name] for name in names)
    count = lax.axis_size(("dp", "fsdp"))
    return lax.ppermute(value, ("dp", "fsdp"), [(i, i ^ mask) for i in range(count)])


ZEDS = (("z2",), ("z1",), ("z1", "z2"))
SIDES = (("x",), ("c", "x"))


def fast_body(partials, scales):
    values, scales = partials[0], scales.transpose(1, 0, 2)
    features, share = values.shape
    own_rows = features // lax.axis_size("dp")
    rank = lax.axis_index("dp")
    at = jnp.stack([rank // 4, rank // 2 % 2, rank % 2, lax.axis_index("fsdp")])
    unit = own_rows // sum(CHUNKS)
    spans, start = [], 0
    for size in CHUNKS:
        spans.append((start, size * unit))
        start += size * unit

    own, table, core_raw, *outs = pack(values, scales, at, own_rows, spans)
    core_raw = flip(core_raw, "c")

    def cross(pair):
        return [flip(out, *side) for out, side in zip(pair, SIDES)]

    outs = [outs[2 * n : 2 * n + 2] for n in range(len(spans))]
    raws = [cross(pair) for pair in outs[:2]]
    heads = raws[0]
    owns, acrosses, held = [], [], []
    made = {}

    def there(step, n):
        return [made[name] for name in AFTER.get((step, n), ())]

    def add_partials(n):
        start, rows = spans[n]
        carry = outs[n + 2] if n + 2 < len(spans) else []
        (keep, *go), carry = dequant(
            at, table, own, core_raw, heads, raws[n], own_rows, start, rows,
            GROUPS[ROUTES[n]], there("sum", n), carry,
        )
        if carry:
            raws.append(cross(carry))
        made["keep", n] = keep
        if ROUTES[n] == "direct":
            made["got", n] = [flip(part, *names) for part, names in zip(go, ZEDS)]
        elif ROUTES[n] == "halves":
            made["got", n] = [flip(part, "z1") for part in go]
            made["near", n], made["last", n] = made["got", n]
        else:
            made["got", n] = flip(go[0], "z1")

    def halve(n):
        keep, got = made["keep", n], made["got", n]
        made["sent", n] = add([keep[1], got[1]], there("halve", n))
        made["half", n] = keep[0] + got[0]

    def finish(n):
        if ROUTES[n] == "direct":
            terms = [made["keep", n], *made["got", n]]
        else:
            terms = [made["half", n], flip(made["sent", n], "z2")]
        made["grad", n] = add(terms, there("finish", n))
        held.append(made["grad", n])
        if n in LEAVE:
            group = jnp.concatenate(held) if len(held) > 1 else held[0]
            across = flip(group, "f")
            made["across", n] = across
            owns.append(group)
            acrosses.append(across)
            if len(owns) == 1:
                (made["base", n],) = gram_part(
                    near_kernel, at, owns, 1, NEAR, "gram_near_early", early=True
                )
            held.clear()

    for step, n in STEPS:
        {"sum": add_partials, "halve": halve, "finish": finish}[step](n)

    own, far = gram_part(
        near_kernel, at, owns[1:], 1, NEAR, "gram_near", made["base", 1]
    )
    core = [flip(far[4:], "c"), flip(far[:4], "c")]
    near_sent = add([own[4:], core[0]], [])
    near_x = flip(near_sent, "x")
    (cross_base,) = gram_part(
        cross_kernel, at, owns[:1] + acrosses[:1], 1, CROSS, "gram_cross_early", early=True,
        after=[near_sent],
    )
    cross_own, far = gram_part(
        cross_kernel, at, owns[1:] + acrosses[1:], 1, CROSS, "gram_cross", cross_base,
        after=[near_sent],
    )
    cross_core = [flip(far[4:], "c"), flip(far[:4], "c")]
    cross_x = flip(add([cross_own[4:], cross_core[0]], []), "x")

    near = own[:4] + core[1] + near_x
    near_z1 = flip(near[2:], "z1")
    near = near[:2] + near_z1
    near_z2 = flip(near, "z2")
    near = add([near, near_z2], [], swap=True)
    near_other = flip(near, "z1")

    cross = add([cross_own[:4], cross_core[1], cross_x], [near_z1])
    cross = add([cross[:2], flip(cross[2:], "z1")], [near_z2])
    cross = add([cross, flip(cross, "z2")], [near_other], swap=True)
    cross_other = flip(cross, "z1")

    near = jnp.concatenate([near, near_other])
    near = jnp.concatenate([near, flip(near, "x")])
    cross = jnp.concatenate([cross, cross_other])
    cross = jnp.concatenate([cross, flip(cross, "f")])
    near_slots = [(z, x, 0, 0) for x in range(2) for z in ORDER]
    cross_slots = [(z, 0, 0, f) for f in range(2) for z in ORDER]
    near = [(near, near_slots), (flip(near, "f"), [(z, x, 0, 1) for z, x, _, _ in near_slots])]
    cross = [(cross, cross_slots), (flip(cross, "x"), [(z, 1, 0, f) for z, _, _, f in cross_slots])]
    for group in (near, cross):
        group += [
            (flip(part, "c"), [(z, x, 1, f) for z, x, _, f in slots]) for part, slots in group
        ]
    scale = float(0.25 * np.sqrt(np.float32(features * 2 * share)))
    return update(at, near, cross, owns, acrosses, scale)


def plain_body(partials, scales):
    values, scales = partials[0], scales[0]
    features, share = values.shape
    dp = lax.axis_size("dp")
    rows = values.reshape(scales.shape[0], -1, share).astype(F32) * scales[:, None, :]
    summed = lax.psum_scatter(
        rows.reshape(features, share), "dp", scatter_dimension=0, tiled=True
    )
    slab = lax.all_gather(summed, "fsdp", axis=1, tiled=True)
    width = slab.shape[1]
    highest = functools.partial(
        jnp.dot, precision=lax.Precision.HIGHEST, preferred_element_type=F32
    )
    half = lax.axis_index("fsdp")
    gram = lax.psum(highest(summed.T, slab), "dp")
    gram = lax.all_gather(gram, "fsdp", axis=0, tiled=True)
    inv = 1.0 / (jnp.sqrt(jnp.trace(gram)) + 1e-07)
    scaled = gram * (inv * inv)
    first = highest(slab * inv, scaled)
    mine = lambda value: lax.dynamic_slice_in_dim(value, half * share, share, 1)
    second = highest(first, mine(scaled))
    result = 3.4445 * (summed * inv) + (-4.775 * mine(first) + 2.0315 * second)
    return (0.25 * jnp.sqrt(F32(features * width)) * result).astype(BF16)


def solution(mesh):
    dp, fsdp = mesh.shape["dp"], mesh.shape["fsdp"]

    def run(partials, scales):
        features, width = partials.shape[1:]
        fast = (
            (dp, fsdp) == (16, 2)
            and features % (dp * GRAIN * sum(CHUNKS)) == 0
            and width == 4 * PIECE
        )
        return jax.shard_map(
            fast_body if fast else plain_body,
            mesh=mesh,
            in_specs=(P("dp", None, "fsdp"), P("dp", None, "fsdp")),
            out_specs=P("dp", "fsdp"),
            check_vma=False,
        )(partials, scales)

    return run
```

```python
import functools

import jax
import jax.numpy as jnp
import numpy as np
from jax import lax
from jax.experimental import pallas as pl
from jax.experimental.pallas import tpu as pltpu
from jax.sharding import PartitionSpec as P

BLOCK = 128
GRAIN = 16
CHUNKS = (2, 5, 4, 4)
LEAVE = (1, 3)
STEPS = (
    ("sum", 0), ("halve", 0), ("sum", 1), ("sum", 2), ("halve", 1), ("finish", 0), ("sum", 3),
    ("halve", 2), ("halve", 3), ("finish", 1), ("finish", 2), ("finish", 3),
)
AFTER = {
    ("sum", 1): (("sent", 0), ("half", 0)),
    ("sum", 2): (("near", 1), ("last", 1)),
    ("halve", 1): (("keep", 2),),
    ("finish", 0): (("keep", 2),),
    ("sum", 3): (("sent", 1), ("grad", 0)),
    ("halve", 2): (("keep", 3),),
    ("finish", 1): (("sent", 2), ("sent", 3)),
    ("finish", 3): (("across", 1),),
}
ORDER = (0, 2, 1, 3)
PIECE = 256
HALF = PIECE // 2
NEAR = HALF + HALF // 2 + HALF
CROSS = 2 * HALF
PACKED = NEAR + CROSS
F32 = jnp.float32
BF16 = jnp.bfloat16
VMEM = 48 * 1024 * 1024
WHOLE = pl.BlockSpec(memory_space=pltpu.VMEM)
SCALARS = pl.BlockSpec(memory_space=pltpu.SMEM)
ANYWHERE = pl.BlockSpec(memory_space=pl.ANY)


def params():
    return pltpu.CompilerParams(vmem_limit_bytes=VMEM)


def split(value):
    high = value.astype(BF16)
    return high, (value - high.astype(F32)).astype(BF16)


def dot3(a, b, contract):
    dims = (contract, ((), ()))

    def one(u, v):
        return lax.dot_general(u, v, dims, preferred_element_type=F32)

    return one(a[0], b[0]) + (one(a[0], b[1]) + one(a[1], b[0]))


def dot_rows(a, high, low, flipped=False):
    return dot3(split(a), (high, low), ((1,), (int(flipped),)))


def slot_row(at, side, slot, own_rows):
    zed, ex, core = at[0], at[1], at[2]
    z = lax.bitwise_xor(zed, ORDER[slot])
    c = lax.bitwise_xor(core, side % 2)
    x = lax.bitwise_xor(ex, side // 2)
    return ((z * 2 + x) * 2 + c) * own_rows


SLOTS = len(ORDER)
GROUPS = {
    "halves": ((0, 1), (2,), (3,)),
    "pair": ((0, 1), (2, 3)),
    "direct": ((0,), (1,), (2,), (3,)),
}
ROUTES = ("halves", "halves", "halves", "halves")
SPAN = 4
TAIL = 3 * SLOTS * SPAN


def pack_kernel(own_rows, spans, at, values, scales, own, table, *refs):
    outs, gathered = refs[:-1], refs[-1]
    blocks = scales.shape[0]

    def copy(side, start, rows, out):
        for slot in range(SLOTS):
            base = pl.multiple_of(slot_row(at, side, slot, own_rows) + start, GRAIN)
            out[slot * rows : (slot + 1) * rows, :] = values[pl.ds(base, rows), :]

    def gather(side, out):
        for slot in range(SLOTS):
            first = slot_row(at, side, slot, own_rows) // BLOCK
            for n in range(SPAN):
                row = jnp.minimum(first + n, blocks - 1)
                out[slot * SPAN + n : slot * SPAN + n + 1, :] = scales[row]

    def tail(side, out):
        gather(side, gathered)
        left = gathered[...]
        for n in range(3):
            part = left.astype(BF16)
            row = out.shape[0] - TAIL + n * SLOTS * SPAN
            out[row : row + SLOTS * SPAN, :] = part
            left = left - part.astype(F32)

    gather(0, table)
    copy(0, 0, own_rows, own)
    copy(1, 0, own_rows, outs[0])
    tail(1, outs[0])
    for n, (start, rows) in enumerate(spans):
        for side in (2, 3):
            out = outs[2 * n + side - 1]
            copy(side, start, rows, out)
            if n == 0:
                tail(side, out)


def pack(values, scales, at, own_rows, spans):
    width = values.shape[1]
    lengths = [SLOTS * own_rows, SLOTS * own_rows + TAIL]
    for n, (_, rows) in enumerate(spans):
        lengths += [SLOTS * rows + (TAIL if n == 0 else 0)] * 2
    return pl.pallas_call(
        functools.partial(pack_kernel, own_rows, spans),
        in_specs=[SCALARS, WHOLE, WHOLE],
        out_specs=[WHOLE] * (1 + len(lengths)),
        out_shape=[jax.ShapeDtypeStruct((lengths[0], width), BF16)]
        + [jax.ShapeDtypeStruct((SLOTS * SPAN, width), F32)]
        + [jax.ShapeDtypeStruct((rows, width), BF16) for rows in lengths[1:]],
        scratch_shapes=[pltpu.VMEM((SLOTS * SPAN, width), F32)],
        compiler_params=params(),
        name="pack_rows",
    )(at, values, scales)


def dequant_kernel(own_rows, start, rows, groups, at, scales, own, core_raw, *refs):
    heads, raws, refs = refs[:2], refs[2:4], refs[4:]
    outs, packed = refs[-1 - len(groups) : -1], refs[-1]
    size = SLOTS * SPAN
    for n, ref in enumerate((core_raw, *heads)):
        row = ref.shape[0] - TAIL
        parts = [
            ref[row + k * size : row + (k + 1) * size, :].astype(F32) for k in range(3)
        ]
        packed[n * size : (n + 1) * size, :] = parts[0] + parts[1] + parts[2]
    for slot in range(SLOTS):
        base = slot_row(at, 0, slot, own_rows)
        for g in range(rows // GRAIN):
            block = (base + (start + g * GRAIN)) // BLOCK
            span = slot * SPAN + block - base // BLOCK
            here = slice(g * GRAIN, (g + 1) * GRAIN)
            row = slot * own_rows + start + g * GRAIN
            there = slice(row, row + GRAIN)
            row = slot * rows + g * GRAIN
            total = own[there, :].astype(F32) * scales[pl.ds(span, 1), :]
            total += core_raw[there, :].astype(F32) * packed[pl.ds(span, 1), :]
            for n, raw in enumerate(raws):
                part = raw[row : row + GRAIN, :].astype(F32)
                total += part * packed[pl.ds((n + 1) * size + span, 1), :]
            for out, group in zip(outs, groups):
                if slot in group and len(group) > 1:
                    out[group.index(slot), here, :] = total
                elif slot in group:
                    out[here, :] = total


def dequant(
    at, scales, own, core_raw, heads, raws, own_rows, start, rows, groups, after, carry
):
    width = own.shape[1]
    shapes = [
        jax.ShapeDtypeStruct((len(group), rows, width)[len(group) == 1 :], F32)
        for group in groups
    ]
    first, count, made = 8 + len(after), len(carry), len(groups)

    def kernel(*refs):
        kept = refs[:8] + refs[first + count : first + count + made] + refs[-1:]
        dequant_kernel(own_rows, start, rows, groups, *kept)

    outs = pl.pallas_call(
        kernel,
        in_specs=[SCALARS] + [WHOLE] * 7 + [ANYWHERE] * (len(after) + count),
        out_specs=[WHOLE] * made + [ANYWHERE] * count,
        out_shape=shapes + [jax.ShapeDtypeStruct(x.shape, x.dtype) for x in carry],
        scratch_shapes=[pltpu.VMEM((3 * SLOTS * SPAN, width), F32)],
        input_output_aliases={first + n: made + n for n in range(count)},
        compiler_params=params(),
        name="dequant_sum",
    )(at, scales, own, core_raw, *heads, *raws, *after, *carry)
    return outs[:made], outs[made:]


def add(terms, after, swap=False):
    def kernel(*refs):
        total = refs[0][...]
        for ref in refs[1 : len(terms) - swap]:
            total = total + ref[...]
        if swap:
            last = refs[len(terms) - 1]
            refs[-1][0] = total[0] + last[1]
            refs[-1][1] = total[1] + last[0]
        else:
            refs[-1][...] = total

    return pl.pallas_call(
        kernel,
        in_specs=[WHOLE] * len(terms) + [ANYWHERE] * len(after),
        out_specs=WHOLE,
        out_shape=jax.ShapeDtypeStruct(terms[0].shape, F32),
        compiler_params=params(),
        name="add_rows",
    )(*terms, *after)


def put_rows(slabs, high, low, column):
    row = 0
    for slab in slabs:
        here, share = slice(row, row + slab.shape[0]), slab.shape[1]
        high[here, column : column + share], low[here, column : column + share] = split(slab[...])
        row += slab.shape[0]


def put_slots(at, flat, out):
    part = out.shape[1]
    for slot in range(8):
        z = lax.bitwise_xor(at[0], ORDER[slot % 4])
        x = lax.bitwise_xor(at[1], slot // 4)
        out[slot] = flat[pl.ds(pl.multiple_of((z * 2 + x) * part, 8), part), :]


def put_out(at, side, bases, flat, outs, early):
    if bases:
        flat[...] += bases[0][side]
    if early:
        outs[0][side] = flat[...]
    else:
        put_slots(at, flat, outs[side])


def near_kernel(count, based, early, at, *refs):
    slabs, bases, (high, low, flat) = refs[:count], refs[count : count + based], refs[-3:]
    outs = refs[-4:-3] if early else refs[-5:-3]
    put_rows(slabs, high, low, 0)

    def take(start, width):
        lanes = pl.ds(pl.multiple_of(start, HALF), width)
        return high[:, lanes], low[:, lanes]

    contract = ((0,), (0,))
    for side in range(2):
        core = lax.bitwise_xor(at[2], side)
        own = take(core * PIECE, PIECE)
        block = dot3(own, own, contract)
        flat[0:HALF, :] = block[0:HALF, :]
        flat[HALF : HALF + HALF // 2, 0:HALF] = block[HALF : HALF + HALF // 2, HALF:]
        flat[HALF : HALF + HALF // 2, HALF:] = block[HALF + HALF // 2 :, HALF:]
        left = take(core * HALF, HALF)
        flat[NEAR - HALF :, :] = dot3(left, take(PIECE, PIECE), contract)
        put_out(at, side, bases, flat, outs, early)


def cross_kernel(count, based, early, at, *refs):
    slabs, bases = refs[: 2 * count], refs[2 * count : 2 * count + based]
    high, low, flat = refs[-3:]
    outs = refs[-4:-3] if early else refs[-5:-3]
    share = slabs[0].shape[1]
    put_rows(slabs[:count], high, low, 0)
    put_rows(slabs[count:], high, low, share)

    def take(start, width):
        lanes = pl.ds(pl.multiple_of(start, HALF), width)
        return high[:, lanes], low[:, lanes]

    contract = ((0,), (0,))
    half = at[3]
    for side in range(2):
        core = lax.bitwise_xor(at[2], side)
        for k in range(2):
            mine = core * PIECE
            other = share + lax.bitwise_xor(core, k) * PIECE
            left = jnp.where(half == 0, mine, other + HALF)
            right = jnp.where(half == 0, other, mine)
            flat[k * HALF : (k + 1) * HALF, :] = dot3(
                take(left, HALF), take(right, PIECE), contract
            )
        put_out(at, side, bases, flat, outs, early)


def gram_part(kernel, at, slabs, count, packed, name, base=None, early=False, after=()):
    rows = sum(slab.shape[0] for slab in slabs[:count])
    width = slabs[0].shape[1] * (len(slabs) // count)
    bases = [] if base is None else [base]
    if early:
        shapes = [jax.ShapeDtypeStruct((2, packed, PIECE), F32)]
    else:
        shapes = [jax.ShapeDtypeStruct((8, packed // 8, PIECE), F32)] * 2
    return pl.pallas_call(
        functools.partial(kernel, count, len(bases), early),
        in_specs=[SCALARS] + [WHOLE] * len(slabs + bases) + [ANYWHERE] * len(after),
        out_specs=[WHOLE] * len(shapes),
        out_shape=shapes,
        scratch_shapes=[pltpu.VMEM((rows, width), BF16)] * 2 + [pltpu.VMEM((packed, PIECE), F32)],
        compiler_params=params(),
        name=name,
    )(at, *slabs, *bases, *after)


def unpack(at, pieces, places, packed, length):
    zed, ex, core, half = at[0], at[1], at[2], at[3]
    for ref, slots in zip(pieces, places):
        part = ref.shape[1]
        for n, (kz, kx, kc, kf) in enumerate(slots):
            quarter = 2 * lax.bitwise_xor(half, kf) + lax.bitwise_xor(core, kc)
            chip = 2 * lax.bitwise_xor(zed, kz) + lax.bitwise_xor(ex, kx)
            row = pl.multiple_of(quarter * length + chip * part, 8)
            packed[pl.ds(row, part), :] = ref[n]


def start_kernel(places, count, at, *refs):
    pieces, refs = refs[: len(places)], refs[len(places) :]
    owns, acrosses, refs = refs[:count], refs[count : 2 * count], refs[2 * count :]
    high, low, inv_out, own_part, far_part, packed = refs
    half = at[3]
    unpack(at, pieces, places, packed, NEAR)
    trace = jnp.zeros((1, 1), F32)
    rows = lax.broadcasted_iota(jnp.int32, (HALF, HALF), 0)
    columns = lax.broadcasted_iota(jnp.int32, (HALF, HALF), 1)

    def put(f, block, row, column):
        here = (f, slice(row, row + block.shape[0]), slice(column, column + block.shape[1]))
        high[here], low[here] = split(block)

    for q in range(4):
        f, edge = q // 2, q % 2 * PIECE
        base = q * NEAR
        top = packed[base : base + HALF, :]
        bottom = packed[base + HALF : base + HALF + HALF // 2, :]
        bottom = jnp.concatenate([bottom[:, :HALF], bottom[:, HALF:]], 0)
        for block in (top[:, :HALF], bottom):
            trace += jnp.sum(jnp.where(rows == columns, block, 0.0), keepdims=True)
        put(f, top, edge, edge)
        put(f, top[:, HALF:].T, edge + HALF, edge)
        put(f, bottom, edge + HALF, edge + HALF)
        block = packed[base + NEAR - HALF : base + NEAR, :]
        first = q % 2 * HALF
        put(f, block, first, PIECE)
        put(f, block.T, PIECE, first)
    inv = 1.0 / (jnp.sqrt(trace) + 1e-07)
    inv_out[...] = jnp.broadcast_to(inv, inv_out.shape)
    unit = jnp.concatenate([own[...] for own in owns], 0) * inv
    far = jnp.concatenate([across[...] for across in acrosses], 0) * inv
    own_part[...] = dot_rows(unit, high[half], low[half])
    far_part[...] = dot_rows(far, high[1 - half], low[1 - half])


def finish_kernel(scale, places, count, at, *refs):
    pieces, refs = refs[: len(places)], refs[len(places) :]
    owns, acrosses, refs = refs[:count], refs[count : 2 * count], refs[2 * count :]
    near_high, near_low, inv_in, own_part, far_part, out, packed, high, low = refs
    half = at[3]
    unpack(at, pieces, places, packed, CROSS)
    for a in range(2):
        for b in range(2, 4):
            row = ((a ^ b) - 2) * HALF
            for first, owner in ((0, a), (HALF, b)):
                base = owner * CROSS + row
                here = (
                    slice(a * PIECE + first, a * PIECE + first + HALF),
                    slice((b - 2) * PIECE, (b - 1) * PIECE),
                )
                high[here], low[here] = split(packed[base : base + HALF, :])
    inv = inv_in[0:1, 0:1]
    unit = jnp.concatenate([own[...] for own in owns], 0) * inv
    far = jnp.concatenate([across[...] for across in acrosses], 0) * inv

    def last(second_half):
        block = (high[...], low[...])
        first = own_part[...] + dot_rows(far, *block, flipped=not second_half)
        other = far_part[...] + dot_rows(unit, *block, flipped=second_half)
        first, other = first * (inv * inv), other * (inv * inv)
        second = dot_rows(first, near_high[half], near_low[half])
        second += dot_rows(other, *block, flipped=not second_half)
        second = second * (inv * inv)
        result = 3.4445 * unit + (-4.775 * first + 2.0315 * second)
        out[...] = (scale * result).astype(out.dtype)

    pl.when(half == 0)(lambda: last(False))
    pl.when(half == 1)(lambda: last(True))


def update(at, near, cross, owns, acrosses, scale):
    rows = sum(own.shape[0] for own in owns)
    share, count = owns[0].shape[1], len(owns)
    pieces, places = zip(*near)
    square = jax.ShapeDtypeStruct((2, share, share), BF16)
    part = jax.ShapeDtypeStruct((rows, share), F32)
    started = pl.pallas_call(
        functools.partial(start_kernel, places, count),
        in_specs=[SCALARS] + [WHOLE] * (len(pieces) + 2 * count),
        out_specs=[WHOLE] * 5,
        out_shape=[square, square, jax.ShapeDtypeStruct((8, 128), F32), part, part],
        scratch_shapes=[pltpu.VMEM((4 * NEAR, PIECE), F32)],
        compiler_params=params(),
        name="update_start",
    )(at, *pieces, *owns, *acrosses)
    pieces, places = zip(*cross)
    return pl.pallas_call(
        functools.partial(finish_kernel, scale, places, count),
        in_specs=[SCALARS] + [WHOLE] * (len(pieces) + 2 * count + 5),
        out_specs=WHOLE,
        out_shape=jax.ShapeDtypeStruct((rows, share), BF16),
        scratch_shapes=[pltpu.VMEM((4 * CROSS, PIECE), F32)]
        + [pltpu.VMEM((share, share), BF16)] * 2,
        compiler_params=params(),
        name="update_finish",
    )(at, *pieces, *owns, *acrosses, *started)


AXIS_BITS = {"f": 1, "c": 2, "x": 4, "z1": 8, "z2": 16}


def flip(value, *names):
    mask = sum(AXIS_BITS[name] for name in names)
    count = lax.axis_size(("dp", "fsdp"))
    return lax.ppermute(value, ("dp", "fsdp"), [(i, i ^ mask) for i in range(count)])


ZEDS = (("z2",), ("z1",), ("z1", "z2"))
SIDES = (("x",), ("c", "x"))


def fast_body(partials, scales):
    values, scales = partials[0], scales.transpose(1, 0, 2)
    features, share = values.shape
    own_rows = features // lax.axis_size("dp")
    rank = lax.axis_index("dp")
    at = jnp.stack([rank // 4, rank // 2 % 2, rank % 2, lax.axis_index("fsdp")])
    unit = own_rows // sum(CHUNKS)
    spans, start = [], 0
    for size in CHUNKS:
        spans.append((start, size * unit))
        start += size * unit

    own, table, core_raw, *outs = pack(values, scales, at, own_rows, spans)
    core_raw = flip(core_raw, "c")

    def cross(pair):
        return [flip(out, *side) for out, side in zip(pair, SIDES)]

    outs = [outs[2 * n : 2 * n + 2] for n in range(len(spans))]
    raws = [cross(pair) for pair in outs[:2]]
    heads = raws[0]
    owns, acrosses, held = [], [], []
    made = {}

    def there(step, n):
        return [made[name] for name in AFTER.get((step, n), ())]

    def add_partials(n):
        start, rows = spans[n]
        carry = outs[n + 2] if n + 2 < len(spans) else []
        (keep, *go), carry = dequant(
            at, table, own, core_raw, heads, raws[n], own_rows, start, rows,
            GROUPS[ROUTES[n]], there("sum", n), carry,
        )
        if carry:
            raws.append(cross(carry))
        made["keep", n] = keep
        if ROUTES[n] == "direct":
            made["got", n] = [flip(part, *names) for part, names in zip(go, ZEDS)]
        elif ROUTES[n] == "halves":
            made["got", n] = [flip(part, "z1") for part in go]
            made["near", n], made["last", n] = made["got", n]
        else:
            made["got", n] = flip(go[0], "z1")

    def halve(n):
        keep, got = made["keep", n], made["got", n]
        made["sent", n] = add([keep[1], got[1]], there("halve", n))
        made["half", n] = keep[0] + got[0]

    def finish(n):
        if ROUTES[n] == "direct":
            terms = [made["keep", n], *made["got", n]]
        else:
            terms = [made["half", n], flip(made["sent", n], "z2")]
        made["grad", n] = add(terms, there("finish", n))
        held.append(made["grad", n])
        if n in LEAVE:
            group = jnp.concatenate(held) if len(held) > 1 else held[0]
            across = flip(group, "f")
            made["across", n] = across
            owns.append(group)
            acrosses.append(across)
            if len(owns) == 1:
                (made["base", n],) = gram_part(
                    near_kernel, at, owns, 1, NEAR, "gram_near_early", early=True
                )
            held.clear()

    for step, n in STEPS:
        {"sum": add_partials, "halve": halve, "finish": finish}[step](n)

    own, far = gram_part(
        near_kernel, at, owns[1:], 1, NEAR, "gram_near", made["base", 1]
    )
    core = [flip(far[4:], "c"), flip(far[:4], "c")]
    near_sent = add([own[4:], core[0]], [])
    near_x = flip(near_sent, "x")
    (cross_base,) = gram_part(
        cross_kernel, at, owns[:1] + acrosses[:1], 1, CROSS, "gram_cross_early", early=True,
        after=[near_sent],
    )
    cross_own, far = gram_part(
        cross_kernel, at, owns[1:] + acrosses[1:], 1, CROSS, "gram_cross", cross_base,
        after=[near_sent],
    )
    cross_core = [flip(far[4:], "c"), flip(far[:4], "c")]
    cross_x = flip(add([cross_own[4:], cross_core[0]], []), "x")

    near = own[:4] + core[1] + near_x
    near_z1 = flip(near[2:], "z1")
    near = near[:2] + near_z1
    near_z2 = flip(near, "z2")
    near = add([near, near_z2], [], swap=True)
    near_other = flip(near, "z1")

    cross = add([cross_own[:4], cross_core[1], cross_x], [near_z1])
    cross = add([cross[:2], flip(cross[2:], "z1")], [near_z2])
    cross = add([cross, flip(cross, "z2")], [near_other], swap=True)
    cross_other = flip(cross, "z1")

    near = jnp.concatenate([near, near_other])
    near = jnp.concatenate([near, flip(near, "x")])
    cross = jnp.concatenate([cross, cross_other])
    cross = jnp.concatenate([cross, flip(cross, "f")])
    near_slots = [(z, x, 0, 0) for x in range(2) for z in ORDER]
    cross_slots = [(z, 0, 0, f) for f in range(2) for z in ORDER]
    near = [(near, near_slots), (flip(near, "f"), [(z, x, 0, 1) for z, x, _, _ in near_slots])]
    cross = [(cross, cross_slots), (flip(cross, "x"), [(z, 1, 0, f) for z, _, _, f in cross_slots])]
    for group in (near, cross):
        group += [
            (flip(part, "c"), [(z, x, 1, f) for z, x, _, f in slots]) for part, slots in group
        ]
    scale = float(0.25 * np.sqrt(np.float32(features * 2 * share)))
    return update(at, near, cross, owns, acrosses, scale)


def plain_body(partials, scales):
    values, scales = partials[0], scales[0]
    features, share = values.shape
    dp = lax.axis_size("dp")
    rows = values.reshape(scales.shape[0], -1, share).astype(F32) * scales[:, None, :]
    summed = lax.psum_scatter(
        rows.reshape(features, share), "dp", scatter_dimension=0, tiled=True
    )
    slab = lax.all_gather(summed, "fsdp", axis=1, tiled=True)
    width = slab.shape[1]
    highest = functools.partial(
        jnp.dot, precision=lax.Precision.HIGHEST, preferred_element_type=F32
    )
    half = lax.axis_index("fsdp")
    gram = lax.psum(highest(summed.T, slab), "dp")
    gram = lax.all_gather(gram, "fsdp", axis=0, tiled=True)
    inv = 1.0 / (jnp.sqrt(jnp.trace(gram)) + 1e-07)
    scaled = gram * (inv * inv)
    first = highest(slab * inv, scaled)
    mine = lambda value: lax.dynamic_slice_in_dim(value, half * share, share, 1)
    second = highest(first, mine(scaled))
    result = 3.4445 * (summed * inv) + (-4.775 * mine(first) + 2.0315 * second)
    return (0.25 * jnp.sqrt(F32(features * width)) * result).astype(BF16)


def solution(mesh):
    dp, fsdp = mesh.shape["dp"], mesh.shape["fsdp"]

    def run(partials, scales):
        features, width = partials.shape[1:]
        fast = (
            (dp, fsdp) == (16, 2)
            and features % (dp * GRAIN * sum(CHUNKS)) == 0
            and width == 4 * PIECE
        )
        return jax.shard_map(
            fast_body if fast else plain_body,
            mesh=mesh,
            in_specs=(P("dp", None, "fsdp"), P("dp", None, "fsdp")),
            out_specs=P("dp", "fsdp"),
            check_vma=False,
        )(partials, scales)

    return run
```

```python
import functools

import jax
import jax.numpy as jnp
import numpy as np
from jax import lax
from jax.experimental import pallas as pl
from jax.experimental.pallas import tpu as pltpu
from jax.sharding import PartitionSpec as P

BLOCK = 128
GRAIN = 16
CHUNKS = (2, 5, 5, 3)
LEAVE = (1, 3)
STEPS = (
    ("sum", 0), ("halve", 0), ("sum", 1), ("sum", 2), ("halve", 1), ("finish", 0), ("sum", 3),
    ("halve", 2), ("halve", 3), ("finish", 1), ("finish", 2), ("finish", 3),
)
AFTER = {
    ("sum", 1): (("sent", 0), ("half", 0)),
    ("sum", 2): (("near", 1), ("last", 1)),
    ("halve", 1): (("keep", 2),),
    ("finish", 0): (("keep", 2),),
    ("sum", 3): (("sent", 1), ("grad", 0)),
    ("halve", 2): (("keep", 3),),
    ("finish", 1): (("sent", 2), ("sent", 3)),
    ("finish", 3): (("across", 1),),
}
ORDER = (0, 2, 1, 3)
PIECE = 256
HALF = PIECE // 2
NEAR = HALF + HALF // 2 + HALF
CROSS = 2 * HALF
PACKED = NEAR + CROSS
F32 = jnp.float32
BF16 = jnp.bfloat16
VMEM = 48 * 1024 * 1024
WHOLE = pl.BlockSpec(memory_space=pltpu.VMEM)
SCALARS = pl.BlockSpec(memory_space=pltpu.SMEM)
ANYWHERE = pl.BlockSpec(memory_space=pl.ANY)


def params():
    return pltpu.CompilerParams(vmem_limit_bytes=VMEM)


def split(value):
    high = value.astype(BF16)
    return high, (value - high.astype(F32)).astype(BF16)


def dot3(a, b, contract):
    dims = (contract, ((), ()))

    def one(u, v):
        return lax.dot_general(u, v, dims, preferred_element_type=F32)

    return one(a[0], b[0]) + (one(a[0], b[1]) + one(a[1], b[0]))


def dot_rows(a, high, low, flipped=False):
    return dot3(split(a), (high, low), ((1,), (int(flipped),)))


def slot_row(at, side, slot, own_rows):
    zed, ex, core = at[0], at[1], at[2]
    z = lax.bitwise_xor(zed, ORDER[slot])
    c = lax.bitwise_xor(core, side % 2)
    x = lax.bitwise_xor(ex, side // 2)
    return ((z * 2 + x) * 2 + c) * own_rows


SLOTS = len(ORDER)
GROUPS = {
    "halves": ((0, 1), (2,), (3,)),
    "pair": ((0, 1), (2, 3)),
    "direct": ((0,), (1,), (2,), (3,)),
}
ROUTES = ("halves", "halves", "halves", "halves")
SPAN = 4
TAIL = 3 * SLOTS * SPAN


def pack_kernel(own_rows, spans, at, values, scales, own, table, *refs):
    outs, gathered = refs[:-1], refs[-1]
    blocks = scales.shape[0]

    def copy(side, start, rows, out):
        for slot in range(SLOTS):
            base = pl.multiple_of(slot_row(at, side, slot, own_rows) + start, GRAIN)
            out[slot * rows : (slot + 1) * rows, :] = values[pl.ds(base, rows), :]

    def gather(side, out):
        for slot in range(SLOTS):
            first = slot_row(at, side, slot, own_rows) // BLOCK
            for n in range(SPAN):
                row = jnp.minimum(first + n, blocks - 1)
                out[slot * SPAN + n : slot * SPAN + n + 1, :] = scales[row]

    def tail(side, out):
        gather(side, gathered)
        left = gathered[...]
        for n in range(3):
            part = left.astype(BF16)
            row = out.shape[0] - TAIL + n * SLOTS * SPAN
            out[row : row + SLOTS * SPAN, :] = part
            left = left - part.astype(F32)

    gather(0, table)
    copy(0, 0, own_rows, own)
    copy(1, 0, own_rows, outs[0])
    tail(1, outs[0])
    for n, (start, rows) in enumerate(spans):
        for side in (2, 3):
            out = outs[2 * n + side - 1]
            copy(side, start, rows, out)
            if n == 0:
                tail(side, out)


def pack(values, scales, at, own_rows, spans):
    width = values.shape[1]
    lengths = [SLOTS * own_rows, SLOTS * own_rows + TAIL]
    for n, (_, rows) in enumerate(spans):
        lengths += [SLOTS * rows + (TAIL if n == 0 else 0)] * 2
    return pl.pallas_call(
        functools.partial(pack_kernel, own_rows, spans),
        in_specs=[SCALARS, WHOLE, WHOLE],
        out_specs=[WHOLE] * (1 + len(lengths)),
        out_shape=[jax.ShapeDtypeStruct((lengths[0], width), BF16)]
        + [jax.ShapeDtypeStruct((SLOTS * SPAN, width), F32)]
        + [jax.ShapeDtypeStruct((rows, width), BF16) for rows in lengths[1:]],
        scratch_shapes=[pltpu.VMEM((SLOTS * SPAN, width), F32)],
        compiler_params=params(),
        name="pack_rows",
    )(at, values, scales)


def dequant_kernel(own_rows, start, rows, groups, at, scales, own, core_raw, *refs):
    heads, raws, refs = refs[:2], refs[2:4], refs[4:]
    outs, packed = refs[-1 - len(groups) : -1], refs[-1]
    size = SLOTS * SPAN
    for n, ref in enumerate((core_raw, *heads)):
        row = ref.shape[0] - TAIL
        parts = [
            ref[row + k * size : row + (k + 1) * size, :].astype(F32) for k in range(3)
        ]
        packed[n * size : (n + 1) * size, :] = parts[0] + parts[1] + parts[2]
    for slot in range(SLOTS):
        base = slot_row(at, 0, slot, own_rows)
        for g in range(rows // GRAIN):
            block = (base + (start + g * GRAIN)) // BLOCK
            span = slot * SPAN + block - base // BLOCK
            here = slice(g * GRAIN, (g + 1) * GRAIN)
            row = slot * own_rows + start + g * GRAIN
            there = slice(row, row + GRAIN)
            row = slot * rows + g * GRAIN
            total = own[there, :].astype(F32) * scales[pl.ds(span, 1), :]
            total += core_raw[there, :].astype(F32) * packed[pl.ds(span, 1), :]
            for n, raw in enumerate(raws):
                part = raw[row : row + GRAIN, :].astype(F32)
                total += part * packed[pl.ds((n + 1) * size + span, 1), :]
            for out, group in zip(outs, groups):
                if slot in group and len(group) > 1:
                    out[group.index(slot), here, :] = total
                elif slot in group:
                    out[here, :] = total


def dequant(
    at, scales, own, core_raw, heads, raws, own_rows, start, rows, groups, after, carry
):
    width = own.shape[1]
    shapes = [
        jax.ShapeDtypeStruct((len(group), rows, width)[len(group) == 1 :], F32)
        for group in groups
    ]
    first, count, made = 8 + len(after), len(carry), len(groups)

    def kernel(*refs):
        kept = refs[:8] + refs[first + count : first + count + made] + refs[-1:]
        dequant_kernel(own_rows, start, rows, groups, *kept)

    outs = pl.pallas_call(
        kernel,
        in_specs=[SCALARS] + [WHOLE] * 7 + [ANYWHERE] * (len(after) + count),
        out_specs=[WHOLE] * made + [ANYWHERE] * count,
        out_shape=shapes + [jax.ShapeDtypeStruct(x.shape, x.dtype) for x in carry],
        scratch_shapes=[pltpu.VMEM((3 * SLOTS * SPAN, width), F32)],
        input_output_aliases={first + n: made + n for n in range(count)},
        compiler_params=params(),
        name="dequant_sum",
    )(at, scales, own, core_raw, *heads, *raws, *after, *carry)
    return outs[:made], outs[made:]


def add(terms, after, swap=False):
    def kernel(*refs):
        total = refs[0][...]
        for ref in refs[1 : len(terms) - swap]:
            total = total + ref[...]
        if swap:
            last = refs[len(terms) - 1]
            refs[-1][0] = total[0] + last[1]
            refs[-1][1] = total[1] + last[0]
        else:
            refs[-1][...] = total

    return pl.pallas_call(
        kernel,
        in_specs=[WHOLE] * len(terms) + [ANYWHERE] * len(after),
        out_specs=WHOLE,
        out_shape=jax.ShapeDtypeStruct(terms[0].shape, F32),
        compiler_params=params(),
        name="add_rows",
    )(*terms, *after)


def put_rows(slabs, high, low, column):
    row = 0
    for slab in slabs:
        here, share = slice(row, row + slab.shape[0]), slab.shape[1]
        high[here, column : column + share], low[here, column : column + share] = split(slab[...])
        row += slab.shape[0]


def put_slots(at, flat, out):
    part = out.shape[1]
    for slot in range(8):
        z = lax.bitwise_xor(at[0], ORDER[slot % 4])
        x = lax.bitwise_xor(at[1], slot // 4)
        out[slot] = flat[pl.ds(pl.multiple_of((z * 2 + x) * part, 8), part), :]


def put_out(at, side, bases, flat, outs, early):
    if bases:
        flat[...] += bases[0][side]
    if early:
        outs[0][side] = flat[...]
    else:
        put_slots(at, flat, outs[side])


def near_kernel(count, based, early, at, *refs):
    slabs, bases, (high, low, flat) = refs[:count], refs[count : count + based], refs[-3:]
    outs = refs[-4:-3] if early else refs[-5:-3]
    put_rows(slabs, high, low, 0)

    def take(start, width):
        lanes = pl.ds(pl.multiple_of(start, HALF), width)
        return high[:, lanes], low[:, lanes]

    contract = ((0,), (0,))
    for side in range(2):
        core = lax.bitwise_xor(at[2], side)
        own = take(core * PIECE, PIECE)
        block = dot3(own, own, contract)
        flat[0:HALF, :] = block[0:HALF, :]
        flat[HALF : HALF + HALF // 2, 0:HALF] = block[HALF : HALF + HALF // 2, HALF:]
        flat[HALF : HALF + HALF // 2, HALF:] = block[HALF + HALF // 2 :, HALF:]
        left = take(core * HALF, HALF)
        flat[NEAR - HALF :, :] = dot3(left, take(PIECE, PIECE), contract)
        put_out(at, side, bases, flat, outs, early)


def cross_kernel(count, based, early, at, *refs):
    slabs, bases = refs[: 2 * count], refs[2 * count : 2 * count + based]
    high, low, flat = refs[-3:]
    outs = refs[-4:-3] if early else refs[-5:-3]
    share = slabs[0].shape[1]
    put_rows(slabs[:count], high, low, 0)
    put_rows(slabs[count:], high, low, share)

    def take(start, width):
        lanes = pl.ds(pl.multiple_of(start, HALF), width)
        return high[:, lanes], low[:, lanes]

    contract = ((0,), (0,))
    half = at[3]
    for side in range(2):
        core = lax.bitwise_xor(at[2], side)
        for k in range(2):
            mine = core * PIECE
            other = share + lax.bitwise_xor(core, k) * PIECE
            left = jnp.where(half == 0, mine, other + HALF)
            right = jnp.where(half == 0, other, mine)
            flat[k * HALF : (k + 1) * HALF, :] = dot3(
                take(left, HALF), take(right, PIECE), contract
            )
        put_out(at, side, bases, flat, outs, early)


def gram_part(kernel, at, slabs, count, packed, name, base=None, early=False, after=()):
    rows = sum(slab.shape[0] for slab in slabs[:count])
    width = slabs[0].shape[1] * (len(slabs) // count)
    bases = [] if base is None else [base]
    if early:
        shapes = [jax.ShapeDtypeStruct((2, packed, PIECE), F32)]
    else:
        shapes = [jax.ShapeDtypeStruct((8, packed // 8, PIECE), F32)] * 2
    return pl.pallas_call(
        functools.partial(kernel, count, len(bases), early),
        in_specs=[SCALARS] + [WHOLE] * len(slabs + bases) + [ANYWHERE] * len(after),
        out_specs=[WHOLE] * len(shapes),
        out_shape=shapes,
        scratch_shapes=[pltpu.VMEM((rows, width), BF16)] * 2 + [pltpu.VMEM((packed, PIECE), F32)],
        compiler_params=params(),
        name=name,
    )(at, *slabs, *bases, *after)


def unpack(at, pieces, places, packed, length):
    zed, ex, core, half = at[0], at[1], at[2], at[3]
    for ref, slots in zip(pieces, places):
        part = ref.shape[1]
        for n, (kz, kx, kc, kf) in enumerate(slots):
            quarter = 2 * lax.bitwise_xor(half, kf) + lax.bitwise_xor(core, kc)
            chip = 2 * lax.bitwise_xor(zed, kz) + lax.bitwise_xor(ex, kx)
            row = pl.multiple_of(quarter * length + chip * part, 8)
            packed[pl.ds(row, part), :] = ref[n]


def start_kernel(places, count, at, *refs):
    pieces, refs = refs[: len(places)], refs[len(places) :]
    owns, acrosses, refs = refs[:count], refs[count : 2 * count], refs[2 * count :]
    high, low, inv_out, own_part, far_part, packed = refs
    half = at[3]
    unpack(at, pieces, places, packed, NEAR)
    trace = jnp.zeros((1, 1), F32)
    rows = lax.broadcasted_iota(jnp.int32, (HALF, HALF), 0)
    columns = lax.broadcasted_iota(jnp.int32, (HALF, HALF), 1)

    def put(f, block, row, column):
        here = (f, slice(row, row + block.shape[0]), slice(column, column + block.shape[1]))
        high[here], low[here] = split(block)

    for q in range(4):
        f, edge = q // 2, q % 2 * PIECE
        base = q * NEAR
        top = packed[base : base + HALF, :]
        bottom = packed[base + HALF : base + HALF + HALF // 2, :]
        bottom = jnp.concatenate([bottom[:, :HALF], bottom[:, HALF:]], 0)
        for block in (top[:, :HALF], bottom):
            trace += jnp.sum(jnp.where(rows == columns, block, 0.0), keepdims=True)
        put(f, top, edge, edge)
        put(f, top[:, HALF:].T, edge + HALF, edge)
        put(f, bottom, edge + HALF, edge + HALF)
        block = packed[base + NEAR - HALF : base + NEAR, :]
        first = q % 2 * HALF
        put(f, block, first, PIECE)
        put(f, block.T, PIECE, first)
    inv = 1.0 / (jnp.sqrt(trace) + 1e-07)
    inv_out[...] = jnp.broadcast_to(inv, inv_out.shape)
    unit = jnp.concatenate([own[...] for own in owns], 0) * inv
    far = jnp.concatenate([across[...] for across in acrosses], 0) * inv
    own_part[...] = dot_rows(unit, high[half], low[half])
    far_part[...] = dot_rows(far, high[1 - half], low[1 - half])


def finish_kernel(scale, places, count, at, *refs):
    pieces, refs = refs[: len(places)], refs[len(places) :]
    owns, acrosses, refs = refs[:count], refs[count : 2 * count], refs[2 * count :]
    near_high, near_low, inv_in, own_part, far_part, out, packed, high, low = refs
    half = at[3]
    unpack(at, pieces, places, packed, CROSS)
    for a in range(2):
        for b in range(2, 4):
            row = ((a ^ b) - 2) * HALF
            for first, owner in ((0, a), (HALF, b)):
                base = owner * CROSS + row
                here = (
                    slice(a * PIECE + first, a * PIECE + first + HALF),
                    slice((b - 2) * PIECE, (b - 1) * PIECE),
                )
                high[here], low[here] = split(packed[base : base + HALF, :])
    inv = inv_in[0:1, 0:1]
    unit = jnp.concatenate([own[...] for own in owns], 0) * inv
    far = jnp.concatenate([across[...] for across in acrosses], 0) * inv

    def last(second_half):
        block = (high[...], low[...])
        first = own_part[...] + dot_rows(far, *block, flipped=not second_half)
        other = far_part[...] + dot_rows(unit, *block, flipped=second_half)
        first, other = first * (inv * inv), other * (inv * inv)
        second = dot_rows(first, near_high[half], near_low[half])
        second += dot_rows(other, *block, flipped=not second_half)
        second = second * (inv * inv)
        result = 3.4445 * unit + (-4.775 * first + 2.0315 * second)
        out[...] = (scale * result).astype(out.dtype)

    pl.when(half == 0)(lambda: last(False))
    pl.when(half == 1)(lambda: last(True))


def update(at, near, cross, owns, acrosses, scale):
    rows = sum(own.shape[0] for own in owns)
    share, count = owns[0].shape[1], len(owns)
    pieces, places = zip(*near)
    square = jax.ShapeDtypeStruct((2, share, share), BF16)
    part = jax.ShapeDtypeStruct((rows, share), F32)
    started = pl.pallas_call(
        functools.partial(start_kernel, places, count),
        in_specs=[SCALARS] + [WHOLE] * (len(pieces) + 2 * count),
        out_specs=[WHOLE] * 5,
        out_shape=[square, square, jax.ShapeDtypeStruct((8, 128), F32), part, part],
        scratch_shapes=[pltpu.VMEM((4 * NEAR, PIECE), F32)],
        compiler_params=params(),
        name="update_start",
    )(at, *pieces, *owns, *acrosses)
    pieces, places = zip(*cross)
    return pl.pallas_call(
        functools.partial(finish_kernel, scale, places, count),
        in_specs=[SCALARS] + [WHOLE] * (len(pieces) + 2 * count + 5),
        out_specs=WHOLE,
        out_shape=jax.ShapeDtypeStruct((rows, share), BF16),
        scratch_shapes=[pltpu.VMEM((4 * CROSS, PIECE), F32)]
        + [pltpu.VMEM((share, share), BF16)] * 2,
        compiler_params=params(),
        name="update_finish",
    )(at, *pieces, *owns, *acrosses, *started)


AXIS_BITS = {"f": 1, "c": 2, "x": 4, "z1": 8, "z2": 16}


def flip(value, *names):
    mask = sum(AXIS_BITS[name] for name in names)
    count = lax.axis_size(("dp", "fsdp"))
    return lax.ppermute(value, ("dp", "fsdp"), [(i, i ^ mask) for i in range(count)])


ZEDS = (("z2",), ("z1",), ("z1", "z2"))
SIDES = (("x",), ("c", "x"))


def fast_body(partials, scales):
    values, scales = partials[0], scales.transpose(1, 0, 2)
    features, share = values.shape
    own_rows = features // lax.axis_size("dp")
    rank = lax.axis_index("dp")
    at = jnp.stack([rank // 4, rank // 2 % 2, rank % 2, lax.axis_index("fsdp")])
    unit = own_rows // sum(CHUNKS)
    spans, start = [], 0
    for size in CHUNKS:
        spans.append((start, size * unit))
        start += size * unit

    own, table, core_raw, *outs = pack(values, scales, at, own_rows, spans)
    core_raw = flip(core_raw, "c")

    def cross(pair):
        return [flip(out, *side) for out, side in zip(pair, SIDES)]

    outs = [outs[2 * n : 2 * n + 2] for n in range(len(spans))]
    raws = [cross(pair) for pair in outs[:2]]
    heads = raws[0]
    owns, acrosses, held = [], [], []
    made = {}

    def there(step, n):
        return [made[name] for name in AFTER.get((step, n), ())]

    def add_partials(n):
        start, rows = spans[n]
        carry = outs[n + 2] if n + 2 < len(spans) else []
        (keep, *go), carry = dequant(
            at, table, own, core_raw, heads, raws[n], own_rows, start, rows,
            GROUPS[ROUTES[n]], there("sum", n), carry,
        )
        if carry:
            raws.append(cross(carry))
        made["keep", n] = keep
        if ROUTES[n] == "direct":
            made["got", n] = [flip(part, *names) for part, names in zip(go, ZEDS)]
        elif ROUTES[n] == "halves":
            made["got", n] = [flip(part, "z1") for part in go]
            made["near", n], made["last", n] = made["got", n]
        else:
            made["got", n] = flip(go[0], "z1")

    def halve(n):
        keep, got = made["keep", n], made["got", n]
        made["sent", n] = add([keep[1], got[1]], there("halve", n))
        made["half", n] = keep[0] + got[0]

    def finish(n):
        if ROUTES[n] == "direct":
            terms = [made["keep", n], *made["got", n]]
        else:
            terms = [made["half", n], flip(made["sent", n], "z2")]
        made["grad", n] = add(terms, there("finish", n))
        held.append(made["grad", n])
        if n in LEAVE:
            group = jnp.concatenate(held) if len(held) > 1 else held[0]
            across = flip(group, "f")
            made["across", n] = across
            owns.append(group)
            acrosses.append(across)
            if len(owns) == 1:
                (made["base", n],) = gram_part(
                    near_kernel, at, owns, 1, NEAR, "gram_near_early", early=True
                )
            held.clear()

    for step, n in STEPS:
        {"sum": add_partials, "halve": halve, "finish": finish}[step](n)

    own, far = gram_part(
        near_kernel, at, owns[1:], 1, NEAR, "gram_near", made["base", 1]
    )
    core = [flip(far[4:], "c"), flip(far[:4], "c")]
    near_sent = add([own[4:], core[0]], [])
    near_x = flip(near_sent, "x")
    (cross_base,) = gram_part(
        cross_kernel, at, owns[:1] + acrosses[:1], 1, CROSS, "gram_cross_early", early=True,
        after=[near_sent],
    )
    cross_own, far = gram_part(
        cross_kernel, at, owns[1:] + acrosses[1:], 1, CROSS, "gram_cross", cross_base,
        after=[near_sent],
    )
    cross_core = [flip(far[4:], "c"), flip(far[:4], "c")]
    cross_x = flip(add([cross_own[4:], cross_core[0]], []), "x")

    near = own[:4] + core[1] + near_x
    near_z1 = flip(near[2:], "z1")
    near = near[:2] + near_z1
    near_z2 = flip(near, "z2")
    near = add([near, near_z2], [], swap=True)
    near_other = flip(near, "z1")

    cross = add([cross_own[:4], cross_core[1], cross_x], [near_z1])
    cross = add([cross[:2], flip(cross[2:], "z1")], [near_z2])
    cross = add([cross, flip(cross, "z2")], [near_other], swap=True)
    cross_other = flip(cross, "z1")

    near = jnp.concatenate([near, near_other])
    near = jnp.concatenate([near, flip(near, "x")])
    cross = jnp.concatenate([cross, cross_other])
    cross = jnp.concatenate([cross, flip(cross, "f")])
    near_slots = [(z, x, 0, 0) for x in range(2) for z in ORDER]
    cross_slots = [(z, 0, 0, f) for f in range(2) for z in ORDER]
    near = [(near, near_slots), (flip(near, "f"), [(z, x, 0, 1) for z, x, _, _ in near_slots])]
    cross = [(cross, cross_slots), (flip(cross, "x"), [(z, 1, 0, f) for z, _, _, f in cross_slots])]
    for group in (near, cross):
        group += [
            (flip(part, "c"), [(z, x, 1, f) for z, x, _, f in slots]) for part, slots in group
        ]
    scale = float(0.25 * np.sqrt(np.float32(features * 2 * share)))
    return update(at, near, cross, owns, acrosses, scale)


def plain_body(partials, scales):
    values, scales = partials[0], scales[0]
    features, share = values.shape
    dp = lax.axis_size("dp")
    rows = values.reshape(scales.shape[0], -1, share).astype(F32) * scales[:, None, :]
    summed = lax.psum_scatter(
        rows.reshape(features, share), "dp", scatter_dimension=0, tiled=True
    )
    slab = lax.all_gather(summed, "fsdp", axis=1, tiled=True)
    width = slab.shape[1]
    highest = functools.partial(
        jnp.dot, precision=lax.Precision.HIGHEST, preferred_element_type=F32
    )
    half = lax.axis_index("fsdp")
    gram = lax.psum(highest(summed.T, slab), "dp")
    gram = lax.all_gather(gram, "fsdp", axis=0, tiled=True)
    inv = 1.0 / (jnp.sqrt(jnp.trace(gram)) + 1e-07)
    scaled = gram * (inv * inv)
    first = highest(slab * inv, scaled)
    mine = lambda value: lax.dynamic_slice_in_dim(value, half * share, share, 1)
    second = highest(first, mine(scaled))
    result = 3.4445 * (summed * inv) + (-4.775 * mine(first) + 2.0315 * second)
    return (0.25 * jnp.sqrt(F32(features * width)) * result).astype(BF16)


def solution(mesh):
    dp, fsdp = mesh.shape["dp"], mesh.shape["fsdp"]

    def run(partials, scales):
        features, width = partials.shape[1:]
        fast = (
            (dp, fsdp) == (16, 2)
            and features % (dp * GRAIN * sum(CHUNKS)) == 0
            and width == 4 * PIECE
        )
        return jax.shard_map(
            fast_body if fast else plain_body,
            mesh=mesh,
            in_specs=(P("dp", None, "fsdp"), P("dp", None, "fsdp")),
            out_specs=P("dp", "fsdp"),
            check_vma=False,
        )(partials, scales)

    return run
```

```python
import functools

import jax
import jax.numpy as jnp
import numpy as np
from jax import lax
from jax.experimental import pallas as pl
from jax.experimental.pallas import tpu as pltpu
from jax.sharding import PartitionSpec as P

BLOCK = 128
GRAIN = 16
CHUNKS = (2, 5, 4, 4)
LEAVE = (1, 2, 3)
STEPS = (
    ("sum", 0), ("halve", 0), ("sum", 1), ("sum", 2), ("halve", 1), ("finish", 0), ("sum", 3),
    ("halve", 2), ("halve", 3), ("finish", 1), ("finish", 2), ("finish", 3),
)
AFTER = {
    ("sum", 1): (("sent", 0), ("half", 0)),
    ("sum", 2): (("near", 1), ("last", 1)),
    ("halve", 1): (("keep", 2),),
    ("finish", 0): (("keep", 2),),
    ("sum", 3): (("sent", 1), ("grad", 0)),
    ("halve", 2): (("keep", 3),),
    ("finish", 1): (("sent", 2), ("sent", 3)),
    ("finish", 3): (("across", 1), ("across", 2)),
}
ORDER = (0, 2, 1, 3)
PIECE = 256
HALF = PIECE // 2
NEAR = HALF + HALF // 2 + HALF
CROSS = 2 * HALF
PACKED = NEAR + CROSS
F32 = jnp.float32
BF16 = jnp.bfloat16
VMEM = 48 * 1024 * 1024
WHOLE = pl.BlockSpec(memory_space=pltpu.VMEM)
SCALARS = pl.BlockSpec(memory_space=pltpu.SMEM)
ANYWHERE = pl.BlockSpec(memory_space=pl.ANY)


def params():
    return pltpu.CompilerParams(vmem_limit_bytes=VMEM)


def split(value):
    high = value.astype(BF16)
    return high, (value - high.astype(F32)).astype(BF16)


def dot3(a, b, contract):
    dims = (contract, ((), ()))

    def one(u, v):
        return lax.dot_general(u, v, dims, preferred_element_type=F32)

    return one(a[0], b[0]) + (one(a[0], b[1]) + one(a[1], b[0]))


def dot_rows(a, high, low, flipped=False):
    return dot3(split(a), (high, low), ((1,), (int(flipped),)))


def slot_row(at, side, slot, own_rows):
    zed, ex, core = at[0], at[1], at[2]
    z = lax.bitwise_xor(zed, ORDER[slot])
    c = lax.bitwise_xor(core, side % 2)
    x = lax.bitwise_xor(ex, side // 2)
    return ((z * 2 + x) * 2 + c) * own_rows


SLOTS = len(ORDER)
GROUPS = {
    "halves": ((0, 1), (2,), (3,)),
    "pair": ((0, 1), (2, 3)),
    "direct": ((0,), (1,), (2,), (3,)),
}
ROUTES = ("halves", "halves", "halves", "halves")
SPAN = 4
TAIL = 3 * SLOTS * SPAN


def pack_kernel(own_rows, spans, at, values, scales, own, table, *refs):
    outs, gathered = refs[:-1], refs[-1]
    blocks = scales.shape[0]

    def copy(side, start, rows, out):
        for slot in range(SLOTS):
            base = pl.multiple_of(slot_row(at, side, slot, own_rows) + start, GRAIN)
            out[slot * rows : (slot + 1) * rows, :] = values[pl.ds(base, rows), :]

    def gather(side, out):
        for slot in range(SLOTS):
            first = slot_row(at, side, slot, own_rows) // BLOCK
            for n in range(SPAN):
                row = jnp.minimum(first + n, blocks - 1)
                out[slot * SPAN + n : slot * SPAN + n + 1, :] = scales[row]

    def tail(side, out):
        gather(side, gathered)
        left = gathered[...]
        for n in range(3):
            part = left.astype(BF16)
            row = out.shape[0] - TAIL + n * SLOTS * SPAN
            out[row : row + SLOTS * SPAN, :] = part
            left = left - part.astype(F32)

    gather(0, table)
    copy(0, 0, own_rows, own)
    copy(1, 0, own_rows, outs[0])
    tail(1, outs[0])
    for n, (start, rows) in enumerate(spans):
        for side in (2, 3):
            out = outs[2 * n + side - 1]
            copy(side, start, rows, out)
            if n == 0:
                tail(side, out)


def pack(values, scales, at, own_rows, spans):
    width = values.shape[1]
    lengths = [SLOTS * own_rows, SLOTS * own_rows + TAIL]
    for n, (_, rows) in enumerate(spans):
        lengths += [SLOTS * rows + (TAIL if n == 0 else 0)] * 2
    return pl.pallas_call(
        functools.partial(pack_kernel, own_rows, spans),
        in_specs=[SCALARS, WHOLE, WHOLE],
        out_specs=[WHOLE] * (1 + len(lengths)),
        out_shape=[jax.ShapeDtypeStruct((lengths[0], width), BF16)]
        + [jax.ShapeDtypeStruct((SLOTS * SPAN, width), F32)]
        + [jax.ShapeDtypeStruct((rows, width), BF16) for rows in lengths[1:]],
        scratch_shapes=[pltpu.VMEM((SLOTS * SPAN, width), F32)],
        compiler_params=params(),
        name="pack_rows",
    )(at, values, scales)


def dequant_kernel(own_rows, start, rows, groups, at, scales, own, core_raw, *refs):
    heads, raws, refs = refs[:2], refs[2:4], refs[4:]
    outs, packed = refs[-1 - len(groups) : -1], refs[-1]
    size = SLOTS * SPAN
    for n, ref in enumerate((core_raw, *heads)):
        row = ref.shape[0] - TAIL
        parts = [
            ref[row + k * size : row + (k + 1) * size, :].astype(F32) for k in range(3)
        ]
        packed[n * size : (n + 1) * size, :] = parts[0] + parts[1] + parts[2]
    for slot in range(SLOTS):
        base = slot_row(at, 0, slot, own_rows)
        for g in range(rows // GRAIN):
            block = (base + (start + g * GRAIN)) // BLOCK
            span = slot * SPAN + block - base // BLOCK
            here = slice(g * GRAIN, (g + 1) * GRAIN)
            row = slot * own_rows + start + g * GRAIN
            there = slice(row, row + GRAIN)
            row = slot * rows + g * GRAIN
            total = own[there, :].astype(F32) * scales[pl.ds(span, 1), :]
            total += core_raw[there, :].astype(F32) * packed[pl.ds(span, 1), :]
            for n, raw in enumerate(raws):
                part = raw[row : row + GRAIN, :].astype(F32)
                total += part * packed[pl.ds((n + 1) * size + span, 1), :]
            for out, group in zip(outs, groups):
                if slot in group and len(group) > 1:
                    out[group.index(slot), here, :] = total
                elif slot in group:
                    out[here, :] = total


def dequant(
    at, scales, own, core_raw, heads, raws, own_rows, start, rows, groups, after, carry
):
    width = own.shape[1]
    shapes = [
        jax.ShapeDtypeStruct((len(group), rows, width)[len(group) == 1 :], F32)
        for group in groups
    ]
    first, count, made = 8 + len(after), len(carry), len(groups)

    def kernel(*refs):
        kept = refs[:8] + refs[first + count : first + count + made] + refs[-1:]
        dequant_kernel(own_rows, start, rows, groups, *kept)

    outs = pl.pallas_call(
        kernel,
        in_specs=[SCALARS] + [WHOLE] * 7 + [ANYWHERE] * (len(after) + count),
        out_specs=[WHOLE] * made + [ANYWHERE] * count,
        out_shape=shapes + [jax.ShapeDtypeStruct(x.shape, x.dtype) for x in carry],
        scratch_shapes=[pltpu.VMEM((3 * SLOTS * SPAN, width), F32)],
        input_output_aliases={first + n: made + n for n in range(count)},
        compiler_params=params(),
        name="dequant_sum",
    )(at, scales, own, core_raw, *heads, *raws, *after, *carry)
    return outs[:made], outs[made:]


def add(terms, after, swap=False):
    def kernel(*refs):
        total = refs[0][...]
        for ref in refs[1 : len(terms) - swap]:
            total = total + ref[...]
        if swap:
            last = refs[len(terms) - 1]
            refs[-1][0] = total[0] + last[1]
            refs[-1][1] = total[1] + last[0]
        else:
            refs[-1][...] = total

    return pl.pallas_call(
        kernel,
        in_specs=[WHOLE] * len(terms) + [ANYWHERE] * len(after),
        out_specs=WHOLE,
        out_shape=jax.ShapeDtypeStruct(terms[0].shape, F32),
        compiler_params=params(),
        name="add_rows",
    )(*terms, *after)


def put_rows(slabs, high, low, column):
    row = 0
    for slab in slabs:
        here, share = slice(row, row + slab.shape[0]), slab.shape[1]
        high[here, column : column + share], low[here, column : column + share] = split(slab[...])
        row += slab.shape[0]


def put_slots(at, flat, out):
    part = out.shape[1]
    for slot in range(8):
        z = lax.bitwise_xor(at[0], ORDER[slot % 4])
        x = lax.bitwise_xor(at[1], slot // 4)
        out[slot] = flat[pl.ds(pl.multiple_of((z * 2 + x) * part, 8), part), :]


def put_out(at, side, bases, flat, outs, early):
    if bases:
        flat[...] += bases[0][side]
    if early:
        outs[0][side] = flat[...]
    else:
        put_slots(at, flat, outs[side])


def near_kernel(count, based, early, at, *refs):
    slabs, bases, (high, low, flat) = refs[:count], refs[count : count + based], refs[-3:]
    outs = refs[-4:-3] if early else refs[-5:-3]
    put_rows(slabs, high, low, 0)

    def take(start, width):
        lanes = pl.ds(pl.multiple_of(start, HALF), width)
        return high[:, lanes], low[:, lanes]

    contract = ((0,), (0,))
    for side in range(2):
        core = lax.bitwise_xor(at[2], side)
        own = take(core * PIECE, PIECE)
        block = dot3(own, own, contract)
        flat[0:HALF, :] = block[0:HALF, :]
        flat[HALF : HALF + HALF // 2, 0:HALF] = block[HALF : HALF + HALF // 2, HALF:]
        flat[HALF : HALF + HALF // 2, HALF:] = block[HALF + HALF // 2 :, HALF:]
        left = take(core * HALF, HALF)
        flat[NEAR - HALF :, :] = dot3(left, take(PIECE, PIECE), contract)
        put_out(at, side, bases, flat, outs, early)


def cross_kernel(count, based, early, at, *refs):
    slabs, bases = refs[: 2 * count], refs[2 * count : 2 * count + based]
    high, low, flat = refs[-3:]
    outs = refs[-4:-3] if early else refs[-5:-3]
    share = slabs[0].shape[1]
    put_rows(slabs[:count], high, low, 0)
    put_rows(slabs[count:], high, low, share)

    def take(start, width):
        lanes = pl.ds(pl.multiple_of(start, HALF), width)
        return high[:, lanes], low[:, lanes]

    contract = ((0,), (0,))
    half = at[3]
    for side in range(2):
        core = lax.bitwise_xor(at[2], side)
        for k in range(2):
            mine = core * PIECE
            other = share + lax.bitwise_xor(core, k) * PIECE
            left = jnp.where(half == 0, mine, other + HALF)
            right = jnp.where(half == 0, other, mine)
            flat[k * HALF : (k + 1) * HALF, :] = dot3(
                take(left, HALF), take(right, PIECE), contract
            )
        put_out(at, side, bases, flat, outs, early)


def gram_part(kernel, at, slabs, count, packed, name, base=None, early=False, after=()):
    rows = sum(slab.shape[0] for slab in slabs[:count])
    width = slabs[0].shape[1] * (len(slabs) // count)
    bases = [] if base is None else [base]
    if early:
        shapes = [jax.ShapeDtypeStruct((2, packed, PIECE), F32)]
    else:
        shapes = [jax.ShapeDtypeStruct((8, packed // 8, PIECE), F32)] * 2
    return pl.pallas_call(
        functools.partial(kernel, count, len(bases), early),
        in_specs=[SCALARS] + [WHOLE] * len(slabs + bases) + [ANYWHERE] * len(after),
        out_specs=[WHOLE] * len(shapes),
        out_shape=shapes,
        scratch_shapes=[pltpu.VMEM((rows, width), BF16)] * 2 + [pltpu.VMEM((packed, PIECE), F32)],
        compiler_params=params(),
        name=name,
    )(at, *slabs, *bases, *after)


def unpack(at, pieces, places, packed, length):
    zed, ex, core, half = at[0], at[1], at[2], at[3]
    for ref, slots in zip(pieces, places):
        part = ref.shape[1]
        for n, (kz, kx, kc, kf) in enumerate(slots):
            quarter = 2 * lax.bitwise_xor(half, kf) + lax.bitwise_xor(core, kc)
            chip = 2 * lax.bitwise_xor(zed, kz) + lax.bitwise_xor(ex, kx)
            row = pl.multiple_of(quarter * length + chip * part, 8)
            packed[pl.ds(row, part), :] = ref[n]


def start_kernel(places, count, at, *refs):
    pieces, refs = refs[: len(places)], refs[len(places) :]
    owns, acrosses, refs = refs[:count], refs[count : 2 * count], refs[2 * count :]
    high, low, inv_out, own_part, far_part, packed = refs
    half = at[3]
    unpack(at, pieces, places, packed, NEAR)
    trace = jnp.zeros((1, 1), F32)
    rows = lax.broadcasted_iota(jnp.int32, (HALF, HALF), 0)
    columns = lax.broadcasted_iota(jnp.int32, (HALF, HALF), 1)

    def put(f, block, row, column):
        here = (f, slice(row, row + block.shape[0]), slice(column, column + block.shape[1]))
        high[here], low[here] = split(block)

    for q in range(4):
        f, edge = q // 2, q % 2 * PIECE
        base = q * NEAR
        top = packed[base : base + HALF, :]
        bottom = packed[base + HALF : base + HALF + HALF // 2, :]
        bottom = jnp.concatenate([bottom[:, :HALF], bottom[:, HALF:]], 0)
        for block in (top[:, :HALF], bottom):
            trace += jnp.sum(jnp.where(rows == columns, block, 0.0), keepdims=True)
        put(f, top, edge, edge)
        put(f, top[:, HALF:].T, edge + HALF, edge)
        put(f, bottom, edge + HALF, edge + HALF)
        block = packed[base + NEAR - HALF : base + NEAR, :]
        first = q % 2 * HALF
        put(f, block, first, PIECE)
        put(f, block.T, PIECE, first)
    inv = 1.0 / (jnp.sqrt(trace) + 1e-07)
    inv_out[...] = jnp.broadcast_to(inv, inv_out.shape)
    unit = jnp.concatenate([own[...] for own in owns], 0) * inv
    far = jnp.concatenate([across[...] for across in acrosses], 0) * inv
    own_part[...] = dot_rows(unit, high[half], low[half])
    far_part[...] = dot_rows(far, high[1 - half], low[1 - half])


def finish_kernel(scale, places, count, at, *refs):
    pieces, refs = refs[: len(places)], refs[len(places) :]
    owns, acrosses, refs = refs[:count], refs[count : 2 * count], refs[2 * count :]
    near_high, near_low, inv_in, own_part, far_part, out, packed, high, low = refs
    half = at[3]
    unpack(at, pieces, places, packed, CROSS)
    for a in range(2):
        for b in range(2, 4):
            row = ((a ^ b) - 2) * HALF
            for first, owner in ((0, a), (HALF, b)):
                base = owner * CROSS + row
                here = (
                    slice(a * PIECE + first, a * PIECE + first + HALF),
                    slice((b - 2) * PIECE, (b - 1) * PIECE),
                )
                high[here], low[here] = split(packed[base : base + HALF, :])
    inv = inv_in[0:1, 0:1]
    unit = jnp.concatenate([own[...] for own in owns], 0) * inv
    far = jnp.concatenate([across[...] for across in acrosses], 0) * inv

    def last(second_half):
        block = (high[...], low[...])
        first = own_part[...] + dot_rows(far, *block, flipped=not second_half)
        other = far_part[...] + dot_rows(unit, *block, flipped=second_half)
        first, other = first * (inv * inv), other * (inv * inv)
        second = dot_rows(first, near_high[half], near_low[half])
        second += dot_rows(other, *block, flipped=not second_half)
        second = second * (inv * inv)
        result = 3.4445 * unit + (-4.775 * first + 2.0315 * second)
        out[...] = (scale * result).astype(out.dtype)

    pl.when(half == 0)(lambda: last(False))
    pl.when(half == 1)(lambda: last(True))


def update(at, near, cross, owns, acrosses, scale):
    rows = sum(own.shape[0] for own in owns)
    share, count = owns[0].shape[1], len(owns)
    pieces, places = zip(*near)
    square = jax.ShapeDtypeStruct((2, share, share), BF16)
    part = jax.ShapeDtypeStruct((rows, share), F32)
    started = pl.pallas_call(
        functools.partial(start_kernel, places, count),
        in_specs=[SCALARS] + [WHOLE] * (len(pieces) + 2 * count),
        out_specs=[WHOLE] * 5,
        out_shape=[square, square, jax.ShapeDtypeStruct((8, 128), F32), part, part],
        scratch_shapes=[pltpu.VMEM((4 * NEAR, PIECE), F32)],
        compiler_params=params(),
        name="update_start",
    )(at, *pieces, *owns, *acrosses)
    pieces, places = zip(*cross)
    return pl.pallas_call(
        functools.partial(finish_kernel, scale, places, count),
        in_specs=[SCALARS] + [WHOLE] * (len(pieces) + 2 * count + 5),
        out_specs=WHOLE,
        out_shape=jax.ShapeDtypeStruct((rows, share), BF16),
        scratch_shapes=[pltpu.VMEM((4 * CROSS, PIECE), F32)]
        + [pltpu.VMEM((share, share), BF16)] * 2,
        compiler_params=params(),
        name="update_finish",
    )(at, *pieces, *owns, *acrosses, *started)


AXIS_BITS = {"f": 1, "c": 2, "x": 4, "z1": 8, "z2": 16}


def flip(value, *names):
    mask = sum(AXIS_BITS[name] for name in names)
    count = lax.axis_size(("dp", "fsdp"))
    return lax.ppermute(value, ("dp", "fsdp"), [(i, i ^ mask) for i in range(count)])


ZEDS = (("z2",), ("z1",), ("z1", "z2"))
SIDES = (("x",), ("c", "x"))


def fast_body(partials, scales):
    values, scales = partials[0], scales.transpose(1, 0, 2)
    features, share = values.shape
    own_rows = features // lax.axis_size("dp")
    rank = lax.axis_index("dp")
    at = jnp.stack([rank // 4, rank // 2 % 2, rank % 2, lax.axis_index("fsdp")])
    unit = own_rows // sum(CHUNKS)
    spans, start = [], 0
    for size in CHUNKS:
        spans.append((start, size * unit))
        start += size * unit

    own, table, core_raw, *outs = pack(values, scales, at, own_rows, spans)
    core_raw = flip(core_raw, "c")

    def cross(pair):
        return [flip(out, *side) for out, side in zip(pair, SIDES)]

    outs = [outs[2 * n : 2 * n + 2] for n in range(len(spans))]
    raws = [cross(pair) for pair in outs[:2]]
    heads = raws[0]
    owns, acrosses, held = [], [], []
    made = {}

    def there(step, n):
        return [made[name] for name in AFTER.get((step, n), ())]

    def add_partials(n):
        start, rows = spans[n]
        carry = outs[n + 2] if n + 2 < len(spans) else []
        (keep, *go), carry = dequant(
            at, table, own, core_raw, heads, raws[n], own_rows, start, rows,
            GROUPS[ROUTES[n]], there("sum", n), carry,
        )
        if carry:
            raws.append(cross(carry))
        made["keep", n] = keep
        if ROUTES[n] == "direct":
            made["got", n] = [flip(part, *names) for part, names in zip(go, ZEDS)]
        elif ROUTES[n] == "halves":
            made["got", n] = [flip(part, "z1") for part in go]
            made["near", n], made["last", n] = made["got", n]
        else:
            made["got", n] = flip(go[0], "z1")

    def halve(n):
        keep, got = made["keep", n], made["got", n]
        made["sent", n] = add([keep[1], got[1]], there("halve", n))
        made["half", n] = keep[0] + got[0]

    def finish(n):
        if ROUTES[n] == "direct":
            terms = [made["keep", n], *made["got", n]]
        else:
            terms = [made["half", n], flip(made["sent", n], "z2")]
        made["grad", n] = add(terms, there("finish", n))
        held.append(made["grad", n])
        if n in LEAVE:
            group = jnp.concatenate(held) if len(held) > 1 else held[0]
            across = flip(group, "f")
            made["across", n] = across
            owns.append(group)
            acrosses.append(across)
            held.clear()

    for step, n in STEPS:
        {"sum": add_partials, "halve": halve, "finish": finish}[step](n)

    count = len(owns)
    (near_base,) = gram_part(
        near_kernel, at, owns[:1], 1, NEAR, "gram_near_early", early=True, after=[made["grad", 2]]
    )
    own, far = gram_part(
        near_kernel, at, owns[1:], count - 1, NEAR, "gram_near", near_base
    )
    core = [flip(far[4:], "c"), flip(far[:4], "c")]
    near_sent = add([own[4:], core[0]], [])
    near_x = flip(near_sent, "x")
    (cross_base,) = gram_part(
        cross_kernel, at, owns[:1] + acrosses[:1], 1, CROSS, "gram_cross_early", early=True,
        after=[near_sent],
    )
    cross_own, far = gram_part(
        cross_kernel, at, owns[1:] + acrosses[1:], count - 1, CROSS, "gram_cross", cross_base,
        after=[near_sent],
    )
    cross_core = [flip(far[4:], "c"), flip(far[:4], "c")]
    cross_x = flip(add([cross_own[4:], cross_core[0]], []), "x")

    near = own[:4] + core[1] + near_x
    near_z1 = flip(near[2:], "z1")
    near = near[:2] + near_z1
    near_z2 = flip(near, "z2")
    near = add([near, near_z2], [], swap=True)
    near_other = flip(near, "z1")

    cross = add([cross_own[:4], cross_core[1], cross_x], [near_z1])
    cross = add([cross[:2], flip(cross[2:], "z1")], [near_z2])
    cross = add([cross, flip(cross, "z2")], [near_other], swap=True)
    cross_other = flip(cross, "z1")

    near = jnp.concatenate([near, near_other])
    near = jnp.concatenate([near, flip(near, "x")])
    cross = jnp.concatenate([cross, cross_other])
    cross = jnp.concatenate([cross, flip(cross, "f")])
    near_slots = [(z, x, 0, 0) for x in range(2) for z in ORDER]
    cross_slots = [(z, 0, 0, f) for f in range(2) for z in ORDER]
    near = [(near, near_slots), (flip(near, "f"), [(z, x, 0, 1) for z, x, _, _ in near_slots])]
    cross = [(cross, cross_slots), (flip(cross, "x"), [(z, 1, 0, f) for z, _, _, f in cross_slots])]
    for group in (near, cross):
        group += [
            (flip(part, "c"), [(z, x, 1, f) for z, x, _, f in slots]) for part, slots in group
        ]
    scale = float(0.25 * np.sqrt(np.float32(features * 2 * share)))
    return update(at, near, cross, owns, acrosses, scale)


def plain_body(partials, scales):
    values, scales = partials[0], scales[0]
    features, share = values.shape
    dp = lax.axis_size("dp")
    rows = values.reshape(scales.shape[0], -1, share).astype(F32) * scales[:, None, :]
    summed = lax.psum_scatter(
        rows.reshape(features, share), "dp", scatter_dimension=0, tiled=True
    )
    slab = lax.all_gather(summed, "fsdp", axis=1, tiled=True)
    width = slab.shape[1]
    highest = functools.partial(
        jnp.dot, precision=lax.Precision.HIGHEST, preferred_element_type=F32
    )
    half = lax.axis_index("fsdp")
    gram = lax.psum(highest(summed.T, slab), "dp")
    gram = lax.all_gather(gram, "fsdp", axis=0, tiled=True)
    inv = 1.0 / (jnp.sqrt(jnp.trace(gram)) + 1e-07)
    scaled = gram * (inv * inv)
    first = highest(slab * inv, scaled)
    mine = lambda value: lax.dynamic_slice_in_dim(value, half * share, share, 1)
    second = highest(first, mine(scaled))
    result = 3.4445 * (summed * inv) + (-4.775 * mine(first) + 2.0315 * second)
    return (0.25 * jnp.sqrt(F32(features * width)) * result).astype(BF16)


def solution(mesh):
    dp, fsdp = mesh.shape["dp"], mesh.shape["fsdp"]

    def run(partials, scales):
        features, width = partials.shape[1:]
        fast = (
            (dp, fsdp) == (16, 2)
            and features % (dp * GRAIN * sum(CHUNKS)) == 0
            and width == 4 * PIECE
        )
        return jax.shard_map(
            fast_body if fast else plain_body,
            mesh=mesh,
            in_specs=(P("dp", None, "fsdp"), P("dp", None, "fsdp")),
            out_specs=P("dp", "fsdp"),
            check_vma=False,
        )(partials, scales)

    return run
```

```python
import functools

import jax
import jax.numpy as jnp
import numpy as np
from jax import lax
from jax.experimental import pallas as pl
from jax.experimental.pallas import tpu as pltpu
from jax.sharding import PartitionSpec as P

BLOCK = 128
GRAIN = 16
CHUNKS = (3, 5, 4, 3)
LEAVE = (1, 3)
STEPS = (
    ("sum", 0), ("halve", 0), ("sum", 1), ("sum", 2), ("halve", 1), ("finish", 0), ("sum", 3),
    ("halve", 2), ("halve", 3), ("finish", 1), ("finish", 2), ("finish", 3),
)
AFTER = {
    ("sum", 1): (("sent", 0), ("half", 0)),
    ("sum", 2): (("near", 1), ("last", 1)),
    ("halve", 1): (("keep", 2),),
    ("finish", 0): (("keep", 2),),
    ("sum", 3): (("sent", 1), ("grad", 0)),
    ("halve", 2): (("keep", 3),),
    ("finish", 1): (("sent", 2), ("sent", 3)),
    ("finish", 3): (("across", 1),),
}
ORDER = (0, 2, 1, 3)
PIECE = 256
HALF = PIECE // 2
NEAR = HALF + HALF // 2 + HALF
CROSS = 2 * HALF
PACKED = NEAR + CROSS
F32 = jnp.float32
BF16 = jnp.bfloat16
VMEM = 48 * 1024 * 1024
WHOLE = pl.BlockSpec(memory_space=pltpu.VMEM)
SCALARS = pl.BlockSpec(memory_space=pltpu.SMEM)
ANYWHERE = pl.BlockSpec(memory_space=pl.ANY)


def params():
    return pltpu.CompilerParams(vmem_limit_bytes=VMEM)


def split(value):
    high = value.astype(BF16)
    return high, (value - high.astype(F32)).astype(BF16)


def dot3(a, b, contract):
    dims = (contract, ((), ()))

    def one(u, v):
        return lax.dot_general(u, v, dims, preferred_element_type=F32)

    return one(a[0], b[0]) + (one(a[0], b[1]) + one(a[1], b[0]))


def dot_rows(a, high, low, flipped=False):
    return dot3(split(a), (high, low), ((1,), (int(flipped),)))


def slot_row(at, side, slot, own_rows):
    zed, ex, core = at[0], at[1], at[2]
    z = lax.bitwise_xor(zed, ORDER[slot])
    c = lax.bitwise_xor(core, side % 2)
    x = lax.bitwise_xor(ex, side // 2)
    return ((z * 2 + x) * 2 + c) * own_rows


SLOTS = len(ORDER)
GROUPS = {
    "halves": ((0, 1), (2,), (3,)),
    "pair": ((0, 1), (2, 3)),
    "direct": ((0,), (1,), (2,), (3,)),
}
ROUTES = ("halves", "halves", "halves", "halves")
SPAN = 4
TAIL = 3 * SLOTS * SPAN


def pack_kernel(own_rows, spans, at, values, scales, own, table, *refs):
    outs, gathered = refs[:-1], refs[-1]
    blocks = scales.shape[0]

    def copy(side, start, rows, out):
        for slot in range(SLOTS):
            base = pl.multiple_of(slot_row(at, side, slot, own_rows) + start, GRAIN)
            out[slot * rows : (slot + 1) * rows, :] = values[pl.ds(base, rows), :]

    def gather(side, out):
        for slot in range(SLOTS):
            first = slot_row(at, side, slot, own_rows) // BLOCK
            for n in range(SPAN):
                row = jnp.minimum(first + n, blocks - 1)
                out[slot * SPAN + n : slot * SPAN + n + 1, :] = scales[row]

    def tail(side, out):
        gather(side, gathered)
        left = gathered[...]
        for n in range(3):
            part = left.astype(BF16)
            row = out.shape[0] - TAIL + n * SLOTS * SPAN
            out[row : row + SLOTS * SPAN, :] = part
            left = left - part.astype(F32)

    gather(0, table)
    copy(0, 0, own_rows, own)
    copy(1, 0, own_rows, outs[0])
    tail(1, outs[0])
    for n, (start, rows) in enumerate(spans):
        for side in (2, 3):
            out = outs[2 * n + side - 1]
            copy(side, start, rows, out)
            if n == 0:
                tail(side, out)


def pack(values, scales, at, own_rows, spans):
    width = values.shape[1]
    lengths = [SLOTS * own_rows, SLOTS * own_rows + TAIL]
    for n, (_, rows) in enumerate(spans):
        lengths += [SLOTS * rows + (TAIL if n == 0 else 0)] * 2
    return pl.pallas_call(
        functools.partial(pack_kernel, own_rows, spans),
        in_specs=[SCALARS, WHOLE, WHOLE],
        out_specs=[WHOLE] * (1 + len(lengths)),
        out_shape=[jax.ShapeDtypeStruct((lengths[0], width), BF16)]
        + [jax.ShapeDtypeStruct((SLOTS * SPAN, width), F32)]
        + [jax.ShapeDtypeStruct((rows, width), BF16) for rows in lengths[1:]],
        scratch_shapes=[pltpu.VMEM((SLOTS * SPAN, width), F32)],
        compiler_params=params(),
        name="pack_rows",
    )(at, values, scales)


def dequant_kernel(own_rows, start, rows, groups, at, scales, own, core_raw, *refs):
    heads, raws, refs = refs[:2], refs[2:4], refs[4:]
    outs, packed = refs[-1 - len(groups) : -1], refs[-1]
    size = SLOTS * SPAN
    for n, ref in enumerate((core_raw, *heads)):
        row = ref.shape[0] - TAIL
        parts = [
            ref[row + k * size : row + (k + 1) * size, :].astype(F32) for k in range(3)
        ]
        packed[n * size : (n + 1) * size, :] = parts[0] + parts[1] + parts[2]
    for slot in range(SLOTS):
        base = slot_row(at, 0, slot, own_rows)
        for g in range(rows // GRAIN):
            block = (base + (start + g * GRAIN)) // BLOCK
            span = slot * SPAN + block - base // BLOCK
            here = slice(g * GRAIN, (g + 1) * GRAIN)
            row = slot * own_rows + start + g * GRAIN
            there = slice(row, row + GRAIN)
            row = slot * rows + g * GRAIN
            total = own[there, :].astype(F32) * scales[pl.ds(span, 1), :]
            total += core_raw[there, :].astype(F32) * packed[pl.ds(span, 1), :]
            for n, raw in enumerate(raws):
                part = raw[row : row + GRAIN, :].astype(F32)
                total += part * packed[pl.ds((n + 1) * size + span, 1), :]
            for out, group in zip(outs, groups):
                if slot in group and len(group) > 1:
                    out[group.index(slot), here, :] = total
                elif slot in group:
                    out[here, :] = total


def dequant(
    at, scales, own, core_raw, heads, raws, own_rows, start, rows, groups, after, carry
):
    width = own.shape[1]
    shapes = [
        jax.ShapeDtypeStruct((len(group), rows, width)[len(group) == 1 :], F32)
        for group in groups
    ]
    first, count, made = 8 + len(after), len(carry), len(groups)

    def kernel(*refs):
        kept = refs[:8] + refs[first + count : first + count + made] + refs[-1:]
        dequant_kernel(own_rows, start, rows, groups, *kept)

    outs = pl.pallas_call(
        kernel,
        in_specs=[SCALARS] + [WHOLE] * 7 + [ANYWHERE] * (len(after) + count),
        out_specs=[WHOLE] * made + [ANYWHERE] * count,
        out_shape=shapes + [jax.ShapeDtypeStruct(x.shape, x.dtype) for x in carry],
        scratch_shapes=[pltpu.VMEM((3 * SLOTS * SPAN, width), F32)],
        input_output_aliases={first + n: made + n for n in range(count)},
        compiler_params=params(),
        name="dequant_sum",
    )(at, scales, own, core_raw, *heads, *raws, *after, *carry)
    return outs[:made], outs[made:]


def add(terms, after, swap=False):
    def kernel(*refs):
        total = refs[0][...]
        for ref in refs[1 : len(terms) - swap]:
            total = total + ref[...]
        if swap:
            last = refs[len(terms) - 1]
            refs[-1][0] = total[0] + last[1]
            refs[-1][1] = total[1] + last[0]
        else:
            refs[-1][...] = total

    return pl.pallas_call(
        kernel,
        in_specs=[WHOLE] * len(terms) + [ANYWHERE] * len(after),
        out_specs=WHOLE,
        out_shape=jax.ShapeDtypeStruct(terms[0].shape, F32),
        compiler_params=params(),
        name="add_rows",
    )(*terms, *after)


def put_rows(slabs, high, low, column):
    row = 0
    for slab in slabs:
        here, share = slice(row, row + slab.shape[0]), slab.shape[1]
        high[here, column : column + share], low[here, column : column + share] = split(slab[...])
        row += slab.shape[0]


def put_slots(at, flat, out):
    part = out.shape[1]
    for slot in range(8):
        z = lax.bitwise_xor(at[0], ORDER[slot % 4])
        x = lax.bitwise_xor(at[1], slot // 4)
        out[slot] = flat[pl.ds(pl.multiple_of((z * 2 + x) * part, 8), part), :]


def put_out(at, side, bases, flat, outs, early):
    if bases:
        flat[...] += bases[0][side]
    if early:
        outs[0][side] = flat[...]
    else:
        put_slots(at, flat, outs[side])


def near_kernel(count, based, early, at, *refs):
    slabs, bases, (high, low, flat) = refs[:count], refs[count : count + based], refs[-3:]
    outs = refs[-4:-3] if early else refs[-5:-3]
    put_rows(slabs, high, low, 0)

    def take(start, width):
        lanes = pl.ds(pl.multiple_of(start, HALF), width)
        return high[:, lanes], low[:, lanes]

    contract = ((0,), (0,))
    for side in range(2):
        core = lax.bitwise_xor(at[2], side)
        own = take(core * PIECE, PIECE)
        block = dot3(own, own, contract)
        flat[0:HALF, :] = block[0:HALF, :]
        flat[HALF : HALF + HALF // 2, 0:HALF] = block[HALF : HALF + HALF // 2, HALF:]
        flat[HALF : HALF + HALF // 2, HALF:] = block[HALF + HALF // 2 :, HALF:]
        left = take(core * HALF, HALF)
        flat[NEAR - HALF :, :] = dot3(left, take(PIECE, PIECE), contract)
        put_out(at, side, bases, flat, outs, early)


def cross_kernel(count, based, early, at, *refs):
    slabs, bases = refs[: 2 * count], refs[2 * count : 2 * count + based]
    high, low, flat = refs[-3:]
    outs = refs[-4:-3] if early else refs[-5:-3]
    share = slabs[0].shape[1]
    put_rows(slabs[:count], high, low, 0)
    put_rows(slabs[count:], high, low, share)

    def take(start, width):
        lanes = pl.ds(pl.multiple_of(start, HALF), width)
        return high[:, lanes], low[:, lanes]

    contract = ((0,), (0,))
    half = at[3]
    for side in range(2):
        core = lax.bitwise_xor(at[2], side)
        for k in range(2):
            mine = core * PIECE
            other = share + lax.bitwise_xor(core, k) * PIECE
            left = jnp.where(half == 0, mine, other + HALF)
            right = jnp.where(half == 0, other, mine)
            flat[k * HALF : (k + 1) * HALF, :] = dot3(
                take(left, HALF), take(right, PIECE), contract
            )
        put_out(at, side, bases, flat, outs, early)


def gram_part(kernel, at, slabs, count, packed, name, base=None, early=False, after=()):
    rows = sum(slab.shape[0] for slab in slabs[:count])
    width = slabs[0].shape[1] * (len(slabs) // count)
    bases = [] if base is None else [base]
    if early:
        shapes = [jax.ShapeDtypeStruct((2, packed, PIECE), F32)]
    else:
        shapes = [jax.ShapeDtypeStruct((8, packed // 8, PIECE), F32)] * 2
    return pl.pallas_call(
        functools.partial(kernel, count, len(bases), early),
        in_specs=[SCALARS] + [WHOLE] * len(slabs + bases) + [ANYWHERE] * len(after),
        out_specs=[WHOLE] * len(shapes),
        out_shape=shapes,
        scratch_shapes=[pltpu.VMEM((rows, width), BF16)] * 2 + [pltpu.VMEM((packed, PIECE), F32)],
        compiler_params=params(),
        name=name,
    )(at, *slabs, *bases, *after)


def unpack(at, pieces, places, packed, length):
    zed, ex, core, half = at[0], at[1], at[2], at[3]
    for ref, slots in zip(pieces, places):
        part = ref.shape[1]
        for n, (kz, kx, kc, kf) in enumerate(slots):
            quarter = 2 * lax.bitwise_xor(half, kf) + lax.bitwise_xor(core, kc)
            chip = 2 * lax.bitwise_xor(zed, kz) + lax.bitwise_xor(ex, kx)
            row = pl.multiple_of(quarter * length + chip * part, 8)
            packed[pl.ds(row, part), :] = ref[n]


def start_kernel(places, count, at, *refs):
    pieces, refs = refs[: len(places)], refs[len(places) :]
    owns, acrosses, refs = refs[:count], refs[count : 2 * count], refs[2 * count :]
    high, low, inv_out, own_part, far_part, packed = refs
    half = at[3]
    unpack(at, pieces, places, packed, NEAR)
    trace = jnp.zeros((1, 1), F32)
    rows = lax.broadcasted_iota(jnp.int32, (HALF, HALF), 0)
    columns = lax.broadcasted_iota(jnp.int32, (HALF, HALF), 1)

    def put(f, block, row, column):
        here = (f, slice(row, row + block.shape[0]), slice(column, column + block.shape[1]))
        high[here], low[here] = split(block)

    for q in range(4):
        f, edge = q // 2, q % 2 * PIECE
        base = q * NEAR
        top = packed[base : base + HALF, :]
        bottom = packed[base + HALF : base + HALF + HALF // 2, :]
        bottom = jnp.concatenate([bottom[:, :HALF], bottom[:, HALF:]], 0)
        for block in (top[:, :HALF], bottom):
            trace += jnp.sum(jnp.where(rows == columns, block, 0.0), keepdims=True)
        put(f, top, edge, edge)
        put(f, top[:, HALF:].T, edge + HALF, edge)
        put(f, bottom, edge + HALF, edge + HALF)
        block = packed[base + NEAR - HALF : base + NEAR, :]
        first = q % 2 * HALF
        put(f, block, first, PIECE)
        put(f, block.T, PIECE, first)
    inv = 1.0 / (jnp.sqrt(trace) + 1e-07)
    inv_out[...] = jnp.broadcast_to(inv, inv_out.shape)
    unit = jnp.concatenate([own[...] for own in owns], 0) * inv
    far = jnp.concatenate([across[...] for across in acrosses], 0) * inv
    own_part[...] = dot_rows(unit, high[half], low[half])
    far_part[...] = dot_rows(far, high[1 - half], low[1 - half])


def finish_kernel(scale, places, count, at, *refs):
    pieces, refs = refs[: len(places)], refs[len(places) :]
    owns, acrosses, refs = refs[:count], refs[count : 2 * count], refs[2 * count :]
    near_high, near_low, inv_in, own_part, far_part, out, packed, high, low = refs
    half = at[3]
    unpack(at, pieces, places, packed, CROSS)
    for a in range(2):
        for b in range(2, 4):
            row = ((a ^ b) - 2) * HALF
            for first, owner in ((0, a), (HALF, b)):
                base = owner * CROSS + row
                here = (
                    slice(a * PIECE + first, a * PIECE + first + HALF),
                    slice((b - 2) * PIECE, (b - 1) * PIECE),
                )
                high[here], low[here] = split(packed[base : base + HALF, :])
    inv = inv_in[0:1, 0:1]
    unit = jnp.concatenate([own[...] for own in owns], 0) * inv
    far = jnp.concatenate([across[...] for across in acrosses], 0) * inv

    def last(second_half):
        block = (high[...], low[...])
        first = own_part[...] + dot_rows(far, *block, flipped=not second_half)
        other = far_part[...] + dot_rows(unit, *block, flipped=second_half)
        first, other = first * (inv * inv), other * (inv * inv)
        second = dot_rows(first, near_high[half], near_low[half])
        second += dot_rows(other, *block, flipped=not second_half)
        second = second * (inv * inv)
        result = 3.4445 * unit + (-4.775 * first + 2.0315 * second)
        out[...] = (scale * result).astype(out.dtype)

    pl.when(half == 0)(lambda: last(False))
    pl.when(half == 1)(lambda: last(True))


def update(at, near, cross, owns, acrosses, scale):
    rows = sum(own.shape[0] for own in owns)
    share, count = owns[0].shape[1], len(owns)
    pieces, places = zip(*near)
    square = jax.ShapeDtypeStruct((2, share, share), BF16)
    part = jax.ShapeDtypeStruct((rows, share), F32)
    started = pl.pallas_call(
        functools.partial(start_kernel, places, count),
        in_specs=[SCALARS] + [WHOLE] * (len(pieces) + 2 * count),
        out_specs=[WHOLE] * 5,
        out_shape=[square, square, jax.ShapeDtypeStruct((8, 128), F32), part, part],
        scratch_shapes=[pltpu.VMEM((4 * NEAR, PIECE), F32)],
        compiler_params=params(),
        name="update_start",
    )(at, *pieces, *owns, *acrosses)
    pieces, places = zip(*cross)
    return pl.pallas_call(
        functools.partial(finish_kernel, scale, places, count),
        in_specs=[SCALARS] + [WHOLE] * (len(pieces) + 2 * count + 5),
        out_specs=WHOLE,
        out_shape=jax.ShapeDtypeStruct((rows, share), BF16),
        scratch_shapes=[pltpu.VMEM((4 * CROSS, PIECE), F32)]
        + [pltpu.VMEM((share, share), BF16)] * 2,
        compiler_params=params(),
        name="update_finish",
    )(at, *pieces, *owns, *acrosses, *started)


AXIS_BITS = {"f": 1, "c": 2, "x": 4, "z1": 8, "z2": 16}


def flip(value, *names):
    mask = sum(AXIS_BITS[name] for name in names)
    count = lax.axis_size(("dp", "fsdp"))
    return lax.ppermute(value, ("dp", "fsdp"), [(i, i ^ mask) for i in range(count)])


ZEDS = (("z2",), ("z1",), ("z1", "z2"))
SIDES = (("x",), ("c", "x"))


def fast_body(partials, scales):
    values, scales = partials[0], scales.transpose(1, 0, 2)
    features, share = values.shape
    own_rows = features // lax.axis_size("dp")
    rank = lax.axis_index("dp")
    at = jnp.stack([rank // 4, rank // 2 % 2, rank % 2, lax.axis_index("fsdp")])
    unit = own_rows // sum(CHUNKS)
    spans, start = [], 0
    for size in CHUNKS:
        spans.append((start, size * unit))
        start += size * unit

    own, table, core_raw, *outs = pack(values, scales, at, own_rows, spans)
    core_raw = flip(core_raw, "c")

    def cross(pair):
        return [flip(out, *side) for out, side in zip(pair, SIDES)]

    outs = [outs[2 * n : 2 * n + 2] for n in range(len(spans))]
    raws = [cross(pair) for pair in outs[:2]]
    heads = raws[0]
    owns, acrosses, held = [], [], []
    made = {}

    def there(step, n):
        return [made[name] for name in AFTER.get((step, n), ())]

    def add_partials(n):
        start, rows = spans[n]
        carry = outs[n + 2] if n + 2 < len(spans) else []
        (keep, *go), carry = dequant(
            at, table, own, core_raw, heads, raws[n], own_rows, start, rows,
            GROUPS[ROUTES[n]], there("sum", n), carry,
        )
        if carry:
            raws.append(cross(carry))
        made["keep", n] = keep
        if ROUTES[n] == "direct":
            made["got", n] = [flip(part, *names) for part, names in zip(go, ZEDS)]
        elif ROUTES[n] == "halves":
            made["got", n] = [flip(part, "z1") for part in go]
            made["near", n], made["last", n] = made["got", n]
        else:
            made["got", n] = flip(go[0], "z1")

    def halve(n):
        keep, got = made["keep", n], made["got", n]
        made["sent", n] = add([keep[1], got[1]], there("halve", n))
        made["half", n] = keep[0] + got[0]

    def finish(n):
        if ROUTES[n] == "direct":
            terms = [made["keep", n], *made["got", n]]
        else:
            terms = [made["half", n], flip(made["sent", n], "z2")]
        made["grad", n] = add(terms, there("finish", n))
        held.append(made["grad", n])
        if n in LEAVE:
            group = jnp.concatenate(held) if len(held) > 1 else held[0]
            across = flip(group, "f")
            made["across", n] = across
            owns.append(group)
            acrosses.append(across)
            if len(owns) == 1:
                (made["base", n],) = gram_part(
                    near_kernel, at, owns, 1, NEAR, "gram_near_early", early=True
                )
            held.clear()

    for step, n in STEPS:
        {"sum": add_partials, "halve": halve, "finish": finish}[step](n)

    own, far = gram_part(
        near_kernel, at, owns[1:], 1, NEAR, "gram_near", made["base", 1]
    )
    core = [flip(far[4:], "c"), flip(far[:4], "c")]
    near_sent = add([own[4:], core[0]], [])
    near_x = flip(near_sent, "x")
    (cross_base,) = gram_part(
        cross_kernel, at, owns[:1] + acrosses[:1], 1, CROSS, "gram_cross_early", early=True,
        after=[near_sent],
    )
    cross_own, far = gram_part(
        cross_kernel, at, owns[1:] + acrosses[1:], 1, CROSS, "gram_cross", cross_base,
        after=[near_sent],
    )
    cross_core = [flip(far[4:], "c"), flip(far[:4], "c")]
    cross_sent = add([cross_own[4:], cross_core[0]], [])
    cross_x = flip(cross_sent, "x")

    near = add([own[:4], core[1], near_x], [cross_sent])
    near_z1 = flip(near[2:], "z1")
    near = near[:2] + near_z1
    near_z2 = flip(near, "z2")
    near = add([near, near_z2], [], swap=True)
    near_other = flip(near, "z1")

    cross = add([cross_own[:4], cross_core[1], cross_x], [near_z1])
    cross = add([cross[:2], flip(cross[2:], "z1")], [near_z2])
    cross = add([cross, flip(cross, "z2")], [near_other], swap=True)
    cross_other = flip(cross, "z1")

    near = jnp.concatenate([near, near_other])
    near = jnp.concatenate([near, flip(near, "x")])
    cross = jnp.concatenate([cross, cross_other])
    cross = jnp.concatenate([cross, flip(cross, "f")])
    near_slots = [(z, x, 0, 0) for x in range(2) for z in ORDER]
    cross_slots = [(z, 0, 0, f) for f in range(2) for z in ORDER]
    near = [(near, near_slots), (flip(near, "f"), [(z, x, 0, 1) for z, x, _, _ in near_slots])]
    cross = [(cross, cross_slots), (flip(cross, "x"), [(z, 1, 0, f) for z, _, _, f in cross_slots])]
    for group in (near, cross):
        group += [
            (flip(part, "c"), [(z, x, 1, f) for z, x, _, f in slots]) for part, slots in group
        ]
    scale = float(0.25 * np.sqrt(np.float32(features * 2 * share)))
    return update(at, near, cross, owns, acrosses, scale)


def plain_body(partials, scales):
    values, scales = partials[0], scales[0]
    features, share = values.shape
    dp = lax.axis_size("dp")
    rows = values.reshape(scales.shape[0], -1, share).astype(F32) * scales[:, None, :]
    summed = lax.psum_scatter(
        rows.reshape(features, share), "dp", scatter_dimension=0, tiled=True
    )
    slab = lax.all_gather(summed, "fsdp", axis=1, tiled=True)
    width = slab.shape[1]
    highest = functools.partial(
        jnp.dot, precision=lax.Precision.HIGHEST, preferred_element_type=F32
    )
    half = lax.axis_index("fsdp")
    gram = lax.psum(highest(summed.T, slab), "dp")
    gram = lax.all_gather(gram, "fsdp", axis=0, tiled=True)
    inv = 1.0 / (jnp.sqrt(jnp.trace(gram)) + 1e-07)
    scaled = gram * (inv * inv)
    first = highest(slab * inv, scaled)
    mine = lambda value: lax.dynamic_slice_in_dim(value, half * share, share, 1)
    second = highest(first, mine(scaled))
    result = 3.4445 * (summed * inv) + (-4.775 * mine(first) + 2.0315 * second)
    return (0.25 * jnp.sqrt(F32(features * width)) * result).astype(BF16)


def solution(mesh):
    dp, fsdp = mesh.shape["dp"], mesh.shape["fsdp"]

    def run(partials, scales):
        features, width = partials.shape[1:]
        fast = (
            (dp, fsdp) == (16, 2)
            and features % (dp * GRAIN * sum(CHUNKS)) == 0
            and width == 4 * PIECE
        )
        return jax.shard_map(
            fast_body if fast else plain_body,
            mesh=mesh,
            in_specs=(P("dp", None, "fsdp"), P("dp", None, "fsdp")),
            out_specs=P("dp", "fsdp"),
            check_vma=False,
        )(partials, scales)

    return run
```
